32 devices in a mesh: dp: 8 (over y, x, core), mp: 4 (over z).
Axes of the slice: x: 2, y: 2, z: 4, core: 2. Of those that a mesh axis runs over, the one named last changes fastest.
Arguments:
- inputs: bfloat16 [8192, 2048], P('dp', 'mp'), may hold values from -6 to 6
- lengths: int32 [8, 4], P('dp'), may hold values from 0 to 1024, as said below
- cotangent: bfloat16 [8192, 2048], P('dp', 'mp'), may hold values from -6 to 6
- gains: float32 [2, 2048], replicated, may hold values from 0.4 to 1.6
- rnn_params: float32 [8, 2560], P(None, 'mp'), may hold values from -3 to 9
- rnn_in: bfloat16 [2048, 2560], P('dp', 'mp'), may hold values from -0.125 to 0.125
- branch_gate: bfloat16 [2048, 2560], P('dp', 'mp'), may hold values from -0.125 to 0.125
- recur_gate: bfloat16 [160, 2560], P('dp', 'mp'), may hold values from -0.5 to 0.5
- input_gate: bfloat16 [160, 2560], P('dp', 'mp'), may hold values from -0.5 to 0.5
- mlp_gate: bfloat16 [2048, 6144], P('dp', 'mp'), may hold values from -0.125 to 0.125
- mlp_up: bfloat16 [2048, 6144], P('dp', 'mp'), may hold values from -0.125 to 0.125
- rnn_out: bfloat16 [2560, 2048], P('mp', 'dp'), may hold values from -0.25 to 0.25
- mlp_down: bfloat16 [6144, 2048], P('mp', 'dp'), may hold values from -0.15625 to 0.15625
Outputs:
- output: bfloat16 [8192, 2048], P('dp', 'mp')
- input_grad: bfloat16 [8192, 2048], P('dp', 'mp')
- grad_gains: float32 [2, 2048], replicated
- grad_rnn_params: float32 [8, 2560], P(None, 'mp')
- grad_rnn_in: float32 [2048, 2560], P('dp', 'mp')
- grad_branch_gate: float32 [2048, 2560], P('dp', 'mp')
- grad_recur_gate: float32 [160, 2560], P('dp', 'mp')
- grad_input_gate: float32 [160, 2560], P('dp', 'mp')
- grad_mlp_gate: float32 [2048, 6144], P('dp', 'mp')
- grad_mlp_up: float32 [2048, 6144], P('dp', 'mp')
- grad_rnn_out: float32 [2560, 2048], P('mp', 'dp')
- grad_mlp_down: float32 [6144, 2048], P('mp', 'dp')
The draws below stay inside these ranges and needn't reach their ends.
Inputs may be any that keep to these rules, and one draw needn't show every extreme that they name: In each bucket the lengths sum to at most 1024 and fill it from its start; slots may be empty; in every draw some bucket holds one sequence of 1024 tokens.
All inputs are finite; a program needn't handle non-finite values.
Results may differ from the reference program's by a relative error of at most 0.018.
Values may be sent and summed in bfloat16 or wider, within the bound.
A program may use at most 256 MiB of HBM per device.

```python
import jax
import jax.numpy as jnp
from jax import lax

D = 2048
BLOCK_W = 160
R = 2560
FF = 6144
CONV = 4
SLOTS = 4
TOK_DEV = 1024
BUCKETS = 8
TOKENS = 8192


def draw_lengths(key, part):
    key = jax.random.fold_in(key, 11)
    first, second, third = jax.random.split(key, 3)
    used = jax.random.randint(first, (BUCKETS,), TOK_DEV // 2, TOK_DEV + 1)
    cuts = jnp.sort(jax.random.randint(second, (BUCKETS, SLOTS - 1), 0, TOK_DEV + 1), axis=1)
    cuts = jnp.minimum(cuts, used[:, None])
    edges = jnp.concatenate([jnp.zeros((BUCKETS, 1), jnp.int32), cuts.astype(jnp.int32), used[:, None].astype(jnp.int32)], axis=1)
    spans = edges[:, 1:] - edges[:, :-1]
    chosen = jax.random.randint(third, (), 0, BUCKETS)
    single = jnp.zeros((SLOTS,), jnp.int32).at[0].set(TOK_DEV)
    rows = jnp.arange(BUCKETS, dtype=jnp.int32)[:, None]
    return jnp.where(rows == chosen, single[None, :], spans).astype(jnp.int32)


def draw_rnn_params(key, part):
    key = jax.random.fold_in(key, 23)
    first, second, third = jax.random.split(key, 3)
    taps = 0.5 * jnp.clip(jax.random.normal(first, (CONV, R), jnp.float32), -3.0, 3.0)
    biases = jnp.clip(jax.random.normal(second, (3, R), jnp.float32), -3.0, 3.0)
    biases = biases * jnp.array([0.3, 1.0, 1.0], jnp.float32)[:, None]
    decay = jax.random.uniform(third, (1, R), jnp.float32, 4.0, 9.0)
    return jnp.concatenate([taps, biases, decay], axis=0).astype(jnp.float32)


def levels(stream_key, extent, cuts, smallest, high):
    def one(position, parts):
        steps = jax.random.uniform(jax.random.fold_in(jax.random.fold_in(stream_key, 6), position), (parts,), jnp.float32, smallest / len(cuts), high / len(cuts))
        return jnp.repeat(jnp.exp(steps), extent[position] // parts).reshape((-1,) + (1,) * (len(extent) - position - 1))

    loudness = one(*cuts[0])
    for cut in cuts[1:]:
        loudness = loudness * one(*cut)
    return loudness


def centred(stream_key, shape, scale, limit, shards=(), kind=jnp.bfloat16):
    values = scale * jax.random.normal(stream_key, shape, jnp.float32)
    if shards:
        values = values * levels(stream_key, shape, shards, -0.22, 0.18)
    return jnp.clip(values, -limit, limit).astype(kind)


def setup_inputs(seed: int = 0) -> dict:
    key_list = jax.random.split(jax.random.key(seed), 14)
    inputs = centred(key_list[0], (TOKENS, D), 1.0, 6.0, ((0, 8), (1, 4)))
    lengths = draw_lengths(jax.random.fold_in(key_list[13], 71), 0)
    cotangent = centred(key_list[2], (TOKENS, D), 1.0, 6.0, ((0, 8), (1, 4)))
    gains = jnp.clip(1.0 + 0.12 * jax.random.normal(key_list[3], (2, D), jnp.float32), 0.4, 1.6)
    rnn_params = draw_rnn_params(jax.random.fold_in(key_list[13], 71), 0)
    rnn_in = centred(key_list[5], (D, R), D ** -0.5, 0.125, ((0, 8), (1, 4)))
    branch_gate = centred(key_list[6], (D, R), D ** -0.5, 0.125, ((0, 8), (1, 4)))
    recur_gate = centred(key_list[7], (BLOCK_W, R), BLOCK_W ** -0.5, 0.5, ((0, 8), (1, 4)))
    input_gate = centred(key_list[8], (BLOCK_W, R), BLOCK_W ** -0.5, 0.5, ((0, 8), (1, 4)))
    mlp_gate = centred(key_list[9], (D, FF), D ** -0.5, 0.125, ((0, 8), (1, 4)))
    mlp_up = centred(key_list[10], (D, FF), D ** -0.5, 0.125, ((0, 8), (1, 4)))
    rnn_out = centred(key_list[11], (R, D), (R // 4) ** -0.5, 0.25, ((0, 4), (1, 8)))
    mlp_down = centred(key_list[12], (FF, D), (FF // 4) ** -0.5, 0.15625, ((0, 4), (1, 8)))
    return dict(inputs=inputs, lengths=lengths, cotangent=cotangent, gains=gains, rnn_params=rnn_params, rnn_in=rnn_in, branch_gate=branch_gate, recur_gate=recur_gate, input_gate=input_gate, mlp_gate=mlp_gate, mlp_up=mlp_up, rnn_out=rnn_out, mlp_down=mlp_down)


EPS = 1e-06
DECAY_SCALE = 8.0
ROOT_FLOOR = 0.0001

@jax.custom_vjp
def low(v):
    return lax.optimization_barrier(v.astype(jnp.bfloat16)).astype(jnp.float32)

@jax.custom_vjp
def low_back(v):
    return v

def low_keep(v):
    return (low(v), None)

def low_pass(kept, grad):
    return (grad,)

def back_keep(v):
    return (v, None)

def back_low(kept, grad):
    return (low(grad),)
low.defvjp(low_keep, low_pass)
low_back.defvjp(back_keep, back_low)

def gelu_tanh(values):
    return jax.nn.gelu(values, approximate=True)

def rms_norm(values, gain):
    return values * lax.rsqrt(lax.optimization_barrier(jnp.mean(values * values, axis=-1, keepdims=True)) + EPS) * gain

def matmul_high(left, right):
    return jnp.dot(left, right, precision=lax.Precision.HIGHEST)

def segment_info(row_lengths, count):
    ends = jnp.cumsum(row_lengths.astype(jnp.int32)).astype(jnp.int32)
    places = jnp.arange(count, dtype=jnp.int32)
    segment = lax.optimization_barrier(jnp.sum((places[:, None] >= ends[None, :]).astype(jnp.int32), axis=1)).astype(jnp.int32)
    before = jnp.concatenate([jnp.full((1,), -1, jnp.int32), segment[:-1]])
    fresh = segment != before
    live = segment < row_lengths.shape[0]
    return (segment, fresh, live)

def shift_down(values, steps, fill):
    head = jnp.full((steps,) + values.shape[1:], fill, values.dtype)
    return jnp.concatenate([head, values[:-steps]], axis=0)

def rnn_core(branch_in, recur_w, input_w, params, segment, fresh):
    taps = params.shape[0] - 4
    conv = params[0] * branch_in
    for step in range(1, taps):
        same = (shift_down(segment, step, -1) == segment)[:, None]
        conv = conv + params[step] * jnp.where(same, shift_down(branch_in, step, 0.0), 0.0)
    conv = conv + params[taps]
    rows, width = conv.shape
    span = recur_w.shape[0]
    grouped = conv.reshape(rows, width // span, span)
    rec = jnp.einsum('tbk,kbj->tbj', grouped, recur_w.reshape(span, width // span, span), precision=lax.Precision.HIGHEST).reshape(rows, width)
    inp = jnp.einsum('tbk,kbj->tbj', grouped, input_w.reshape(span, width // span, span), precision=lax.Precision.HIGHEST).reshape(rows, width)
    gate_r = jax.nn.sigmoid(rec + params[taps + 1])
    gate_i = jax.nn.sigmoid(inp + params[taps + 2])
    log_a = -DECAY_SCALE * gate_r * jax.nn.softplus(-params[taps + 3])
    starts = fresh[:, None]
    decay = jnp.where(starts, 0.0, jnp.exp(log_a))
    scale = jnp.where(starts, 1.0, jnp.sqrt(jnp.maximum(-jnp.expm1(2.0 * log_a), ROOT_FLOOR)))
    drive = scale * gate_i * conv

    def combine(earlier, later):
        return (earlier[0] * later[0], later[0] * earlier[1] + later[1])
    unused, state = lax.associative_scan(combine, (decay, drive), axis=0)
    return state

def forward(weights, values, segment, fresh):
    gains, params, rnn_in, branch_gate, recur_gate, input_gate, mlp_gate, mlp_up, rnn_out, mlp_down = weights
    normed = low(rms_norm(values, gains[0]))
    branch_in = low_back(matmul_high(normed, rnn_in))
    branch_pre = low_back(matmul_high(normed, branch_gate))
    state = rnn_core(branch_in, recur_gate, input_gate, params, segment, fresh)
    mixed = low(state * gelu_tanh(branch_pre))
    middle = values + low_back(matmul_high(mixed, rnn_out))
    normed2 = low(rms_norm(middle, gains[1]))
    gate_pre = low_back(matmul_high(normed2, mlp_gate))
    up_pre = low_back(matmul_high(normed2, mlp_up))
    hidden = low(gelu_tanh(gate_pre) * up_pre)
    return middle + low_back(matmul_high(hidden, mlp_down))

def reference(inputs, lengths, cotangent, gains, rnn_params, rnn_in, branch_gate, recur_gate, input_gate, mlp_gate, mlp_up, rnn_out, mlp_down):
    weights = tuple((value.astype(jnp.float32) for value in (gains, rnn_params, rnn_in, branch_gate, recur_gate, input_gate, mlp_gate, mlp_up, rnn_out, mlp_down)))
    bucket_in = inputs.astype(jnp.float32).reshape(BUCKETS, TOK_DEV, D)
    bucket_cot = cotangent.astype(jnp.float32).reshape(BUCKETS, TOK_DEV, D)

    def bucket(totals, item):
        rows_in, row_lengths, rows_cot = item
        segment, fresh, live = segment_info(row_lengths, TOK_DEV)

        def layer(params, values):
            return forward(params, values, segment, fresh)
        result, pullback = jax.vjp(layer, weights, rows_in)
        grad_params, grad_rows = pullback(rows_cot * live[:, None].astype(jnp.float32))
        totals = jax.tree.map(lambda left, right: left + right, totals, grad_params)
        return (totals, (result.astype(jnp.bfloat16), grad_rows.astype(jnp.bfloat16)))
    zeros = jax.tree.map(jnp.zeros_like, weights)
    grads, outputs = lax.scan(bucket, zeros, (bucket_in, lengths, bucket_cot))
    output = outputs[0].reshape(TOKENS, D)
    input_grad = outputs[1].reshape(TOKENS, D)
    return (output, input_grad, grads[0], grads[1], grads[2], grads[3], grads[4], grads[5], grads[6], grads[7], grads[8], grads[9])
```

```python
import functools

import jax
import jax.numpy as jnp
from jax import lax
from jax.experimental import pallas as pl
from jax.experimental.pallas import tpu as pltpu
from jax.sharding import PartitionSpec as P

EPS = 1e-06
DECAY_SCALE = 8.0
ROOT_FLOOR = 0.0001
TAPS = 4
LANES = 8
CHUNKS = 2
TILE = 32
F32 = jnp.float32
BF16 = jnp.bfloat16
VMEM_BYTES = 56 * 1024 * 1024


def matmul(left, right):
    return jnp.dot(left, right, preferred_element_type=F32)


def inner_rows(left, right):
    return lax.dot_general(left, right, (((0,), (0,)), ((), ())), preferred_element_type=F32)


def inner_cols(left, right):
    return lax.dot_general(left, right, (((1,), (1,)), ((), ())), preferred_element_type=F32)


def gelu_and_slope(values):
    outer = 0.7978845608028654
    inner = 0.044715
    square = values * values
    bent = jnp.tanh(outer * values * (1.0 + inner * square))
    half = 0.5 * (1.0 + bent)
    slope = half + 0.5 * values * (1.0 - bent * bent) * outer * (1.0 + 3.0 * inner * square)
    return values * half, slope


def gelu(values):
    outer = 0.7978845608028654
    inner = 0.044715
    bent = jnp.tanh(outer * values * (1.0 + inner * values * values))
    return values * (0.5 * (1.0 + bent))


def one_less_exp(values):
    near = -values * (1.0 + 0.5 * values * (1.0 + (values / 3.0) * (1.0 + 0.25 * values)))
    return jnp.where(values > -0.02, near, 1.0 - jnp.exp(values))


def after(value, *earlier):
    return lax.optimization_barrier((value,) + earlier)[0]


def line_gather(mine, axis, size):
    place = lax.axis_index(axis)
    width = mine.shape[1]
    right, left = mine, mine
    rights, lefts = {}, {}
    for step in range(1, size):
        right = lax.ppermute(right, axis, [(i, i + 1) for i in range(step - 1, size - 1)])
        left = lax.ppermute(left, axis, [(i + 1, i) for i in range(size - step)])
        rights[step], lefts[step] = right, left
    whole = jnp.zeros((mine.shape[0], size * width), mine.dtype)
    for step in range(size):
        block = mine if step == 0 else lefts[step] + rights[size - step]
        spot = lax.rem(place + step, size) * width
        whole = lax.dynamic_update_slice_in_dim(whole, block, spot, 1)
    return whole


def line_scatter(part, axis, size):
    place = lax.axis_index(axis)
    width = part.shape[1] // size

    def block(index):
        spot = jnp.clip(index, 0, size - 1) * width
        return lax.dynamic_slice_in_dim(part, spot, width, 1).astype(F32)

    right, left = None, None
    for step in range(1, size):
        going = block(size - step + place)
        if right is not None:
            going = going + right.astype(F32)
        right = lax.ppermute(going.astype(BF16), axis, [(i, i + 1) for i in range(step)])
        going = block(place - (size - step))
        if left is not None:
            going = going + left.astype(F32)
        left = lax.ppermute(
            going.astype(BF16), axis, [(i, i - 1) for i in range(size - step, size)]
        )
    return block(place) + right.astype(F32) + left.astype(F32)


def line_sum(value, axis, size):
    bit = 1
    while bit < size:
        value = value + lax.ppermute(value, axis, [(i, i ^ bit) for i in range(size)])
        bit *= 2
    return value


def pair_gather(mine, axis, size):
    place = lax.axis_index(axis)
    bit = 1
    while bit < size:
        other = lax.ppermute(mine, axis, [(i, i ^ bit) for i in range(size)])
        upper = (place & bit) != 0
        mine = jnp.concatenate(
            [jnp.where(upper, other, mine), jnp.where(upper, mine, other)], axis=0
        )
        bit *= 2
    return mine


def pair_scatter(part, axis, size):
    place = lax.axis_index(axis)
    part = part.astype(F32)
    bit = size // 2
    while bit >= 1:
        upper = (place & bit) != 0
        low, high = jnp.split(part, 2, axis=0)
        going = jnp.where(upper, low, high).astype(BF16)
        came = lax.ppermute(going, axis, [(i, i ^ bit) for i in range(size)])
        part = jnp.where(upper, high, low) + came.astype(F32)
        bit //= 2
    return part


def swap(size, bit):
    return [(i, i ^ bit) for i in range(size)]


def cross(size):
    return [(i, i ^ 4 if i % 2 == 0 else i ^ 2) for i in range(size)]


def square_gather(mine, axis, size):
    if size != 8:
        return pair_gather(mine, axis, size)
    place = lax.axis_index(axis)
    rows = mine.shape[0]
    by_x = lax.ppermute(mine, axis, swap(size, 2))
    by_y = lax.ppermute(mine, axis, swap(size, 4))
    onward = jnp.where((place & 1) == 0, by_x, by_y)
    far = lax.ppermute(onward, axis, cross(size))
    held = {0: mine, 2: by_x, 4: by_y, 6: far}
    for bits in (0, 2, 4, 6):
        held[bits + 1] = lax.ppermute(held[bits], axis, swap(size, 1))
    whole = jnp.zeros((size * rows,) + mine.shape[1:], mine.dtype)
    for bits, block in held.items():
        whole = lax.dynamic_update_slice_in_dim(whole, block, (place ^ bits) * rows, 0)
    return whole


def square_scatter(part, axis, size):
    if size != 8:
        return pair_scatter(part, axis, size)
    place = lax.axis_index(axis)
    core = place & 1
    chip = lax.shift_right_logical(place, 1)
    split = part.reshape(size // 2, 2, part.shape[0] // size, part.shape[1])
    going = lax.dynamic_index_in_dim(split, 1 - core, 1, keepdims=False)
    came = lax.ppermute(going, axis, swap(size, 1))
    kept = lax.dynamic_index_in_dim(split, core, 1, keepdims=False)
    both = (kept.astype(F32) + came.astype(F32)).astype(BF16)

    def pick(index):
        return lax.dynamic_index_in_dim(both, index, 0, keepdims=False)

    far = lax.ppermute(pick(chip ^ 3), axis, cross(size)).astype(F32)
    none = jnp.zeros((), F32)
    to_x = pick(chip ^ 1).astype(F32) + jnp.where(core == 0, far, none)
    to_y = pick(chip ^ 2).astype(F32) + jnp.where(core == 1, far, none)
    by_x = lax.ppermute(to_x.astype(BF16), axis, swap(size, 2))
    by_y = lax.ppermute(to_y.astype(BF16), axis, swap(size, 4))
    return pick(chip).astype(F32) + by_x.astype(F32) + by_y.astype(F32)


def tile_loop(count, body):
    lax.fori_loop(0, count, lambda i, c: (body(i), c)[1], 0)


def rows_at(index, size):
    return pl.ds(pl.multiple_of(index * size, size), size)


def put(ref, rows, values):
    for j in range(ref.shape[0]):
        ref[j, rows, :] = values[:, j * 128 : (j + 1) * 128]


def get(ref, rows):
    return jnp.concatenate([ref[j, rows, :] for j in range(ref.shape[0])], axis=1)


def rnn_forward_kernel(
    both_ref, halo_ref, start_ref, mask_ref, gates_ref, params_ref,
    mixed_ref, conv_ref, r_ref, i_ref, state_ref, end_ref,
    padded, high, low, decay, drive,
):
    count, width = conv_ref.shape
    seg = count // 8
    tiles = count // TILE
    padded[0:8, :] = halo_ref[...]
    padded[8:, :] = both_ref[:, 0:width]

    def convolve(t):
        span = padded[pl.ds(pl.multiple_of(t * TILE, TILE), TILE + 8), :]
        mask = mask_ref[rows_at(t, TILE), :]
        conv = params_ref[0:1, :] * span[8:, :] + params_ref[TAPS : TAPS + 1, :]
        for k in range(1, TAPS):
            moved = span[8 - k : 8 - k + TILE, :]
            conv = conv + params_ref[k : k + 1, :] * (moved * mask[:, k : k + 1])
        conv_ref[rows_at(t, TILE), :] = conv
        top = conv.astype(BF16)
        high[rows_at(t, TILE), :] = top
        low[rows_at(t, TILE), :] = (conv - top.astype(F32)).astype(BF16)

    tile_loop(tiles, convolve)

    block = min(256, count)

    def gate(t):
        rows = rows_at(t, block)
        weights = gates_ref[...]
        both = jnp.dot(high[rows, :], weights, preferred_element_type=F32)
        both = both + jnp.dot(low[rows, :], weights, preferred_element_type=F32)
        r_ref[rows, :] = both[:, 0:width]
        i_ref[rows, :] = both[:, width:]

    tile_loop(count // block, gate)

    strength = DECAY_SCALE * jax.nn.softplus(-params_ref[TAPS + 3 : TAPS + 4, :])

    def prepare(t):
        rows = rows_at(t, TILE)
        keep = mask_ref[rows, :][:, 0:1]
        r = jax.nn.sigmoid(r_ref[rows, :] + params_ref[TAPS + 1 : TAPS + 2, :])
        i = jax.nn.sigmoid(i_ref[rows, :] + params_ref[TAPS + 2 : TAPS + 3, :])
        log_a = -strength * r
        scale = jnp.sqrt(jnp.maximum(one_less_exp(2.0 * log_a), ROOT_FLOOR))
        scale = jnp.where(keep > 0.0, scale, 1.0)
        put(decay, rows, jnp.exp(log_a) * keep)
        put(drive, rows, scale * i * conv_ref[rows, :])
        r_ref[rows, :] = r
        i_ref[rows, :] = i

    tile_loop(tiles, prepare)

    def scan(t, carry):
        held, prod = carry
        rows = pl.ds(t, 8, stride=seg)
        a = get(decay, rows)
        held = a * held + get(drive, rows)
        prod = a * prod
        put(drive, rows, held)
        put(decay, rows, prod)
        return held, prod

    shape = (8, width)
    held, prod = lax.fori_loop(0, seg, scan, (jnp.zeros(shape, F32), jnp.ones(shape, F32)))
    carry = start_ref[0:1, :]
    carries = []
    for s in range(8):
        carries.append(carry)
        carry = prod[s : s + 1, :] * carry + held[s : s + 1, :]
    end_ref[...] = jnp.broadcast_to(carry, shape)

    small = min(TILE, seg)
    for s in range(8):

        def finish(t, s=s):
            rows = pl.ds(pl.multiple_of(s * seg + t * small, small), small)
            state = get(drive, rows) + get(decay, rows) * carries[s]
            state_ref[rows, :] = state
            mixed_ref[rows, :] = (state * gelu(both_ref[rows, width:])).astype(BF16)

        tile_loop(seg // small, finish)


def rnn_forward(both, halo, start, mask, gates, params):
    count, width = both.shape[0], both.shape[1] // 2
    full = jax.ShapeDtypeStruct((count, width), F32)
    return pl.pallas_call(
        rnn_forward_kernel,
        out_shape=(
            jax.ShapeDtypeStruct((count, width), BF16),
            full, full, full, full,
            jax.ShapeDtypeStruct((8, width), F32),
        ),
        scratch_shapes=[
            pltpu.VMEM((count + 8, width), F32),
            pltpu.VMEM((count, width), BF16),
            pltpu.VMEM((count, width), BF16),
            pltpu.VMEM((width // 128, count, 128), F32),
            pltpu.VMEM((width // 128, count, 128), F32),
        ],
        compiler_params=pltpu.CompilerParams(vmem_limit_bytes=VMEM_BYTES),
        cost_estimate=pl.CostEstimate(
            flops=4 * count * width * 2 * width, bytes_accessed=count * width * 30,
            transcendentals=count * width * 6,
        ),
        name="rnn_forward",
    )(both, halo, start, mask, gates, params)


def rnn_backward_kernel(
    gm_ref, both_ref, halo_ref, start_ref, conv_ref, r_ref, i_ref, state_ref, mask_ref,
    gates_ref, params_ref, back_ref, tail_ref,
    grads_ref, rates_ref, dparams_ref, back_out_ref, tail_out_ref,
    padded, before, decay, adjoint, coef, dconv, sums,
):
    count, width = conv_ref.shape
    seg = count // 8
    tiles = count // TILE
    padded[0:8, :] = halo_ref[...]
    padded[8:, :] = both_ref[:, 0:width]
    before[0:8, :] = start_ref[...]
    before[8:, :] = state_ref[...]
    strength = DECAY_SCALE * jax.nn.softplus(-params_ref[TAPS + 3 : TAPS + 4, :])

    def prepare(t):
        rows = rows_at(t, TILE)
        keep = mask_ref[rows, :][:, 0:1]
        gm = gm_ref[rows, :]
        value, slope = gelu_and_slope(both_ref[rows, width:])
        put(adjoint, rows, gm * value)
        grads_ref[rows, width:] = (gm * state_ref[rows, :] * slope).astype(BF16)
        put(decay, rows, jnp.exp(-strength * r_ref[rows, :]) * keep)

    tile_loop(tiles, prepare)

    def scan(t, carry):
        held, prod = carry
        rows = pl.ds(seg - 1 - t, 8, stride=seg)
        a = get(decay, rows)
        total = get(adjoint, rows) + held
        put(adjoint, rows, total)
        put(coef, rows, prod)
        return a * total, a * prod

    shape = (8, width)
    held, prod = lax.fori_loop(0, seg, scan, (jnp.zeros(shape, F32), jnp.ones(shape, F32)))
    carry = back_ref[0:1, :]
    carries = [None] * 8
    for s in reversed(range(8)):
        carries[s] = carry
        carry = prod[s : s + 1, :] * carry + held[s : s + 1, :]
    back_out_ref[...] = jnp.broadcast_to(carry, shape)

    sums[...] = jnp.zeros_like(sums)

    def fold(values):
        return jnp.sum(values.reshape(-1, 8, width), axis=0)

    small = min(TILE, seg)
    for s in range(8):

        def chain(t, s=s):
            base = pl.multiple_of(s * seg + t * small, small)
            rows = pl.ds(base, small)
            keep = mask_ref[rows, :][:, 0:1]
            a = get(adjoint, rows) + get(coef, rows) * carries[s]
            r, i, conv = r_ref[rows, :], i_ref[rows, :], conv_ref[rows, :]
            fall = get(decay, rows)
            prior = before[pl.ds(base, small + 8), :][7 : 7 + small, :]
            room = one_less_exp(-2.0 * strength * r)
            bound = jnp.maximum(room, ROOT_FLOOR)
            inverse = lax.rsqrt(bound)
            live = keep > 0.0
            scale = jnp.where(live, bound * inverse, 1.0)
            open_ = jnp.where(room > ROOT_FLOOR, inverse, 0.0)
            driven = a * i
            dlog = fall * (a * prior - fall * driven * conv * open_)
            common = a * scale
            drec = dlog * (-strength) * r * (1.0 - r)
            dinp = common * conv * i * (1.0 - i)
            rates_ref[rows, 0:width] = drec.astype(BF16)
            rates_ref[rows, width:] = dinp.astype(BF16)
            dconv[rows, :] = common * i
            sums[5] += fold(drec)
            sums[6] += fold(dinp)
            sums[7] += fold(dlog * r)

        tile_loop(seg // small, chain)

    block = min(256, count)

    def spread(t):
        rows = rows_at(t, block)
        dconv[rows, :] += lax.dot_general(
            rates_ref[rows, :], gates_ref[...], (((1,), (1,)), ((), ())),
            preferred_element_type=F32,
        )

    tile_loop(count // block, spread)
    dconv[count:, :] = tail_ref[...]
    tail_out_ref[...] = dconv[0:8, :]

    def unconvolve(t):
        base = pl.multiple_of(t * TILE, TILE)
        rows = pl.ds(base, TILE)
        span = dconv[pl.ds(base, TILE + 8), :]
        mask = mask_ref[pl.ds(base, TILE + 8), :]
        source = padded[pl.ds(base, TILE + 8), :]
        here = span[0:TILE, :]
        out = params_ref[0:1, :] * here
        sums[0] += fold(here * source[8:, :])
        sums[4] += fold(here)
        for k in range(1, TAPS):
            kept = span * mask[:, k : k + 1]
            out = out + params_ref[k : k + 1, :] * kept[k : k + TILE, :]
            sums[k] += fold(kept[0:TILE, :] * source[8 - k : 8 - k + TILE, :])
        grads_ref[rows, 0:width] = out.astype(BF16)

    tile_loop(tiles, unconvolve)
    for k in range(8):
        dparams_ref[k : k + 1, :] = jnp.sum(sums[k], axis=0, keepdims=True)
    dparams_ref[TAPS + 3 : TAPS + 4, :] = (
        DECAY_SCALE
        * jax.nn.sigmoid(-params_ref[TAPS + 3 : TAPS + 4, :])
        * jnp.sum(sums[TAPS + 3], axis=0, keepdims=True)
    )


def rnn_backward(gm, both, halo, start, saved, mask, gates, params, back, tail):
    conv, r, i, state = saved
    count, width = conv.shape
    return pl.pallas_call(
        rnn_backward_kernel,
        out_shape=(
            jax.ShapeDtypeStruct((count, 2 * width), BF16),
            jax.ShapeDtypeStruct((count, 2 * width), BF16),
            jax.ShapeDtypeStruct((8, width), F32),
            jax.ShapeDtypeStruct((8, width), F32),
            jax.ShapeDtypeStruct((8, width), F32),
        ),
        scratch_shapes=[
            pltpu.VMEM((count + 8, width), F32),
            pltpu.VMEM((count + 8, width), F32),
            pltpu.VMEM((width // 128, count, 128), F32),
            pltpu.VMEM((width // 128, count, 128), F32),
            pltpu.VMEM((width // 128, count, 128), F32),
            pltpu.VMEM((count + 8, width), F32),
            pltpu.VMEM((8, 8, width), F32),
        ],
        compiler_params=pltpu.CompilerParams(vmem_limit_bytes=VMEM_BYTES),
        cost_estimate=pl.CostEstimate(
            flops=2 * count * width * 2 * width, bytes_accessed=count * width * 36,
            transcendentals=count * width * 6,
        ),
        name="rnn_backward",
    )(gm, both, halo, start, conv, r, i, state, mask, gates, params, back, tail)


def make_masks(row_lengths, count):
    ends = jnp.cumsum(row_lengths)
    places = jnp.arange(-TAPS, count, dtype=jnp.int32)
    segment = jnp.sum((places[:, None] >= ends[None, :]).astype(jnp.int32), axis=1)
    segment = jnp.where(places < 0, -1, segment)
    now = segment[TAPS:]
    same = [(segment[TAPS - k : TAPS - k + count] == now).astype(F32) for k in range(1, TAPS)]
    blank = jnp.zeros((count,), F32)
    columns = [same[0]] + same + [blank] * (LANES - TAPS)
    live = now < row_lengths.shape[0]
    return jnp.stack(columns, axis=1), live


def dense_gates(gates, width):
    span = gates.shape[0]
    tiled = jnp.tile(gates, (width // span, 1))
    row = lax.broadcasted_iota(jnp.int32, tiled.shape, 0) // span
    column = (lax.broadcasted_iota(jnp.int32, tiled.shape, 1) % width) // span
    return jnp.where(row == column, tiled, jnp.zeros((), tiled.dtype))


def diagonal_blocks(dense, span):
    width = dense.shape[0]
    column = (lax.broadcasted_iota(jnp.int32, (1, 2 * width), 1) % width) // span
    total = jnp.zeros((span, 2 * width), F32)
    for b in range(width // span):
        total = total + jnp.where(column == b, dense[b * span : (b + 1) * span], 0.0)
    return total


def per_device(
    dp, mp,
    inputs, lengths, cotangent, gains, rnn_params, rnn_in, branch_gate, recur_gate, input_gate,
    mlp_gate, mlp_up, rnn_out, mlp_down,
):
    count, part = inputs.shape
    width = rnn_in.shape[1]
    hidden_width = mlp_gate.shape[1]
    span = recur_gate.shape[0] * dp
    features = part * mp
    step = count // CHUNKS
    spot = lax.axis_index("mp") * part

    def cut(values):
        return [values[c * step : (c + 1) * step] for c in range(CHUNKS)]

    def mine(values):
        return lax.dynamic_slice_in_dim(values, spot, part, values.ndim - 1)

    gates = pair_gather(jnp.concatenate([recur_gate, input_gate], axis=1), "dp", dp)
    w_in = square_gather(jnp.concatenate([rnn_in, branch_gate], axis=1), "dp", dp)
    w_out = square_gather(after(rnn_out.T, w_in), "dp", dp)
    w_up = square_gather(
        after(jnp.concatenate([mlp_gate, mlp_up], axis=1), w_out), "dp", dp
    )
    w_down = square_gather(after(mlp_down.T, w_up), "dp", dp)

    in_parts = cut(inputs)
    wholes = []
    for c in range(CHUNKS):
        source = in_parts[c] if c == 0 else after(in_parts[c], wholes[-1])
        wholes.append(line_gather(source, "mp", mp))
    cots = []
    cot_parts = cut(cotangent)
    for c in range(CHUNKS):
        cots.append(line_gather(after(cot_parts[c], wholes[-1], *cots[-1:]), "mp", mp))

    mask, live = make_masks(lengths[0], count)
    masks = cut(mask)
    mask_tail = jnp.concatenate([mask, jnp.zeros((8, LANES), F32)], axis=0)
    tail_masks = [mask_tail[c * step : (c + 1) * step + 8] for c in range(CHUNKS)]
    lives = cut(live[:, None])
    dense = dense_gates(gates, width)

    blank = jnp.zeros((8, width), F32)
    halo, start = blank, blank
    halos, starts, boths, saves, mixes, norms, scales1 = [], [], [], [], [], [], []
    for c in range(CHUNKS):
        values = wholes[c].astype(F32)
        s1 = lax.rsqrt(jnp.mean(values * values, axis=1, keepdims=True) + EPS)
        normed = (values * s1 * gains[0]).astype(BF16)
        both = matmul(normed, w_in)
        mixed, conv, r, i, state, end = rnn_forward(
            both, halo, start, masks[c], dense, rnn_params
        )
        halos.append(halo)
        starts.append(start)
        halo, start = both[-8:, :width], end
        boths.append(both)
        saves.append((conv, r, i, state))
        mixes.append(mixed)
        norms.append(normed)
        scales1.append(s1)

    outputs, hiddens, gates_up, norms2, gbos, locals_, gms = [], [], [], [], [], [], []
    gain2_total = 0.0
    for c in range(CHUNKS):
        branch = line_scatter(inner_cols(mixes[c], w_out).astype(BF16), "mp", mp)
        middle_mine = in_parts[c].astype(F32) + branch
        middle = line_gather(middle_mine.astype(BF16), "mp", mp).astype(F32)
        s2 = lax.rsqrt(jnp.mean(middle * middle, axis=1, keepdims=True) + EPS)
        normed2 = (middle * s2 * gains[1]).astype(BF16)
        pre = matmul(normed2, w_up)
        gate_pre, up_pre = pre[:, :hidden_width], pre[:, hidden_width:]
        value, slope = gelu_and_slope(gate_pre)
        hidden = (value * up_pre).astype(BF16)
        grad_y = jnp.where(lives[c], cots[c], jnp.zeros((), BF16))
        grad_hidden = matmul(grad_y, w_down)
        pulled = jnp.concatenate(
            [
                (grad_hidden * up_pre * slope).astype(BF16),
                (grad_hidden * value).astype(BF16),
            ],
            axis=1,
        )
        gn2_part = inner_cols(pulled, w_up).astype(BF16)
        gn2_mine = line_scatter(gn2_part, "mp", mp)
        gn2 = line_gather(gn2_mine.astype(BF16), "mp", mp).astype(F32)
        g = gn2 * gains[1]
        mean = jnp.mean(g * middle, axis=1, keepdims=True)
        gbo = (grad_y.astype(F32) + s2 * g - middle * (s2 * s2 * s2 * mean)).astype(BF16)
        gain2_total = gain2_total + jnp.sum(gn2 * (middle * s2), axis=0)
        local = (
            jnp.where(lives[c], cotangent[c * step : (c + 1) * step].astype(F32), 0.0)
            + s2 * (gn2_mine * mine(gains[1]))
            - middle_mine * (s2 * s2 * s2 * mean)
        )
        mlp = line_scatter(inner_cols(hidden, w_down).astype(BF16), "mp", mp)
        outputs.append((middle_mine + mlp).astype(BF16))
        hiddens.append(hidden)
        gates_up.append(pulled)
        norms2.append(normed2)
        gbos.append(gbo)
        locals_.append(local)
        gms.append(matmul(gbo, w_out))
        cots[c] = grad_y

    grad_up = square_scatter(
        inner_rows(jnp.concatenate(norms2), jnp.concatenate(gates_up)).astype(BF16), "dp", dp
    )
    grad_down = square_scatter(
        inner_rows(jnp.concatenate(cots), jnp.concatenate(hiddens)).astype(BF16), "dp", dp
    )
    grad_out = square_scatter(
        inner_rows(jnp.concatenate(gbos), jnp.concatenate(mixes)).astype(BF16), "dp", dp
    )

    back, tail = blank, blank
    pulls, rates, grads_in = [None] * CHUNKS, [None] * CHUNKS, [None] * CHUNKS
    gain1_total, params_total = 0.0, 0.0
    for c in reversed(range(CHUNKS)):
        pull, rate, dparams, back, tail = rnn_backward(
            gms[c], boths[c], halos[c], starts[c], saves[c], tail_masks[c], dense, rnn_params,
            back, tail,
        )
        params_total = params_total + dparams
        pulls[c], rates[c] = pull, rate
        gn1_part = inner_cols(pull, w_in).astype(BF16)
        values = wholes[c].astype(F32)
        scaled = gn1_part.astype(F32) * values
        gain1_total = gain1_total + jnp.sum(scaled * scales1[c], axis=0)
        dots = jnp.sum(scaled * gains[0], axis=1).reshape(8, -1)
        mean = (line_sum(dots, "mp", mp) / features).reshape(-1, 1)
        gn1_mine = line_scatter(gn1_part, "mp", mp)
        s1 = scales1[c]
        grad = (
            locals_[c]
            + s1 * (gn1_mine * mine(gains[0]))
            - in_parts[c].astype(F32) * (s1 * s1 * s1 * mean)
        )
        grads_in[c] = grad.astype(BF16)

    grad_in = square_scatter(
        inner_rows(jnp.concatenate(norms), jnp.concatenate(pulls)).astype(BF16), "dp", dp
    )
    convs = jnp.concatenate([s[0] for s in saves]).astype(BF16)
    grad_gates = pair_scatter(
        diagonal_blocks(inner_rows(convs, jnp.concatenate(rates)), span), "dp", dp
    )
    grad_params = line_sum(params_total, "dp", dp)
    grad_gain1 = line_sum(line_sum(gain1_total.reshape(8, -1), "dp", dp), "mp", mp)
    grad_gain2 = line_sum(gain2_total.reshape(8, -1), "dp", dp)
    return (
        jnp.concatenate(outputs),
        jnp.concatenate(grads_in),
        jnp.stack([grad_gain1.reshape(-1), grad_gain2.reshape(-1)]),
        grad_params,
        grad_in[:, :width],
        grad_in[:, width:],
        grad_gates[:, :width],
        grad_gates[:, width:],
        grad_up[:, :hidden_width],
        grad_up[:, hidden_width:],
        grad_out.T,
        grad_down.T,
    )


def solution(mesh):
    return jax.shard_map(
        functools.partial(per_device, mesh.shape["dp"], mesh.shape["mp"]),
        mesh=mesh,
        in_specs=(
            P("dp", "mp"),
            P("dp", None),
            P("dp", "mp"),
            P(),
            P(None, "mp"),
            P("dp", "mp"),
            P("dp", "mp"),
            P("dp", "mp"),
            P("dp", "mp"),
            P("dp", "mp"),
            P("dp", "mp"),
            P("mp", "dp"),
            P("mp", "dp"),
        ),
        out_specs=(
            P("dp", "mp"),
            P("dp", "mp"),
            P(),
            P(None, "mp"),
            P("dp", "mp"),
            P("dp", "mp"),
            P("dp", "mp"),
            P("dp", "mp"),
            P("dp", "mp"),
            P("dp", "mp"),
            P("mp", "dp"),
            P("mp", "dp"),
        ),
        check_vma=False,
    )
```

```python
import functools

import jax
import jax.numpy as jnp
from jax import lax
from jax.experimental import pallas as pl
from jax.experimental.pallas import tpu as pltpu
from jax.sharding import PartitionSpec as P

EPS = 1e-06
DECAY_SCALE = 8.0
ROOT_FLOOR = 0.0001
TAPS = 4
LANES = 8
CHUNKS = 2
TILE = 32
F32 = jnp.float32
BF16 = jnp.bfloat16
VMEM_BYTES = 56 * 1024 * 1024


def matmul(left, right):
    return jnp.dot(left, right, preferred_element_type=F32)


def inner_rows(left, right):
    return lax.dot_general(left, right, (((0,), (0,)), ((), ())), preferred_element_type=F32)


def inner_cols(left, right):
    return lax.dot_general(left, right, (((1,), (1,)), ((), ())), preferred_element_type=F32)


def gelu_and_slope(values):
    outer = 0.7978845608028654
    inner = 0.044715
    square = values * values
    bent = jnp.tanh(outer * values * (1.0 + inner * square))
    half = 0.5 * (1.0 + bent)
    slope = half + 0.5 * values * (1.0 - bent * bent) * outer * (1.0 + 3.0 * inner * square)
    return values * half, slope


def gelu(values):
    outer = 0.7978845608028654
    inner = 0.044715
    bent = jnp.tanh(outer * values * (1.0 + inner * values * values))
    return values * (0.5 * (1.0 + bent))


def one_less_exp(values):
    near = -values * (1.0 + 0.5 * values * (1.0 + (values / 3.0) * (1.0 + 0.25 * values)))
    return jnp.where(values > -0.02, near, 1.0 - jnp.exp(values))


def after(value, *earlier):
    return lax.optimization_barrier((value,) + earlier)[0]


def line_gather(mine, axis, size):
    place = lax.axis_index(axis)
    width = mine.shape[1]
    right, left = mine, mine
    rights, lefts = {}, {}
    for step in range(1, size):
        right = lax.ppermute(right, axis, [(i, i + 1) for i in range(step - 1, size - 1)])
        left = lax.ppermute(left, axis, [(i + 1, i) for i in range(size - step)])
        rights[step], lefts[step] = right, left
    whole = jnp.zeros((mine.shape[0], size * width), mine.dtype)
    for step in range(size):
        block = mine if step == 0 else lefts[step] + rights[size - step]
        spot = lax.rem(place + step, size) * width
        whole = lax.dynamic_update_slice_in_dim(whole, block, spot, 1)
    return whole


def line_scatter(part, axis, size):
    place = lax.axis_index(axis)
    width = part.shape[1] // size

    def block(index):
        spot = jnp.clip(index, 0, size - 1) * width
        return lax.dynamic_slice_in_dim(part, spot, width, 1).astype(F32)

    right, left = None, None
    for step in range(1, size):
        going = block(size - step + place)
        if right is not None:
            going = going + right.astype(F32)
        right = lax.ppermute(going.astype(BF16), axis, [(i, i + 1) for i in range(step)])
        going = block(place - (size - step))
        if left is not None:
            going = going + left.astype(F32)
        left = lax.ppermute(
            going.astype(BF16), axis, [(i, i - 1) for i in range(size - step, size)]
        )
    return block(place) + right.astype(F32) + left.astype(F32)


def line_sum(value, axis, size):
    bit = 1
    while bit < size:
        value = value + lax.ppermute(value, axis, [(i, i ^ bit) for i in range(size)])
        bit *= 2
    return value


def pair_gather(mine, axis, size):
    place = lax.axis_index(axis)
    bit = 1
    while bit < size:
        other = lax.ppermute(mine, axis, [(i, i ^ bit) for i in range(size)])
        upper = (place & bit) != 0
        mine = jnp.concatenate(
            [jnp.where(upper, other, mine), jnp.where(upper, mine, other)], axis=0
        )
        bit *= 2
    return mine


def pair_scatter(part, axis, size):
    place = lax.axis_index(axis)
    part = part.astype(F32)
    bit = size // 2
    while bit >= 1:
        upper = (place & bit) != 0
        low, high = jnp.split(part, 2, axis=0)
        going = jnp.where(upper, low, high).astype(BF16)
        came = lax.ppermute(going, axis, [(i, i ^ bit) for i in range(size)])
        part = jnp.where(upper, high, low) + came.astype(F32)
        bit //= 2
    return part


def swap(size, bit):
    return [(i, i ^ bit) for i in range(size)]


def cross(size):
    return [(i, i ^ 4 if i % 2 == 0 else i ^ 2) for i in range(size)]


def square_gather(mine, axis, size):
    if size != 8:
        return pair_gather(mine, axis, size)
    place = lax.axis_index(axis)
    rows = mine.shape[0]
    by_x = lax.ppermute(mine, axis, swap(size, 2))
    by_y = lax.ppermute(mine, axis, swap(size, 4))
    onward = jnp.where((place & 1) == 0, by_x, by_y)
    far = lax.ppermute(onward, axis, cross(size))
    held = {0: mine, 2: by_x, 4: by_y, 6: far}
    for bits in (0, 2, 4, 6):
        held[bits + 1] = lax.ppermute(held[bits], axis, swap(size, 1))
    whole = jnp.zeros((size * rows,) + mine.shape[1:], mine.dtype)
    for bits, block in held.items():
        whole = lax.dynamic_update_slice_in_dim(whole, block, (place ^ bits) * rows, 0)
    return whole


def square_scatter(part, axis, size):
    if size != 8:
        return pair_scatter(part, axis, size)
    place = lax.axis_index(axis)
    core = place & 1
    chip = lax.shift_right_logical(place, 1)
    split = part.reshape(size // 2, 2, part.shape[0] // size, part.shape[1])
    going = lax.dynamic_index_in_dim(split, 1 - core, 1, keepdims=False)
    came = lax.ppermute(going, axis, swap(size, 1))
    kept = lax.dynamic_index_in_dim(split, core, 1, keepdims=False)
    both = (kept.astype(F32) + came.astype(F32)).astype(BF16)

    def pick(index):
        return lax.dynamic_index_in_dim(both, index, 0, keepdims=False)

    far = lax.ppermute(pick(chip ^ 3), axis, cross(size)).astype(F32)
    none = jnp.zeros((), F32)
    to_x = pick(chip ^ 1).astype(F32) + jnp.where(core == 0, far, none)
    to_y = pick(chip ^ 2).astype(F32) + jnp.where(core == 1, far, none)
    by_x = lax.ppermute(to_x.astype(BF16), axis, swap(size, 2))
    by_y = lax.ppermute(to_y.astype(BF16), axis, swap(size, 4))
    return pick(chip).astype(F32) + by_x.astype(F32) + by_y.astype(F32)


def tile_loop(count, body):
    lax.fori_loop(0, count, lambda i, c: (body(i), c)[1], 0)


def rows_at(index, size):
    return pl.ds(pl.multiple_of(index * size, size), size)


def put(ref, rows, values):
    for j in range(ref.shape[0]):
        ref[j, rows, :] = values[:, j * 128 : (j + 1) * 128]


def get(ref, rows):
    return jnp.concatenate([ref[j, rows, :] for j in range(ref.shape[0])], axis=1)


def rnn_forward_kernel(
    both_ref, halo_ref, start_ref, mask_ref, gates_ref, params_ref,
    mixed_ref, conv_ref, r_ref, i_ref, state_ref, end_ref,
    padded, high, low, decay, drive,
):
    count, width = conv_ref.shape
    seg = count // 8
    tiles = count // TILE
    padded[0:8, :] = halo_ref[...]
    padded[8:, :] = both_ref[:, 0:width]

    def convolve(t):
        span = padded[pl.ds(pl.multiple_of(t * TILE, TILE), TILE + 8), :]
        mask = mask_ref[rows_at(t, TILE), :]
        conv = params_ref[0:1, :] * span[8:, :] + params_ref[TAPS : TAPS + 1, :]
        for k in range(1, TAPS):
            moved = span[8 - k : 8 - k + TILE, :]
            conv = conv + params_ref[k : k + 1, :] * (moved * mask[:, k : k + 1])
        conv_ref[rows_at(t, TILE), :] = conv
        top = conv.astype(BF16)
        high[rows_at(t, TILE), :] = top
        low[rows_at(t, TILE), :] = (conv - top.astype(F32)).astype(BF16)

    tile_loop(tiles, convolve)

    block = min(256, count)

    def gate(t):
        rows = rows_at(t, block)
        weights = gates_ref[...]
        both = jnp.dot(high[rows, :], weights, preferred_element_type=F32)
        both = both + jnp.dot(low[rows, :], weights, preferred_element_type=F32)
        r_ref[rows, :] = both[:, 0:width]
        i_ref[rows, :] = both[:, width:]

    tile_loop(count // block, gate)

    strength = DECAY_SCALE * jax.nn.softplus(-params_ref[TAPS + 3 : TAPS + 4, :])

    def prepare(t):
        rows = rows_at(t, TILE)
        keep = mask_ref[rows, :][:, 0:1]
        r = jax.nn.sigmoid(r_ref[rows, :] + params_ref[TAPS + 1 : TAPS + 2, :])
        i = jax.nn.sigmoid(i_ref[rows, :] + params_ref[TAPS + 2 : TAPS + 3, :])
        log_a = -strength * r
        scale = jnp.sqrt(jnp.maximum(one_less_exp(2.0 * log_a), ROOT_FLOOR))
        scale = jnp.where(keep > 0.0, scale, 1.0)
        put(decay, rows, jnp.exp(log_a) * keep)
        put(drive, rows, scale * i * conv_ref[rows, :])
        r_ref[rows, :] = r
        i_ref[rows, :] = i

    tile_loop(tiles, prepare)

    def scan(t, carry):
        held, prod = carry
        rows = pl.ds(t, 8, stride=seg)
        a = get(decay, rows)
        held = a * held + get(drive, rows)
        prod = a * prod
        put(drive, rows, held)
        put(decay, rows, prod)
        return held, prod

    shape = (8, width)
    held, prod = lax.fori_loop(0, seg, scan, (jnp.zeros(shape, F32), jnp.ones(shape, F32)))
    carry = start_ref[0:1, :]
    carries = []
    for s in range(8):
        carries.append(carry)
        carry = prod[s : s + 1, :] * carry + held[s : s + 1, :]
    end_ref[...] = jnp.broadcast_to(carry, shape)

    small = min(TILE, seg)
    for s in range(8):

        def finish(t, s=s):
            rows = pl.ds(pl.multiple_of(s * seg + t * small, small), small)
            state = get(drive, rows) + get(decay, rows) * carries[s]
            state_ref[rows, :] = state
            mixed_ref[rows, :] = (state * gelu(both_ref[rows, width:])).astype(BF16)

        tile_loop(seg // small, finish)


def rnn_forward(both, halo, start, mask, gates, params):
    count, width = both.shape[0], both.shape[1] // 2
    full = jax.ShapeDtypeStruct((count, width), F32)
    return pl.pallas_call(
        rnn_forward_kernel,
        out_shape=(
            jax.ShapeDtypeStruct((count, width), BF16),
            full, full, full, full,
            jax.ShapeDtypeStruct((8, width), F32),
        ),
        scratch_shapes=[
            pltpu.VMEM((count + 8, width), F32),
            pltpu.VMEM((count, width), BF16),
            pltpu.VMEM((count, width), BF16),
            pltpu.VMEM((width // 128, count, 128), F32),
            pltpu.VMEM((width // 128, count, 128), F32),
        ],
        compiler_params=pltpu.CompilerParams(vmem_limit_bytes=VMEM_BYTES),
        cost_estimate=pl.CostEstimate(
            flops=4 * count * width * 2 * width, bytes_accessed=count * width * 30,
            transcendentals=count * width * 6,
        ),
        name="rnn_forward",
    )(both, halo, start, mask, gates, params)


def rnn_backward_kernel(
    gm_ref, both_ref, halo_ref, start_ref, conv_ref, r_ref, i_ref, state_ref, mask_ref,
    gates_ref, params_ref, back_ref, tail_ref,
    grads_ref, rates_ref, dparams_ref, back_out_ref, tail_out_ref,
    padded, before, decay, adjoint, coef, dconv, sums,
):
    count, width = conv_ref.shape
    seg = count // 8
    tiles = count // TILE
    padded[0:8, :] = halo_ref[...]
    padded[8:, :] = both_ref[:, 0:width]
    before[0:8, :] = start_ref[...]
    before[8:, :] = state_ref[...]
    strength = DECAY_SCALE * jax.nn.softplus(-params_ref[TAPS + 3 : TAPS + 4, :])

    def prepare(t):
        rows = rows_at(t, TILE)
        keep = mask_ref[rows, :][:, 0:1]
        gm = gm_ref[rows, :]
        value, slope = gelu_and_slope(both_ref[rows, width:])
        put(adjoint, rows, gm * value)
        grads_ref[rows, width:] = (gm * state_ref[rows, :] * slope).astype(BF16)
        put(decay, rows, jnp.exp(-strength * r_ref[rows, :]) * keep)

    tile_loop(tiles, prepare)

    def scan(t, carry):
        held, prod = carry
        rows = pl.ds(seg - 1 - t, 8, stride=seg)
        a = get(decay, rows)
        total = get(adjoint, rows) + held
        put(adjoint, rows, total)
        put(coef, rows, prod)
        return a * total, a * prod

    shape = (8, width)
    held, prod = lax.fori_loop(0, seg, scan, (jnp.zeros(shape, F32), jnp.ones(shape, F32)))
    carry = back_ref[0:1, :]
    carries = [None] * 8
    for s in reversed(range(8)):
        carries[s] = carry
        carry = prod[s : s + 1, :] * carry + held[s : s + 1, :]
    back_out_ref[...] = jnp.broadcast_to(carry, shape)

    sums[...] = jnp.zeros_like(sums)

    def fold(values):
        return jnp.sum(values.reshape(-1, 8, width), axis=0)

    small = min(TILE, seg)
    for s in range(8):

        def chain(t, s=s):
            base = pl.multiple_of(s * seg + t * small, small)
            rows = pl.ds(base, small)
            keep = mask_ref[rows, :][:, 0:1]
            a = get(adjoint, rows) + get(coef, rows) * carries[s]
            r, i, conv = r_ref[rows, :], i_ref[rows, :], conv_ref[rows, :]
            fall = get(decay, rows)
            prior = before[pl.ds(base, small + 8), :][7 : 7 + small, :]
            room = one_less_exp(-2.0 * strength * r)
            bound = jnp.maximum(room, ROOT_FLOOR)
            inverse = lax.rsqrt(bound)
            live = keep > 0.0
            scale = jnp.where(live, bound * inverse, 1.0)
            open_ = jnp.where(room > ROOT_FLOOR, inverse, 0.0)
            driven = a * i
            dlog = fall * (a * prior - fall * driven * conv * open_)
            common = a * scale
            drec = dlog * (-strength) * r * (1.0 - r)
            dinp = common * conv * i * (1.0 - i)
            rates_ref[rows, 0:width] = drec.astype(BF16)
            rates_ref[rows, width:] = dinp.astype(BF16)
            dconv[rows, :] = common * i
            sums[5] += fold(drec)
            sums[6] += fold(dinp)
            sums[7] += fold(dlog * r)

        tile_loop(seg // small, chain)

    block = min(256, count)

    def spread(t):
        rows = rows_at(t, block)
        dconv[rows, :] += lax.dot_general(
            rates_ref[rows, :], gates_ref[...], (((1,), (1,)), ((), ())),
            preferred_element_type=F32,
        )

    tile_loop(count // block, spread)
    dconv[count:, :] = tail_ref[...]
    tail_out_ref[...] = dconv[0:8, :]

    def unconvolve(t):
        base = pl.multiple_of(t * TILE, TILE)
        rows = pl.ds(base, TILE)
        span = dconv[pl.ds(base, TILE + 8), :]
        mask = mask_ref[pl.ds(base, TILE + 8), :]
        source = padded[pl.ds(base, TILE + 8), :]
        here = span[0:TILE, :]
        out = params_ref[0:1, :] * here
        sums[0] += fold(here * source[8:, :])
        sums[4] += fold(here)
        for k in range(1, TAPS):
            kept = span * mask[:, k : k + 1]
            out = out + params_ref[k : k + 1, :] * kept[k : k + TILE, :]
            sums[k] += fold(kept[0:TILE, :] * source[8 - k : 8 - k + TILE, :])
        grads_ref[rows, 0:width] = out.astype(BF16)

    tile_loop(tiles, unconvolve)
    for k in range(8):
        dparams_ref[k : k + 1, :] = jnp.sum(sums[k], axis=0, keepdims=True)
    dparams_ref[TAPS + 3 : TAPS + 4, :] = (
        DECAY_SCALE
        * jax.nn.sigmoid(-params_ref[TAPS + 3 : TAPS + 4, :])
        * jnp.sum(sums[TAPS + 3], axis=0, keepdims=True)
    )


def rnn_backward(gm, both, halo, start, saved, mask, gates, params, back, tail):
    conv, r, i, state = saved
    count, width = conv.shape
    return pl.pallas_call(
        rnn_backward_kernel,
        out_shape=(
            jax.ShapeDtypeStruct((count, 2 * width), BF16),
            jax.ShapeDtypeStruct((count, 2 * width), BF16),
            jax.ShapeDtypeStruct((8, width), F32),
            jax.ShapeDtypeStruct((8, width), F32),
            jax.ShapeDtypeStruct((8, width), F32),
        ),
        scratch_shapes=[
            pltpu.VMEM((count + 8, width), F32),
            pltpu.VMEM((count + 8, width), F32),
            pltpu.VMEM((width // 128, count, 128), F32),
            pltpu.VMEM((width // 128, count, 128), F32),
            pltpu.VMEM((width // 128, count, 128), F32),
            pltpu.VMEM((count + 8, width), F32),
            pltpu.VMEM((8, 8, width), F32),
        ],
        compiler_params=pltpu.CompilerParams(vmem_limit_bytes=VMEM_BYTES),
        cost_estimate=pl.CostEstimate(
            flops=2 * count * width * 2 * width, bytes_accessed=count * width * 36,
            transcendentals=count * width * 6,
        ),
        name="rnn_backward",
    )(gm, both, halo, start, conv, r, i, state, mask, gates, params, back, tail)


MESH = pl.DeviceIdType.MESH


class Spread:
    def __init__(self, place, size, blocks, sent, came):
        self.place, self.size = place, size
        self.blocks, self.sent, self.came = blocks, sent, came

    def copy(self, slot, j, way, k):
        ref = self.blocks.at[slot, j]
        return pltpu.make_async_remote_copy(
            src_ref=ref, dst_ref=ref, send_sem=self.sent.at[slot, k],
            recv_sem=self.came.at[slot, j], device_id={"mp": self.place + way},
            device_id_type=MESH,
        )

    def moves(self, s):
        z, n = self.place, self.size
        return (
            ((z - s >= 0) & (z < n - 1), z - s, 1, 2 * s),
            ((z + s <= n - 1) & (z > 0), z + s, -1, 2 * s + 1),
        )

    def step(self, slot, s):
        for valid, j, way, k in self.moves(s):

            @pl.when(valid)
            def _(j=j, way=way, k=k):
                copy = self.copy(slot, j, way, k)
                if s > 0:
                    copy.wait_recv()
                copy.start()

    def finish(self, slot):
        z, n = self.place, self.size

        @pl.when(z == 0)
        def _():
            for j in range(1, n):
                self.copy(slot, j, 1, 0).wait_recv()

        @pl.when(z == n - 1)
        def _():
            for j in range(n - 1):
                self.copy(slot, j, -1, 0).wait_recv()

    def drain(self, slot):
        for s in range(self.size - 1):
            for valid, j, way, k in self.moves(s):

                @pl.when(valid)
                def _(j=j, way=way, k=k):
                    self.copy(slot, j, way, k).wait_send()


class Fold:
    def __init__(self, place, size, parts, rights, lefts, sent, came_right, came_left):
        self.place, self.size = place, size
        self.parts, self.rights, self.lefts = parts, rights, lefts
        self.sent, self.came_right, self.came_left = sent, came_right, came_left

    def right(self, slot, j, k):
        return pltpu.make_async_remote_copy(
            src_ref=self.parts.at[slot, j], dst_ref=self.rights.at[slot, k],
            send_sem=self.sent.at[slot, j], recv_sem=self.came_right.at[slot, k],
            device_id={"mp": self.place + 1}, device_id_type=MESH,
        )

    def left(self, slot, j, k):
        return pltpu.make_async_remote_copy(
            src_ref=self.parts.at[slot, j], dst_ref=self.lefts.at[slot, k],
            send_sem=self.sent.at[slot, j], recv_sem=self.came_left.at[slot, k],
            device_id={"mp": self.place - 1}, device_id_type=MESH,
        )

    def clear(self):
        for slot in range(self.parts.shape[0]):
            last = self.size - 2
            blank = jnp.zeros(self.rights.shape[2:], BF16)
            self.rights[slot, last] = blank
            self.lefts[slot, last] = blank

    def start(self, slot):
        z, n = self.place, self.size

        @pl.when(z == 0)
        def _():
            for j in reversed(range(1, n)):
                self.right(slot, j, n - 1 - j).start()

        @pl.when(z == n - 1)
        def _():
            for j in range(n - 1):
                self.left(slot, j, j).start()

    def step(self, slot, s):
        z, n = self.place, self.size
        back = n - 1 - z

        @pl.when((z >= 1) & (z <= n - 2) & (s >= z))
        def _():
            j = n - 1 + z - s
            self.right(slot, j, s - 1).wait_recv()
            self.add(slot, j, self.rights, s - 1)
            self.right(slot, j, s).start()

        @pl.when((back >= 1) & (back <= n - 2) & (s >= back))
        def _():
            j = s - back
            self.left(slot, j, s - 1).wait_recv()
            self.add(slot, j, self.lefts, s - 1)
            self.left(slot, j, s).start()

    def add(self, slot, j, came, k):
        self.parts[slot, j] = (
            self.parts[slot, j].astype(F32) + came[slot, k].astype(F32)
        ).astype(BF16)

    def finish(self, slot):
        z, n = self.place, self.size

        @pl.when(z >= 1)
        def _():
            self.right(slot, z, n - 2).wait_recv()

        @pl.when(z <= n - 2)
        def _():
            self.left(slot, z, n - 2).wait_recv()

    def total(self, slot, rows):
        z, n = self.place, self.size
        return (
            self.parts[slot, z, rows, :].astype(F32)
            + self.rights[slot, n - 2, rows, :].astype(F32)
            + self.lefts[slot, n - 2, rows, :].astype(F32)
        )

    def drain(self, slot):
        for j in range(self.size):

            @pl.when(j != self.place)
            def _(j=j):
                self.right(slot, j, 0).wait_send()


def partners(d):
    core, x, y = lax.rem(d, 2), lax.rem(lax.div(d, 2), 2), lax.div(d, 4)
    return core, d + 1 - 2 * core, d + 2 - 4 * x, d + 4 - 8 * y


class Square:
    def __init__(self, d, shard, whole, sent, came, own):
        self.d, self.shard, self.whole = d, shard, whole
        self.sent, self.came, self.own = sent, came, own
        self.core, self.by_core, self.by_x, self.by_y = partners(d)

    def rows(self, d):
        count = self.shard.shape[0]
        return self.whole.at[pl.ds(pl.multiple_of(d * count, count), count), :]

    def copy(self, src, origin, target, sent, came):
        return pltpu.make_async_remote_copy(
            src_ref=src, dst_ref=self.rows(origin), send_sem=self.sent.at[sent],
            recv_sem=self.came.at[came], device_id={"dp": target}, device_id_type=MESH,
        )

    def local(self):
        return pltpu.make_async_copy(self.shard, self.rows(self.d), self.own)

    def far(self):
        return partners(self.by_x)[3]

    def first(self):
        return (
            self.copy(self.shard, self.d, self.by_x, 0, 2),
            self.copy(self.shard, self.d, self.by_y, 1, 4),
            self.copy(self.shard, self.d, self.by_core, 2, 1),
        )

    def start(self):
        for copy in self.first():
            copy.start()
        self.local().start()

    def step_one(self):
        x_rows, y_rows = self.rows(self.by_x), self.rows(self.by_y)
        by_x = self.copy(x_rows, self.by_x, self.by_core, 3, 2)
        by_y = self.copy(y_rows, self.by_y, self.by_core, 4, 4)
        by_x.wait_recv()

        @pl.when(self.core == 0)
        def _():
            self.copy(x_rows, self.by_x, self.by_y, 5, 6).start()

        self.copy(x_rows, self.by_x, self.by_core, 3, 3).start()
        by_y.wait_recv()

        @pl.when(self.core == 1)
        def _():
            self.copy(y_rows, self.by_y, self.by_x, 5, 6).start()

        self.copy(y_rows, self.by_y, self.by_core, 4, 5).start()

    def step_two(self):
        far = self.far()
        rows = self.rows(far)
        self.copy(rows, far, self.by_core, 6, 6).wait_recv()
        self.copy(rows, far, self.by_core, 6, 7).start()

    def finish(self):
        for k in (1, 3, 5, 7):
            self.copy(self.shard, self.d, self.by_core, 0, k).wait_recv()
        self.local().wait()

    def drain(self):
        for k in range(7):
            self.copy(self.shard, self.d, self.by_core, k, 0).wait_send()


def middle_kernel(dp, mp, chunks, *refs):
    (
        mixed_ref, x_ref, cot_ref, live_ref, gains_ref, mine_ref, wout_ref, up_ref, down_ref,
        output_ref, gm_ref, gbo_ref, local_ref, hidden_ref, pulled_ref, norm_ref, grady_ref,
        gain_ref,
        w_up, w_down, cots, mids, gn2s, mid_mine, gn2_mine,
        parts1, rights1, lefts1, parts2, rights2, lefts2, parts3, rights3, lefts3,
        norm, hidden, pulled, gbo, gm, local, out,
        spread_sent, spread_came, fold_sent, fold_right, fold_left,
        square_sent, square_came, square_own, load_sem, store_sem,
    ) = refs
    step, part = x_ref.shape[0] // chunks, x_ref.shape[1]
    features = part * mp
    hidden_width = w_down.shape[1]
    z, d = lax.axis_index("mp"), lax.axis_index("dp")
    square = dp == 8

    folds = [
        Fold(z, mp, p, r, l, fold_sent.at[k], fold_right.at[k], fold_left.at[k])
        for k, (p, r, l) in enumerate(
            ((parts1, rights1, lefts1), (parts2, rights2, lefts2), (parts3, rights3, lefts3))
        )
    ]
    rs1, rs2, rs3 = folds
    ag2, ag3, ag4 = [
        Spread(z, mp, b, spread_sent.at[k], spread_came.at[k])
        for k, b in enumerate((cots, mids, gn2s))
    ]
    for fold in folds:
        fold.clear()

    barrier = pltpu.get_barrier_semaphore()

    @pl.when(z > 0)
    def _():
        pl.semaphore_signal(barrier, inc=1, device_id={"mp": z - 1}, device_id_type=MESH)

    @pl.when(z < mp - 1)
    def _():
        pl.semaphore_signal(barrier, inc=1, device_id={"mp": z + 1}, device_id_type=MESH)

    count = jnp.where((z > 0) & (z < mp - 1), 2, 1)
    if square:
        for other in partners(d)[1:]:
            pl.semaphore_signal(barrier, inc=1, device_id={"dp": other}, device_id_type=MESH)
        count = count + 3
    pl.semaphore_wait(barrier, count)

    if square:
        squares = [
            Square(d, up_ref, w_up, square_sent.at[0], square_came.at[0], square_own.at[0]),
            Square(d, down_ref, w_down, square_sent.at[1], square_came.at[1], square_own.at[1]),
        ]
        for item in squares:
            item.start()
    else:
        loads = [
            pltpu.make_async_copy(up_ref, w_up, square_own.at[0]),
            pltpu.make_async_copy(down_ref, w_down, square_own.at[1]),
        ]
        for item in loads:
            item.start()

    def chunk_rows(c):
        return pl.ds(c * step, step)

    def store(buffer, target, c, k):
        return pltpu.make_async_copy(buffer, target.at[chunk_rows(c), :], store_sem.at[k])

    def own_cot(c):
        return pltpu.make_async_copy(cot_ref.at[chunk_rows(c), :], cots.at[c, z], load_sem.at[c])

    for c in range(chunks):
        own_cot(c).start()

    gain_ref[...] = jnp.zeros_like(gain_ref)
    tiles = step // TILE

    def fill(fold, slot, left, weights):
        def body(j):
            rows = pl.ds(pl.multiple_of(j * part, part), part)
            fold.parts[slot, j] = inner_cols(left, weights[rows, :]).astype(BF16)

        tile_loop(mp, body)

    def branch(c):
        fill(rs1, c % 2, mixed_ref[chunk_rows(c), :], wout_ref)

    def join(c):
        def body(t):
            rows = rows_at(t, TILE)
            base = pl.ds(pl.multiple_of(c * step + t * TILE, TILE), TILE)
            total = x_ref[base, :].astype(F32) + rs1.total(c % 2, rows)
            mid_mine[c, rows, :] = total
            mids[c, z, rows, :] = total.astype(BF16)

        tile_loop(tiles, body)

    def stats(c, rows):
        blocks = [mids[c, j, rows, :].astype(F32) for j in range(mp)]
        square_sum = sum(jnp.sum(b * b, axis=1, keepdims=True) for b in blocks)
        return blocks, lax.rsqrt(square_sum / features + EPS)

    def block_cols(j):
        return slice(j * part, (j + 1) * part)

    def normalise(c):
        def body(t):
            rows = rows_at(t, TILE)
            base = pl.ds(pl.multiple_of(c * step + t * TILE, TILE), TILE)
            blocks, s2 = stats(c, rows)
            live = live_ref[base, :][:, 0:1]
            for j in range(mp):
                norm[rows, block_cols(j)] = (
                    blocks[j] * s2 * gains_ref[1:2, block_cols(j)]
                ).astype(BF16)
                cots[c, j, rows, :] = (cots[c, j, rows, :].astype(F32) * live).astype(BF16)

        tile_loop(tiles, body)

    def grad_y_copies(c):
        return [
            pltpu.make_async_copy(
                cots.at[c, j], grady_ref.at[chunk_rows(c), pl.ds(j * part, part)],
                store_sem.at[8 + j],
            )
            for j in range(mp)
        ]

    def mlp_first(c):
        if c > 0:
            store(norm, norm_ref, c, 0).wait()
            store(hidden, hidden_ref, c, 1).wait()
            store(pulled, pulled_ref, c, 2).wait()
            for copy in grad_y_copies(c - 1):
                copy.wait()
        ag2.drain(c)
        normalise(c)
        store(norm, norm_ref, c, 0).start()
        for copy in grad_y_copies(c):
            copy.start()
        size = 256

        def body(t):
            near = pl.ds(pl.multiple_of(t * size, size), size)
            off = pl.ds(pl.multiple_of(hidden_width + t * size, size), size)
            gate = matmul(norm[...], w_up[:, near])
            up = matmul(norm[...], w_up[:, off])
            grad = sum(
                matmul(cots[c, j], w_down[block_cols(j), near]) for j in range(mp)
            )
            value, slope = gelu_and_slope(gate)
            hidden[:, near] = (value * up).astype(BF16)
            pulled[:, near] = (grad * up * slope).astype(BF16)
            pulled[:, off] = (grad * value).astype(BF16)

        tile_loop(hidden_width // size, body)
        store(hidden, hidden_ref, c, 1).start()
        store(pulled, pulled_ref, c, 2).start()

    def mlp_second(c):
        slot = c % 2
        if c > 1:
            rs3.drain(slot)
        fill(rs3, slot, pulled[...], w_up)
        rs3.start(slot)

    def mlp_third(c):
        slot = c % 2
        if c > 1:
            rs2.drain(slot)
        fill(rs2, slot, hidden[...], w_down)

    def gather_grad(c):
        slot = c % 2

        def body(t):
            rows = rows_at(t, TILE)
            total = rs3.total(slot, rows)
            gn2_mine[slot, rows, :] = total
            gn2s[slot, z, rows, :] = total.astype(BF16)

        tile_loop(tiles, body)
        ag4.step(slot, 0)

    def norm_back(c):
        slot = c % 2
        if c > 0:
            store(gbo, gbo_ref, c, 3).wait()
            store(local, local_ref, c, 4).wait()
            store(gm, gm_ref, c, 5).wait()

        def body(t):
            rows = rows_at(t, TILE)
            blocks, s2 = stats(c, rows)
            grads = [gn2s[slot, j, rows, :].astype(F32) for j in range(mp)]
            scaled = [grads[j] * gains_ref[1:2, block_cols(j)] for j in range(mp)]
            mean = (
                sum(jnp.sum(scaled[j] * blocks[j], axis=1, keepdims=True) for j in range(mp))
                / features
            )
            fall = s2 * s2 * s2 * mean
            for j in range(mp):
                grad_y = cots[c, j, rows, :].astype(F32)
                gbo[rows, block_cols(j)] = (
                    grad_y + s2 * scaled[j] - blocks[j] * fall
                ).astype(BF16)
                gain_ref[:, block_cols(j)] += jnp.sum(
                    (grads[j] * (blocks[j] * s2)).reshape(-1, 8, part), axis=0
                )
            local[rows, :] = (
                cots[c, z, rows, :].astype(F32)
                + s2 * (gn2_mine[slot, rows, :] * mine_ref[1:2, :])
                - mid_mine[c, rows, :] * fall
            )

        tile_loop(tiles, body)
        gm[...] = matmul(gbo[...], wout_ref[...])
        store(gbo, gbo_ref, c, 3).start()
        store(local, local_ref, c, 4).start()
        store(gm, gm_ref, c, 5).start()

    def make_output(c):
        if c > 0:
            store(out, output_ref, c, 6).wait()

        def body(t):
            rows = rows_at(t, TILE)
            out[rows, :] = (mid_mine[c, rows, :] + rs2.total(c % 2, rows)).astype(BF16)

        tile_loop(tiles, body)
        store(out, output_ref, c, 6).start()

    def has(c):
        return 0 <= c < chunks

    for r in range(chunks + 3):
        if has(r):
            if r > 1:
                rs1.drain(r % 2)
            branch(r)
            rs1.start(r % 2)
            own_cot(r).wait()
        if has(r - 1):
            ag3.step(r - 1, 0)
        if has(r):
            ag2.step(r, 0)
        if has(r - 3):
            gather_grad(r - 3)
            rs2.start((r - 3) % 2)
        if r == 0 and square:
            squares[0].step_one()
        if r == 1 and square:
            squares[1].step_one()
        if r == 2:
            if square:
                squares[0].step_two()
                squares[1].step_two()
                for item in squares:
                    item.finish()
            else:
                for item in loads:
                    item.wait()
        if has(r - 2):
            mlp_first(r - 2)
        for s in range(1, mp - 1):
            if has(r):
                rs1.step(r % 2, s)
            if has(r - 1):
                ag3.step(r - 1, s)
            if has(r - 3):
                ag4.step((r - 3) % 2, s)
            if has(r):
                ag2.step(r, s)
            if has(r - 3):
                rs2.step((r - 3) % 2, s)
            if s == 1 and has(r - 2):
                mlp_second(r - 2)
        if has(r):
            rs1.finish(r % 2)
            join(r)
        if has(r - 1):
            ag3.finish(r - 1)
        if has(r):
            ag2.finish(r)
        if has(r - 2):
            rs3.step((r - 2) % 2, 1)
            mlp_third(r - 2)
        if has(r - 3):
            ag4.finish((r - 3) % 2)
            norm_back(r - 3)
            ag4.drain((r - 3) % 2)
        if has(r - 2):
            for s in range(2, mp - 1):
                rs3.step((r - 2) % 2, s)
        if has(r - 3):
            rs2.finish((r - 3) % 2)
            make_output(r - 3)
        if has(r - 2):
            rs3.finish((r - 2) % 2)

    last = chunks - 1
    for k, (buffer, target) in enumerate(
        (
            (norm, norm_ref), (hidden, hidden_ref), (pulled, pulled_ref), (gbo, gbo_ref),
            (local, local_ref), (gm, gm_ref), (out, output_ref),
        )
    ):
        store(buffer, target, last, k).wait()
    for copy in grad_y_copies(last):
        copy.wait()
    for c in range(chunks):
        ag3.drain(c)
    for slot in range(2):
        for fold in folds:
            fold.drain(slot)
    if square:
        for item in squares:
            item.drain()


def middle(dp, mp, chunks, mixed, inputs, cotangent, live, gains, mine, w_out, up, down):
    count, part = inputs.shape
    width, hidden_width = mixed.shape[1], down.shape[1]
    step, features = count // chunks, part * mp

    def fold_buffers():
        return [
            pltpu.VMEM((2, mp, step, part), BF16),
            pltpu.VMEM((2, mp - 1, step, part), BF16),
            pltpu.VMEM((2, mp - 1, step, part), BF16),
        ]

    dma = pltpu.SemaphoreType.DMA
    any_, vmem = pl.BlockSpec(memory_space=pl.ANY), pl.BlockSpec(memory_space=pltpu.VMEM)
    return pl.pallas_call(
        functools.partial(middle_kernel, dp, mp, chunks),
        in_specs=[vmem, vmem, any_, vmem, vmem, vmem, vmem, any_, any_],
        out_specs=[any_] * 8 + [vmem],
        out_shape=(
            jax.ShapeDtypeStruct((count, part), BF16),
            jax.ShapeDtypeStruct((count, width), F32),
            jax.ShapeDtypeStruct((count, features), BF16),
            jax.ShapeDtypeStruct((count, part), F32),
            jax.ShapeDtypeStruct((count, hidden_width), BF16),
            jax.ShapeDtypeStruct((count, 2 * hidden_width), BF16),
            jax.ShapeDtypeStruct((count, features), BF16),
            jax.ShapeDtypeStruct((count, features), BF16),
            jax.ShapeDtypeStruct((8, features), F32),
        ),
        scratch_shapes=[
            pltpu.VMEM((features, 2 * hidden_width), BF16),
            pltpu.VMEM((features, hidden_width), BF16),
            pltpu.VMEM((chunks, mp, step, part), BF16),
            pltpu.VMEM((chunks, mp, step, part), BF16),
            pltpu.VMEM((2, mp, step, part), BF16),
            pltpu.VMEM((chunks, step, part), F32),
            pltpu.VMEM((2, step, part), F32),
        ]
        + fold_buffers() + fold_buffers() + fold_buffers()
        + [
            pltpu.VMEM((step, features), BF16),
            pltpu.VMEM((step, hidden_width), BF16),
            pltpu.VMEM((step, 2 * hidden_width), BF16),
            pltpu.VMEM((step, features), BF16),
            pltpu.VMEM((step, width), F32),
            pltpu.VMEM((step, part), F32),
            pltpu.VMEM((step, part), BF16),
            dma((3, chunks, 2 * mp)),
            dma((3, chunks, mp)),
            dma((3, 2, mp)),
            dma((3, 2, mp)),
            dma((3, 2, mp)),
            dma((2, 8)),
            dma((2, 8)),
            dma((2,)),
            dma((chunks,)),
            dma((12,)),
        ],
        compiler_params=pltpu.CompilerParams(
            collective_id=0, has_side_effects=True, vmem_limit_bytes=62 * 1024 * 1024
        ),
        name="middle",
    )(mixed, inputs, cotangent, live, gains, mine, w_out, up, down)


def make_masks(row_lengths, count):
    ends = jnp.cumsum(row_lengths)
    places = jnp.arange(-TAPS, count, dtype=jnp.int32)
    segment = jnp.sum((places[:, None] >= ends[None, :]).astype(jnp.int32), axis=1)
    segment = jnp.where(places < 0, -1, segment)
    now = segment[TAPS:]
    same = [(segment[TAPS - k : TAPS - k + count] == now).astype(F32) for k in range(1, TAPS)]
    blank = jnp.zeros((count,), F32)
    columns = [same[0]] + same + [blank] * (LANES - TAPS)
    live = now < row_lengths.shape[0]
    return jnp.stack(columns, axis=1), live


def dense_gates(gates, width):
    span = gates.shape[0]
    tiled = jnp.tile(gates, (width // span, 1))
    row = lax.broadcasted_iota(jnp.int32, tiled.shape, 0) // span
    column = (lax.broadcasted_iota(jnp.int32, tiled.shape, 1) % width) // span
    return jnp.where(row == column, tiled, jnp.zeros((), tiled.dtype))


def diagonal_blocks(dense, span):
    width = dense.shape[0]
    column = (lax.broadcasted_iota(jnp.int32, (1, 2 * width), 1) % width) // span
    total = jnp.zeros((span, 2 * width), F32)
    for b in range(width // span):
        total = total + jnp.where(column == b, dense[b * span : (b + 1) * span], 0.0)
    return total


def per_device(
    dp, mp,
    inputs, lengths, cotangent, gains, rnn_params, rnn_in, branch_gate, recur_gate, input_gate,
    mlp_gate, mlp_up, rnn_out, mlp_down,
):
    count, part = inputs.shape
    width = rnn_in.shape[1]
    hidden_width = mlp_gate.shape[1]
    span = recur_gate.shape[0] * dp
    features = part * mp
    step = count // CHUNKS
    spot = lax.axis_index("mp") * part

    def cut(values):
        return [values[c * step : (c + 1) * step] for c in range(CHUNKS)]

    def mine(values):
        return lax.dynamic_slice_in_dim(values, spot, part, values.ndim - 1)

    gates = pair_gather(jnp.concatenate([recur_gate, input_gate], axis=1), "dp", dp)
    w_in = square_gather(jnp.concatenate([rnn_in, branch_gate], axis=1), "dp", dp)
    w_out = square_gather(after(rnn_out.T, w_in), "dp", dp)
    up = jnp.concatenate([mlp_gate, mlp_up], axis=1)
    down = mlp_down.T
    if dp != 8:
        up, down = square_gather(up, "dp", dp), square_gather(down, "dp", dp)

    in_parts = cut(inputs)
    wholes = []
    for c in range(CHUNKS):
        source = in_parts[c] if c == 0 else after(in_parts[c], wholes[-1])
        wholes.append(line_gather(source, "mp", mp))
    mask, live = make_masks(lengths[0], count)
    masks = cut(mask)
    mask_tail = jnp.concatenate([mask, jnp.zeros((8, LANES), F32)], axis=0)
    tail_masks = [mask_tail[c * step : (c + 1) * step + 8] for c in range(CHUNKS)]
    live = jnp.broadcast_to(live[:, None], (count, LANES)).astype(F32)
    dense = dense_gates(gates, width)

    blank = jnp.zeros((8, width), F32)
    halo, start = blank, blank
    halos, starts, boths, saves, mixes, norms, scales1 = [], [], [], [], [], [], []
    for c in range(CHUNKS):
        values = wholes[c].astype(F32)
        s1 = lax.rsqrt(jnp.mean(values * values, axis=1, keepdims=True) + EPS)
        normed = (values * s1 * gains[0]).astype(BF16)
        both = matmul(normed, w_in)
        mixed, conv, r, i, state, end = rnn_forward(
            both, halo, start, masks[c], dense, rnn_params
        )
        halos.append(halo)
        starts.append(start)
        halo, start = both[-8:, :width], end
        boths.append(both)
        saves.append((conv, r, i, state))
        mixes.append(mixed)
        norms.append(normed)
        scales1.append(s1)

    output, gm, gbo, local, hidden, pulled, normed2, grad_y, gain2 = middle(
        dp, mp, 4, jnp.concatenate(mixes), inputs, cotangent, live, gains, mine(gains), w_out,
        up, down,
    )
    gms, locals_ = cut(gm), cut(local)

    grad_up = square_scatter(
        inner_rows(normed2, pulled).astype(BF16), "dp", dp
    )
    grad_down = square_scatter(
        inner_rows(grad_y, hidden).astype(BF16), "dp", dp
    )
    grad_out = square_scatter(
        inner_rows(gbo, jnp.concatenate(mixes)).astype(BF16), "dp", dp
    )

    back, tail = blank, blank
    pulls, rates, grads_in = [None] * CHUNKS, [None] * CHUNKS, [None] * CHUNKS
    gain1_total, params_total = 0.0, 0.0
    for c in reversed(range(CHUNKS)):
        pull, rate, dparams, back, tail = rnn_backward(
            gms[c], boths[c], halos[c], starts[c], saves[c], tail_masks[c], dense, rnn_params,
            back, tail,
        )
        params_total = params_total + dparams
        pulls[c], rates[c] = pull, rate
        gn1_part = inner_cols(pull, w_in).astype(BF16)
        values = wholes[c].astype(F32)
        scaled = gn1_part.astype(F32) * values
        gain1_total = gain1_total + jnp.sum(scaled * scales1[c], axis=0)
        dots = jnp.sum(scaled * gains[0], axis=1).reshape(8, -1)
        mean = (line_sum(dots, "mp", mp) / features).reshape(-1, 1)
        gn1_mine = line_scatter(gn1_part, "mp", mp)
        s1 = scales1[c]
        grad = (
            locals_[c]
            + s1 * (gn1_mine * mine(gains[0]))
            - in_parts[c].astype(F32) * (s1 * s1 * s1 * mean)
        )
        grads_in[c] = grad.astype(BF16)

    grad_in = square_scatter(
        inner_rows(jnp.concatenate(norms), jnp.concatenate(pulls)).astype(BF16), "dp", dp
    )
    convs = jnp.concatenate([s[0] for s in saves]).astype(BF16)
    grad_gates = pair_scatter(
        diagonal_blocks(inner_rows(convs, jnp.concatenate(rates)), span), "dp", dp
    )
    grad_params = line_sum(params_total, "dp", dp)
    grad_gain1 = line_sum(line_sum(gain1_total.reshape(8, -1), "dp", dp), "mp", mp)
    grad_gain2 = line_sum(jnp.sum(gain2, axis=0).reshape(8, -1), "dp", dp)
    return (
        output,
        jnp.concatenate(grads_in),
        jnp.stack([grad_gain1.reshape(-1), grad_gain2.reshape(-1)]),
        grad_params,
        grad_in[:, :width],
        grad_in[:, width:],
        grad_gates[:, :width],
        grad_gates[:, width:],
        grad_up[:, :hidden_width],
        grad_up[:, hidden_width:],
        grad_out.T,
        grad_down.T,
    )


def solution(mesh):
    return jax.shard_map(
        functools.partial(per_device, mesh.shape["dp"], mesh.shape["mp"]),
        mesh=mesh,
        in_specs=(
            P("dp", "mp"),
            P("dp", None),
            P("dp", "mp"),
            P(),
            P(None, "mp"),
            P("dp", "mp"),
            P("dp", "mp"),
            P("dp", "mp"),
            P("dp", "mp"),
            P("dp", "mp"),
            P("dp", "mp"),
            P("mp", "dp"),
            P("mp", "dp"),
        ),
        out_specs=(
            P("dp", "mp"),
            P("dp", "mp"),
            P(),
            P(None, "mp"),
            P("dp", "mp"),
            P("dp", "mp"),
            P("dp", "mp"),
            P("dp", "mp"),
            P("dp", "mp"),
            P("dp", "mp"),
            P("mp", "dp"),
            P("mp", "dp"),
        ),
        check_vma=False,
    )
```

```python
import functools

import jax
import jax.numpy as jnp
from jax import lax
from jax.experimental import pallas as pl
from jax.experimental.pallas import tpu as pltpu
from jax.sharding import PartitionSpec as P

EPS = 1e-06
DECAY_SCALE = 8.0
ROOT_FLOOR = 0.0001
TAPS = 4
LANES = 8
CHUNKS = 1
TILE = 32
F32 = jnp.float32
BF16 = jnp.bfloat16
VMEM_BYTES = 56 * 1024 * 1024


def matmul(left, right):
    return jnp.dot(left, right, preferred_element_type=F32)


def inner_rows(left, right):
    return lax.dot_general(left, right, (((0,), (0,)), ((), ())), preferred_element_type=F32)


def inner_cols(left, right):
    return lax.dot_general(left, right, (((1,), (1,)), ((), ())), preferred_element_type=F32)


def gelu_and_slope(values):
    outer = 0.7978845608028654
    inner = 0.044715
    square = values * values
    bent = jnp.tanh(outer * values * (1.0 + inner * square))
    half = 0.5 * (1.0 + bent)
    slope = half + 0.5 * values * (1.0 - bent * bent) * outer * (1.0 + 3.0 * inner * square)
    return values * half, slope


def gelu(values):
    outer = 0.7978845608028654
    inner = 0.044715
    bent = jnp.tanh(outer * values * (1.0 + inner * values * values))
    return values * (0.5 * (1.0 + bent))


def one_less_exp(values):
    near = -values * (1.0 + 0.5 * values * (1.0 + (values / 3.0) * (1.0 + 0.25 * values)))
    return jnp.where(values > -0.02, near, 1.0 - jnp.exp(values))


def after(value, *earlier):
    return lax.optimization_barrier((value,) + earlier)[0]


def line_gather(mine, axis, size):
    place = lax.axis_index(axis)
    width = mine.shape[1]
    right, left = mine, mine
    rights, lefts = {}, {}
    for step in range(1, size):
        right = lax.ppermute(right, axis, [(i, i + 1) for i in range(step - 1, size - 1)])
        left = lax.ppermute(left, axis, [(i + 1, i) for i in range(size - step)])
        rights[step], lefts[step] = right, left
    whole = jnp.zeros((mine.shape[0], size * width), mine.dtype)
    for step in range(size):
        block = mine if step == 0 else lefts[step] + rights[size - step]
        spot = lax.rem(place + step, size) * width
        whole = lax.dynamic_update_slice_in_dim(whole, block, spot, 1)
    return whole


def line_scatter(part, axis, size):
    place = lax.axis_index(axis)
    width = part.shape[1] // size

    def block(index):
        spot = jnp.clip(index, 0, size - 1) * width
        return lax.dynamic_slice_in_dim(part, spot, width, 1).astype(F32)

    right, left = None, None
    for step in range(1, size):
        going = block(size - step + place)
        if right is not None:
            going = going + right.astype(F32)
        right = lax.ppermute(going.astype(BF16), axis, [(i, i + 1) for i in range(step)])
        going = block(place - (size - step))
        if left is not None:
            going = going + left.astype(F32)
        left = lax.ppermute(
            going.astype(BF16), axis, [(i, i - 1) for i in range(size - step, size)]
        )
    return block(place) + right.astype(F32) + left.astype(F32)


def line_sum(value, axis, size):
    bit = 1
    while bit < size:
        value = value + lax.ppermute(value, axis, [(i, i ^ bit) for i in range(size)])
        bit *= 2
    return value


def pair_gather(mine, axis, size):
    place = lax.axis_index(axis)
    bit = 1
    while bit < size:
        other = lax.ppermute(mine, axis, [(i, i ^ bit) for i in range(size)])
        upper = (place & bit) != 0
        mine = jnp.concatenate(
            [jnp.where(upper, other, mine), jnp.where(upper, mine, other)], axis=0
        )
        bit *= 2
    return mine


def pair_scatter(part, axis, size):
    place = lax.axis_index(axis)
    part = part.astype(F32)
    bit = size // 2
    while bit >= 1:
        upper = (place & bit) != 0
        low, high = jnp.split(part, 2, axis=0)
        going = jnp.where(upper, low, high).astype(BF16)
        came = lax.ppermute(going, axis, [(i, i ^ bit) for i in range(size)])
        part = jnp.where(upper, high, low) + came.astype(F32)
        bit //= 2
    return part


def swap(size, bit):
    return [(i, i ^ bit) for i in range(size)]


def cross(size):
    return [(i, i ^ 4 if i % 2 == 0 else i ^ 2) for i in range(size)]


def square_gather(mine, axis, size):
    if size != 8:
        return pair_gather(mine, axis, size)
    place = lax.axis_index(axis)
    rows = mine.shape[0]
    by_x = lax.ppermute(mine, axis, swap(size, 2))
    by_y = lax.ppermute(mine, axis, swap(size, 4))
    onward = jnp.where((place & 1) == 0, by_x, by_y)
    far = lax.ppermute(onward, axis, cross(size))
    held = {0: mine, 2: by_x, 4: by_y, 6: far}
    for bits in (0, 2, 4, 6):
        held[bits + 1] = lax.ppermute(held[bits], axis, swap(size, 1))
    whole = jnp.zeros((size * rows,) + mine.shape[1:], mine.dtype)
    for bits, block in held.items():
        whole = lax.dynamic_update_slice_in_dim(whole, block, (place ^ bits) * rows, 0)
    return whole


def square_scatter(part, axis, size):
    if size != 8:
        return pair_scatter(part, axis, size)
    place = lax.axis_index(axis)
    core = place & 1
    chip = lax.shift_right_logical(place, 1)
    split = part.reshape(size // 2, 2, part.shape[0] // size, part.shape[1])
    going = lax.dynamic_index_in_dim(split, 1 - core, 1, keepdims=False)
    came = lax.ppermute(going, axis, swap(size, 1))
    kept = lax.dynamic_index_in_dim(split, core, 1, keepdims=False)
    both = (kept.astype(F32) + came.astype(F32)).astype(BF16)

    def pick(index):
        return lax.dynamic_index_in_dim(both, index, 0, keepdims=False)

    far = lax.ppermute(pick(chip ^ 3), axis, cross(size)).astype(F32)
    none = jnp.zeros((), F32)
    to_x = pick(chip ^ 1).astype(F32) + jnp.where(core == 0, far, none)
    to_y = pick(chip ^ 2).astype(F32) + jnp.where(core == 1, far, none)
    by_x = lax.ppermute(to_x.astype(BF16), axis, swap(size, 2))
    by_y = lax.ppermute(to_y.astype(BF16), axis, swap(size, 4))
    return pick(chip).astype(F32) + by_x.astype(F32) + by_y.astype(F32)


def tile_loop(count, body):
    lax.fori_loop(0, count, lambda i, c: (body(i), c)[1], 0)


def rows_at(index, size):
    return pl.ds(pl.multiple_of(index * size, size), size)


def put(ref, rows, values):
    for j in range(ref.shape[0]):
        ref[j, rows, :] = values[:, j * 128 : (j + 1) * 128]


def get(ref, rows):
    return jnp.concatenate([ref[j, rows, :] for j in range(ref.shape[0])], axis=1)


def rnn_forward_kernel(
    both_ref, halo_ref, start_ref, mask_ref, gates_ref, params_ref,
    mixed_ref, conv_ref, r_ref, i_ref, state_ref, end_ref,
    padded, high, low, decay, drive,
):
    count, width = conv_ref.shape
    seg = count // 8
    tiles = count // TILE
    padded[0:8, :] = halo_ref[...]
    padded[8:, :] = both_ref[:, 0:width]

    def convolve(t):
        span = padded[pl.ds(pl.multiple_of(t * TILE, TILE), TILE + 8), :]
        mask = mask_ref[rows_at(t, TILE), :]
        conv = params_ref[0:1, :] * span[8:, :] + params_ref[TAPS : TAPS + 1, :]
        for k in range(1, TAPS):
            moved = span[8 - k : 8 - k + TILE, :]
            conv = conv + params_ref[k : k + 1, :] * (moved * mask[:, k : k + 1])
        conv_ref[rows_at(t, TILE), :] = conv
        top = conv.astype(BF16)
        high[rows_at(t, TILE), :] = top
        low[rows_at(t, TILE), :] = (conv - top.astype(F32)).astype(BF16)

    tile_loop(tiles, convolve)

    block = min(256, count)

    def gate(t):
        rows = rows_at(t, block)
        weights = gates_ref[...]
        both = jnp.dot(high[rows, :], weights, preferred_element_type=F32)
        both = both + jnp.dot(low[rows, :], weights, preferred_element_type=F32)
        r_ref[rows, :] = both[:, 0:width]
        i_ref[rows, :] = both[:, width:]

    tile_loop(count // block, gate)

    strength = DECAY_SCALE * jax.nn.softplus(-params_ref[TAPS + 3 : TAPS + 4, :])

    def prepare(t):
        rows = rows_at(t, TILE)
        keep = mask_ref[rows, :][:, 0:1]
        r = jax.nn.sigmoid(r_ref[rows, :] + params_ref[TAPS + 1 : TAPS + 2, :])
        i = jax.nn.sigmoid(i_ref[rows, :] + params_ref[TAPS + 2 : TAPS + 3, :])
        log_a = -strength * r
        scale = jnp.sqrt(jnp.maximum(one_less_exp(2.0 * log_a), ROOT_FLOOR))
        scale = jnp.where(keep > 0.0, scale, 1.0)
        put(decay, rows, jnp.exp(log_a) * keep)
        put(drive, rows, scale * i * conv_ref[rows, :])
        r_ref[rows, :] = r
        i_ref[rows, :] = i

    tile_loop(tiles, prepare)

    def scan(t, carry):
        held, prod = carry
        rows = pl.ds(t, 8, stride=seg)
        a = get(decay, rows)
        held = a * held + get(drive, rows)
        prod = a * prod
        put(drive, rows, held)
        put(decay, rows, prod)
        return held, prod

    shape = (8, width)
    held, prod = lax.fori_loop(0, seg, scan, (jnp.zeros(shape, F32), jnp.ones(shape, F32)))
    carry = start_ref[0:1, :]
    carries = []
    for s in range(8):
        carries.append(carry)
        carry = prod[s : s + 1, :] * carry + held[s : s + 1, :]
    end_ref[...] = jnp.broadcast_to(carry, shape)

    small = min(TILE, seg)
    for s in range(8):

        def finish(t, s=s):
            rows = pl.ds(pl.multiple_of(s * seg + t * small, small), small)
            state = get(drive, rows) + get(decay, rows) * carries[s]
            state_ref[rows, :] = state
            mixed_ref[rows, :] = (state * gelu(both_ref[rows, width:])).astype(BF16)

        tile_loop(seg // small, finish)


def rnn_forward(both, halo, start, mask, gates, params):
    count, width = both.shape[0], both.shape[1] // 2
    full = jax.ShapeDtypeStruct((count, width), F32)
    return pl.pallas_call(
        rnn_forward_kernel,
        out_shape=(
            jax.ShapeDtypeStruct((count, width), BF16),
            full, full, full, full,
            jax.ShapeDtypeStruct((8, width), F32),
        ),
        scratch_shapes=[
            pltpu.VMEM((count + 8, width), F32),
            pltpu.VMEM((count, width), BF16),
            pltpu.VMEM((count, width), BF16),
            pltpu.VMEM((width // 128, count, 128), F32),
            pltpu.VMEM((width // 128, count, 128), F32),
        ],
        compiler_params=pltpu.CompilerParams(vmem_limit_bytes=VMEM_BYTES),
        cost_estimate=pl.CostEstimate(
            flops=4 * count * width * 2 * width, bytes_accessed=count * width * 30,
            transcendentals=count * width * 6,
        ),
        name="rnn_forward",
    )(both, halo, start, mask, gates, params)


def rnn_backward_kernel(
    gm_ref, both_ref, halo_ref, start_ref, conv_ref, r_ref, i_ref, state_ref, mask_ref,
    gates_ref, params_ref, back_ref, tail_ref,
    grads_ref, rates_ref, dparams_ref, back_out_ref, tail_out_ref, dots_ref,
    padded, before, decay, adjoint, coef, dconv, sums,
):
    count, width = conv_ref.shape
    seg = count // 8
    tiles = count // TILE
    padded[0:8, :] = halo_ref[...]
    padded[8:, :] = both_ref[:, 0:width]
    before[0:8, :] = start_ref[...]
    before[8:, :] = state_ref[...]
    strength = DECAY_SCALE * jax.nn.softplus(-params_ref[TAPS + 3 : TAPS + 4, :])

    def prepare(t):
        rows = rows_at(t, TILE)
        keep = mask_ref[rows, :][:, 0:1]
        gm = gm_ref[rows, :]
        value, slope = gelu_and_slope(both_ref[rows, width:])
        put(adjoint, rows, gm * value)
        grads_ref[rows, width:] = (gm * state_ref[rows, :] * slope).astype(BF16)
        put(decay, rows, jnp.exp(-strength * r_ref[rows, :]) * keep)

    tile_loop(tiles, prepare)

    def scan(t, carry):
        held, prod = carry
        rows = pl.ds(seg - 1 - t, 8, stride=seg)
        a = get(decay, rows)
        total = get(adjoint, rows) + held
        put(adjoint, rows, total)
        put(coef, rows, prod)
        return a * total, a * prod

    shape = (8, width)
    held, prod = lax.fori_loop(0, seg, scan, (jnp.zeros(shape, F32), jnp.ones(shape, F32)))
    carry = back_ref[0:1, :]
    carries = [None] * 8
    for s in reversed(range(8)):
        carries[s] = carry
        carry = prod[s : s + 1, :] * carry + held[s : s + 1, :]
    back_out_ref[...] = jnp.broadcast_to(carry, shape)

    sums[...] = jnp.zeros_like(sums)

    def fold(values):
        return jnp.sum(values.reshape(-1, 8, width), axis=0)

    small = min(TILE, seg)
    for s in range(8):

        def chain(t, s=s):
            base = pl.multiple_of(s * seg + t * small, small)
            rows = pl.ds(base, small)
            keep = mask_ref[rows, :][:, 0:1]
            a = get(adjoint, rows) + get(coef, rows) * carries[s]
            r, i, conv = r_ref[rows, :], i_ref[rows, :], conv_ref[rows, :]
            fall = get(decay, rows)
            prior = before[pl.ds(base, small + 8), :][7 : 7 + small, :]
            room = one_less_exp(-2.0 * strength * r)
            bound = jnp.maximum(room, ROOT_FLOOR)
            inverse = lax.rsqrt(bound)
            live = keep > 0.0
            scale = jnp.where(live, bound * inverse, 1.0)
            open_ = jnp.where(room > ROOT_FLOOR, inverse, 0.0)
            driven = a * i
            dlog = fall * (a * prior - fall * driven * conv * open_)
            common = a * scale
            drec = dlog * (-strength) * r * (1.0 - r)
            dinp = common * conv * i * (1.0 - i)
            rates_ref[rows, 0:width] = drec.astype(BF16)
            rates_ref[rows, width:] = dinp.astype(BF16)
            dconv[rows, :] = common * i
            sums[5] += fold(drec)
            sums[6] += fold(dinp)
            sums[7] += fold(dlog * r)

        tile_loop(seg // small, chain)

    block = min(256, count)

    def spread(t):
        rows = rows_at(t, block)
        dconv[rows, :] += lax.dot_general(
            rates_ref[rows, :], gates_ref[...], (((1,), (1,)), ((), ())),
            preferred_element_type=F32,
        )

    tile_loop(count // block, spread)
    dconv[count:, :] = tail_ref[...]
    tail_out_ref[...] = dconv[0:8, :]

    def unconvolve(t):
        base = pl.multiple_of(t * TILE, TILE)
        rows = pl.ds(base, TILE)
        span = dconv[pl.ds(base, TILE + 8), :]
        mask = mask_ref[pl.ds(base, TILE + 8), :]
        source = padded[pl.ds(base, TILE + 8), :]
        here = span[0:TILE, :]
        out = params_ref[0:1, :] * here
        sums[0] += fold(here * source[8:, :])
        sums[4] += fold(here)
        for k in range(1, TAPS):
            kept = span * mask[:, k : k + 1]
            out = out + params_ref[k : k + 1, :] * kept[k : k + TILE, :]
            sums[k] += fold(kept[0:TILE, :] * source[8 - k : 8 - k + TILE, :])
        grads_ref[rows, 0:width] = out.astype(BF16)
        dot = jnp.sum(
            out * source[8:, :] + grads_ref[rows, width:].astype(F32) * both_ref[rows, width:],
            axis=1, keepdims=True,
        )
        dots_ref[rows, :] = jnp.broadcast_to(dot, (TILE, 128))

    tile_loop(tiles, unconvolve)
    for k in range(8):
        dparams_ref[k : k + 1, :] = jnp.sum(sums[k], axis=0, keepdims=True)
    dparams_ref[TAPS + 3 : TAPS + 4, :] = (
        DECAY_SCALE
        * jax.nn.sigmoid(-params_ref[TAPS + 3 : TAPS + 4, :])
        * jnp.sum(sums[TAPS + 3], axis=0, keepdims=True)
    )


def rnn_backward(gm, both, halo, start, saved, mask, gates, params, back, tail):
    conv, r, i, state = saved
    count, width = conv.shape
    return pl.pallas_call(
        rnn_backward_kernel,
        out_shape=(
            jax.ShapeDtypeStruct((count, 2 * width), BF16),
            jax.ShapeDtypeStruct((count, 2 * width), BF16),
            jax.ShapeDtypeStruct((8, width), F32),
            jax.ShapeDtypeStruct((8, width), F32),
            jax.ShapeDtypeStruct((8, width), F32),
            jax.ShapeDtypeStruct((count, 128), F32),
        ),
        scratch_shapes=[
            pltpu.VMEM((count + 8, width), F32),
            pltpu.VMEM((count + 8, width), F32),
            pltpu.VMEM((width // 128, count, 128), F32),
            pltpu.VMEM((width // 128, count, 128), F32),
            pltpu.VMEM((width // 128, count, 128), F32),
            pltpu.VMEM((count + 8, width), F32),
            pltpu.VMEM((8, 8, width), F32),
        ],
        compiler_params=pltpu.CompilerParams(vmem_limit_bytes=VMEM_BYTES),
        cost_estimate=pl.CostEstimate(
            flops=2 * count * width * 2 * width, bytes_accessed=count * width * 36,
            transcendentals=count * width * 6,
        ),
        name="rnn_backward",
    )(gm, both, halo, start, conv, r, i, state, mask, gates, params, back, tail)


MESH = pl.DeviceIdType.MESH


class Spread:
    def __init__(self, place, size, blocks, sent, came):
        self.place, self.size = place, size
        self.blocks, self.sent, self.came = blocks, sent, came

    def copy(self, slot, j, way, k):
        ref = self.blocks.at[slot, j]
        return pltpu.make_async_remote_copy(
            src_ref=ref, dst_ref=ref, send_sem=self.sent.at[slot, k],
            recv_sem=self.came.at[slot, j], device_id={"mp": self.place + way},
            device_id_type=MESH,
        )

    def moves(self, s):
        z, n = self.place, self.size
        return (
            ((z - s >= 0) & (z < n - 1), z - s, 1, 2 * s),
            ((z + s <= n - 1) & (z > 0), z + s, -1, 2 * s + 1),
        )

    def step(self, slot, s):
        for valid, j, way, k in self.moves(s):

            @pl.when(valid)
            def _(j=j, way=way, k=k):
                copy = self.copy(slot, j, way, k)
                if s > 0:
                    copy.wait_recv()
                copy.start()

    def finish(self, slot):
        z, n = self.place, self.size

        @pl.when(z == 0)
        def _():
            for j in range(1, n):
                self.copy(slot, j, 1, 0).wait_recv()

        @pl.when(z == n - 1)
        def _():
            for j in range(n - 1):
                self.copy(slot, j, -1, 0).wait_recv()

    def drain(self, slot):
        for s in range(self.size - 1):
            for valid, j, way, k in self.moves(s):

                @pl.when(valid)
                def _(j=j, way=way, k=k):
                    self.copy(slot, j, way, k).wait_send()


class Fold:
    def __init__(self, place, size, parts, rights, lefts, sent, came_right, came_left):
        self.place, self.size = place, size
        self.parts, self.rights, self.lefts = parts, rights, lefts
        self.sent, self.came_right, self.came_left = sent, came_right, came_left

    def right(self, slot, j, k):
        return pltpu.make_async_remote_copy(
            src_ref=self.parts.at[slot, j], dst_ref=self.rights.at[slot, k],
            send_sem=self.sent.at[slot, j], recv_sem=self.came_right.at[slot, k],
            device_id={"mp": self.place + 1}, device_id_type=MESH,
        )

    def left(self, slot, j, k):
        return pltpu.make_async_remote_copy(
            src_ref=self.parts.at[slot, j], dst_ref=self.lefts.at[slot, k],
            send_sem=self.sent.at[slot, j], recv_sem=self.came_left.at[slot, k],
            device_id={"mp": self.place - 1}, device_id_type=MESH,
        )

    def clear(self):
        for slot in range(self.parts.shape[0]):
            last = self.size - 2
            blank = jnp.zeros(self.rights.shape[2:], BF16)
            self.rights[slot, last] = blank
            self.lefts[slot, last] = blank

    def start(self, slot):
        z, n = self.place, self.size

        @pl.when(z == 0)
        def _():
            for j in reversed(range(1, n)):
                self.right(slot, j, n - 1 - j).start()

        @pl.when(z == n - 1)
        def _():
            for j in range(n - 1):
                self.left(slot, j, j).start()

    def step(self, slot, s):
        z, n = self.place, self.size
        back = n - 1 - z

        @pl.when((z >= 1) & (z <= n - 2) & (s >= z))
        def _():
            j = n - 1 + z - s
            self.right(slot, j, s - 1).wait_recv()
            self.add(slot, j, self.rights, s - 1)
            self.right(slot, j, s).start()

        @pl.when((back >= 1) & (back <= n - 2) & (s >= back))
        def _():
            j = s - back
            self.left(slot, j, s - 1).wait_recv()
            self.add(slot, j, self.lefts, s - 1)
            self.left(slot, j, s).start()

    def add(self, slot, j, came, k):
        self.parts[slot, j] = (
            self.parts[slot, j].astype(F32) + came[slot, k].astype(F32)
        ).astype(BF16)

    def finish(self, slot):
        z, n = self.place, self.size

        @pl.when(z >= 1)
        def _():
            self.right(slot, z, n - 2).wait_recv()

        @pl.when(z <= n - 2)
        def _():
            self.left(slot, z, n - 2).wait_recv()

    def total(self, slot, rows):
        z, n = self.place, self.size
        return (
            self.parts[slot, z, rows, :].astype(F32)
            + self.rights[slot, n - 2, rows, :].astype(F32)
            + self.lefts[slot, n - 2, rows, :].astype(F32)
        )

    def drain(self, slot):
        for j in range(self.size):

            @pl.when(j != self.place)
            def _(j=j):
                self.right(slot, j, 0).wait_send()


def partners(d):
    core, x, y = lax.rem(d, 2), lax.rem(lax.div(d, 2), 2), lax.div(d, 4)
    return core, d + 1 - 2 * core, d + 2 - 4 * x, d + 4 - 8 * y


class Square:
    def __init__(self, d, shard, whole, sent, came, own):
        self.d, self.shard, self.whole = d, shard, whole
        self.sent, self.came, self.own = sent, came, own
        self.core, self.by_core, self.by_x, self.by_y = partners(d)

    def rows(self, d):
        count = self.shard.shape[0]
        return self.whole.at[pl.ds(pl.multiple_of(d * count, count), count), :]

    def copy(self, src, origin, target, sent, came):
        return pltpu.make_async_remote_copy(
            src_ref=src, dst_ref=self.rows(origin), send_sem=self.sent.at[sent],
            recv_sem=self.came.at[came], device_id={"dp": target}, device_id_type=MESH,
        )

    def local(self):
        return pltpu.make_async_copy(self.shard, self.rows(self.d), self.own)

    def far(self):
        return partners(self.by_x)[3]

    def first(self):
        return (
            self.copy(self.shard, self.d, self.by_x, 0, 2),
            self.copy(self.shard, self.d, self.by_y, 1, 4),
            self.copy(self.shard, self.d, self.by_core, 2, 1),
        )

    def start(self):
        for copy in self.first():
            copy.start()
        self.local().start()

    def step_one(self):
        x_rows, y_rows = self.rows(self.by_x), self.rows(self.by_y)
        by_x = self.copy(x_rows, self.by_x, self.by_core, 3, 2)
        by_y = self.copy(y_rows, self.by_y, self.by_core, 4, 4)
        by_x.wait_recv()

        @pl.when(self.core == 0)
        def _():
            self.copy(x_rows, self.by_x, self.by_y, 5, 6).start()

        self.copy(x_rows, self.by_x, self.by_core, 3, 3).start()
        by_y.wait_recv()

        @pl.when(self.core == 1)
        def _():
            self.copy(y_rows, self.by_y, self.by_x, 5, 6).start()

        self.copy(y_rows, self.by_y, self.by_core, 4, 5).start()

    def step_two(self):
        far = self.far()
        rows = self.rows(far)
        self.copy(rows, far, self.by_core, 6, 6).wait_recv()
        self.copy(rows, far, self.by_core, 6, 7).start()

    def finish(self):
        for k in (1, 3, 5, 7):
            self.copy(self.shard, self.d, self.by_core, 0, k).wait_recv()
        self.local().wait()

    def drain(self):
        for k in range(7):
            self.copy(self.shard, self.d, self.by_core, k, 0).wait_send()


def head_kernel(dp, mp, names, *refs):
    ref = dict(zip(names, refs))
    blocks, w_in, norm, both = ref["blocks"], ref["w_in_here"], ref["norm"], ref["both_here"]
    chunks, _, step, part = blocks.shape
    features, width = part * mp, ref["mixed_here"].shape[2]
    z, d = lax.axis_index("mp"), lax.axis_index("dp")
    square = dp == 8
    gather = Spread(z, mp, blocks, ref["spread_sent"], ref["spread_came"])

    barrier = pltpu.get_barrier_semaphore()

    @pl.when(z > 0)
    def _():
        pl.semaphore_signal(barrier, inc=1, device_id={"mp": z - 1}, device_id_type=MESH)

    @pl.when(z < mp - 1)
    def _():
        pl.semaphore_signal(barrier, inc=1, device_id={"mp": z + 1}, device_id_type=MESH)

    count = jnp.where((z > 0) & (z < mp - 1), 2, 1)
    if square:
        for other in partners(d)[1:]:
            pl.semaphore_signal(barrier, inc=1, device_id={"dp": other}, device_id_type=MESH)
        count = count + 3

    def chunk_rows(c):
        return pl.ds(c * step, step)

    def own_block(c):
        return pltpu.make_async_copy(
            ref["x"].at[chunk_rows(c), :], blocks.at[c, z], ref["load_sem"].at[c]
        )

    for c in range(chunks):
        own_block(c).start()
    pl.semaphore_wait(barrier, count)

    wholes = (("gates_shard", ref["gates_here"]), ("in_shard", w_in), ("out_shard", ref["w_out"]))
    if square:
        squares = [
            Square(
                d, ref[name], whole, ref["square_sent"].at[k], ref["square_came"].at[k],
                ref["square_own"].at[k],
            )
            for k, (name, whole) in enumerate(wholes)
        ]
        for item in squares:
            item.start()
    else:
        loads = [
            pltpu.make_async_copy(ref[name], whole, ref["square_own"].at[k])
            for k, (name, whole) in enumerate(wholes)
        ]
        for item in loads:
            item.start()

    def begin(c):
        own_block(c).wait()
        gather.step(c, 0)

    begin(0)
    if chunks > 1:
        begin(1)

    def expand():
        span = ref["gates_flat"].shape[0]
        rows = span // 8
        for k in range(8):
            ref["gates_flat"][k * rows : (k + 1) * rows, :] = ref["gates_here"][
                k * 32 : k * 32 + 32, :
            ].astype(F32)[0:rows, :]
        column = lax.broadcasted_iota(jnp.int32, (span, 2 * width), 1)
        column = jnp.where(column >= width, column - width, column)
        for b in range(width // span):
            inside = (column >= b * span) & (column < (b + 1) * span)
            ref["dense_here"][b * span : (b + 1) * span, :] = jnp.where(
                inside, ref["gates_flat"][...], 0.0
            ).astype(BF16)

    stores = (
        ("norm", "norm"), ("both", "both_here"), ("conv", "conv_here"), ("r", "r_here"),
        ("i", "i_here"), ("state", "state_here"), ("mixed", "mixed_here"), ("s1", "s1_here"),
    )

    def store_all(c):
        return [
            pltpu.make_async_copy(
                ref[near].at[c % 2], ref[far + "_out"].at[chunk_rows(c), :],
                ref["store_sem"].at[c % 2, k],
            )
            for k, (far, near) in enumerate(stores)
        ]

    ref["halo"][...] = jnp.zeros_like(ref["halo"])
    ref["start"][...] = jnp.zeros_like(ref["start"])

    def compute(c):
        slot = c % 2
        if c > 1:
            for copy in store_all(c - 2):
                copy.wait()

        def body(t):
            rows = rows_at(t, TILE)
            values = [blocks[c, j, rows, :].astype(F32) for j in range(mp)]
            total = sum(jnp.sum(v * v, axis=1, keepdims=True) for v in values)
            s1 = lax.rsqrt(total / features + EPS)
            for j in range(mp):
                cols = slice(j * part, (j + 1) * part)
                norm[slot, rows, cols] = (values[j] * s1 * ref["gains"][0:1, cols]).astype(BF16)
            ref["s1_here"][slot, rows, :] = jnp.broadcast_to(s1, (TILE, 128))

        tile_loop(step // TILE, body)
        for k in range(2):
            cols = slice(k * width, (k + 1) * width)
            both[slot, :, cols] = matmul(norm[slot], w_in[:, cols])
        rnn_forward_kernel(
            both.at[slot], ref["halo"], ref["start"], ref["mask"].at[chunk_rows(c), :],
            ref["dense_here"], ref["params"],
            ref["mixed_here"].at[slot], ref["conv_here"].at[slot], ref["r_here"].at[slot],
            ref["i_here"].at[slot], ref["state_here"].at[slot], ref["end"],
            ref["padded"], ref["high"], ref["low"], ref["decay"], ref["drive"],
        )
        ref["halo"][...] = both[slot, step - 8 :, 0:width]
        ref["start"][...] = ref["end"][...]
        for copy in store_all(c):
            copy.start()

    for s in range(1, mp - 1):
        gather.step(0, s)
        if s == 1 and chunks > 2:
            begin(2)
    if square:
        for item in squares[:2]:
            item.step_one()
        for item in squares[:2]:
            item.step_two()
    gather.finish(0)
    for c in range(chunks):
        if c + 1 < chunks:
            gather.step(c + 1, 1)
        if c == 0:
            if square:
                for item in squares[:2]:
                    item.finish()
                squares[2].step_one()
            else:
                for item in loads:
                    item.wait()
            expand()
            pass_on = [
                pltpu.make_async_copy(w_in, ref["w_in"], ref["pass_sem"].at[0]),
                pltpu.make_async_copy(ref["dense_here"], ref["dense"], ref["pass_sem"].at[1]),
            ]
            for copy in pass_on:
                copy.start()
        if c == 1 and square:
            squares[2].step_two()
        compute(c)
        if c + 3 < chunks:
            begin(c + 3)
        if c + 1 < chunks:
            for s in range(2, mp - 1):
                gather.step(c + 1, s)
            gather.finish(c + 1)
    if square:
        squares[2].finish()
        for item in squares:
            item.drain()
    for copy in pass_on:
        copy.wait()
    for c in range(max(0, chunks - 2), chunks):
        for copy in store_all(c):
            copy.wait()
    for c in range(chunks):
        gather.drain(c)


def head(dp, mp, chunks, x, gains, params, mask, in_shard, out_shard, gates_shard, span):
    count, part = x.shape
    features, width = part * mp, params.shape[1]
    step = count // chunks
    dma = pltpu.SemaphoreType.DMA
    any_, vmem = pl.BlockSpec(memory_space=pl.ANY), pl.BlockSpec(memory_space=pltpu.VMEM)
    ins = [
        ("x", x, any_), ("gains", gains, vmem), ("params", params, vmem), ("mask", mask, vmem),
        ("in_shard", in_shard, any_), ("out_shard", out_shard, any_),
        ("gates_shard", gates_shard, any_),
    ]
    shape = jax.ShapeDtypeStruct
    outs = [
        ("w_in", shape((features, 2 * width), BF16)), ("w_out", shape((features, width), BF16)),
        ("dense", shape((width, 2 * width), BF16)), ("norm_out", shape((count, features), BF16)),
        ("both_out", shape((count, 2 * width), F32)), ("conv_out", shape((count, width), F32)),
        ("r_out", shape((count, width), F32)), ("i_out", shape((count, width), F32)),
        ("state_out", shape((count, width), F32)), ("mixed_out", shape((count, width), BF16)),
        ("s1_out", shape((count, 128), F32)),
    ]
    wide = pltpu.VMEM((2, step, width), F32)
    columns = pltpu.VMEM((width // 128, step, 128), F32)
    scratch = [
        ("blocks", pltpu.VMEM((chunks, mp, step, part), BF16)),
        ("w_in_here", pltpu.VMEM((features, 2 * width), BF16)),
        ("gates_here", pltpu.VMEM((256, 2 * width), BF16)),
        ("gates_flat", pltpu.VMEM((span, 2 * width), F32)),
        ("dense_here", pltpu.VMEM((width, 2 * width), BF16)),
        ("norm", pltpu.VMEM((2, step, features), BF16)),
        ("both_here", pltpu.VMEM((2, step, 2 * width), F32)),
        ("conv_here", wide), ("r_here", wide), ("i_here", wide), ("state_here", wide),
        ("mixed_here", pltpu.VMEM((2, step, width), BF16)),
        ("s1_here", pltpu.VMEM((2, step, 128), F32)),
        ("halo", pltpu.VMEM((8, width), F32)), ("start", pltpu.VMEM((8, width), F32)),
        ("end", pltpu.VMEM((8, width), F32)),
        ("padded", pltpu.VMEM((step + 8, width), F32)),
        ("high", pltpu.VMEM((step, width), BF16)), ("low", pltpu.VMEM((step, width), BF16)),
        ("decay", columns), ("drive", columns),
        ("spread_sent", dma((chunks, 2 * mp))), ("spread_came", dma((chunks, mp))),
        ("square_sent", dma((3, 8))), ("square_came", dma((3, 8))), ("square_own", dma((3,))),
        ("load_sem", dma((chunks,))), ("store_sem", dma((2, 8))), ("pass_sem", dma((2,))),
    ]
    names = [i[0] for i in ins] + [o[0] for o in outs] + [k[0] for k in scratch]
    return pl.pallas_call(
        functools.partial(head_kernel, dp, mp, tuple(names)),
        in_specs=[i[2] for i in ins],
        out_specs=[any_] * len(outs),
        out_shape=[o[1] for o in outs],
        scratch_shapes=[k[1] for k in scratch],
        compiler_params=pltpu.CompilerParams(
            collective_id=2, has_side_effects=True, vmem_limit_bytes=60 * 1024 * 1024
        ),
        name="head",
    )(*[i[1] for i in ins])


def middle_kernel(dp, mp, chunks, *refs):
    (
        mixed_ref, x_ref, cot_ref, live_ref, gains_ref, mine_ref, wout_ref, up_ref, down_ref,
        output_ref, gm_ref, gbo_ref, local_ref, hidden_ref, pulled_ref, norm_ref, grady_ref,
        gain_ref,
        w_up, w_down, cots, mids, gn2s, mid_mine, gn2_mine,
        parts1, rights1, lefts1, parts2, rights2, lefts2, parts3, rights3, lefts3,
        norm, hidden, pulled, gbo, gm, local, out,
        spread_sent, spread_came, fold_sent, fold_right, fold_left,
        square_sent, square_came, square_own, load_sem, store_sem,
    ) = refs
    step, part = x_ref.shape[0] // chunks, x_ref.shape[1]
    features = part * mp
    hidden_width = w_down.shape[1]
    z, d = lax.axis_index("mp"), lax.axis_index("dp")
    square = dp == 8

    folds = [
        Fold(z, mp, p, r, l, fold_sent.at[k], fold_right.at[k], fold_left.at[k])
        for k, (p, r, l) in enumerate(
            ((parts1, rights1, lefts1), (parts2, rights2, lefts2), (parts3, rights3, lefts3))
        )
    ]
    rs1, rs2, rs3 = folds
    ag2, ag3, ag4 = [
        Spread(z, mp, b, spread_sent.at[k], spread_came.at[k])
        for k, b in enumerate((cots, mids, gn2s))
    ]
    for fold in folds:
        fold.clear()

    barrier = pltpu.get_barrier_semaphore()

    @pl.when(z > 0)
    def _():
        pl.semaphore_signal(barrier, inc=1, device_id={"mp": z - 1}, device_id_type=MESH)

    @pl.when(z < mp - 1)
    def _():
        pl.semaphore_signal(barrier, inc=1, device_id={"mp": z + 1}, device_id_type=MESH)

    count = jnp.where((z > 0) & (z < mp - 1), 2, 1)
    if square:
        for other in partners(d)[1:]:
            pl.semaphore_signal(barrier, inc=1, device_id={"dp": other}, device_id_type=MESH)
        count = count + 3
    pl.semaphore_wait(barrier, count)

    if square:
        squares = [
            Square(d, up_ref, w_up, square_sent.at[0], square_came.at[0], square_own.at[0]),
            Square(d, down_ref, w_down, square_sent.at[1], square_came.at[1], square_own.at[1]),
        ]
        for item in squares:
            item.start()
    else:
        loads = [
            pltpu.make_async_copy(up_ref, w_up, square_own.at[0]),
            pltpu.make_async_copy(down_ref, w_down, square_own.at[1]),
        ]
        for item in loads:
            item.start()

    def chunk_rows(c):
        return pl.ds(c * step, step)

    def store(buffer, target, c, k):
        return pltpu.make_async_copy(buffer, target.at[chunk_rows(c), :], store_sem.at[k])

    def own_cot(c):
        return pltpu.make_async_copy(cot_ref.at[chunk_rows(c), :], cots.at[c, z], load_sem.at[c])

    for c in range(chunks):
        own_cot(c).start()

    gain_ref[...] = jnp.zeros_like(gain_ref)
    tiles = step // TILE

    def fill(fold, slot, left, weights):
        def body(j):
            rows = pl.ds(pl.multiple_of(j * part, part), part)
            fold.parts[slot, j] = inner_cols(left, weights[rows, :]).astype(BF16)

        tile_loop(mp, body)

    def branch(c):
        fill(rs1, c % 2, mixed_ref[chunk_rows(c), :], wout_ref)

    def join(c):
        def body(t):
            rows = rows_at(t, TILE)
            base = pl.ds(pl.multiple_of(c * step + t * TILE, TILE), TILE)
            total = x_ref[base, :].astype(F32) + rs1.total(c % 2, rows)
            mid_mine[c, rows, :] = total
            mids[c, z, rows, :] = total.astype(BF16)

        tile_loop(tiles, body)

    def stats(c, rows):
        blocks = [mids[c, j, rows, :].astype(F32) for j in range(mp)]
        square_sum = sum(jnp.sum(b * b, axis=1, keepdims=True) for b in blocks)
        return blocks, lax.rsqrt(square_sum / features + EPS)

    def block_cols(j):
        return slice(j * part, (j + 1) * part)

    def normalise(c):
        def body(t):
            rows = rows_at(t, TILE)
            base = pl.ds(pl.multiple_of(c * step + t * TILE, TILE), TILE)
            blocks, s2 = stats(c, rows)
            live = live_ref[base, :][:, 0:1]
            for j in range(mp):
                norm[rows, block_cols(j)] = (
                    blocks[j] * s2 * gains_ref[1:2, block_cols(j)]
                ).astype(BF16)
                cots[c, j, rows, :] = (cots[c, j, rows, :].astype(F32) * live).astype(BF16)

        tile_loop(tiles, body)

    def grad_y_copies(c):
        return [
            pltpu.make_async_copy(
                cots.at[c, j], grady_ref.at[chunk_rows(c), pl.ds(j * part, part)],
                store_sem.at[8 + j],
            )
            for j in range(mp)
        ]

    def mlp_first(c):
        if c > 0:
            store(norm, norm_ref, c, 0).wait()
            store(hidden, hidden_ref, c, 1).wait()
            store(pulled, pulled_ref, c, 2).wait()
            for copy in grad_y_copies(c - 1):
                copy.wait()
        ag2.drain(c)
        normalise(c)
        store(norm, norm_ref, c, 0).start()
        for copy in grad_y_copies(c):
            copy.start()
        size = 256

        def body(t):
            near = pl.ds(pl.multiple_of(t * size, size), size)
            off = pl.ds(pl.multiple_of(hidden_width + t * size, size), size)
            gate = matmul(norm[...], w_up[:, near])
            up = matmul(norm[...], w_up[:, off])
            grad = sum(
                matmul(cots[c, j], w_down[block_cols(j), near]) for j in range(mp)
            )
            value, slope = gelu_and_slope(gate)
            hidden[:, near] = (value * up).astype(BF16)
            pulled[:, near] = (grad * up * slope).astype(BF16)
            pulled[:, off] = (grad * value).astype(BF16)

        tile_loop(hidden_width // size, body)
        store(hidden, hidden_ref, c, 1).start()
        store(pulled, pulled_ref, c, 2).start()

    def mlp_second(c):
        slot = c % 2
        if c > 1:
            rs3.drain(slot)
        fill(rs3, slot, pulled[...], w_up)
        rs3.start(slot)

    def mlp_third(c):
        slot = c % 2
        if c > 1:
            rs2.drain(slot)
        fill(rs2, slot, hidden[...], w_down)

    def gather_grad(c):
        slot = c % 2

        def body(t):
            rows = rows_at(t, TILE)
            total = rs3.total(slot, rows)
            gn2_mine[slot, rows, :] = total
            gn2s[slot, z, rows, :] = total.astype(BF16)

        tile_loop(tiles, body)
        ag4.step(slot, 0)

    def norm_back(c):
        slot = c % 2
        if c > 0:
            store(gbo, gbo_ref, c, 3).wait()
            store(local, local_ref, c, 4).wait()
            store(gm, gm_ref, c, 5).wait()

        def body(t):
            rows = rows_at(t, TILE)
            blocks, s2 = stats(c, rows)
            grads = [gn2s[slot, j, rows, :].astype(F32) for j in range(mp)]
            scaled = [grads[j] * gains_ref[1:2, block_cols(j)] for j in range(mp)]
            mean = (
                sum(jnp.sum(scaled[j] * blocks[j], axis=1, keepdims=True) for j in range(mp))
                / features
            )
            fall = s2 * s2 * s2 * mean
            for j in range(mp):
                grad_y = cots[c, j, rows, :].astype(F32)
                gbo[rows, block_cols(j)] = (
                    grad_y + s2 * scaled[j] - blocks[j] * fall
                ).astype(BF16)
                gain_ref[:, block_cols(j)] += jnp.sum(
                    (grads[j] * (blocks[j] * s2)).reshape(-1, 8, part), axis=0
                )
            local[rows, :] = (
                cots[c, z, rows, :].astype(F32)
                + s2 * (gn2_mine[slot, rows, :] * mine_ref[1:2, :])
                - mid_mine[c, rows, :] * fall
            )

        tile_loop(tiles, body)
        gm[...] = matmul(gbo[...], wout_ref[...])
        store(gbo, gbo_ref, c, 3).start()
        store(local, local_ref, c, 4).start()
        store(gm, gm_ref, c, 5).start()

    def make_output(c):
        if c > 0:
            store(out, output_ref, c, 6).wait()

        def body(t):
            rows = rows_at(t, TILE)
            out[rows, :] = (mid_mine[c, rows, :] + rs2.total(c % 2, rows)).astype(BF16)

        tile_loop(tiles, body)
        store(out, output_ref, c, 6).start()

    def has(c):
        return 0 <= c < chunks

    for r in range(chunks + 3):
        if has(r):
            if r > 1:
                rs1.drain(r % 2)
            branch(r)
            rs1.start(r % 2)
            own_cot(r).wait()
        if has(r - 1):
            ag3.step(r - 1, 0)
        if has(r):
            ag2.step(r, 0)
        if has(r - 3):
            gather_grad(r - 3)
            rs2.start((r - 3) % 2)
        if r == 0 and square:
            squares[0].step_one()
        if r == 1 and square:
            squares[1].step_one()
        if r == 2:
            if square:
                squares[0].step_two()
                squares[1].step_two()
                for item in squares:
                    item.finish()
            else:
                for item in loads:
                    item.wait()
        if has(r - 2):
            mlp_first(r - 2)
        for s in range(1, mp - 1):
            if has(r):
                rs1.step(r % 2, s)
            if has(r - 1):
                ag3.step(r - 1, s)
            if has(r - 3):
                ag4.step((r - 3) % 2, s)
            if has(r):
                ag2.step(r, s)
            if has(r - 3):
                rs2.step((r - 3) % 2, s)
            if s == 1 and has(r - 2):
                mlp_second(r - 2)
        if has(r):
            rs1.finish(r % 2)
            join(r)
        if has(r - 1):
            ag3.finish(r - 1)
        if has(r):
            ag2.finish(r)
        if has(r - 2):
            rs3.step((r - 2) % 2, 1)
            mlp_third(r - 2)
        if has(r - 3):
            ag4.finish((r - 3) % 2)
            norm_back(r - 3)
            ag4.drain((r - 3) % 2)
        if has(r - 2):
            for s in range(2, mp - 1):
                rs3.step((r - 2) % 2, s)
        if has(r - 3):
            rs2.finish((r - 3) % 2)
            make_output(r - 3)
        if has(r - 2):
            rs3.finish((r - 2) % 2)

    last = chunks - 1
    for k, (buffer, target) in enumerate(
        (
            (norm, norm_ref), (hidden, hidden_ref), (pulled, pulled_ref), (gbo, gbo_ref),
            (local, local_ref), (gm, gm_ref), (out, output_ref),
        )
    ):
        store(buffer, target, last, k).wait()
    for copy in grad_y_copies(last):
        copy.wait()
    for c in range(chunks):
        ag3.drain(c)
    for slot in range(2):
        for fold in folds:
            fold.drain(slot)
    if square:
        for item in squares:
            item.drain()


def middle(dp, mp, chunks, mixed, inputs, cotangent, live, gains, mine, w_out, up, down):
    count, part = inputs.shape
    width, hidden_width = mixed.shape[1], down.shape[1]
    step, features = count // chunks, part * mp

    def fold_buffers():
        return [
            pltpu.VMEM((2, mp, step, part), BF16),
            pltpu.VMEM((2, mp - 1, step, part), BF16),
            pltpu.VMEM((2, mp - 1, step, part), BF16),
        ]

    dma = pltpu.SemaphoreType.DMA
    any_, vmem = pl.BlockSpec(memory_space=pl.ANY), pl.BlockSpec(memory_space=pltpu.VMEM)
    return pl.pallas_call(
        functools.partial(middle_kernel, dp, mp, chunks),
        in_specs=[vmem, vmem, any_, vmem, vmem, vmem, vmem, any_, any_],
        out_specs=[any_] * 8 + [vmem],
        out_shape=(
            jax.ShapeDtypeStruct((count, part), BF16),
            jax.ShapeDtypeStruct((count, width), F32),
            jax.ShapeDtypeStruct((count, features), BF16),
            jax.ShapeDtypeStruct((count, part), F32),
            jax.ShapeDtypeStruct((count, hidden_width), BF16),
            jax.ShapeDtypeStruct((count, 2 * hidden_width), BF16),
            jax.ShapeDtypeStruct((count, features), BF16),
            jax.ShapeDtypeStruct((count, features), BF16),
            jax.ShapeDtypeStruct((8, features), F32),
        ),
        scratch_shapes=[
            pltpu.VMEM((features, 2 * hidden_width), BF16),
            pltpu.VMEM((features, hidden_width), BF16),
            pltpu.VMEM((chunks, mp, step, part), BF16),
            pltpu.VMEM((chunks, mp, step, part), BF16),
            pltpu.VMEM((2, mp, step, part), BF16),
            pltpu.VMEM((chunks, step, part), F32),
            pltpu.VMEM((2, step, part), F32),
        ]
        + fold_buffers() + fold_buffers() + fold_buffers()
        + [
            pltpu.VMEM((step, features), BF16),
            pltpu.VMEM((step, hidden_width), BF16),
            pltpu.VMEM((step, 2 * hidden_width), BF16),
            pltpu.VMEM((step, features), BF16),
            pltpu.VMEM((step, width), F32),
            pltpu.VMEM((step, part), F32),
            pltpu.VMEM((step, part), BF16),
            dma((3, chunks, 2 * mp)),
            dma((3, chunks, mp)),
            dma((3, 2, mp)),
            dma((3, 2, mp)),
            dma((3, 2, mp)),
            dma((2, 8)),
            dma((2, 8)),
            dma((2,)),
            dma((chunks,)),
            dma((12,)),
        ],
        compiler_params=pltpu.CompilerParams(
            collective_id=0, has_side_effects=True, vmem_limit_bytes=62 * 1024 * 1024
        ),
        name="middle",
    )(mixed, inputs, cotangent, live, gains, mine, w_out, up, down)


class Scatter:
    def __init__(self, d, count, compute, held, far, first, second, sent, came):
        self.d, self.count, self.compute = d, count, compute
        self.held, self.far_in, self.first_in, self.second_in = held, far, first, second
        self.sent, self.came = sent, came
        self.core, self.by_core, by_x, by_y = partners(d)
        even = self.core == 0
        self.first = jnp.where(even, by_y, by_x)
        self.second = jnp.where(even, by_x, by_y)
        self.first_at, self.second_at = 2 - self.core, 1 + self.core
        other = partners(self.by_core)
        self.away = (self.by_core, other[2], other[3], partners(other[2])[3])
        self.distant = partners(by_x)[3]

    def copy(self, src, dst, target, sent, came):
        return pltpu.make_async_remote_copy(
            src_ref=src, dst_ref=dst, send_sem=self.sent.at[sent], recv_sem=self.came.at[came],
            device_id={"dp": target}, device_id_type=MESH,
        )

    def to_core(self, buffer, k):
        return self.copy(buffer, self.held.at[k], self.by_core, k, k)

    def to_far(self):
        return self.copy(self.held.at[3], self.far_in, self.first, 4, 4)

    def to_first(self):
        return self.copy(self.held.at[self.first_at], self.first_in, self.first, 5, 5)

    def to_second(self):
        return self.copy(self.held.at[self.second_at], self.second_in, self.second, 6, 6)

    def add_block(self, k, owner):
        self.copy(self.held.at[k], self.held.at[k], self.by_core, k, k).wait_recv()
        self.compute(owner, self.held.at[k], True)

    def near_core(self):
        self.add_block(3, self.distant)
        self.to_far().start()
        self.add_block(self.first_at, self.first)
        self.to_first().start()
        self.add_block(0, self.d)
        self.add_block(self.second_at, self.second)

    def onward(self):
        self.to_far().wait_recv()
        at = self.second_at

        def body(t):
            rows = rows_at(t, 16)
            self.held[at, rows, :] = (
                self.held[at, rows, :].astype(F32) + self.far_in[rows, :].astype(F32)
            ).astype(BF16)

        tile_loop(self.count // 16, body)
        self.to_second().start()

    def finish(self, target):
        self.to_first().wait_recv()
        self.to_second().wait_recv()

        def body(t):
            rows = rows_at(t, 16)
            target[rows, :] = (
                self.held[0, rows, :].astype(F32)
                + self.first_in[rows, :].astype(F32)
                + self.second_in[rows, :].astype(F32)
            )

        tile_loop(self.count // 16, body)

    def drain(self):
        self.to_far().wait_send()
        self.to_first().wait_send()
        self.to_second().wait_send()


def tail_kernel(mp, tasks, names, *refs):
    ref = dict(zip(names, refs))
    pull, w_in, norm1 = ref["pull"], ref["w_in"], ref["norm1"]
    count, part = ref["x"].shape
    features = part * mp
    halves = ref["parts"].shape[0]
    step = count // halves
    own = features // 8
    z, d = lax.axis_index("mp"), lax.axis_index("dp")
    core, by_core, by_x, by_y = partners(d)
    fold = Fold(
        z, mp, ref["parts"], ref["rights"], ref["lefts"], ref["fold_sent"], ref["fold_right"],
        ref["fold_left"],
    )
    fold.clear()
    near = z + 1 - 2 * lax.rem(z, 2)
    apart = z + 2 - 4 * lax.div(z, 2)

    barrier = pltpu.get_barrier_semaphore()

    @pl.when(z > 0)
    def _():
        pl.semaphore_signal(barrier, inc=1, device_id={"mp": z - 1}, device_id_type=MESH)

    @pl.when(z < mp - 1)
    def _():
        pl.semaphore_signal(barrier, inc=1, device_id={"mp": z + 1}, device_id_type=MESH)

    pl.semaphore_signal(barrier, inc=1, device_id={"mp": apart}, device_id_type=MESH)
    for other in (by_core, by_x, by_y):
        pl.semaphore_signal(barrier, inc=1, device_id={"dp": other}, device_id_type=MESH)
    pl.semaphore_wait(barrier, jnp.where((z > 0) & (z < mp - 1), 6, 5))

    rhs, lhs, sends = ref["rhs"], ref["lhs"], ref["sends"]
    load_sem, lhs_sem, store_sem = ref["load_sem"], ref["lhs_sem"], ref["store_sem"]
    loaded = [k for k, t in enumerate(tasks) if t[2] not in ("pull", "gates")]

    def load(k):
        _, _, right, first, width, _ = tasks[k]
        slot = loaded.index(k) % 2
        return pltpu.make_async_copy(
            ref[right].at[:, pl.ds(first, width)], rhs.at[slot, :, pl.ds(0, width)],
            load_sem.at[slot],
        )

    load(loaded[0]).start()
    load(loaded[1]).start()

    other = partners(by_core)
    far_here, far_there = partners(by_x)[3], partners(other[2])[3]
    first_dev = jnp.where(core == 0, by_y, by_x)
    second_dev = jnp.where(core == 0, by_x, by_y)
    order = (
        far_there, other[2], other[3], by_core, far_here, first_dev, d, second_dev,
    )
    plan = [
        (k, owner) for k, t in enumerate(tasks) if t[1] not in (None, "norm1") for owner in order
    ]
    turn = [0]

    def lhs_copy(index):
        k, owner = plan[index]
        cols = pl.ds(pl.multiple_of(owner * own, own), own)
        return pltpu.make_async_copy(
            ref[tasks[k][1]].at[:, cols], lhs.at[index % 2], lhs_sem.at[index % 2]
        )

    lhs_copy(0).start()

    def build(k):
        _, left, right, first, width, _ = tasks[k]

        def compute(owner, target, add):
            if left is None:
                rows = pl.ds(pl.multiple_of(owner * 32, 32), 32)
                value = ref["gates"][rows, first : first + width].astype(F32)
            else:
                if left == "norm1":
                    source = norm1.at[:, pl.ds(pl.multiple_of(owner * own, own), own)]
                else:
                    index = turn[0]
                    turn[0] += 1
                    if index + 1 < len(plan):
                        lhs_copy(index + 1).start()
                    lhs_copy(index).wait()
                    source = lhs.at[index % 2]
                if right == "pull":
                    operand = pull[:, first : first + width]
                else:
                    operand = rhs[loaded.index(k) % 2, :, 0:width]
                value = inner_rows(source[...], operand)
            if add:
                value = value + target[...].astype(F32)
            target[...] = value.astype(BF16)

        return Scatter(
            d, 32 if left is None else own, compute, ref["held%d" % k], ref["far%d" % k],
            ref["first%d" % k], ref["second%d" % k], ref["task_sent"].at[k],
            ref["task_came"].at[k],
        )

    scatters = [build(k) for k in range(len(tasks))]
    sending = [None, None]

    def far_core(k):
        scatter = scatters[k]
        width = tasks[k][4]
        for i, rel in enumerate((3, 1, 2, 0)):
            slot = i % 2
            buffer = sends.at[slot, pl.ds(0, scatter.count), pl.ds(0, width)]
            if sending[slot] is not None:
                sending[slot].wait_send()
            scatter.compute(scatter.away[rel], buffer, False)
            copy = scatter.to_core(buffer, rel)
            copy.start()
            sending[slot] = copy

    stage, stage_wait = ref["stage"], [None, None]

    def finish(k):
        scatter = scatters[k]
        name, width, column = tasks[k][0], tasks[k][4], tasks[k][5]
        slot = k % 2
        if stage_wait[slot] is not None:
            stage_wait[slot].wait()
        view = stage.at[slot, pl.ds(0, scatter.count), pl.ds(0, width)]
        scatter.finish(view)
        target = ref["grad_" + name].at[:, pl.ds(column, width)]
        copy = pltpu.make_async_copy(view, target, store_sem.at[slot])
        copy.start()
        stage_wait[slot] = copy

    dots, dots_in = ref["dots_row"], ref["dots_in"]
    for q in range(count // 128):
        turned = jnp.transpose(ref["dots"][q * 128 : (q + 1) * 128, :])
        dots[:, q * 128 : (q + 1) * 128] = turned[0:8, :]

    def dots_copy(k):
        return pltpu.make_async_remote_copy(
            src_ref=dots, dst_ref=dots_in.at[k], send_sem=ref["dots_sent"].at[k],
            recv_sem=ref["dots_came"].at[k], device_id={"mp": near if k == 0 else apart},
            device_id_type=MESH,
        )

    def dots_add(k):
        dots_copy(k).wait()
        dots[...] += dots_in[k]

    dots_copy(0).start()
    gain = ref["gain"]
    gain[...] = jnp.zeros_like(gain)
    for c in range(halves):

        def body(j, c=c):
            rows = pl.ds(pl.multiple_of(j * part, part), part)
            for q in range(step // 256):
                tokens = pl.ds(c * step + q * 256, 256)
                value = inner_cols(pull[tokens, :], w_in[rows, :])
                fold.parts[c, j, q * 256 : (q + 1) * 256, :] = value.astype(BF16)
                gain[:, rows] += jnp.sum(
                    (value * norm1[tokens, rows].astype(F32)).reshape(-1, 8, part), axis=0
                )

        tile_loop(mp, body)
        if c == 0:
            dots_add(0)
            dots_copy(1).start()
        fold.start(c)

    small, small_in = ref["small"], ref["small_in"]
    small[...] = ref["small_start"][...]
    small[0:1, :] = jnp.sum(gain[...], axis=0, keepdims=True) / ref["gains"][0:1, :]
    targets = (
        {"dp": by_core}, {"dp": by_x}, {"dp": by_y}, {"mp": near}, {"mp": apart},
    )

    def small_copy(k):
        rows = pl.ds(0, 16 if k < 3 else 8)
        return pltpu.make_async_remote_copy(
            src_ref=small.at[rows, :], dst_ref=small_in.at[k, rows, :],
            send_sem=ref["small_sent"].at[k], recv_sem=ref["small_came"].at[k],
            device_id=targets[k], device_id_type=MESH,
        )

    def small_add(k):
        rows = 16 if k < 3 else 8
        small_copy(k).wait()
        small[0:rows, :] += small_in[k, 0:rows, :]

    def local_copy(c):
        return pltpu.make_async_copy(
            ref["local"].at[pl.ds(c * step, step), :], ref["near_local"], ref["local_sem"]
        )

    local_copy(0).start()

    def input_grad(c):
        fold.finish(c)
        local_copy(c).wait()

        def body(t):
            rows = rows_at(t, TILE)
            base = pl.ds(pl.multiple_of(c * step + t * TILE, TILE), TILE)
            s1 = ref["s1"][base, :][:, 0:1]
            dot = ref["dots_col"][base, :][:, 0:1]
            grad = (
                ref["near_local"][rows, :]
                + s1 * (fold.total(c, rows) * ref["mine"][0:1, :])
                - ref["x"][base, :].astype(F32) * (s1 * s1 * dot * (1.0 / features))
            )
            ref["grad_x"][base, :] = grad.astype(BF16)

        tile_loop(step // TILE, body)
        if c + 1 < halves:
            local_copy(c + 1).start()

    def dots_back():
        for q in range(count // 128):
            wide = jnp.broadcast_to(dots[0:1, q * 128 : (q + 1) * 128], (128, 128))
            ref["dots_col"][q * 128 : (q + 1) * 128, :] = jnp.transpose(wide)

    small_copy(0).start()
    last = len(tasks) - 1
    for k in range(len(tasks)):
        if k in loaded:
            load(k).wait()
        far_core(k)
        if k == 0:
            for i in range(3):
                small_add(i)
                if i < 2:
                    small_copy(i + 1).start()
        scatters[k].near_core()
        if k in loaded and loaded.index(k) + 2 < len(loaded):
            load(loaded[loaded.index(k) + 2]).start()
        if k == 0:
            dots_add(1)
            dots_back()
        if k == 1:
            fold.step(0, 1)
        if k == 2:
            fold.step(0, 2)
        if k == 3:
            input_grad(0)
        if k == 4:
            fold.step(1, 1)
        if k == 6:
            fold.step(1, 2)
        if k == 8:
            input_grad(1)
            small_copy(3).start()
        if k > 0:
            scatters[k - 1].onward()
        if k > 5:
            finish(k - 6)
    scatters[last].onward()
    small_add(3)
    small_copy(4).start()
    for k in range(last - 5, last + 1):
        finish(k)
    small_add(4)
    for copy in stage_wait:
        copy.wait()
    for copy in sending:
        copy.wait_send()
    for scatter in scatters:
        scatter.drain()
    for c in range(halves):
        fold.drain(c)


def tail(mp, pull, w_in, norm1, norm2, pulled, grady, hidden, gbo, mixed, gates, dots, s1, x,
         local, gains, mine, small):
    count, part = x.shape
    features = part * mp
    own = features // 8
    halves = 2
    step = count // halves
    widths = {
        "gate": hidden.shape[1], "up": hidden.shape[1], "down": hidden.shape[1],
        "in": pull.shape[1], "out": mixed.shape[1], "block": pull.shape[1],
    }
    heights = {name: 32 if name == "block" else own for name in widths}
    operands = {
        "gate": ("norm2", "pulled", 0), "up": ("norm2", "pulled", hidden.shape[1]),
        "down": ("grady", "hidden", 0), "in": ("norm1", "pull", 0), "out": ("gbo", "mixed", 0),
        "block": (None, "gates", 0),
    }
    tasks = []
    for name, width in widths.items():
        left, right, first = operands[name]
        pieces = 1 if name == "out" else 2
        for piece in range(pieces):
            column = piece * (width // pieces)
            tasks.append((name, left, right, first + column, width // pieces, column))
    widest = max(t[4] for t in tasks)
    dma = pltpu.SemaphoreType.DMA
    any_, vmem = pl.BlockSpec(memory_space=pl.ANY), pl.BlockSpec(memory_space=pltpu.VMEM)
    ins = [
        ("pull", pull, vmem), ("w_in", w_in, vmem), ("norm1", norm1, vmem),
        ("norm2", norm2, any_), ("pulled", pulled, any_), ("grady", grady, any_),
        ("hidden", hidden, any_), ("gbo", gbo, any_), ("mixed", mixed, any_),
        ("gates", gates, vmem), ("dots", dots, vmem), ("s1", s1, vmem), ("x", x, vmem),
        ("local", local, any_), ("gains", gains, vmem), ("mine", mine, vmem),
        ("small_start", small, vmem),
    ]
    outs = [("grad_x", jax.ShapeDtypeStruct((count, part), BF16), vmem)]
    for name, width in widths.items():
        outs.append(("grad_" + name, jax.ShapeDtypeStruct((heights[name], width), F32), any_))
    outs.append(("small", jax.ShapeDtypeStruct((16, features), F32), vmem))
    scratch = [
        ("parts", pltpu.VMEM((halves, mp, step, part), BF16)),
        ("rights", pltpu.VMEM((halves, mp - 1, step, part), BF16)),
        ("lefts", pltpu.VMEM((halves, mp - 1, step, part), BF16)),
        ("rhs", pltpu.VMEM((2, count, widest), BF16)),
        ("lhs", pltpu.VMEM((2, count, own), BF16)),
        ("sends", pltpu.VMEM((2, own, widest), BF16)),
        ("stage", pltpu.VMEM((2, own, widest), F32)),
        ("near_local", pltpu.VMEM((step, part), F32)),
        ("local_sem", dma),
        ("gain", pltpu.VMEM((8, features), F32)),
        ("dots_row", pltpu.VMEM((8, count), F32)),
        ("dots_in", pltpu.VMEM((2, 8, count), F32)),
        ("dots_col", pltpu.VMEM((count, 128), F32)),
        ("small_in", pltpu.VMEM((5, 16, features), F32)),
        ("fold_sent", dma((halves, mp))),
        ("fold_right", dma((halves, mp))),
        ("fold_left", dma((halves, mp))),
        ("task_sent", dma((len(tasks), 8))),
        ("task_came", dma((len(tasks), 8))),
        ("load_sem", dma((2,))),
        ("lhs_sem", dma((2,))),
        ("store_sem", dma((2,))),
        ("dots_sent", dma((2,))),
        ("dots_came", dma((2,))),
        ("small_sent", dma((5,))),
        ("small_came", dma((5,))),
    ]
    for k, (name, _, _, _, width, _) in enumerate(tasks):
        tall = heights[name]
        scratch.append(("held%d" % k, pltpu.VMEM((4, tall, width), BF16)))
        for kind in ("far", "first", "second"):
            scratch.append(("%s%d" % (kind, k), pltpu.VMEM((tall, width), BF16)))
    names = [i[0] for i in ins] + [o[0] for o in outs] + [k[0] for k in scratch]
    return pl.pallas_call(
        functools.partial(tail_kernel, mp, tuple(tasks), tuple(names)),
        in_specs=[i[2] for i in ins],
        out_specs=[o[2] for o in outs],
        out_shape=[o[1] for o in outs],
        scratch_shapes=[k[1] for k in scratch],
        compiler_params=pltpu.CompilerParams(
            collective_id=1, has_side_effects=True, vmem_limit_bytes=63 * 1024 * 1024
        ),
        name="tail",
    )(*[i[1] for i in ins])


def make_masks(row_lengths, count):
    ends = jnp.cumsum(row_lengths)
    places = jnp.arange(-TAPS, count, dtype=jnp.int32)
    segment = jnp.sum((places[:, None] >= ends[None, :]).astype(jnp.int32), axis=1)
    segment = jnp.where(places < 0, -1, segment)
    now = segment[TAPS:]
    same = [(segment[TAPS - k : TAPS - k + count] == now).astype(F32) for k in range(1, TAPS)]
    blank = jnp.zeros((count,), F32)
    columns = [same[0]] + same + [blank] * (LANES - TAPS)
    live = now < row_lengths.shape[0]
    return jnp.stack(columns, axis=1), live


def dense_gates(gates, width):
    span = gates.shape[0]
    tiled = jnp.tile(gates, (width // span, 1))
    row = lax.broadcasted_iota(jnp.int32, tiled.shape, 0) // span
    column = (lax.broadcasted_iota(jnp.int32, tiled.shape, 1) % width) // span
    return jnp.where(row == column, tiled, jnp.zeros((), tiled.dtype))


def diagonal_blocks(dense, span):
    width = dense.shape[0]
    column = (lax.broadcasted_iota(jnp.int32, (1, 2 * width), 1) % width) // span
    total = jnp.zeros((span, 2 * width), F32)
    for b in range(width // span):
        total = total + jnp.where(column == b, dense[b * span : (b + 1) * span], 0.0)
    return total


def per_device(
    dp, mp,
    inputs, lengths, cotangent, gains, rnn_params, rnn_in, branch_gate, recur_gate, input_gate,
    mlp_gate, mlp_up, rnn_out, mlp_down,
):
    count, part = inputs.shape
    width = rnn_in.shape[1]
    hidden_width = mlp_gate.shape[1]
    span = recur_gate.shape[0] * dp
    features = part * mp
    step = count // CHUNKS
    spot = lax.axis_index("mp") * part

    def cut(values):
        return [values[c * step : (c + 1) * step] for c in range(CHUNKS)]

    def mine(values):
        return lax.dynamic_slice_in_dim(values, spot, part, values.ndim - 1)

    in_shard = jnp.concatenate([rnn_in, branch_gate], axis=1)
    out_shard = rnn_out.T
    gates_shard = jnp.concatenate([recur_gate, input_gate], axis=1)
    up = jnp.concatenate([mlp_gate, mlp_up], axis=1)
    down = mlp_down.T
    if dp == 8:
        gates_shard = jnp.pad(gates_shard, ((0, 32 - span // 8), (0, 0)))
    else:
        in_shard, out_shard = square_gather(in_shard, "dp", dp), square_gather(out_shard, "dp", dp)
        up, down = square_gather(up, "dp", dp), square_gather(down, "dp", dp)
        gates_shard = pair_gather(gates_shard, "dp", dp).reshape(8, span // 8, 2 * width)
        gates_shard = jnp.pad(gates_shard, ((0, 0), (0, 32 - span // 8), (0, 0)))
        gates_shard = gates_shard.reshape(256, 2 * width)

    mask, live = make_masks(lengths[0], count)
    mask_tail = jnp.concatenate([mask, jnp.zeros((8, LANES), F32)], axis=0)
    tail_masks = [mask_tail[c * step : (c + 1) * step + 8] for c in range(CHUNKS)]
    live = jnp.broadcast_to(live[:, None], (count, LANES)).astype(F32)
    w_in, w_out, dense, normed, both, conv, r, i, state, mixed, s1 = head(
        dp, mp, 4, inputs, gains, rnn_params, mask, in_shard, out_shard, gates_shard, span
    )
    output, gm, gbo, local, hidden, pulled, normed2, grad_y, gain2 = middle(
        dp, mp, 4, mixed, inputs, cotangent, live, gains, mine(gains), w_out,
        up, down,
    )
    blank = jnp.zeros((8, width), F32)
    back, tail_rows = blank, blank
    pulls, rates, dots = [None] * CHUNKS, [None] * CHUNKS, [None] * CHUNKS
    params_total = 0.0
    gms, boths = cut(gm), cut(both)
    saves = list(zip(cut(conv), cut(r), cut(i), cut(state)))
    for c in reversed(range(CHUNKS)):
        low = c * step
        halo = blank if c == 0 else both[low - 8 : low, :width]
        start = blank if c == 0 else state[low - 8 : low]
        pull, rate, dparams, back, tail_rows, dot = rnn_backward(
            gms[c], boths[c], halo, start, saves[c], tail_masks[c], dense, rnn_params,
            back, tail_rows,
        )
        params_total = params_total + dparams
        pulls[c], rates[c], dots[c] = pull, rate, dot
    pull = jnp.concatenate(pulls)
    dots = jnp.concatenate(dots)
    grad_gates = diagonal_blocks(inner_rows(conv.astype(BF16), jnp.concatenate(rates)), span)
    gain2 = jnp.sum(gain2, axis=0, keepdims=True)

    if dp == 8:
        rows = span // dp
        padded = jnp.pad(
            grad_gates.astype(BF16).reshape(dp, rows, 2 * width), ((0, 0), (0, 32 - rows), (0, 0))
        ).reshape(dp * 32, 2 * width)
        small = jnp.concatenate(
            [
                jnp.zeros((1, features), F32), gain2 / mp, jnp.zeros((6, features), F32),
                jnp.pad(params_total, ((0, 0), (0, features - width))),
            ]
        )
        input_grad, grad_gate, grad_up, grad_down, grad_in, grad_out, grad_gates, small = tail(
            mp, pull, w_in, normed, normed2, pulled, grad_y, hidden, gbo, mixed, padded, dots,
            s1, inputs, local, gains, mine(gains), small,
        )
        grad_gates = grad_gates[:rows]
        grad_gains, grad_params = small[0:2], small[8:16, :width]
    else:
        parts = []
        gain1 = 0.0
        norms, s1 = cut(normed), s1[:, 0:1]
        for c in range(CHUNKS):
            gn1_part = inner_cols(pulls[c], w_in).astype(BF16)
            gain1 = gain1 + jnp.sum(gn1_part.astype(F32) * norms[c].astype(F32), axis=0)
            parts.append(line_scatter(gn1_part, "mp", mp))
        dot = line_sum(dots[:, 0].reshape(8, -1), "mp", mp).reshape(-1, 1)
        input_grad = (
            local + s1 * (jnp.concatenate(parts) * mine(gains[0]))
            - inputs.astype(F32) * (s1 * s1 * dot / features)
        ).astype(BF16)
        grad_both = square_scatter(inner_rows(normed2, pulled).astype(BF16), "dp", dp)
        grad_gate, grad_up = grad_both[:, :hidden_width], grad_both[:, hidden_width:]
        grad_down = square_scatter(inner_rows(grad_y, hidden).astype(BF16), "dp", dp)
        grad_out = square_scatter(inner_rows(gbo, mixed).astype(BF16), "dp", dp)
        grad_in = square_scatter(inner_rows(normed, pull).astype(BF16), "dp", dp)
        grad_gates = pair_scatter(grad_gates, "dp", dp)
        grad_params = line_sum(params_total, "dp", dp)
        both_gains = jnp.concatenate([(gain1 / gains[0])[None], gain2])
        both_gains = line_sum(both_gains, "dp", dp)
        grad_gains = jnp.concatenate([line_sum(both_gains[:1], "mp", mp), both_gains[1:]])
    return (
        output,
        input_grad,
        grad_gains,
        grad_params,
        grad_in[:, :width],
        grad_in[:, width:],
        grad_gates[:, :width],
        grad_gates[:, width:],
        grad_gate,
        grad_up,
        grad_out.T,
        grad_down.T,
    )


def solution(mesh):
    return jax.shard_map(
        functools.partial(per_device, mesh.shape["dp"], mesh.shape["mp"]),
        mesh=mesh,
        in_specs=(
            P("dp", "mp"),
            P("dp", None),
            P("dp", "mp"),
            P(),
            P(None, "mp"),
            P("dp", "mp"),
            P("dp", "mp"),
            P("dp", "mp"),
            P("dp", "mp"),
            P("dp", "mp"),
            P("dp", "mp"),
            P("mp", "dp"),
            P("mp", "dp"),
        ),
        out_specs=(
            P("dp", "mp"),
            P("dp", "mp"),
            P(),
            P(None, "mp"),
            P("dp", "mp"),
            P("dp", "mp"),
            P("dp", "mp"),
            P("dp", "mp"),
            P("dp", "mp"),
            P("dp", "mp"),
            P("mp", "dp"),
            P("mp", "dp"),
        ),
        check_vma=False,
    )
```

```python
import functools

import jax
import jax.numpy as jnp
from jax import lax
from jax.experimental import pallas as pl
from jax.experimental.pallas import tpu as pltpu
from jax.sharding import PartitionSpec as P

EPS = 1e-06
DECAY_SCALE = 8.0
ROOT_FLOOR = 0.0001
TAPS = 4
LANES = 8
CHUNKS = 1
TILE = 32
F32 = jnp.float32
BF16 = jnp.bfloat16
VMEM_BYTES = 56 * 1024 * 1024


def matmul(left, right):
    return jnp.dot(left, right, preferred_element_type=F32)


def inner_rows(left, right):
    return lax.dot_general(left, right, (((0,), (0,)), ((), ())), preferred_element_type=F32)


def inner_cols(left, right):
    return lax.dot_general(left, right, (((1,), (1,)), ((), ())), preferred_element_type=F32)


def gelu_and_slope(values):
    outer = 0.7978845608028654
    inner = 0.044715
    square = values * values
    bent = jnp.tanh(outer * values * (1.0 + inner * square))
    half = 0.5 * (1.0 + bent)
    slope = half + 0.5 * values * (1.0 - bent * bent) * outer * (1.0 + 3.0 * inner * square)
    return values * half, slope


def gelu(values):
    outer = 0.7978845608028654
    inner = 0.044715
    bent = jnp.tanh(outer * values * (1.0 + inner * values * values))
    return values * (0.5 * (1.0 + bent))


def one_less_exp(values):
    near = -values * (1.0 + 0.5 * values * (1.0 + (values / 3.0) * (1.0 + 0.25 * values)))
    return jnp.where(values > -0.02, near, 1.0 - jnp.exp(values))


def after(value, *earlier):
    return lax.optimization_barrier((value,) + earlier)[0]


def line_gather(mine, axis, size):
    place = lax.axis_index(axis)
    width = mine.shape[1]
    right, left = mine, mine
    rights, lefts = {}, {}
    for step in range(1, size):
        right = lax.ppermute(right, axis, [(i, i + 1) for i in range(step - 1, size - 1)])
        left = lax.ppermute(left, axis, [(i + 1, i) for i in range(size - step)])
        rights[step], lefts[step] = right, left
    whole = jnp.zeros((mine.shape[0], size * width), mine.dtype)
    for step in range(size):
        block = mine if step == 0 else lefts[step] + rights[size - step]
        spot = lax.rem(place + step, size) * width
        whole = lax.dynamic_update_slice_in_dim(whole, block, spot, 1)
    return whole


def line_scatter(part, axis, size):
    place = lax.axis_index(axis)
    width = part.shape[1] // size

    def block(index):
        spot = jnp.clip(index, 0, size - 1) * width
        return lax.dynamic_slice_in_dim(part, spot, width, 1).astype(F32)

    right, left = None, None
    for step in range(1, size):
        going = block(size - step + place)
        if right is not None:
            going = going + right.astype(F32)
        right = lax.ppermute(going.astype(BF16), axis, [(i, i + 1) for i in range(step)])
        going = block(place - (size - step))
        if left is not None:
            going = going + left.astype(F32)
        left = lax.ppermute(
            going.astype(BF16), axis, [(i, i - 1) for i in range(size - step, size)]
        )
    return block(place) + right.astype(F32) + left.astype(F32)


def line_sum(value, axis, size):
    bit = 1
    while bit < size:
        value = value + lax.ppermute(value, axis, [(i, i ^ bit) for i in range(size)])
        bit *= 2
    return value


def pair_gather(mine, axis, size):
    place = lax.axis_index(axis)
    bit = 1
    while bit < size:
        other = lax.ppermute(mine, axis, [(i, i ^ bit) for i in range(size)])
        upper = (place & bit) != 0
        mine = jnp.concatenate(
            [jnp.where(upper, other, mine), jnp.where(upper, mine, other)], axis=0
        )
        bit *= 2
    return mine


def pair_scatter(part, axis, size):
    place = lax.axis_index(axis)
    part = part.astype(F32)
    bit = size // 2
    while bit >= 1:
        upper = (place & bit) != 0
        low, high = jnp.split(part, 2, axis=0)
        going = jnp.where(upper, low, high).astype(BF16)
        came = lax.ppermute(going, axis, [(i, i ^ bit) for i in range(size)])
        part = jnp.where(upper, high, low) + came.astype(F32)
        bit //= 2
    return part


def swap(size, bit):
    return [(i, i ^ bit) for i in range(size)]


def cross(size):
    return [(i, i ^ 4 if i % 2 == 0 else i ^ 2) for i in range(size)]


def square_gather(mine, axis, size):
    if size != 8:
        return pair_gather(mine, axis, size)
    place = lax.axis_index(axis)
    rows = mine.shape[0]
    by_x = lax.ppermute(mine, axis, swap(size, 2))
    by_y = lax.ppermute(mine, axis, swap(size, 4))
    onward = jnp.where((place & 1) == 0, by_x, by_y)
    far = lax.ppermute(onward, axis, cross(size))
    held = {0: mine, 2: by_x, 4: by_y, 6: far}
    for bits in (0, 2, 4, 6):
        held[bits + 1] = lax.ppermute(held[bits], axis, swap(size, 1))
    whole = jnp.zeros((size * rows,) + mine.shape[1:], mine.dtype)
    for bits, block in held.items():
        whole = lax.dynamic_update_slice_in_dim(whole, block, (place ^ bits) * rows, 0)
    return whole


def square_scatter(part, axis, size):
    if size != 8:
        return pair_scatter(part, axis, size)
    place = lax.axis_index(axis)
    core = place & 1
    chip = lax.shift_right_logical(place, 1)
    split = part.reshape(size // 2, 2, part.shape[0] // size, part.shape[1])
    going = lax.dynamic_index_in_dim(split, 1 - core, 1, keepdims=False)
    came = lax.ppermute(going, axis, swap(size, 1))
    kept = lax.dynamic_index_in_dim(split, core, 1, keepdims=False)
    both = (kept.astype(F32) + came.astype(F32)).astype(BF16)

    def pick(index):
        return lax.dynamic_index_in_dim(both, index, 0, keepdims=False)

    far = lax.ppermute(pick(chip ^ 3), axis, cross(size)).astype(F32)
    none = jnp.zeros((), F32)
    to_x = pick(chip ^ 1).astype(F32) + jnp.where(core == 0, far, none)
    to_y = pick(chip ^ 2).astype(F32) + jnp.where(core == 1, far, none)
    by_x = lax.ppermute(to_x.astype(BF16), axis, swap(size, 2))
    by_y = lax.ppermute(to_y.astype(BF16), axis, swap(size, 4))
    return pick(chip).astype(F32) + by_x.astype(F32) + by_y.astype(F32)


def tile_loop(count, body):
    lax.fori_loop(0, count, lambda i, c: (body(i), c)[1], 0)


def rows_at(index, size):
    return pl.ds(pl.multiple_of(index * size, size), size)


def put(ref, rows, values):
    for j in range(ref.shape[0]):
        ref[j, rows, :] = values[:, j * 128 : (j + 1) * 128]


def get(ref, rows):
    return jnp.concatenate([ref[j, rows, :] for j in range(ref.shape[0])], axis=1)


def rnn_forward_kernel(
    both_ref, halo_ref, start_ref, mask_ref, gates_ref, params_ref,
    mixed_ref, conv_ref, r_ref, i_ref, state_ref, end_ref,
    padded, high, low, decay, drive,
):
    count, width = conv_ref.shape
    seg = count // 8
    tiles = count // TILE
    padded[0:8, :] = halo_ref[...]
    padded[8:, :] = both_ref[:, 0:width]

    def convolve(t):
        span = padded[pl.ds(pl.multiple_of(t * TILE, TILE), TILE + 8), :]
        mask = mask_ref[rows_at(t, TILE), :]
        conv = params_ref[0:1, :] * span[8:, :] + params_ref[TAPS : TAPS + 1, :]
        for k in range(1, TAPS):
            moved = span[8 - k : 8 - k + TILE, :]
            conv = conv + params_ref[k : k + 1, :] * (moved * mask[:, k : k + 1])
        conv_ref[rows_at(t, TILE), :] = conv
        top = conv.astype(BF16)
        high[rows_at(t, TILE), :] = top
        low[rows_at(t, TILE), :] = (conv - top.astype(F32)).astype(BF16)

    tile_loop(tiles, convolve)

    block = min(256, count)

    def gate(t):
        rows = rows_at(t, block)
        weights = gates_ref[...]
        both = jnp.dot(high[rows, :], weights, preferred_element_type=F32)
        both = both + jnp.dot(low[rows, :], weights, preferred_element_type=F32)
        r_ref[rows, :] = both[:, 0:width]
        i_ref[rows, :] = both[:, width:]

    tile_loop(count // block, gate)

    strength = DECAY_SCALE * jax.nn.softplus(-params_ref[TAPS + 3 : TAPS + 4, :])

    def prepare(t):
        rows = rows_at(t, TILE)
        keep = mask_ref[rows, :][:, 0:1]
        r = jax.nn.sigmoid(r_ref[rows, :] + params_ref[TAPS + 1 : TAPS + 2, :])
        i = jax.nn.sigmoid(i_ref[rows, :] + params_ref[TAPS + 2 : TAPS + 3, :])
        log_a = -strength * r
        scale = jnp.sqrt(jnp.maximum(one_less_exp(2.0 * log_a), ROOT_FLOOR))
        scale = jnp.where(keep > 0.0, scale, 1.0)
        put(decay, rows, jnp.exp(log_a) * keep)
        put(drive, rows, scale * i * conv_ref[rows, :])
        r_ref[rows, :] = r
        i_ref[rows, :] = i

    tile_loop(tiles, prepare)

    def scan(t, carry):
        held, prod = carry
        rows = pl.ds(t, 8, stride=seg)
        a = get(decay, rows)
        held = a * held + get(drive, rows)
        prod = a * prod
        put(drive, rows, held)
        put(decay, rows, prod)
        return held, prod

    shape = (8, width)
    held, prod = lax.fori_loop(0, seg, scan, (jnp.zeros(shape, F32), jnp.ones(shape, F32)))
    carry = start_ref[0:1, :]
    carries = []
    for s in range(8):
        carries.append(carry)
        carry = prod[s : s + 1, :] * carry + held[s : s + 1, :]
    end_ref[...] = jnp.broadcast_to(carry, shape)

    small = min(TILE, seg)
    for s in range(8):

        def finish(t, s=s):
            rows = pl.ds(pl.multiple_of(s * seg + t * small, small), small)
            state = get(drive, rows) + get(decay, rows) * carries[s]
            state_ref[rows, :] = state
            mixed_ref[rows, :] = (state * gelu(both_ref[rows, width:])).astype(BF16)

        tile_loop(seg // small, finish)


def rnn_forward(both, halo, start, mask, gates, params):
    count, width = both.shape[0], both.shape[1] // 2
    full = jax.ShapeDtypeStruct((count, width), F32)
    return pl.pallas_call(
        rnn_forward_kernel,
        out_shape=(
            jax.ShapeDtypeStruct((count, width), BF16),
            full, full, full, full,
            jax.ShapeDtypeStruct((8, width), F32),
        ),
        scratch_shapes=[
            pltpu.VMEM((count + 8, width), F32),
            pltpu.VMEM((count, width), BF16),
            pltpu.VMEM((count, width), BF16),
            pltpu.VMEM((width // 128, count, 128), F32),
            pltpu.VMEM((width // 128, count, 128), F32),
        ],
        compiler_params=pltpu.CompilerParams(vmem_limit_bytes=VMEM_BYTES),
        cost_estimate=pl.CostEstimate(
            flops=4 * count * width * 2 * width, bytes_accessed=count * width * 30,
            transcendentals=count * width * 6,
        ),
        name="rnn_forward",
    )(both, halo, start, mask, gates, params)


def rnn_backward_kernel(
    gm_ref, both_ref, halo_ref, start_ref, conv_ref, r_ref, i_ref, state_ref, mask_ref,
    gates_ref, params_ref, back_ref, tail_ref,
    grads_ref, rates_ref, dparams_ref, back_out_ref, tail_out_ref, dots_ref,
    padded, before, decay, adjoint, coef, dconv, sums,
):
    count, width = conv_ref.shape
    seg = count // 8
    tiles = count // TILE
    padded[0:8, :] = halo_ref[...]
    padded[8:, :] = both_ref[:, 0:width]
    before[0:8, :] = start_ref[...]
    before[8:, :] = state_ref[...]
    strength = DECAY_SCALE * jax.nn.softplus(-params_ref[TAPS + 3 : TAPS + 4, :])

    def prepare(t):
        rows = rows_at(t, TILE)
        keep = mask_ref[rows, :][:, 0:1]
        gm = gm_ref[rows, :]
        value, slope = gelu_and_slope(both_ref[rows, width:])
        put(adjoint, rows, gm * value)
        grads_ref[rows, width:] = (gm * state_ref[rows, :] * slope).astype(BF16)
        put(decay, rows, jnp.exp(-strength * r_ref[rows, :]) * keep)

    tile_loop(tiles, prepare)

    def scan(t, carry):
        held, prod = carry
        rows = pl.ds(seg - 1 - t, 8, stride=seg)
        a = get(decay, rows)
        total = get(adjoint, rows) + held
        put(adjoint, rows, total)
        put(coef, rows, prod)
        return a * total, a * prod

    shape = (8, width)
    held, prod = lax.fori_loop(0, seg, scan, (jnp.zeros(shape, F32), jnp.ones(shape, F32)))
    carry = back_ref[0:1, :]
    carries = [None] * 8
    for s in reversed(range(8)):
        carries[s] = carry
        carry = prod[s : s + 1, :] * carry + held[s : s + 1, :]
    back_out_ref[...] = jnp.broadcast_to(carry, shape)

    sums[...] = jnp.zeros_like(sums)

    def fold(values):
        return jnp.sum(values.reshape(-1, 8, width), axis=0)

    small = min(TILE, seg)
    for s in range(8):

        def chain(t, s=s):
            base = pl.multiple_of(s * seg + t * small, small)
            rows = pl.ds(base, small)
            keep = mask_ref[rows, :][:, 0:1]
            a = get(adjoint, rows) + get(coef, rows) * carries[s]
            r, i, conv = r_ref[rows, :], i_ref[rows, :], conv_ref[rows, :]
            fall = get(decay, rows)
            prior = before[pl.ds(base, small + 8), :][7 : 7 + small, :]
            room = one_less_exp(-2.0 * strength * r)
            bound = jnp.maximum(room, ROOT_FLOOR)
            inverse = lax.rsqrt(bound)
            live = keep > 0.0
            scale = jnp.where(live, bound * inverse, 1.0)
            open_ = jnp.where(room > ROOT_FLOOR, inverse, 0.0)
            driven = a * i
            dlog = fall * (a * prior - fall * driven * conv * open_)
            common = a * scale
            drec = dlog * (-strength) * r * (1.0 - r)
            dinp = common * conv * i * (1.0 - i)
            rates_ref[rows, 0:width] = drec.astype(BF16)
            rates_ref[rows, width:] = dinp.astype(BF16)
            dconv[rows, :] = common * i
            sums[5] += fold(drec)
            sums[6] += fold(dinp)
            sums[7] += fold(dlog * r)

        tile_loop(seg // small, chain)

    block = min(256, count)

    def spread(t):
        rows = rows_at(t, block)
        dconv[rows, :] += lax.dot_general(
            rates_ref[rows, :], gates_ref[...], (((1,), (1,)), ((), ())),
            preferred_element_type=F32,
        )

    tile_loop(count // block, spread)
    dconv[count:, :] = tail_ref[...]
    tail_out_ref[...] = dconv[0:8, :]

    def unconvolve(t):
        base = pl.multiple_of(t * TILE, TILE)
        rows = pl.ds(base, TILE)
        span = dconv[pl.ds(base, TILE + 8), :]
        mask = mask_ref[pl.ds(base, TILE + 8), :]
        source = padded[pl.ds(base, TILE + 8), :]
        here = span[0:TILE, :]
        out = params_ref[0:1, :] * here
        sums[0] += fold(here * source[8:, :])
        sums[4] += fold(here)
        for k in range(1, TAPS):
            kept = span * mask[:, k : k + 1]
            out = out + params_ref[k : k + 1, :] * kept[k : k + TILE, :]
            sums[k] += fold(kept[0:TILE, :] * source[8 - k : 8 - k + TILE, :])
        grads_ref[rows, 0:width] = out.astype(BF16)
        dot = jnp.sum(
            out * source[8:, :] + grads_ref[rows, width:].astype(F32) * both_ref[rows, width:],
            axis=1, keepdims=True,
        )
        dots_ref[rows, :] = jnp.broadcast_to(dot, (TILE, 128))

    tile_loop(tiles, unconvolve)
    for k in range(8):
        dparams_ref[k : k + 1, :] = jnp.sum(sums[k], axis=0, keepdims=True)
    dparams_ref[TAPS + 3 : TAPS + 4, :] = (
        DECAY_SCALE
        * jax.nn.sigmoid(-params_ref[TAPS + 3 : TAPS + 4, :])
        * jnp.sum(sums[TAPS + 3], axis=0, keepdims=True)
    )


def rnn_backward(gm, both, halo, start, saved, mask, gates, params, back, tail):
    conv, r, i, state = saved
    count, width = conv.shape
    return pl.pallas_call(
        rnn_backward_kernel,
        out_shape=(
            jax.ShapeDtypeStruct((count, 2 * width), BF16),
            jax.ShapeDtypeStruct((count, 2 * width), BF16),
            jax.ShapeDtypeStruct((8, width), F32),
            jax.ShapeDtypeStruct((8, width), F32),
            jax.ShapeDtypeStruct((8, width), F32),
            jax.ShapeDtypeStruct((count, 128), F32),
        ),
        scratch_shapes=[
            pltpu.VMEM((count + 8, width), F32),
            pltpu.VMEM((count + 8, width), F32),
            pltpu.VMEM((width // 128, count, 128), F32),
            pltpu.VMEM((width // 128, count, 128), F32),
            pltpu.VMEM((width // 128, count, 128), F32),
            pltpu.VMEM((count + 8, width), F32),
            pltpu.VMEM((8, 8, width), F32),
        ],
        compiler_params=pltpu.CompilerParams(vmem_limit_bytes=VMEM_BYTES),
        cost_estimate=pl.CostEstimate(
            flops=2 * count * width * 2 * width, bytes_accessed=count * width * 36,
            transcendentals=count * width * 6,
        ),
        name="rnn_backward",
    )(gm, both, halo, start, conv, r, i, state, mask, gates, params, back, tail)


MESH = pl.DeviceIdType.MESH


class Spread:
    def __init__(self, place, size, blocks, sent, came):
        self.place, self.size = place, size
        self.blocks, self.sent, self.came = blocks, sent, came

    def copy(self, slot, j, way, k):
        ref = self.blocks.at[slot, j]
        return pltpu.make_async_remote_copy(
            src_ref=ref, dst_ref=ref, send_sem=self.sent.at[slot, k],
            recv_sem=self.came.at[slot, j], device_id={"mp": self.place + way},
            device_id_type=MESH,
        )

    def moves(self, s):
        z, n = self.place, self.size
        return (
            ((z - s >= 0) & (z < n - 1), z - s, 1, 2 * s),
            ((z + s <= n - 1) & (z > 0), z + s, -1, 2 * s + 1),
        )

    def step(self, slot, s):
        for valid, j, way, k in self.moves(s):

            @pl.when(valid)
            def _(j=j, way=way, k=k):
                copy = self.copy(slot, j, way, k)
                if s > 0:
                    copy.wait_recv()
                copy.start()

    def finish(self, slot):
        z, n = self.place, self.size

        @pl.when(z == 0)
        def _():
            for j in range(1, n):
                self.copy(slot, j, 1, 0).wait_recv()

        @pl.when(z == n - 1)
        def _():
            for j in range(n - 1):
                self.copy(slot, j, -1, 0).wait_recv()

    def drain(self, slot):
        for s in range(self.size - 1):
            for valid, j, way, k in self.moves(s):

                @pl.when(valid)
                def _(j=j, way=way, k=k):
                    self.copy(slot, j, way, k).wait_send()


class Fold:
    def __init__(self, place, size, parts, rights, lefts, sent, came_right, came_left):
        self.place, self.size = place, size
        self.parts, self.rights, self.lefts = parts, rights, lefts
        self.sent, self.came_right, self.came_left = sent, came_right, came_left

    def right(self, slot, j, k):
        return pltpu.make_async_remote_copy(
            src_ref=self.parts.at[slot, j], dst_ref=self.rights.at[slot, k],
            send_sem=self.sent.at[slot, j], recv_sem=self.came_right.at[slot, k],
            device_id={"mp": self.place + 1}, device_id_type=MESH,
        )

    def left(self, slot, j, k):
        return pltpu.make_async_remote_copy(
            src_ref=self.parts.at[slot, j], dst_ref=self.lefts.at[slot, k],
            send_sem=self.sent.at[slot, j], recv_sem=self.came_left.at[slot, k],
            device_id={"mp": self.place - 1}, device_id_type=MESH,
        )

    def clear(self):
        for slot in range(self.parts.shape[0]):
            last = self.size - 2
            blank = jnp.zeros(self.rights.shape[2:], BF16)
            self.rights[slot, last] = blank
            self.lefts[slot, last] = blank

    def start(self, slot):
        z, n = self.place, self.size

        @pl.when(z == 0)
        def _():
            for j in reversed(range(1, n)):
                self.right(slot, j, n - 1 - j).start()

        @pl.when(z == n - 1)
        def _():
            for j in range(n - 1):
                self.left(slot, j, j).start()

    def step(self, slot, s):
        z, n = self.place, self.size
        back = n - 1 - z

        @pl.when((z >= 1) & (z <= n - 2) & (s >= z))
        def _():
            j = n - 1 + z - s
            self.right(slot, j, s - 1).wait_recv()
            self.add(slot, j, self.rights, s - 1)
            self.right(slot, j, s).start()

        @pl.when((back >= 1) & (back <= n - 2) & (s >= back))
        def _():
            j = s - back
            self.left(slot, j, s - 1).wait_recv()
            self.add(slot, j, self.lefts, s - 1)
            self.left(slot, j, s).start()

    def add(self, slot, j, came, k):
        self.parts[slot, j] = (
            self.parts[slot, j].astype(F32) + came[slot, k].astype(F32)
        ).astype(BF16)

    def finish(self, slot):
        z, n = self.place, self.size

        @pl.when(z >= 1)
        def _():
            self.right(slot, z, n - 2).wait_recv()

        @pl.when(z <= n - 2)
        def _():
            self.left(slot, z, n - 2).wait_recv()

    def total(self, slot, rows):
        z, n = self.place, self.size
        return (
            self.parts[slot, z, rows, :].astype(F32)
            + self.rights[slot, n - 2, rows, :].astype(F32)
            + self.lefts[slot, n - 2, rows, :].astype(F32)
        )

    def drain(self, slot):
        for j in range(self.size):

            @pl.when(j != self.place)
            def _(j=j):
                self.right(slot, j, 0).wait_send()


def partners(d):
    core, x, y = lax.rem(d, 2), lax.rem(lax.div(d, 2), 2), lax.div(d, 4)
    return core, d + 1 - 2 * core, d + 2 - 4 * x, d + 4 - 8 * y


class Square:
    def __init__(self, d, shard, whole, sent, came, own):
        self.d, self.shard, self.whole = d, shard, whole
        self.sent, self.came, self.own = sent, came, own
        self.core, self.by_core, self.by_x, self.by_y = partners(d)

    def rows(self, d):
        count = self.shard.shape[0]
        return self.whole.at[pl.ds(pl.multiple_of(d * count, count), count), :]

    def copy(self, src, origin, target, sent, came):
        return pltpu.make_async_remote_copy(
            src_ref=src, dst_ref=self.rows(origin), send_sem=self.sent.at[sent],
            recv_sem=self.came.at[came], device_id={"dp": target}, device_id_type=MESH,
        )

    def local(self):
        return pltpu.make_async_copy(self.shard, self.rows(self.d), self.own)

    def far(self):
        return partners(self.by_x)[3]

    def first(self):
        return (
            self.copy(self.shard, self.d, self.by_x, 0, 2),
            self.copy(self.shard, self.d, self.by_y, 1, 4),
            self.copy(self.shard, self.d, self.by_core, 2, 1),
        )

    def start(self):
        for copy in self.first():
            copy.start()
        self.local().start()

    def step_one(self):
        x_rows, y_rows = self.rows(self.by_x), self.rows(self.by_y)
        by_x = self.copy(x_rows, self.by_x, self.by_core, 3, 2)
        by_y = self.copy(y_rows, self.by_y, self.by_core, 4, 4)
        by_x.wait_recv()

        @pl.when(self.core == 0)
        def _():
            self.copy(x_rows, self.by_x, self.by_y, 5, 6).start()

        self.copy(x_rows, self.by_x, self.by_core, 3, 3).start()
        by_y.wait_recv()

        @pl.when(self.core == 1)
        def _():
            self.copy(y_rows, self.by_y, self.by_x, 5, 6).start()

        self.copy(y_rows, self.by_y, self.by_core, 4, 5).start()

    def step_two(self):
        far = self.far()
        rows = self.rows(far)
        self.copy(rows, far, self.by_core, 6, 6).wait_recv()
        self.copy(rows, far, self.by_core, 6, 7).start()

    def finish(self):
        for k in (1, 3, 5, 7):
            self.copy(self.shard, self.d, self.by_core, 0, k).wait_recv()
        self.local().wait()

    def drain(self):
        for k in range(7):
            self.copy(self.shard, self.d, self.by_core, k, 0).wait_send()


class Scatter:
    def __init__(self, d, count, compute, held, far, first, second, sent, came):
        self.d, self.count, self.compute = d, count, compute
        self.held, self.far_in, self.first_in, self.second_in = held, far, first, second
        self.sent, self.came = sent, came
        self.core, self.by_core, by_x, by_y = partners(d)
        even = self.core == 0
        self.first = jnp.where(even, by_y, by_x)
        self.second = jnp.where(even, by_x, by_y)
        self.first_at, self.second_at = 2 - self.core, 1 + self.core
        other = partners(self.by_core)
        self.away = (self.by_core, other[2], other[3], partners(other[2])[3])
        self.distant = partners(by_x)[3]

    def owners(self):
        return [self.away[k] for k in (3, 1, 2, 0)] + [
            self.distant, self.first, self.d, self.second
        ]

    def copy(self, src, dst, target, sent, came):
        return pltpu.make_async_remote_copy(
            src_ref=src, dst_ref=dst, send_sem=self.sent.at[sent], recv_sem=self.came.at[came],
            device_id={"dp": target}, device_id_type=MESH,
        )

    def to_core(self, buffer, k):
        return self.copy(buffer, self.held(k), self.by_core, k, k)

    def to_far(self):
        return self.copy(self.held(3), self.far_in, self.first, 4, 4)

    def to_first(self):
        return self.copy(self.held(self.first_at), self.first_in, self.first, 5, 5)

    def to_second(self):
        return self.copy(self.held(self.second_at), self.second_in, self.second, 6, 6)

    def far_core(self, buffers, sending):
        for slot, k in enumerate((3, 1, 2, 0)):
            if sending[slot] is not None:
                sending[slot].wait_send()
            self.compute(self.away[k], buffers[slot], False)
            copy = self.to_core(buffers[slot], k)
            copy.start()
            sending[slot] = copy

    def add_block(self, k, came, owner):
        self.copy(self.held(k), self.held(k), self.by_core, k, came).wait_recv()
        self.compute(owner, self.held(k), True)

    def near_core(self):
        self.add_block(3, 3, self.distant)
        self.to_far().start()
        self.add_block(self.first_at, self.first_at, self.first)
        self.to_first().start()
        self.add_block(0, 0, self.d)
        self.add_block(self.second_at, self.second_at, self.second)

    def onward(self):
        self.to_far().wait_recv()
        held = self.held(self.second_at)

        def body(t):
            rows = rows_at(t, 16)
            held[rows, :] = (
                held[rows, :].astype(F32) + self.far_in[rows, :].astype(F32)
            ).astype(BF16)

        tile_loop(self.count // 16, body)
        self.to_second().start()

    def finish(self, target):
        self.to_first().wait_recv()
        self.to_second().wait_recv()
        held = self.held(0)

        def body(t):
            rows = rows_at(t, 16)
            target[rows, :] = (
                held[rows, :].astype(F32)
                + self.first_in[rows, :].astype(F32)
                + self.second_in[rows, :].astype(F32)
            )

        tile_loop(self.count // 16, body)

    def drain(self):
        self.to_far().wait_send()
        self.to_first().wait_send()
        self.to_second().wait_send()


def head_kernel(dp, mp, names, *refs):
    ref = dict(zip(names, refs))
    blocks, w_in, norm, both = ref["blocks"], ref["w_in_here"], ref["norm"], ref["both_here"]
    chunks, _, step, part = blocks.shape
    features, width = part * mp, ref["mixed_here"].shape[2]
    z, d = lax.axis_index("mp"), lax.axis_index("dp")
    square = dp == 8
    gather = Spread(z, mp, blocks, ref["spread_sent"], ref["spread_came"])

    barrier = pltpu.get_barrier_semaphore()

    @pl.when(z > 0)
    def _():
        pl.semaphore_signal(barrier, inc=1, device_id={"mp": z - 1}, device_id_type=MESH)

    @pl.when(z < mp - 1)
    def _():
        pl.semaphore_signal(barrier, inc=1, device_id={"mp": z + 1}, device_id_type=MESH)

    count = jnp.where((z > 0) & (z < mp - 1), 2, 1)
    if square:
        for other in partners(d)[1:]:
            pl.semaphore_signal(barrier, inc=1, device_id={"dp": other}, device_id_type=MESH)
        count = count + 3

    def chunk_rows(c):
        return pl.ds(c * step, step)

    def own_block(c):
        return pltpu.make_async_copy(
            ref["x"].at[chunk_rows(c), :], blocks.at[c, z], ref["load_sem"].at[c]
        )

    for c in range(chunks):
        own_block(c).start()
    pl.semaphore_wait(barrier, count)

    wholes = (
        ("gates_shard", ref["gates_here"]), ("in_shard", w_in), ("out_shard", ref["w_out"]),
        ("gate_shard", ref["w_gate"]),
    )
    if square:
        squares = [
            Square(
                d, ref[name], whole, ref["square_sent"].at[k], ref["square_came"].at[k],
                ref["square_own"].at[k],
            )
            for k, (name, whole) in enumerate(wholes)
        ]
        for item in squares[:2]:
            item.start()
    else:
        loads = [
            pltpu.make_async_copy(ref[name], whole, ref["square_own"].at[k])
            for k, (name, whole) in enumerate(wholes)
        ]
        for item in loads:
            item.start()

    def begin(c):
        own_block(c).wait()
        gather.step(c, 0)

    begin(0)
    if chunks > 1:
        begin(1)

    def expand():
        span = ref["gates_flat"].shape[0]
        rows = span // 8
        for k in range(8):
            ref["gates_flat"][k * rows : (k + 1) * rows, :] = ref["gates_here"][
                k * 32 : k * 32 + 32, :
            ].astype(F32)[0:rows, :]
        column = lax.broadcasted_iota(jnp.int32, (span, 2 * width), 1)
        column = jnp.where(column >= width, column - width, column)
        for b in range(width // span):
            inside = (column >= b * span) & (column < (b + 1) * span)
            ref["dense_here"][b * span : (b + 1) * span, :] = jnp.where(
                inside, ref["gates_flat"][...], 0.0
            ).astype(BF16)

    stores = (
        ("norm", "norm"), ("both", "both_here"), ("conv", "conv_here"), ("r", "r_here"),
        ("i", "i_here"), ("state", "state_here"), ("mixed", "mixed_here"), ("s1", "s1_here"),
    )

    def store_all(c):
        return [
            pltpu.make_async_copy(
                ref[near].at[c % 2], ref[far + "_out"].at[chunk_rows(c), :],
                ref["store_sem"].at[c % 2, k],
            )
            for k, (far, near) in enumerate(stores)
        ]

    ref["halo"][...] = jnp.zeros_like(ref["halo"])
    ref["start"][...] = jnp.zeros_like(ref["start"])

    def compute(c):
        slot = c % 2
        if c > 1:
            for copy in store_all(c - 2):
                copy.wait()

        def body(t):
            rows = rows_at(t, TILE)
            values = [blocks[c, j, rows, :].astype(F32) for j in range(mp)]
            total = sum(jnp.sum(v * v, axis=1, keepdims=True) for v in values)
            s1 = lax.rsqrt(total / features + EPS)
            for j in range(mp):
                cols = slice(j * part, (j + 1) * part)
                norm[slot, rows, cols] = (values[j] * s1 * ref["gains"][0:1, cols]).astype(BF16)
            ref["s1_here"][slot, rows, :] = jnp.broadcast_to(s1, (TILE, 128))

        tile_loop(step // TILE, body)
        for k in range(2):
            cols = slice(k * width, (k + 1) * width)
            both[slot, :, cols] = matmul(norm[slot], w_in[:, cols])
        rnn_forward_kernel(
            both.at[slot], ref["halo"], ref["start"], ref["mask"].at[chunk_rows(c), :],
            ref["dense_here"], ref["params"],
            ref["mixed_here"].at[slot], ref["conv_here"].at[slot], ref["r_here"].at[slot],
            ref["i_here"].at[slot], ref["state_here"].at[slot], ref["end"],
            ref["padded"], ref["high"], ref["low"], ref["decay"], ref["drive"],
        )
        ref["halo"][...] = both[slot, step - 8 :, 0:width]
        ref["start"][...] = ref["end"][...]
        for copy in store_all(c):
            copy.start()

    for s in range(1, mp - 1):
        gather.step(0, s)
        if s == 1 and chunks > 2:
            begin(2)
    if square:
        for item in squares[:2]:
            item.step_one()
        squares[2].start()
        for item in squares[:2]:
            item.step_two()
    gather.finish(0)
    for c in range(chunks):
        if c + 1 < chunks:
            gather.step(c + 1, 1)
        if c == 0:
            if square:
                for item in squares[:2]:
                    item.finish()
            else:
                for item in loads:
                    item.wait()
            expand()
            pass_on = [
                pltpu.make_async_copy(w_in, ref["w_in"], ref["pass_sem"].at[0]),
                pltpu.make_async_copy(ref["dense_here"], ref["dense"], ref["pass_sem"].at[1]),
            ]
            for copy in pass_on:
                copy.start()
        if c == 3 and square:
            squares[3].step_one()
        compute(c)
        if c == 0 and square:
            squares[2].step_one()
            squares[3].start()
        if c == 1 and square:
            squares[2].step_two()
        if c + 3 < chunks:
            begin(c + 3)
        if c + 1 < chunks:
            for s in range(2, mp - 1):
                gather.step(c + 1, s)
            gather.finish(c + 1)
    if square:
        squares[3].step_two()
        squares[2].finish()
        squares[3].finish()
        for item in squares:
            item.drain()
    for copy in pass_on:
        copy.wait()
    for c in range(max(0, chunks - 2), chunks):
        for copy in store_all(c):
            copy.wait()
    for c in range(chunks):
        gather.drain(c)


def head(
    dp, mp, chunks, x, gains, params, mask, in_shard, out_shard, gate_shard, gates_shard, span
):
    count, part = x.shape
    features, width = part * mp, params.shape[1]
    step = count // chunks
    dma = pltpu.SemaphoreType.DMA
    any_, vmem = pl.BlockSpec(memory_space=pl.ANY), pl.BlockSpec(memory_space=pltpu.VMEM)
    ins = [
        ("x", x, any_), ("gains", gains, vmem), ("params", params, vmem), ("mask", mask, vmem),
        ("in_shard", in_shard, any_), ("out_shard", out_shard, any_),
        ("gate_shard", gate_shard, any_), ("gates_shard", gates_shard, any_),
    ]
    gate_width = gate_shard.shape[1]
    shape = jax.ShapeDtypeStruct
    outs = [
        ("w_in", shape((features, 2 * width), BF16)), ("w_out", shape((features, width), BF16)),
        ("w_gate", shape((features, gate_width), BF16)), ("dense", shape((width, 2 * width), BF16)), ("norm_out", shape((count, features), BF16)),
        ("both_out", shape((count, 2 * width), F32)), ("conv_out", shape((count, width), F32)),
        ("r_out", shape((count, width), F32)), ("i_out", shape((count, width), F32)),
        ("state_out", shape((count, width), F32)), ("mixed_out", shape((count, width), BF16)),
        ("s1_out", shape((count, 128), F32)),
    ]
    wide = pltpu.VMEM((2, step, width), F32)
    columns = pltpu.VMEM((width // 128, step, 128), F32)
    scratch = [
        ("blocks", pltpu.VMEM((chunks, mp, step, part), BF16)),
        ("w_in_here", pltpu.VMEM((features, 2 * width), BF16)),
        ("gates_here", pltpu.VMEM((256, 2 * width), BF16)),
        ("gates_flat", pltpu.VMEM((span, 2 * width), F32)),
        ("dense_here", pltpu.VMEM((width, 2 * width), BF16)),
        ("norm", pltpu.VMEM((2, step, features), BF16)),
        ("both_here", pltpu.VMEM((2, step, 2 * width), F32)),
        ("conv_here", wide), ("r_here", wide), ("i_here", wide), ("state_here", wide),
        ("mixed_here", pltpu.VMEM((2, step, width), BF16)),
        ("s1_here", pltpu.VMEM((2, step, 128), F32)),
        ("halo", pltpu.VMEM((8, width), F32)), ("start", pltpu.VMEM((8, width), F32)),
        ("end", pltpu.VMEM((8, width), F32)),
        ("padded", pltpu.VMEM((step + 8, width), F32)),
        ("high", pltpu.VMEM((step, width), BF16)), ("low", pltpu.VMEM((step, width), BF16)),
        ("decay", columns), ("drive", columns),
        ("spread_sent", dma((chunks, 2 * mp))), ("spread_came", dma((chunks, mp))),
        ("square_sent", dma((4, 8))), ("square_came", dma((4, 8))), ("square_own", dma((4,))),
        ("load_sem", dma((chunks,))), ("store_sem", dma((2, 8))), ("pass_sem", dma((2,))),
    ]
    names = [i[0] for i in ins] + [o[0] for o in outs] + [k[0] for k in scratch]
    return pl.pallas_call(
        functools.partial(head_kernel, dp, mp, tuple(names)),
        in_specs=[i[2] for i in ins],
        out_specs=[any_] * len(outs),
        out_shape=[o[1] for o in outs],
        scratch_shapes=[k[1] for k in scratch],
        compiler_params=pltpu.CompilerParams(
            collective_id=2, has_side_effects=True, vmem_limit_bytes=60 * 1024 * 1024
        ),
        name="head",
    )(*[i[1] for i in ins])


MIDDLE_ORDER = (
    ("d", 0, 0), ("A", 0, 0), ("d", 0, 1), ("d", 0, 2), ("a", 1, 0), ("d", 1, 0), ("a", 2, 0),
    ("d", 0, 3), ("J", 0, 0), ("d", 2, 0), ("e", 0, 0), ("A", 0, 1), ("e", 1, 0), ("e", 2, 0),
    ("a", 1, 1), ("d", 1, 2), ("e", 3, 0), ("A", 0, 2), ("S", 1, 0), ("a", 2, 1), ("d", 1, 1),
    ("S", 2, 0), ("d", 2, 2), ("J", 0, 1), ("d", 3, 0), ("a", 1, 2), ("e", 0, 1), ("S", 3, 0),
    ("H", 0, 0), ("a", 2, 2), ("d", 1, 3), ("d", 2, 1), ("G", 0, 0), ("d", 3, 2), ("c", 1, 0),
    ("e", 1, 1), ("J", 0, 2), ("e", 0, 2), ("d", 3, 1), ("e", 2, 1), ("O", 0, 0), ("e", 3, 1),
    ("b", 1, 0), ("c", 2, 0), ("A", 0, 3), ("e", 1, 2), ("K", 0, 0), ("a", 1, 3), ("b", 2, 0),
    ("e", 2, 2), ("H", 0, 1), ("d", 2, 3), ("G", 0, 1), ("e", 3, 2), ("O", 0, 1), ("f", 1, 0),
    ("c", 1, 1), ("a", 2, 3), ("c", 2, 1), ("Y", 0, 0), ("f", 2, 0), ("b", 1, 1), ("J", 0, 3),
    ("K", 0, 1), ("H", 0, 2), ("e", 0, 3), ("B", 0, 0), ("f", 1, 1), ("G", 0, 2), ("e", 1, 3),
    ("f", 2, 1), ("c", 1, 2), ("b", 2, 1), ("c", 2, 2), ("B", 0, 1), ("e", 2, 3), ("Y", 0, 1),
    ("K", 0, 2), ("O", 0, 2), ("e", 3, 3), ("f", 1, 2), ("d", 3, 3), ("H", 0, 3), ("f", 2, 2),
    ("G", 0, 3), ("b", 1, 2), ("B", 0, 2), ("O", 0, 3), ("D", 0, 0), ("c", 1, 3), ("W", 0, 0),
    ("D", 0, 1), ("c", 2, 3), ("D", 0, 2), ("K", 0, 3), ("W", 0, 1), ("b", 2, 2), ("D", 0, 3),
    ("W", 0, 2), ("D", 0, 4), ("Z", 0, 0), ("W", 0, 3), ("f", 1, 3), ("D", 0, 5), ("b", 1, 3),
    ("f", 2, 3), ("Z", 0, 1), ("b", 2, 3), ("W", 0, 4), ("B", 0, 3), ("W", 0, 5), ("Y", 0, 2),
    ("Z", 0, 2), ("Y", 0, 3), ("Z", 0, 3), ("Z", 0, 4), ("Z", 0, 5),
)


def middle_kernel(dp, mp, chunks, *refs):
    (
        mixed_ref, x_ref, cot_ref, live_ref, gains_ref, mine_ref, wout_ref, gate_ref, up_ref,
        down_ref,
        output_ref, gm_ref, gbo_ref, local_ref, hidden_ref, pulled_ref, norm_ref, grady_ref,
        grad_gate_ref, grad_up_ref, gain_ref,
        w_up, w_down, cots, mids, gn2s, mid_mine, gn2_mine,
        parts1, rights1, lefts1, parts2, rights2, lefts2, parts3, rights3, lefts3,
        norm, hidden, pulled, gbo, gm, local, out,
        spread_sent, spread_came, fold_sent, fold_right, fold_left,
        square_sent, square_came, square_own, load_sem, store_sem,
        stage, free_sem, task_sent, task_came, left_sem, right_sem, stage_sem,
    ) = refs
    step, part = x_ref.shape[0] // chunks, x_ref.shape[1]
    features = part * mp
    hidden_width = w_down.shape[1]
    z, d = lax.axis_index("mp"), lax.axis_index("dp")
    square = dp == 8
    up_half = w_up.at[:, pl.ds(hidden_width, hidden_width)]

    folds = [
        Fold(z, mp, p, r, l, fold_sent.at[k], fold_right.at[k], fold_left.at[k])
        for k, (p, r, l) in enumerate(
            ((parts1, rights1, lefts1), (parts2, rights2, lefts2), (parts3, rights3, lefts3))
        )
    ]
    rs1, rs2, rs3 = folds
    ag2, ag3, ag4 = [
        Spread(z, mp, b, spread_sent.at[k], spread_came.at[k])
        for k, b in enumerate((cots, mids, gn2s))
    ]
    for fold in folds:
        fold.clear()

    barrier = pltpu.get_barrier_semaphore()

    @pl.when(z > 0)
    def _():
        pl.semaphore_signal(barrier, inc=1, device_id={"mp": z - 1}, device_id_type=MESH)

    @pl.when(z < mp - 1)
    def _():
        pl.semaphore_signal(barrier, inc=1, device_id={"mp": z + 1}, device_id_type=MESH)

    count = jnp.where((z > 0) & (z < mp - 1), 2, 1)
    if square:
        for other in partners(d)[1:]:
            pl.semaphore_signal(barrier, inc=1, device_id={"dp": other}, device_id_type=MESH)
        count = count + 3
    pl.semaphore_wait(barrier, count)

    if square:
        squares = [
            Square(
                d, shard, whole, square_sent.at[k], square_came.at[k], square_own.at[k]
            )
            for k, (shard, whole) in enumerate(((up_ref, up_half), (down_ref, w_down)))
        ]
        for item in squares:
            item.start()
    else:
        loads = [
            pltpu.make_async_copy(up_ref, up_half, square_own.at[0]),
            pltpu.make_async_copy(down_ref, w_down, square_own.at[1]),
        ]
        for item in loads:
            item.start()
    load_gate = pltpu.make_async_copy(
        gate_ref, w_up.at[:, pl.ds(0, hidden_width)], square_own.at[2]
    )
    load_gate.start()

    def chunk_rows(c):
        return pl.ds(c * step, step)

    def store(buffer, target, c, k):
        return pltpu.make_async_copy(buffer, target.at[chunk_rows(c), :], store_sem.at[k])

    def own_cot(c):
        return pltpu.make_async_copy(cot_ref.at[chunk_rows(c), :], cots.at[c, z], load_sem.at[c])

    for c in range(chunks):
        own_cot(c).start()

    gain_ref[...] = jnp.zeros_like(gain_ref)
    tiles = step // TILE

    def fill(fold, slot, left, weights):
        def body(j):
            rows = pl.ds(pl.multiple_of(j * part, part), part)
            fold.parts[slot, j] = inner_cols(left, weights[rows, :]).astype(BF16)

        tile_loop(mp, body)

    def branch(c):
        if c > 1:
            rs1.drain(c % 2)
        fill(rs1, c % 2, mixed_ref[chunk_rows(c), :], wout_ref)
        rs1.start(c % 2)

    def join(c):
        rs1.finish(c % 2)

        def body(t):
            rows = rows_at(t, TILE)
            base = pl.ds(pl.multiple_of(c * step + t * TILE, TILE), TILE)
            total = x_ref[base, :].astype(F32) + rs1.total(c % 2, rows)
            mid_mine[c, rows, :] = total
            mids[c, z, rows, :] = total.astype(BF16)

        tile_loop(tiles, body)

    def stats(c, rows):
        blocks = [mids[c, j, rows, :].astype(F32) for j in range(mp)]
        square_sum = sum(jnp.sum(b * b, axis=1, keepdims=True) for b in blocks)
        return blocks, lax.rsqrt(square_sum / features + EPS)

    def block_cols(j):
        return slice(j * part, (j + 1) * part)

    def normalise(c):
        def body(t):
            rows = rows_at(t, TILE)
            base = pl.ds(pl.multiple_of(c * step + t * TILE, TILE), TILE)
            blocks, s2 = stats(c, rows)
            live = live_ref[base, :][:, 0:1]
            for j in range(mp):
                norm[rows, block_cols(j)] = (
                    blocks[j] * s2 * gains_ref[1:2, block_cols(j)]
                ).astype(BF16)
                cots[c, j, rows, :] = (cots[c, j, rows, :].astype(F32) * live).astype(BF16)

        tile_loop(tiles, body)

    def grad_y_copies(c):
        return [
            pltpu.make_async_copy(
                cots.at[c, j], grady_ref.at[chunk_rows(c), pl.ds(j * part, part)],
                store_sem.at[8 + j],
            )
            for j in range(mp)
        ]

    def mlp_first(c):
        if c > 0:
            store(norm, norm_ref, c, 0).wait()
            store(hidden, hidden_ref, c, 1).wait()
            store(pulled, pulled_ref, c, 2).wait()
            for copy in grad_y_copies(c - 1):
                copy.wait()
        if c == 0:
            load_gate.wait()
            for item in squares if square else ():
                item.finish()
            for item in () if square else loads:
                item.wait()
        ag2.drain(c)
        normalise(c)
        store(norm, norm_ref, c, 0).start()
        for copy in grad_y_copies(c):
            copy.start()
        size = 256

        def body(t):
            near = pl.ds(pl.multiple_of(t * size, size), size)
            off = pl.ds(pl.multiple_of(hidden_width + t * size, size), size)
            gate = matmul(norm[...], w_up[:, near])
            up = matmul(norm[...], w_up[:, off])
            grad = sum(
                matmul(cots[c, j], w_down[block_cols(j), near]) for j in range(mp)
            )
            value, slope = gelu_and_slope(gate)
            hidden[:, near] = (value * up).astype(BF16)
            pulled[:, near] = (grad * up * slope).astype(BF16)
            pulled[:, off] = (grad * value).astype(BF16)

        tile_loop(hidden_width // size, body)
        store(hidden, hidden_ref, c, 1).start()
        store(pulled, pulled_ref, c, 2).start()

    def mlp_second(c):
        slot = c % 2
        if c > 1:
            rs3.drain(slot)
        fill(rs3, slot, pulled[...], w_up)
        rs3.start(slot)
        if square and c == chunks - 1:
            for item in squares:
                item.drain()
            for k, other in enumerate(partners(d)[1:]):
                pl.semaphore_signal(
                    free_sem.at[k], inc=1, device_id={"dp": other}, device_id_type=MESH
                )

    def mlp_third(c):
        slot = c % 2
        if c > 1:
            rs2.drain(slot)
        fill(rs2, slot, hidden[...], w_down)
        rs2.start(slot)

    def gather_grad(c):
        slot = c % 2
        rs3.finish(slot)

        def body(t):
            rows = rows_at(t, TILE)
            total = rs3.total(slot, rows)
            gn2_mine[slot, rows, :] = total
            gn2s[c, z, rows, :] = total.astype(BF16)

        tile_loop(tiles, body)
        ag4.step(c, 0)

    def norm_back(c):
        slot = c % 2
        ag4.finish(c)
        if c > 0:
            store(gbo, gbo_ref, c, 3).wait()
            store(local, local_ref, c, 4).wait()
            store(gm, gm_ref, c, 5).wait()

        def body(t):
            rows = rows_at(t, TILE)
            blocks, s2 = stats(c, rows)
            grads = [gn2s[c, j, rows, :].astype(F32) for j in range(mp)]
            scaled = [grads[j] * gains_ref[1:2, block_cols(j)] for j in range(mp)]
            mean = (
                sum(jnp.sum(scaled[j] * blocks[j], axis=1, keepdims=True) for j in range(mp))
                / features
            )
            fall = s2 * s2 * s2 * mean
            for j in range(mp):
                grad_y = cots[c, j, rows, :].astype(F32)
                gbo[rows, block_cols(j)] = (
                    grad_y + s2 * scaled[j] - blocks[j] * fall
                ).astype(BF16)
                gain_ref[:, block_cols(j)] += jnp.sum(
                    (grads[j] * (blocks[j] * s2)).reshape(-1, 8, part), axis=0
                )
            local[rows, :] = (
                cots[c, z, rows, :].astype(F32)
                + s2 * (gn2_mine[slot, rows, :] * mine_ref[1:2, :])
                - mid_mine[c, rows, :] * fall
            )

        tile_loop(tiles, body)
        gm[...] = matmul(gbo[...], wout_ref[...])
        store(gbo, gbo_ref, c, 3).start()
        store(local, local_ref, c, 4).start()
        store(gm, gm_ref, c, 5).start()

    def make_output(c):
        rs2.finish(c % 2)
        if c > 0:
            store(out, output_ref, c, 6).wait()

        def body(t):
            rows = rows_at(t, TILE)
            out[rows, :] = (mid_mine[c, rows, :] + rs2.total(c % 2, rows)).astype(BF16)

        tile_loop(tiles, body)
        store(out, output_ref, c, 6).start()

    own = features // 8
    count_tasks = 2 * hidden_width // part
    scatters, sending = [], [None] * 4
    buffers = [rights1.at[i // 2, i % 2] for i in range(4)]
    staged = [None]

    def left_block(i):
        return (cots if i < 2 else mids).at[i % 2]

    def left_copies():
        return [
            pltpu.make_async_copy(
                norm_ref.at[chunk_rows(i), pl.ds(j * part, part)], left_block(i).at[j],
                left_sem.at[i, j],
            )
            for i in range(chunks)
            for j in range(mp)
        ]

    def right_copies(k):
        return [
            pltpu.make_async_copy(
                pulled_ref.at[chunk_rows(i), pl.ds(k * part, part)], parts1.at[k % 2, i],
                right_sem.at[k % 2, i],
            )
            for i in range(chunks)
        ]

    def make_scatter(k):
        def compute(owner, target, add):
            j = lax.div(owner, 2)
            near = pl.ds(pl.multiple_of(lax.rem(owner, 2) * own, own), own)
            value = sum(
                inner_rows(left_block(i)[j, :, near], parts1[k % 2, i]) for i in range(chunks)
            )
            if add:
                value = value + target[...].astype(F32)
            target[...] = value.astype(BF16)

        cols = pl.ds(k * part, part)

        def place(first):
            return w_up.at[pl.ds(first, own), cols]

        def held(i):
            return w_up.at[pl.ds(pl.multiple_of(i * own, own), own), cols]

        return Scatter(
            d, own, compute, held, place(4 * own), place(5 * own), place(6 * own),
            task_sent.at[k], task_came.at[k],
        )

    def weight_first(k):
        if not square:
            return
        if k == 0:
            store(norm, norm_ref, chunks - 1, 0).wait()
            store(pulled, pulled_ref, chunks - 1, 2).wait()
            for slot in range(2):
                rs1.drain(slot)
            for c in range(2):
                ag3.drain(c)
            scatters.extend(make_scatter(i) for i in range(count_tasks))
            for copy in right_copies(0) + left_copies():
                copy.start()
            for i in range(3):
                pl.semaphore_wait(free_sem.at[i], 1)
        if k + 1 < count_tasks:
            for copy in right_copies(k + 1):
                copy.start()
        for copy in right_copies(k) + (left_copies() if k == 0 else []):
            copy.wait()
        scatters[k].far_core(buffers, sending)
        scatters[k].near_core()

    def weight_second(k):
        if square:
            scatters[k].onward()

    def weight_third(k):
        if not square:
            return
        if staged[0] is not None:
            staged[0].wait()
        scatters[k].finish(stage)
        half = count_tasks // 2
        target = grad_gate_ref if k < half else grad_up_ref
        staged[0] = pltpu.make_async_copy(
            stage, target.at[:, pl.ds((k % half) * part, part)], stage_sem
        )
        staged[0].start()

    steps = {
        "A": branch, "J": join, "H": mlp_first, "G": mlp_second, "O": mlp_third,
        "K": gather_grad, "B": norm_back, "Y": make_output, "D": weight_first,
        "W": weight_second, "Z": weight_third,
    }
    moves = {"a": (rs1, 2), "b": (rs2, 2), "c": (rs3, 2), "d": (ag2, 0), "e": (ag3, 0), "f": (ag4, 0)}
    for name, s, c in MIDDLE_ORDER:
        if name == "S":
            if square and s < 3:
                squares[s - 1].step_one()
            if square and s == 3:
                squares[0].step_two()
                squares[1].step_two()
        elif name in steps:
            steps[name](c)
        else:
            line, parity = moves[name]
            if s == mp - 1:
                line.finish(c)
                continue
            if name == "d" and s == 0:
                own_cot(c).wait()
            line.step(c % parity if parity else c, s)

    last = chunks - 1
    for k, (buffer, target) in enumerate(
        (
            (norm, norm_ref), (hidden, hidden_ref), (pulled, pulled_ref), (gbo, gbo_ref),
            (local, local_ref), (gm, gm_ref), (out, output_ref),
        )
    ):
        if not (square and k in (0, 2)):
            store(buffer, target, last, k).wait()
    for copy in grad_y_copies(last):
        copy.wait()
    for c in range(chunks):
        if c > 1 or not square:
            ag3.drain(c)
        ag4.drain(c)
    for slot in range(2):
        for fold in folds[1:] if square else folds:
            fold.drain(slot)
    if square:
        staged[0].wait()
        for copy in sending:
            copy.wait_send()
        for scatter in scatters:
            scatter.drain()


def middle(dp, mp, chunks, mixed, inputs, cotangent, live, gains, mine, w_out, gate, up, down):
    count, part = inputs.shape
    width, hidden_width = mixed.shape[1], down.shape[1]
    step, features = count // chunks, part * mp

    def fold_buffers():
        return [
            pltpu.VMEM((2, mp, step, part), BF16),
            pltpu.VMEM((2, mp - 1, step, part), BF16),
            pltpu.VMEM((2, mp - 1, step, part), BF16),
        ]

    dma = pltpu.SemaphoreType.DMA
    any_, vmem = pl.BlockSpec(memory_space=pl.ANY), pl.BlockSpec(memory_space=pltpu.VMEM)
    return pl.pallas_call(
        functools.partial(middle_kernel, dp, mp, chunks),
        in_specs=[vmem, vmem, any_, vmem, vmem, vmem, vmem, any_, any_, any_],
        out_specs=[any_] * 10 + [vmem],
        out_shape=(
            jax.ShapeDtypeStruct((count, part), BF16),
            jax.ShapeDtypeStruct((count, width), F32),
            jax.ShapeDtypeStruct((count, features), BF16),
            jax.ShapeDtypeStruct((count, part), F32),
            jax.ShapeDtypeStruct((count, hidden_width), BF16),
            jax.ShapeDtypeStruct((count, 2 * hidden_width), BF16),
            jax.ShapeDtypeStruct((count, features), BF16),
            jax.ShapeDtypeStruct((count, features), BF16),
            jax.ShapeDtypeStruct((features // 8, hidden_width), F32),
            jax.ShapeDtypeStruct((features // 8, hidden_width), F32),
            jax.ShapeDtypeStruct((8, features), F32),
        ),
        scratch_shapes=[
            pltpu.VMEM((features, 2 * hidden_width), BF16),
            pltpu.VMEM((features, hidden_width), BF16),
            pltpu.VMEM((chunks, mp, step, part), BF16),
            pltpu.VMEM((chunks, mp, step, part), BF16),
            pltpu.VMEM((chunks, mp, step, part), BF16),
            pltpu.VMEM((chunks, step, part), F32),
            pltpu.VMEM((2, step, part), F32),
        ]
        + fold_buffers() + fold_buffers() + fold_buffers()
        + [
            pltpu.VMEM((step, features), BF16),
            pltpu.VMEM((step, hidden_width), BF16),
            pltpu.VMEM((step, 2 * hidden_width), BF16),
            pltpu.VMEM((step, features), BF16),
            pltpu.VMEM((step, width), F32),
            pltpu.VMEM((step, part), F32),
            pltpu.VMEM((step, part), BF16),
            dma((3, chunks, 2 * mp)),
            dma((3, chunks, mp)),
            dma((3, 2, mp)),
            dma((3, 2, mp)),
            dma((3, 2, mp)),
            dma((2, 8)),
            dma((2, 8)),
            dma((3,)),
            dma((chunks,)),
            dma((12,)),
            pltpu.VMEM((features // 8, part), F32),
            pltpu.SemaphoreType.REGULAR((3,)),
            dma((2 * hidden_width // part, 8)),
            dma((2 * hidden_width // part, 8)),
            dma((chunks, mp)),
            dma((2, chunks)),
            dma,
        ],
        compiler_params=pltpu.CompilerParams(
            collective_id=0, has_side_effects=True, vmem_limit_bytes=62 * 1024 * 1024
        ),
        name="middle",
    )(mixed, inputs, cotangent, live, gains, mine, w_out, gate, up, down)


def tail_kernel(mp, tasks, loaded, names, *refs):
    ref = dict(zip(names, refs))
    pull, w_in, norm1 = ref["pull"], ref["w_in"], ref["norm1_here"]
    count, part = ref["x"].shape
    features = part * mp
    halves = ref["parts"].shape[0]
    step = count // halves
    own = features // 8
    z, d = lax.axis_index("mp"), lax.axis_index("dp")
    core, by_core, by_x, by_y = partners(d)
    fold = Fold(
        z, mp, ref["parts"], ref["rights"], ref["lefts"], ref["fold_sent"], ref["fold_right"],
        ref["fold_left"],
    )
    fold.clear()
    near = z + 1 - 2 * lax.rem(z, 2)
    apart = z + 2 - 4 * lax.div(z, 2)

    barrier = pltpu.get_barrier_semaphore()

    @pl.when(z > 0)
    def _():
        pl.semaphore_signal(barrier, inc=1, device_id={"mp": z - 1}, device_id_type=MESH)

    @pl.when(z < mp - 1)
    def _():
        pl.semaphore_signal(barrier, inc=1, device_id={"mp": z + 1}, device_id_type=MESH)

    pl.semaphore_signal(barrier, inc=1, device_id={"mp": apart}, device_id_type=MESH)
    for other in (by_core, by_x, by_y):
        pl.semaphore_signal(barrier, inc=1, device_id={"dp": other}, device_id_type=MESH)
    pl.semaphore_wait(barrier, jnp.where((z > 0) & (z < mp - 1), 6, 5))

    sends, store_sem = ref["sends"], ref["store_sem"]
    loads = {
        name: pltpu.make_async_copy(ref[name], ref[name + "_here"], ref["load_sem"].at[k])
        for k, name in enumerate(loaded)
    }
    for copy in loads.values():
        copy.start()

    def ready(name):
        if name in loads:
            loads.pop(name).wait()

    def operand(name):
        return ref[name + "_here"] if name in loaded else ref[name]

    def build(k):
        _, left, right, first, width, _ = tasks[k]

        def compute(owner, target, add):
            if left is None:
                rows = pl.ds(pl.multiple_of(owner * 32, 32), 32)
                value = ref["gates"][rows, first : first + width].astype(F32)
            else:
                cols = pl.ds(pl.multiple_of(owner * own, own), own)
                value = inner_rows(
                    operand(left)[:, cols], operand(right)[:, first : first + width]
                )
            if add:
                value = value + target[...].astype(F32)
            target[...] = value.astype(BF16)

        return Scatter(
            d, 32 if left is None else own, compute, ref["held%d" % k].at.__getitem__,
            ref["far%d" % k], ref["first%d" % k], ref["second%d" % k], ref["task_sent"].at[k],
            ref["task_came"].at[k],
        )

    scatters = [build(k) for k in range(len(tasks))]
    sending = [None] * 4

    def far_core(k):
        height, width = scatters[k].count, tasks[k][4]
        scatters[k].far_core(
            [sends.at[slot, pl.ds(0, height), pl.ds(0, width)] for slot in range(4)], sending
        )

    stage, stage_wait = ref["stage"], [None, None]

    def finish(k):
        scatter = scatters[k]
        name, width, column = tasks[k][0], tasks[k][4], tasks[k][5]
        slot = k % 2
        if stage_wait[slot] is not None:
            stage_wait[slot].wait()
        view = stage.at[slot, pl.ds(0, scatter.count), pl.ds(0, width)]
        scatter.finish(view)
        target = ref["grad_" + name].at[:, pl.ds(column, width)]
        copy = pltpu.make_async_copy(view, target, store_sem.at[slot])
        copy.start()
        stage_wait[slot] = copy

    dots, dots_in = ref["dots_row"], ref["dots_in"]
    for q in range(count // 128):
        turned = jnp.transpose(ref["dots"][q * 128 : (q + 1) * 128, :])
        dots[:, q * 128 : (q + 1) * 128] = turned[0:8, :]

    def dots_copy(k):
        return pltpu.make_async_remote_copy(
            src_ref=dots, dst_ref=dots_in.at[k], send_sem=ref["dots_sent"].at[k],
            recv_sem=ref["dots_came"].at[k], device_id={"mp": near if k == 0 else apart},
            device_id_type=MESH,
        )

    def dots_add(k):
        dots_copy(k).wait()
        dots[...] += dots_in[k]

    dots_copy(0).start()
    gain = ref["gain"]
    gain[...] = jnp.zeros_like(gain)
    ready("norm1")
    for c in range(halves):

        def body(j, c=c):
            rows = pl.ds(pl.multiple_of(j * part, part), part)
            for q in range(step // 256):
                tokens = pl.ds(c * step + q * 256, 256)
                value = inner_cols(pull[tokens, :], w_in[rows, :])
                fold.parts[c, j, q * 256 : (q + 1) * 256, :] = value.astype(BF16)
                gain[:, rows] += jnp.sum(
                    (value * norm1[tokens, rows].astype(F32)).reshape(-1, 8, part), axis=0
                )

        tile_loop(mp, body)
        if c == 0:
            dots_add(0)
            dots_copy(1).start()
        fold.start(c)

    small, small_in = ref["small"], ref["small_in"]
    small[...] = ref["small_start"][...]
    small[0:1, :] = jnp.sum(gain[...], axis=0, keepdims=True) / ref["gains"][0:1, :]
    targets = (
        {"dp": by_core}, {"dp": by_x}, {"dp": by_y}, {"mp": near}, {"mp": apart},
    )

    def small_copy(k):
        rows = pl.ds(0, 16 if k < 3 else 8)
        return pltpu.make_async_remote_copy(
            src_ref=small.at[rows, :], dst_ref=small_in.at[k, rows, :],
            send_sem=ref["small_sent"].at[k], recv_sem=ref["small_came"].at[k],
            device_id=targets[k], device_id_type=MESH,
        )

    def small_add(k):
        rows = 16 if k < 3 else 8
        small_copy(k).wait()
        small[0:rows, :] += small_in[k, 0:rows, :]

    ready("x")
    ready("s1")

    def local_copy(c):
        return pltpu.make_async_copy(
            ref["local"].at[pl.ds(c * step, step), :], ref["near_local"], ref["local_sem"]
        )

    local_copy(0).start()

    def input_grad(c):
        fold.finish(c)
        local_copy(c).wait()

        def body(t):
            rows = rows_at(t, TILE)
            base = pl.ds(pl.multiple_of(c * step + t * TILE, TILE), TILE)
            s1 = ref["s1_here"][base, :][:, 0:1]
            dot = ref["dots_col"][base, :][:, 0:1]
            grad = (
                ref["near_local"][rows, :]
                + s1 * (fold.total(c, rows) * ref["mine"][0:1, :])
                - ref["x_here"][base, :].astype(F32) * (s1 * s1 * dot * (1.0 / features))
            )
            ref["grad_x"][base, :] = grad.astype(BF16)

        tile_loop(step // TILE, body)
        if c + 1 < halves:
            local_copy(c + 1).start()

    def dots_back():
        for q in range(count // 128):
            wide = jnp.broadcast_to(dots[0:1, q * 128 : (q + 1) * 128], (128, 128))
            ref["dots_col"][q * 128 : (q + 1) * 128, :] = jnp.transpose(wide)

    small_copy(0).start()
    last = len(tasks) - 1
    for k in range(len(tasks)):
        for name in tasks[k][1:3]:
            ready(name)
        far_core(k)
        if k == 0:
            for i in range(3):
                small_add(i)
                if i < 2:
                    small_copy(i + 1).start()
        scatters[k].near_core()
        if k == 0:
            dots_add(1)
            dots_back()
            fold.step(0, 1)
        if k == 1:
            fold.step(0, 2)
        if k == 3:
            input_grad(0)
        if k > 0:
            scatters[k - 1].onward()
        if k == 4:
            fold.step(1, 1)
            finish(0)
    scatters[last].onward()
    finish(1)
    fold.step(1, 2)
    small_copy(3).start()
    for k in range(2, last + 1):
        finish(k)
    small_add(3)
    small_copy(4).start()
    input_grad(1)
    small_add(4)
    for copy in stage_wait:
        copy.wait()
    for copy in sending:
        copy.wait_send()
    for scatter in scatters:
        scatter.drain()
    for c in range(halves):
        fold.drain(c)


def tail(mp, pull, w_in, norm1, grady, hidden, gbo, mixed, gates, dots, s1, x, local, gains, mine,
         small):
    count, part = x.shape
    features = part * mp
    own = features // 8
    halves = 2
    step = count // halves
    widths = {
        "down": hidden.shape[1], "in": pull.shape[1], "out": mixed.shape[1],
        "block": pull.shape[1],
    }
    heights = {name: 32 if name == "block" else own for name in widths}
    operands = {
        "down": ("grady", "hidden", 0), "in": ("norm1", "pull", 0), "out": ("gbo", "mixed", 0),
        "block": (None, "gates", 0),
    }
    tasks = []
    for name, width in widths.items():
        left, right, first = operands[name]
        pieces = 1 if name == "out" else 2
        for piece in range(pieces):
            column = piece * (width // pieces)
            tasks.append((name, left, right, first + column, width // pieces, column))
    widest = max(t[4] for t in tasks)
    dma = pltpu.SemaphoreType.DMA
    any_, vmem = pl.BlockSpec(memory_space=pl.ANY), pl.BlockSpec(memory_space=pltpu.VMEM)
    ins = [
        ("pull", pull, vmem), ("w_in", w_in, vmem), ("norm1", norm1, any_),
        ("grady", grady, any_),
        ("hidden", hidden, any_), ("gbo", gbo, any_), ("mixed", mixed, any_),
        ("gates", gates, vmem), ("dots", dots, vmem), ("s1", s1, any_), ("x", x, any_),
        ("local", local, any_), ("gains", gains, vmem), ("mine", mine, vmem),
        ("small_start", small, vmem),
    ]
    outs = [("grad_x", jax.ShapeDtypeStruct((count, part), BF16), vmem)]
    for name, width in widths.items():
        outs.append(("grad_" + name, jax.ShapeDtypeStruct((heights[name], width), F32), any_))
    outs.append(("small", jax.ShapeDtypeStruct((16, features), F32), vmem))
    scratch = [
        ("parts", pltpu.VMEM((halves, mp, step, part), BF16)),
        ("rights", pltpu.VMEM((halves, mp - 1, step, part), BF16)),
        ("lefts", pltpu.VMEM((halves, mp - 1, step, part), BF16)),
        ("sends", pltpu.VMEM((4, own, widest), BF16)),
        ("stage", pltpu.VMEM((2, own, widest), F32)),
        ("near_local", pltpu.VMEM((step, part), F32)),
        ("local_sem", dma),
        ("gain", pltpu.VMEM((8, features), F32)),
        ("dots_row", pltpu.VMEM((8, count), F32)),
        ("dots_in", pltpu.VMEM((2, 8, count), F32)),
        ("dots_col", pltpu.VMEM((count, 128), F32)),
        ("small_in", pltpu.VMEM((5, 16, features), F32)),
        ("fold_sent", dma((halves, mp))),
        ("fold_right", dma((halves, mp))),
        ("fold_left", dma((halves, mp))),
        ("task_sent", dma((len(tasks), 8))),
        ("task_came", dma((len(tasks), 8))),
        ("load_sem", dma((8,))),
        ("store_sem", dma((2,))),
        ("dots_sent", dma((2,))),
        ("dots_came", dma((2,))),
        ("small_sent", dma((5,))),
        ("small_came", dma((5,))),
    ]
    loaded = ("norm1", "grady", "hidden", "x", "s1", "gbo", "mixed")
    for name, value, _ in ins:
        if name in loaded:
            scratch.append((name + "_here", pltpu.VMEM(value.shape, value.dtype)))
    for k, (name, _, _, _, width, _) in enumerate(tasks):
        tall = heights[name]
        scratch.append(("held%d" % k, pltpu.VMEM((4, tall, width), BF16)))
        for kind in ("far", "first", "second"):
            scratch.append(("%s%d" % (kind, k), pltpu.VMEM((tall, width), BF16)))
    names = [i[0] for i in ins] + [o[0] for o in outs] + [k[0] for k in scratch]
    return pl.pallas_call(
        functools.partial(tail_kernel, mp, tuple(tasks), loaded, tuple(names)),
        in_specs=[i[2] for i in ins],
        out_specs=[o[2] for o in outs],
        out_shape=[o[1] for o in outs],
        scratch_shapes=[k[1] for k in scratch],
        compiler_params=pltpu.CompilerParams(
            collective_id=1, has_side_effects=True, vmem_limit_bytes=63 * 1024 * 1024
        ),
        name="tail",
    )(*[i[1] for i in ins])


def make_masks(row_lengths, count):
    ends = jnp.cumsum(row_lengths)
    places = jnp.arange(-TAPS, count, dtype=jnp.int32)
    segment = jnp.sum((places[:, None] >= ends[None, :]).astype(jnp.int32), axis=1)
    segment = jnp.where(places < 0, -1, segment)
    now = segment[TAPS:]
    same = [(segment[TAPS - k : TAPS - k + count] == now).astype(F32) for k in range(1, TAPS)]
    blank = jnp.zeros((count,), F32)
    columns = [same[0]] + same + [blank] * (LANES - TAPS)
    live = now < row_lengths.shape[0]
    return jnp.stack(columns, axis=1), live


def dense_gates(gates, width):
    span = gates.shape[0]
    tiled = jnp.tile(gates, (width // span, 1))
    row = lax.broadcasted_iota(jnp.int32, tiled.shape, 0) // span
    column = (lax.broadcasted_iota(jnp.int32, tiled.shape, 1) % width) // span
    return jnp.where(row == column, tiled, jnp.zeros((), tiled.dtype))


def diagonal_blocks(dense, span):
    width = dense.shape[0]
    column = (lax.broadcasted_iota(jnp.int32, (1, 2 * width), 1) % width) // span
    total = jnp.zeros((span, 2 * width), F32)
    for b in range(width // span):
        total = total + jnp.where(column == b, dense[b * span : (b + 1) * span], 0.0)
    return total


def per_device(
    dp, mp,
    inputs, lengths, cotangent, gains, rnn_params, rnn_in, branch_gate, recur_gate, input_gate,
    mlp_gate, mlp_up, rnn_out, mlp_down,
):
    count, part = inputs.shape
    width = rnn_in.shape[1]
    hidden_width = mlp_gate.shape[1]
    span = recur_gate.shape[0] * dp
    features = part * mp
    step = count // CHUNKS
    spot = lax.axis_index("mp") * part

    def cut(values):
        return [values[c * step : (c + 1) * step] for c in range(CHUNKS)]

    def mine(values):
        return lax.dynamic_slice_in_dim(values, spot, part, values.ndim - 1)

    in_shard = jnp.concatenate([rnn_in, branch_gate], axis=1)
    out_shard = rnn_out.T
    gates_shard = jnp.concatenate([recur_gate, input_gate], axis=1)
    gate, up, down = mlp_gate, mlp_up, mlp_down.T
    if dp == 8:
        gates_shard = jnp.pad(gates_shard, ((0, 32 - span // 8), (0, 0)))
    else:
        in_shard, out_shard = square_gather(in_shard, "dp", dp), square_gather(out_shard, "dp", dp)
        gate, up, down = [square_gather(w, "dp", dp) for w in (gate, up, down)]
        gates_shard = pair_gather(gates_shard, "dp", dp).reshape(8, span // 8, 2 * width)
        gates_shard = jnp.pad(gates_shard, ((0, 0), (0, 32 - span // 8), (0, 0)))
        gates_shard = gates_shard.reshape(256, 2 * width)

    mask, live = make_masks(lengths[0], count)
    mask_tail = jnp.concatenate([mask, jnp.zeros((8, LANES), F32)], axis=0)
    tail_masks = [mask_tail[c * step : (c + 1) * step + 8] for c in range(CHUNKS)]
    live = jnp.broadcast_to(live[:, None], (count, LANES)).astype(F32)
    w_in, w_out, w_gate, dense, normed, both, conv, r, i, state, mixed, s1 = head(
        dp, mp, 4, inputs, gains, rnn_params, mask, in_shard, out_shard, gate, gates_shard, span
    )
    (
        output, gm, gbo, local, hidden, pulled, normed2, grad_y, grad_gate, grad_up, gain2,
    ) = middle(
        dp, mp, 4, mixed, inputs, cotangent, live, gains, mine(gains), w_out,
        w_gate, up, down,
    )
    blank = jnp.zeros((8, width), F32)
    back, tail_rows = blank, blank
    pulls, rates, dots = [None] * CHUNKS, [None] * CHUNKS, [None] * CHUNKS
    params_total = 0.0
    gms, boths = cut(gm), cut(both)
    saves = list(zip(cut(conv), cut(r), cut(i), cut(state)))
    for c in reversed(range(CHUNKS)):
        low = c * step
        halo = blank if c == 0 else both[low - 8 : low, :width]
        start = blank if c == 0 else state[low - 8 : low]
        pull, rate, dparams, back, tail_rows, dot = rnn_backward(
            gms[c], boths[c], halo, start, saves[c], tail_masks[c], dense, rnn_params,
            back, tail_rows,
        )
        params_total = params_total + dparams
        pulls[c], rates[c], dots[c] = pull, rate, dot
    pull = jnp.concatenate(pulls)
    dots = jnp.concatenate(dots)
    grad_gates = diagonal_blocks(inner_rows(conv.astype(BF16), jnp.concatenate(rates)), span)
    gain2 = jnp.sum(gain2, axis=0, keepdims=True)

    if dp == 8:
        rows = span // dp
        padded = jnp.pad(
            grad_gates.astype(BF16).reshape(dp, rows, 2 * width), ((0, 0), (0, 32 - rows), (0, 0))
        ).reshape(dp * 32, 2 * width)
        small = jnp.concatenate(
            [
                jnp.zeros((1, features), F32), gain2 / mp, jnp.zeros((6, features), F32),
                jnp.pad(params_total, ((0, 0), (0, features - width))),
            ]
        )
        input_grad, grad_down, grad_in, grad_out, grad_gates, small = tail(
            mp, pull, w_in, normed, grad_y, hidden, gbo, mixed, padded, dots,
            s1, inputs, local, gains, mine(gains), small,
        )
        grad_gates = grad_gates[:rows]
        grad_gains, grad_params = small[0:2], small[8:16, :width]
    else:
        parts = []
        gain1 = 0.0
        norms, s1 = cut(normed), s1[:, 0:1]
        for c in range(CHUNKS):
            gn1_part = inner_cols(pulls[c], w_in).astype(BF16)
            gain1 = gain1 + jnp.sum(gn1_part.astype(F32) * norms[c].astype(F32), axis=0)
            parts.append(line_scatter(gn1_part, "mp", mp))
        dot = line_sum(dots[:, 0].reshape(8, -1), "mp", mp).reshape(-1, 1)
        input_grad = (
            local + s1 * (jnp.concatenate(parts) * mine(gains[0]))
            - inputs.astype(F32) * (s1 * s1 * dot / features)
        ).astype(BF16)
        grad_both = square_scatter(inner_rows(normed2, pulled).astype(BF16), "dp", dp)
        grad_gate, grad_up = grad_both[:, :hidden_width], grad_both[:, hidden_width:]
        grad_down = square_scatter(inner_rows(grad_y, hidden).astype(BF16), "dp", dp)
        grad_out = square_scatter(inner_rows(gbo, mixed).astype(BF16), "dp", dp)
        grad_in = square_scatter(inner_rows(normed, pull).astype(BF16), "dp", dp)
        grad_gates = pair_scatter(grad_gates, "dp", dp)
        grad_params = line_sum(params_total, "dp", dp)
        both_gains = jnp.concatenate([(gain1 / gains[0])[None], gain2])
        both_gains = line_sum(both_gains, "dp", dp)
        grad_gains = jnp.concatenate([line_sum(both_gains[:1], "mp", mp), both_gains[1:]])
    return (
        output,
        input_grad,
        grad_gains,
        grad_params,
        grad_in[:, :width],
        grad_in[:, width:],
        grad_gates[:, :width],
        grad_gates[:, width:],
        grad_gate,
        grad_up,
        grad_out.T,
        grad_down.T,
    )


def solution(mesh):
    return jax.shard_map(
        functools.partial(per_device, mesh.shape["dp"], mesh.shape["mp"]),
        mesh=mesh,
        in_specs=(
            P("dp", "mp"),
            P("dp", None),
            P("dp", "mp"),
            P(),
            P(None, "mp"),
            P("dp", "mp"),
            P("dp", "mp"),
            P("dp", "mp"),
            P("dp", "mp"),
            P("dp", "mp"),
            P("dp", "mp"),
            P("mp", "dp"),
            P("mp", "dp"),
        ),
        out_specs=(
            P("dp", "mp"),
            P("dp", "mp"),
            P(),
            P(None, "mp"),
            P("dp", "mp"),
            P("dp", "mp"),
            P("dp", "mp"),
            P("dp", "mp"),
            P("dp", "mp"),
            P("dp", "mp"),
            P("mp", "dp"),
            P("mp", "dp"),
        ),
        check_vma=False,
    )
```

```python
import functools

import jax
import jax.numpy as jnp
from jax import lax
from jax.experimental import pallas as pl
from jax.experimental.pallas import tpu as pltpu
from jax.sharding import PartitionSpec as P

EPS = 1e-06
DECAY_SCALE = 8.0
ROOT_FLOOR = 0.0001
TAPS = 4
LANES = 8
CHUNKS = 1
TILE = 32
F32 = jnp.float32
BF16 = jnp.bfloat16
VMEM_BYTES = 56 * 1024 * 1024


def matmul(left, right):
    return jnp.dot(left, right, preferred_element_type=F32)


def inner_rows(left, right):
    return lax.dot_general(left, right, (((0,), (0,)), ((), ())), preferred_element_type=F32)


def inner_cols(left, right):
    return lax.dot_general(left, right, (((1,), (1,)), ((), ())), preferred_element_type=F32)


def gelu_and_slope(values):
    outer = 0.7978845608028654
    inner = 0.044715
    square = values * values
    bent = jnp.tanh(outer * values * (1.0 + inner * square))
    half = 0.5 * (1.0 + bent)
    slope = half + 0.5 * values * (1.0 - bent * bent) * outer * (1.0 + 3.0 * inner * square)
    return values * half, slope


def gelu(values):
    outer = 0.7978845608028654
    inner = 0.044715
    bent = jnp.tanh(outer * values * (1.0 + inner * values * values))
    return values * (0.5 * (1.0 + bent))


def one_less_exp(values):
    near = -values * (1.0 + 0.5 * values * (1.0 + (values / 3.0) * (1.0 + 0.25 * values)))
    return jnp.where(values > -0.02, near, 1.0 - jnp.exp(values))


def after(value, *earlier):
    return lax.optimization_barrier((value,) + earlier)[0]


def line_gather(mine, axis, size):
    place = lax.axis_index(axis)
    width = mine.shape[1]
    right, left = mine, mine
    rights, lefts = {}, {}
    for step in range(1, size):
        right = lax.ppermute(right, axis, [(i, i + 1) for i in range(step - 1, size - 1)])
        left = lax.ppermute(left, axis, [(i + 1, i) for i in range(size - step)])
        rights[step], lefts[step] = right, left
    whole = jnp.zeros((mine.shape[0], size * width), mine.dtype)
    for step in range(size):
        block = mine if step == 0 else lefts[step] + rights[size - step]
        spot = lax.rem(place + step, size) * width
        whole = lax.dynamic_update_slice_in_dim(whole, block, spot, 1)
    return whole


def line_scatter(part, axis, size):
    place = lax.axis_index(axis)
    width = part.shape[1] // size

    def block(index):
        spot = jnp.clip(index, 0, size - 1) * width
        return lax.dynamic_slice_in_dim(part, spot, width, 1).astype(F32)

    right, left = None, None
    for step in range(1, size):
        going = block(size - step + place)
        if right is not None:
            going = going + right.astype(F32)
        right = lax.ppermute(going.astype(BF16), axis, [(i, i + 1) for i in range(step)])
        going = block(place - (size - step))
        if left is not None:
            going = going + left.astype(F32)
        left = lax.ppermute(
            going.astype(BF16), axis, [(i, i - 1) for i in range(size - step, size)]
        )
    return block(place) + right.astype(F32) + left.astype(F32)


def line_sum(value, axis, size):
    bit = 1
    while bit < size:
        value = value + lax.ppermute(value, axis, [(i, i ^ bit) for i in range(size)])
        bit *= 2
    return value


def pair_gather(mine, axis, size):
    place = lax.axis_index(axis)
    bit = 1
    while bit < size:
        other = lax.ppermute(mine, axis, [(i, i ^ bit) for i in range(size)])
        upper = (place & bit) != 0
        mine = jnp.concatenate(
            [jnp.where(upper, other, mine), jnp.where(upper, mine, other)], axis=0
        )
        bit *= 2
    return mine


def pair_scatter(part, axis, size):
    place = lax.axis_index(axis)
    part = part.astype(F32)
    bit = size // 2
    while bit >= 1:
        upper = (place & bit) != 0
        low, high = jnp.split(part, 2, axis=0)
        going = jnp.where(upper, low, high).astype(BF16)
        came = lax.ppermute(going, axis, [(i, i ^ bit) for i in range(size)])
        part = jnp.where(upper, high, low) + came.astype(F32)
        bit //= 2
    return part


def swap(size, bit):
    return [(i, i ^ bit) for i in range(size)]


def cross(size):
    return [(i, i ^ 4 if i % 2 == 0 else i ^ 2) for i in range(size)]


def square_gather(mine, axis, size):
    if size != 8:
        return pair_gather(mine, axis, size)
    place = lax.axis_index(axis)
    rows = mine.shape[0]
    by_x = lax.ppermute(mine, axis, swap(size, 2))
    by_y = lax.ppermute(mine, axis, swap(size, 4))
    onward = jnp.where((place & 1) == 0, by_x, by_y)
    far = lax.ppermute(onward, axis, cross(size))
    held = {0: mine, 2: by_x, 4: by_y, 6: far}
    for bits in (0, 2, 4, 6):
        held[bits + 1] = lax.ppermute(held[bits], axis, swap(size, 1))
    whole = jnp.zeros((size * rows,) + mine.shape[1:], mine.dtype)
    for bits, block in held.items():
        whole = lax.dynamic_update_slice_in_dim(whole, block, (place ^ bits) * rows, 0)
    return whole


def square_scatter(part, axis, size):
    if size != 8:
        return pair_scatter(part, axis, size)
    place = lax.axis_index(axis)
    core = place & 1
    chip = lax.shift_right_logical(place, 1)
    split = part.reshape(size // 2, 2, part.shape[0] // size, part.shape[1])
    going = lax.dynamic_index_in_dim(split, 1 - core, 1, keepdims=False)
    came = lax.ppermute(going, axis, swap(size, 1))
    kept = lax.dynamic_index_in_dim(split, core, 1, keepdims=False)
    both = (kept.astype(F32) + came.astype(F32)).astype(BF16)

    def pick(index):
        return lax.dynamic_index_in_dim(both, index, 0, keepdims=False)

    far = lax.ppermute(pick(chip ^ 3), axis, cross(size)).astype(F32)
    none = jnp.zeros((), F32)
    to_x = pick(chip ^ 1).astype(F32) + jnp.where(core == 0, far, none)
    to_y = pick(chip ^ 2).astype(F32) + jnp.where(core == 1, far, none)
    by_x = lax.ppermute(to_x.astype(BF16), axis, swap(size, 2))
    by_y = lax.ppermute(to_y.astype(BF16), axis, swap(size, 4))
    return pick(chip).astype(F32) + by_x.astype(F32) + by_y.astype(F32)


def tile_loop(count, body):
    lax.fori_loop(0, count, lambda i, c: (body(i), c)[1], 0)


def rows_at(index, size):
    return pl.ds(pl.multiple_of(index * size, size), size)


def put(ref, rows, values):
    for j in range(ref.shape[0]):
        ref[j, rows, :] = values[:, j * 128 : (j + 1) * 128]


def get(ref, rows):
    return jnp.concatenate([ref[j, rows, :] for j in range(ref.shape[0])], axis=1)


def rnn_forward_kernel(
    both_ref, halo_ref, start_ref, mask_ref, gates_ref, params_ref,
    mixed_ref, conv_ref, r_ref, i_ref, state_ref, end_ref,
    padded, high, low, decay, drive,
):
    count, width = conv_ref.shape
    seg = count // 8
    tiles = count // TILE
    padded[0:8, :] = halo_ref[...]
    padded[8:, :] = both_ref[:, 0:width]

    def convolve(t):
        span = padded[pl.ds(pl.multiple_of(t * TILE, TILE), TILE + 8), :]
        mask = mask_ref[rows_at(t, TILE), :]
        conv = params_ref[0:1, :] * span[8:, :] + params_ref[TAPS : TAPS + 1, :]
        for k in range(1, TAPS):
            moved = span[8 - k : 8 - k + TILE, :]
            conv = conv + params_ref[k : k + 1, :] * (moved * mask[:, k : k + 1])
        conv_ref[rows_at(t, TILE), :] = conv
        top = conv.astype(BF16)
        high[rows_at(t, TILE), :] = top
        low[rows_at(t, TILE), :] = (conv - top.astype(F32)).astype(BF16)

    tile_loop(tiles, convolve)

    block = min(256, count)

    def gate(t):
        rows = rows_at(t, block)
        weights = gates_ref[...]
        both = jnp.dot(high[rows, :], weights, preferred_element_type=F32)
        both = both + jnp.dot(low[rows, :], weights, preferred_element_type=F32)
        r_ref[rows, :] = both[:, 0:width]
        i_ref[rows, :] = both[:, width:]

    tile_loop(count // block, gate)

    strength = DECAY_SCALE * jax.nn.softplus(-params_ref[TAPS + 3 : TAPS + 4, :])

    def prepare(t):
        rows = rows_at(t, TILE)
        keep = mask_ref[rows, :][:, 0:1]
        r = jax.nn.sigmoid(r_ref[rows, :] + params_ref[TAPS + 1 : TAPS + 2, :])
        i = jax.nn.sigmoid(i_ref[rows, :] + params_ref[TAPS + 2 : TAPS + 3, :])
        log_a = -strength * r
        scale = jnp.sqrt(jnp.maximum(one_less_exp(2.0 * log_a), ROOT_FLOOR))
        scale = jnp.where(keep > 0.0, scale, 1.0)
        put(decay, rows, jnp.exp(log_a) * keep)
        put(drive, rows, scale * i * conv_ref[rows, :])
        r_ref[rows, :] = r
        i_ref[rows, :] = i

    tile_loop(tiles, prepare)

    def scan(t, carry):
        held, prod = carry
        rows = pl.ds(t, 8, stride=seg)
        a = get(decay, rows)
        held = a * held + get(drive, rows)
        prod = a * prod
        put(drive, rows, held)
        put(decay, rows, prod)
        return held, prod

    shape = (8, width)
    held, prod = lax.fori_loop(0, seg, scan, (jnp.zeros(shape, F32), jnp.ones(shape, F32)))
    carry = start_ref[0:1, :]
    carries = []
    for s in range(8):
        carries.append(carry)
        carry = prod[s : s + 1, :] * carry + held[s : s + 1, :]
    end_ref[...] = jnp.broadcast_to(carry, shape)

    small = min(TILE, seg)
    for s in range(8):

        def finish(t, s=s):
            rows = pl.ds(pl.multiple_of(s * seg + t * small, small), small)
            state = get(drive, rows) + get(decay, rows) * carries[s]
            state_ref[rows, :] = state
            mixed_ref[rows, :] = (state * gelu(both_ref[rows, width:])).astype(BF16)

        tile_loop(seg // small, finish)


def rnn_forward(both, halo, start, mask, gates, params):
    count, width = both.shape[0], both.shape[1] // 2
    full = jax.ShapeDtypeStruct((count, width), F32)
    return pl.pallas_call(
        rnn_forward_kernel,
        out_shape=(
            jax.ShapeDtypeStruct((count, width), BF16),
            full, full, full, full,
            jax.ShapeDtypeStruct((8, width), F32),
        ),
        scratch_shapes=[
            pltpu.VMEM((count + 8, width), F32),
            pltpu.VMEM((count, width), BF16),
            pltpu.VMEM((count, width), BF16),
            pltpu.VMEM((width // 128, count, 128), F32),
            pltpu.VMEM((width // 128, count, 128), F32),
        ],
        compiler_params=pltpu.CompilerParams(vmem_limit_bytes=VMEM_BYTES),
        cost_estimate=pl.CostEstimate(
            flops=4 * count * width * 2 * width, bytes_accessed=count * width * 30,
            transcendentals=count * width * 6,
        ),
        name="rnn_forward",
    )(both, halo, start, mask, gates, params)


def rnn_backward_kernel(
    gm_ref, both_ref, halo_ref, start_ref, conv_ref, r_ref, i_ref, state_ref, mask_ref,
    gates_ref, params_ref, back_ref, tail_ref,
    grads_ref, rates_ref, dparams_ref, back_out_ref, tail_out_ref, dots_ref,
    padded, before, decay, adjoint, coef, dconv, sums,
):
    count, width = conv_ref.shape
    seg = count // 8
    tiles = count // TILE
    padded[0:8, :] = halo_ref[...]
    padded[8:, :] = both_ref[:, 0:width]
    before[0:8, :] = start_ref[...]
    before[8:, :] = state_ref[...]
    strength = DECAY_SCALE * jax.nn.softplus(-params_ref[TAPS + 3 : TAPS + 4, :])

    def prepare(t):
        rows = rows_at(t, TILE)
        keep = mask_ref[rows, :][:, 0:1]
        gm = gm_ref[rows, :]
        value, slope = gelu_and_slope(both_ref[rows, width:])
        put(adjoint, rows, gm * value)
        grads_ref[rows, width:] = (gm * state_ref[rows, :] * slope).astype(BF16)
        put(decay, rows, jnp.exp(-strength * r_ref[rows, :]) * keep)

    tile_loop(tiles, prepare)

    def scan(t, carry):
        held, prod = carry
        rows = pl.ds(seg - 1 - t, 8, stride=seg)
        a = get(decay, rows)
        total = get(adjoint, rows) + held
        put(adjoint, rows, total)
        put(coef, rows, prod)
        return a * total, a * prod

    shape = (8, width)
    held, prod = lax.fori_loop(0, seg, scan, (jnp.zeros(shape, F32), jnp.ones(shape, F32)))
    carry = back_ref[0:1, :]
    carries = [None] * 8
    for s in reversed(range(8)):
        carries[s] = carry
        carry = prod[s : s + 1, :] * carry + held[s : s + 1, :]
    back_out_ref[...] = jnp.broadcast_to(carry, shape)

    sums[...] = jnp.zeros_like(sums)

    def fold(values):
        return jnp.sum(values.reshape(-1, 8, width), axis=0)

    small = min(TILE, seg)
    for s in range(8):

        def chain(t, s=s):
            base = pl.multiple_of(s * seg + t * small, small)
            rows = pl.ds(base, small)
            keep = mask_ref[rows, :][:, 0:1]
            a = get(adjoint, rows) + get(coef, rows) * carries[s]
            r, i, conv = r_ref[rows, :], i_ref[rows, :], conv_ref[rows, :]
            fall = get(decay, rows)
            prior = before[pl.ds(base, small + 8), :][7 : 7 + small, :]
            room = one_less_exp(-2.0 * strength * r)
            bound = jnp.maximum(room, ROOT_FLOOR)
            inverse = lax.rsqrt(bound)
            live = keep > 0.0
            scale = jnp.where(live, bound * inverse, 1.0)
            open_ = jnp.where(room > ROOT_FLOOR, inverse, 0.0)
            driven = a * i
            dlog = fall * (a * prior - fall * driven * conv * open_)
            common = a * scale
            drec = dlog * (-strength) * r * (1.0 - r)
            dinp = common * conv * i * (1.0 - i)
            rates_ref[rows, 0:width] = drec.astype(BF16)
            rates_ref[rows, width:] = dinp.astype(BF16)
            dconv[rows, :] = common * i
            sums[5] += fold(drec)
            sums[6] += fold(dinp)
            sums[7] += fold(dlog * r)

        tile_loop(seg // small, chain)

    block = min(256, count)

    def spread(t):
        rows = rows_at(t, block)
        dconv[rows, :] += lax.dot_general(
            rates_ref[rows, :], gates_ref[...], (((1,), (1,)), ((), ())),
            preferred_element_type=F32,
        )

    tile_loop(count // block, spread)
    dconv[count:, :] = tail_ref[...]
    tail_out_ref[...] = dconv[0:8, :]

    def unconvolve(t):
        base = pl.multiple_of(t * TILE, TILE)
        rows = pl.ds(base, TILE)
        span = dconv[pl.ds(base, TILE + 8), :]
        mask = mask_ref[pl.ds(base, TILE + 8), :]
        source = padded[pl.ds(base, TILE + 8), :]
        here = span[0:TILE, :]
        out = params_ref[0:1, :] * here
        sums[0] += fold(here * source[8:, :])
        sums[4] += fold(here)
        for k in range(1, TAPS):
            kept = span * mask[:, k : k + 1]
            out = out + params_ref[k : k + 1, :] * kept[k : k + TILE, :]
            sums[k] += fold(kept[0:TILE, :] * source[8 - k : 8 - k + TILE, :])
        grads_ref[rows, 0:width] = out.astype(BF16)
        dot = jnp.sum(
            out * source[8:, :] + grads_ref[rows, width:].astype(F32) * both_ref[rows, width:],
            axis=1, keepdims=True,
        )
        dots_ref[rows, :] = jnp.broadcast_to(dot, (TILE, 128))

    tile_loop(tiles, unconvolve)
    for k in range(8):
        dparams_ref[k : k + 1, :] = jnp.sum(sums[k], axis=0, keepdims=True)
    dparams_ref[TAPS + 3 : TAPS + 4, :] = (
        DECAY_SCALE
        * jax.nn.sigmoid(-params_ref[TAPS + 3 : TAPS + 4, :])
        * jnp.sum(sums[TAPS + 3], axis=0, keepdims=True)
    )


def rnn_backward(gm, both, halo, start, saved, mask, gates, params, back, tail):
    conv, r, i, state = saved
    count, width = conv.shape
    return pl.pallas_call(
        rnn_backward_kernel,
        out_shape=(
            jax.ShapeDtypeStruct((count, 2 * width), BF16),
            jax.ShapeDtypeStruct((count, 2 * width), BF16),
            jax.ShapeDtypeStruct((8, width), F32),
            jax.ShapeDtypeStruct((8, width), F32),
            jax.ShapeDtypeStruct((8, width), F32),
            jax.ShapeDtypeStruct((count, 128), F32),
        ),
        scratch_shapes=[
            pltpu.VMEM((count + 8, width), F32),
            pltpu.VMEM((count + 8, width), F32),
            pltpu.VMEM((width // 128, count, 128), F32),
            pltpu.VMEM((width // 128, count, 128), F32),
            pltpu.VMEM((width // 128, count, 128), F32),
            pltpu.VMEM((count + 8, width), F32),
            pltpu.VMEM((8, 8, width), F32),
        ],
        compiler_params=pltpu.CompilerParams(vmem_limit_bytes=VMEM_BYTES),
        cost_estimate=pl.CostEstimate(
            flops=2 * count * width * 2 * width, bytes_accessed=count * width * 36,
            transcendentals=count * width * 6,
        ),
        name="rnn_backward",
    )(gm, both, halo, start, conv, r, i, state, mask, gates, params, back, tail)


MESH = pl.DeviceIdType.MESH


class Spread:
    def __init__(self, place, size, blocks, sent, came):
        self.place, self.size = place, size
        self.blocks, self.sent, self.came = blocks, sent, came

    def copy(self, slot, j, way, k):
        ref = self.blocks.at[slot, j]
        return pltpu.make_async_remote_copy(
            src_ref=ref, dst_ref=ref, send_sem=self.sent.at[slot, k],
            recv_sem=self.came.at[slot, j], device_id={"mp": self.place + way},
            device_id_type=MESH,
        )

    def moves(self, s):
        z, n = self.place, self.size
        return (
            ((z - s >= 0) & (z < n - 1), z - s, 1, 2 * s),
            ((z + s <= n - 1) & (z > 0), z + s, -1, 2 * s + 1),
        )

    def step(self, slot, s):
        for valid, j, way, k in self.moves(s):

            @pl.when(valid)
            def _(j=j, way=way, k=k):
                copy = self.copy(slot, j, way, k)
                if s > 0:
                    copy.wait_recv()
                copy.start()

    def finish(self, slot):
        z, n = self.place, self.size

        @pl.when(z == 0)
        def _():
            for j in range(1, n):
                self.copy(slot, j, 1, 0).wait_recv()

        @pl.when(z == n - 1)
        def _():
            for j in range(n - 1):
                self.copy(slot, j, -1, 0).wait_recv()

    def drain(self, slot):
        for s in range(self.size - 1):
            for valid, j, way, k in self.moves(s):

                @pl.when(valid)
                def _(j=j, way=way, k=k):
                    self.copy(slot, j, way, k).wait_send()


class Fold:
    def __init__(self, place, size, parts, rights, lefts, sent, came_right, came_left):
        self.place, self.size = place, size
        self.parts, self.rights, self.lefts = parts, rights, lefts
        self.sent, self.came_right, self.came_left = sent, came_right, came_left

    def right(self, slot, j, k):
        return pltpu.make_async_remote_copy(
            src_ref=self.parts.at[slot, j], dst_ref=self.rights.at[slot, k],
            send_sem=self.sent.at[slot, j], recv_sem=self.came_right.at[slot, k],
            device_id={"mp": self.place + 1}, device_id_type=MESH,
        )

    def left(self, slot, j, k):
        return pltpu.make_async_remote_copy(
            src_ref=self.parts.at[slot, j], dst_ref=self.lefts.at[slot, k],
            send_sem=self.sent.at[slot, j], recv_sem=self.came_left.at[slot, k],
            device_id={"mp": self.place - 1}, device_id_type=MESH,
        )

    def clear(self):
        for slot in range(self.parts.shape[0]):
            last = self.size - 2
            blank = jnp.zeros(self.rights.shape[2:], BF16)
            self.rights[slot, last] = blank
            self.lefts[slot, last] = blank

    def start(self, slot):
        z, n = self.place, self.size

        @pl.when(z == 0)
        def _():
            for j in reversed(range(1, n)):
                self.right(slot, j, n - 1 - j).start()

        @pl.when(z == n - 1)
        def _():
            for j in range(n - 1):
                self.left(slot, j, j).start()

    def step(self, slot, s):
        z, n = self.place, self.size
        back = n - 1 - z

        @pl.when((z >= 1) & (z <= n - 2) & (s >= z))
        def _():
            j = n - 1 + z - s
            self.right(slot, j, s - 1).wait_recv()
            self.add(slot, j, self.rights, s - 1)
            self.right(slot, j, s).start()

        @pl.when((back >= 1) & (back <= n - 2) & (s >= back))
        def _():
            j = s - back
            self.left(slot, j, s - 1).wait_recv()
            self.add(slot, j, self.lefts, s - 1)
            self.left(slot, j, s).start()

    def add(self, slot, j, came, k):
        self.parts[slot, j] = (
            self.parts[slot, j].astype(F32) + came[slot, k].astype(F32)
        ).astype(BF16)

    def finish(self, slot):
        z, n = self.place, self.size

        @pl.when(z >= 1)
        def _():
            self.right(slot, z, n - 2).wait_recv()

        @pl.when(z <= n - 2)
        def _():
            self.left(slot, z, n - 2).wait_recv()

    def total(self, slot, rows):
        z, n = self.place, self.size
        return (
            self.parts[slot, z, rows, :].astype(F32)
            + self.rights[slot, n - 2, rows, :].astype(F32)
            + self.lefts[slot, n - 2, rows, :].astype(F32)
        )

    def drain(self, slot):
        for j in range(self.size):

            @pl.when(j != self.place)
            def _(j=j):
                self.right(slot, j, 0).wait_send()


def partners(d):
    core, x, y = lax.rem(d, 2), lax.rem(lax.div(d, 2), 2), lax.div(d, 4)
    return core, d + 1 - 2 * core, d + 2 - 4 * x, d + 4 - 8 * y


class Square:
    def __init__(self, d, shard, whole, sent, came, own):
        self.d, self.shard, self.whole = d, shard, whole
        self.sent, self.came, self.own = sent, came, own
        self.core, self.by_core, self.by_x, self.by_y = partners(d)

    def rows(self, d):
        count = self.shard.shape[0]
        return self.whole.at[pl.ds(pl.multiple_of(d * count, count), count), :]

    def copy(self, src, origin, target, sent, came):
        return pltpu.make_async_remote_copy(
            src_ref=src, dst_ref=self.rows(origin), send_sem=self.sent.at[sent],
            recv_sem=self.came.at[came], device_id={"dp": target}, device_id_type=MESH,
        )

    def local(self):
        return pltpu.make_async_copy(self.shard, self.rows(self.d), self.own)

    def far(self):
        return partners(self.by_x)[3]

    def first(self):
        return (
            self.copy(self.shard, self.d, self.by_x, 0, 2),
            self.copy(self.shard, self.d, self.by_y, 1, 4),
            self.copy(self.shard, self.d, self.by_core, 2, 1),
        )

    def start(self):
        for copy in self.first():
            copy.start()
        self.local().start()

    def step_one(self):
        x_rows, y_rows = self.rows(self.by_x), self.rows(self.by_y)
        by_x = self.copy(x_rows, self.by_x, self.by_core, 3, 2)
        by_y = self.copy(y_rows, self.by_y, self.by_core, 4, 4)
        by_x.wait_recv()

        @pl.when(self.core == 0)
        def _():
            self.copy(x_rows, self.by_x, self.by_y, 5, 6).start()

        self.copy(x_rows, self.by_x, self.by_core, 3, 3).start()
        by_y.wait_recv()

        @pl.when(self.core == 1)
        def _():
            self.copy(y_rows, self.by_y, self.by_x, 5, 6).start()

        self.copy(y_rows, self.by_y, self.by_core, 4, 5).start()

    def step_two(self):
        far = self.far()
        rows = self.rows(far)
        self.copy(rows, far, self.by_core, 6, 6).wait_recv()
        self.copy(rows, far, self.by_core, 6, 7).start()

    def finish(self):
        for k in (1, 3, 5, 7):
            self.copy(self.shard, self.d, self.by_core, 0, k).wait_recv()
        self.local().wait()

    def drain(self):
        for k in range(7):
            self.copy(self.shard, self.d, self.by_core, k, 0).wait_send()


class Scatter:
    def __init__(self, d, count, compute, held, far, first, second, sent, came):
        self.d, self.count, self.compute = d, count, compute
        self.held, self.far_in, self.first_in, self.second_in = held, far, first, second
        self.sent, self.came = sent, came
        self.core, self.by_core, by_x, by_y = partners(d)
        even = self.core == 0
        self.first = jnp.where(even, by_y, by_x)
        self.second = jnp.where(even, by_x, by_y)
        self.first_at, self.second_at = 2 - self.core, 1 + self.core
        other = partners(self.by_core)
        self.away = (self.by_core, other[2], other[3], partners(other[2])[3])
        self.distant = partners(by_x)[3]

    def owners(self):
        return [self.away[k] for k in (3, 1, 2, 0)] + [
            self.distant, self.first, self.d, self.second
        ]

    def copy(self, src, dst, target, sent, came):
        return pltpu.make_async_remote_copy(
            src_ref=src, dst_ref=dst, send_sem=self.sent.at[sent], recv_sem=self.came.at[came],
            device_id={"dp": target}, device_id_type=MESH,
        )

    def to_core(self, buffer, k):
        return self.copy(buffer, self.held(k), self.by_core, k, k)

    def to_far(self):
        return self.copy(self.held(3), self.far_in, self.first, 4, 4)

    def to_first(self):
        return self.copy(self.held(self.first_at), self.first_in, self.first, 5, 5)

    def to_second(self):
        return self.copy(self.held(self.second_at), self.second_in, self.second, 6, 6)

    def far_core(self, buffers, sending):
        for slot, k in enumerate((3, 1, 2, 0)):
            if sending[slot] is not None:
                sending[slot].wait_send()
            self.compute(self.away[k], buffers[slot], False)
            copy = self.to_core(buffers[slot], k)
            copy.start()
            sending[slot] = copy

    def add_block(self, k, came, owner):
        self.copy(self.held(k), self.held(k), self.by_core, k, came).wait_recv()
        self.compute(owner, self.held(k), True)

    def near_core(self):
        self.add_block(3, 3, self.distant)
        self.to_far().start()
        self.add_block(self.first_at, self.first_at, self.first)
        self.to_first().start()
        self.add_block(0, 0, self.d)
        self.add_block(self.second_at, self.second_at, self.second)

    def onward(self):
        self.to_far().wait_recv()
        held = self.held(self.second_at)

        def body(t):
            rows = rows_at(t, 16)
            held[rows, :] = (
                held[rows, :].astype(F32) + self.far_in[rows, :].astype(F32)
            ).astype(BF16)

        tile_loop(self.count // 16, body)
        self.to_second().start()

    def finish(self, target):
        self.to_first().wait_recv()
        self.to_second().wait_recv()
        held = self.held(0)

        def body(t):
            rows = rows_at(t, 16)
            target[rows, :] = (
                held[rows, :].astype(F32)
                + self.first_in[rows, :].astype(F32)
                + self.second_in[rows, :].astype(F32)
            )

        tile_loop(self.count // 16, body)

    def drain(self):
        self.to_far().wait_send()
        self.to_first().wait_send()
        self.to_second().wait_send()


def head_kernel(dp, mp, names, *refs):
    ref = dict(zip(names, refs))
    blocks, w_in, norm, both = ref["blocks"], ref["w_in_here"], ref["norm"], ref["both_here"]
    chunks, _, step, part = blocks.shape
    features, width = part * mp, ref["mixed_here"].shape[2]
    z, d = lax.axis_index("mp"), lax.axis_index("dp")
    square = dp == 8
    gather = Spread(z, mp, blocks, ref["spread_sent"], ref["spread_came"])

    barrier = pltpu.get_barrier_semaphore()

    @pl.when(z > 0)
    def _():
        pl.semaphore_signal(barrier, inc=1, device_id={"mp": z - 1}, device_id_type=MESH)

    @pl.when(z < mp - 1)
    def _():
        pl.semaphore_signal(barrier, inc=1, device_id={"mp": z + 1}, device_id_type=MESH)

    count = jnp.where((z > 0) & (z < mp - 1), 2, 1)
    if square:
        for other in partners(d)[1:]:
            pl.semaphore_signal(barrier, inc=1, device_id={"dp": other}, device_id_type=MESH)
        count = count + 3

    def chunk_rows(c):
        return pl.ds(c * step, step)

    def own_block(c):
        return pltpu.make_async_copy(
            ref["x"].at[chunk_rows(c), :], blocks.at[c, z], ref["load_sem"].at[c]
        )

    for c in range(chunks):
        own_block(c).start()
    pl.semaphore_wait(barrier, count)

    wholes = (
        ("gates_shard", ref["gates_here"]), ("in_shard", w_in), ("out_shard", ref["w_out"]),
        ("gate_shard", ref["w_gate"]),
    )
    if square:
        squares = [
            Square(
                d, ref[name], whole, ref["square_sent"].at[k], ref["square_came"].at[k],
                ref["square_own"].at[k],
            )
            for k, (name, whole) in enumerate(wholes)
        ]
        for item in squares[:2]:
            item.start()
    else:
        loads = [
            pltpu.make_async_copy(ref[name], whole, ref["square_own"].at[k])
            for k, (name, whole) in enumerate(wholes)
        ]
        for item in loads:
            item.start()

    def begin(c):
        own_block(c).wait()
        gather.step(c, 0)

    begin(0)
    if chunks > 1:
        begin(1)

    def expand():
        span = ref["gates_flat"].shape[0]
        rows = span // 8
        for k in range(8):
            ref["gates_flat"][k * rows : (k + 1) * rows, :] = ref["gates_here"][
                k * 32 : k * 32 + 32, :
            ].astype(F32)[0:rows, :]
        column = lax.broadcasted_iota(jnp.int32, (span, 2 * width), 1)
        column = jnp.where(column >= width, column - width, column)
        for b in range(width // span):
            inside = (column >= b * span) & (column < (b + 1) * span)
            ref["dense_here"][b * span : (b + 1) * span, :] = jnp.where(
                inside, ref["gates_flat"][...], 0.0
            ).astype(BF16)

    stores = (
        ("norm", "norm"), ("both", "both_here"), ("conv", "conv_here"), ("r", "r_here"),
        ("i", "i_here"), ("state", "state_here"), ("mixed", "mixed_here"), ("s1", "s1_here"),
    )

    def store_all(c):
        return [
            pltpu.make_async_copy(
                ref[near].at[c % 2], ref[far + "_out"].at[chunk_rows(c), :],
                ref["store_sem"].at[c % 2, k],
            )
            for k, (far, near) in enumerate(stores)
        ]

    ref["halo"][...] = jnp.zeros_like(ref["halo"])
    ref["start"][...] = jnp.zeros_like(ref["start"])

    def compute(c):
        slot = c % 2
        if c > 1:
            for copy in store_all(c - 2):
                copy.wait()

        def body(t):
            rows = rows_at(t, TILE)
            values = [blocks[c, j, rows, :].astype(F32) for j in range(mp)]
            total = sum(jnp.sum(v * v, axis=1, keepdims=True) for v in values)
            s1 = lax.rsqrt(total / features + EPS)
            for j in range(mp):
                cols = slice(j * part, (j + 1) * part)
                norm[slot, rows, cols] = (values[j] * s1 * ref["gains"][0:1, cols]).astype(BF16)
            ref["s1_here"][slot, rows, :] = jnp.broadcast_to(s1, (TILE, 128))

        tile_loop(step // TILE, body)
        for k in range(2):
            cols = slice(k * width, (k + 1) * width)
            both[slot, :, cols] = matmul(norm[slot], w_in[:, cols])
        rnn_forward_kernel(
            both.at[slot], ref["halo"], ref["start"], ref["mask"].at[chunk_rows(c), :],
            ref["dense_here"], ref["params"],
            ref["mixed_here"].at[slot], ref["conv_here"].at[slot], ref["r_here"].at[slot],
            ref["i_here"].at[slot], ref["state_here"].at[slot], ref["end"],
            ref["padded"], ref["high"], ref["low"], ref["decay"], ref["drive"],
        )
        ref["halo"][...] = both[slot, step - 8 :, 0:width]
        ref["start"][...] = ref["end"][...]
        for copy in store_all(c):
            copy.start()

    for s in range(1, mp - 1):
        gather.step(0, s)
        if s == 1 and chunks > 2:
            begin(2)
    if square:
        for item in squares[:2]:
            item.step_one()
        squares[2].start()
        for item in squares[:2]:
            item.step_two()
    gather.finish(0)
    for c in range(chunks):
        if c + 1 < chunks:
            gather.step(c + 1, 1)
        if c == 0:
            if square:
                for item in squares[:2]:
                    item.finish()
            else:
                for item in loads:
                    item.wait()
            expand()
            pass_on = [
                pltpu.make_async_copy(w_in, ref["w_in"], ref["pass_sem"].at[0]),
                pltpu.make_async_copy(ref["dense_here"], ref["dense"], ref["pass_sem"].at[1]),
            ]
            for copy in pass_on:
                copy.start()
        if c == 3 and square:
            squares[3].step_one()
        compute(c)
        if c == 0 and square:
            squares[2].step_one()
            squares[3].start()
        if c == 1 and square:
            squares[2].step_two()
        if c + 3 < chunks:
            begin(c + 3)
        if c + 1 < chunks:
            for s in range(2, mp - 1):
                gather.step(c + 1, s)
            gather.finish(c + 1)
    if square:
        squares[3].step_two()
        squares[2].finish()
        squares[3].finish()
        for item in squares:
            item.drain()
    for copy in pass_on:
        copy.wait()
    for c in range(max(0, chunks - 2), chunks):
        for copy in store_all(c):
            copy.wait()
    for c in range(chunks):
        gather.drain(c)


def head(
    dp, mp, chunks, x, gains, params, mask, in_shard, out_shard, gate_shard, gates_shard, span
):
    count, part = x.shape
    features, width = part * mp, params.shape[1]
    step = count // chunks
    dma = pltpu.SemaphoreType.DMA
    any_, vmem = pl.BlockSpec(memory_space=pl.ANY), pl.BlockSpec(memory_space=pltpu.VMEM)
    ins = [
        ("x", x, any_), ("gains", gains, vmem), ("params", params, vmem), ("mask", mask, vmem),
        ("in_shard", in_shard, any_), ("out_shard", out_shard, any_),
        ("gate_shard", gate_shard, any_), ("gates_shard", gates_shard, any_),
    ]
    gate_width = gate_shard.shape[1]
    shape = jax.ShapeDtypeStruct
    outs = [
        ("w_in", shape((features, 2 * width), BF16)), ("w_out", shape((features, width), BF16)),
        ("w_gate", shape((features, gate_width), BF16)), ("dense", shape((width, 2 * width), BF16)), ("norm_out", shape((count, features), BF16)),
        ("both_out", shape((count, 2 * width), F32)), ("conv_out", shape((count, width), F32)),
        ("r_out", shape((count, width), F32)), ("i_out", shape((count, width), F32)),
        ("state_out", shape((count, width), F32)), ("mixed_out", shape((count, width), BF16)),
        ("s1_out", shape((count, 128), F32)),
    ]
    wide = pltpu.VMEM((2, step, width), F32)
    columns = pltpu.VMEM((width // 128, step, 128), F32)
    scratch = [
        ("blocks", pltpu.VMEM((chunks, mp, step, part), BF16)),
        ("w_in_here", pltpu.VMEM((features, 2 * width), BF16)),
        ("gates_here", pltpu.VMEM((256, 2 * width), BF16)),
        ("gates_flat", pltpu.VMEM((span, 2 * width), F32)),
        ("dense_here", pltpu.VMEM((width, 2 * width), BF16)),
        ("norm", pltpu.VMEM((2, step, features), BF16)),
        ("both_here", pltpu.VMEM((2, step, 2 * width), F32)),
        ("conv_here", wide), ("r_here", wide), ("i_here", wide), ("state_here", wide),
        ("mixed_here", pltpu.VMEM((2, step, width), BF16)),
        ("s1_here", pltpu.VMEM((2, step, 128), F32)),
        ("halo", pltpu.VMEM((8, width), F32)), ("start", pltpu.VMEM((8, width), F32)),
        ("end", pltpu.VMEM((8, width), F32)),
        ("padded", pltpu.VMEM((step + 8, width), F32)),
        ("high", pltpu.VMEM((step, width), BF16)), ("low", pltpu.VMEM((step, width), BF16)),
        ("decay", columns), ("drive", columns),
        ("spread_sent", dma((chunks, 2 * mp))), ("spread_came", dma((chunks, mp))),
        ("square_sent", dma((4, 8))), ("square_came", dma((4, 8))), ("square_own", dma((4,))),
        ("load_sem", dma((chunks,))), ("store_sem", dma((2, 8))), ("pass_sem", dma((2,))),
    ]
    names = [i[0] for i in ins] + [o[0] for o in outs] + [k[0] for k in scratch]
    return pl.pallas_call(
        functools.partial(head_kernel, dp, mp, tuple(names)),
        in_specs=[i[2] for i in ins],
        out_specs=[any_] * len(outs),
        out_shape=[o[1] for o in outs],
        scratch_shapes=[k[1] for k in scratch],
        compiler_params=pltpu.CompilerParams(
            collective_id=2, has_side_effects=True, vmem_limit_bytes=60 * 1024 * 1024
        ),
        name="head",
    )(*[i[1] for i in ins])


MIDDLE_ORDER = (
    ("d", 0, 0), ("A", 0, 0), ("d", 0, 1), ("d", 0, 2), ("a", 1, 0), ("d", 1, 0), ("a", 2, 0),
    ("d", 0, 3), ("J", 0, 0), ("d", 2, 0), ("e", 0, 0), ("A", 0, 1), ("e", 1, 0), ("e", 2, 0),
    ("a", 1, 1), ("d", 1, 2), ("e", 3, 0), ("A", 0, 2), ("S", 1, 0), ("a", 2, 1), ("d", 1, 1),
    ("S", 2, 0), ("d", 2, 2), ("J", 0, 1), ("d", 3, 0), ("a", 1, 2), ("e", 0, 1), ("S", 3, 0),
    ("H", 0, 0), ("a", 2, 2), ("d", 1, 3), ("d", 2, 1), ("G", 0, 0), ("d", 3, 2), ("c", 1, 0),
    ("e", 1, 1), ("J", 0, 2), ("e", 0, 2), ("d", 3, 1), ("e", 2, 1), ("O", 0, 0), ("e", 3, 1),
    ("b", 1, 0), ("c", 2, 0), ("A", 0, 3), ("e", 1, 2), ("K", 0, 0), ("a", 1, 3), ("b", 2, 0),
    ("e", 2, 2), ("H", 0, 1), ("d", 2, 3), ("G", 0, 1), ("e", 3, 2), ("O", 0, 1), ("f", 1, 0),
    ("c", 1, 1), ("a", 2, 3), ("c", 2, 1), ("Y", 0, 0), ("f", 2, 0), ("b", 1, 1), ("J", 0, 3),
    ("K", 0, 1), ("H", 0, 2), ("e", 0, 3), ("B", 0, 0), ("f", 1, 1), ("G", 0, 2), ("e", 1, 3),
    ("f", 2, 1), ("c", 1, 2), ("b", 2, 1), ("c", 2, 2), ("B", 0, 1), ("e", 2, 3), ("Y", 0, 1),
    ("K", 0, 2), ("O", 0, 2), ("e", 3, 3), ("f", 1, 2), ("d", 3, 3), ("H", 0, 3), ("f", 2, 2),
    ("G", 0, 3), ("b", 1, 2), ("B", 0, 2), ("O", 0, 3), ("D", 0, 0), ("c", 1, 3), ("W", 0, 0),
    ("D", 0, 1), ("c", 2, 3), ("D", 0, 2), ("K", 0, 3), ("W", 0, 1), ("b", 2, 2), ("D", 0, 3),
    ("W", 0, 2), ("D", 0, 4), ("Z", 0, 0), ("W", 0, 3), ("f", 1, 3), ("D", 0, 5), ("b", 1, 3),
    ("f", 2, 3), ("Z", 0, 1), ("b", 2, 3), ("W", 0, 4), ("B", 0, 3), ("W", 0, 5), ("Y", 0, 2),
    ("Z", 0, 2), ("Y", 0, 3), ("Z", 0, 3), ("Z", 0, 4), ("Z", 0, 5),
)


def middle_kernel(dp, mp, chunks, *refs):
    (
        mixed_ref, x_ref, cot_ref, live_ref, gains_ref, mine_ref, wout_ref, gate_ref, up_ref,
        down_ref,
        output_ref, gm_ref, gbo_ref, local_ref, hidden_ref, pulled_ref, norm_ref, grady_ref,
        grad_gate_ref, grad_up_ref, gain_ref,
        w_up, w_down, cots, mids, gn2s, mid_mine, gn2_mine,
        parts1, rights1, lefts1, parts2, rights2, lefts2, parts3, rights3, lefts3,
        norm, hidden, pulled, gbo, gm, local, out,
        spread_sent, spread_came, fold_sent, fold_right, fold_left,
        square_sent, square_came, square_own, load_sem, store_sem,
        stage, free_sem, task_sent, task_came, left_sem, right_sem, stage_sem,
    ) = refs
    step, part = x_ref.shape[0] // chunks, x_ref.shape[1]
    features = part * mp
    hidden_width = w_down.shape[1]
    z, d = lax.axis_index("mp"), lax.axis_index("dp")
    square = dp == 8
    up_half = w_up.at[:, pl.ds(hidden_width, hidden_width)]

    folds = [
        Fold(z, mp, p, r, l, fold_sent.at[k], fold_right.at[k], fold_left.at[k])
        for k, (p, r, l) in enumerate(
            ((parts1, rights1, lefts1), (parts2, rights2, lefts2), (parts3, rights3, lefts3))
        )
    ]
    rs1, rs2, rs3 = folds
    ag2, ag3, ag4 = [
        Spread(z, mp, b, spread_sent.at[k], spread_came.at[k])
        for k, b in enumerate((cots, mids, gn2s))
    ]
    for fold in folds:
        fold.clear()

    barrier = pltpu.get_barrier_semaphore()

    @pl.when(z > 0)
    def _():
        pl.semaphore_signal(barrier, inc=1, device_id={"mp": z - 1}, device_id_type=MESH)

    @pl.when(z < mp - 1)
    def _():
        pl.semaphore_signal(barrier, inc=1, device_id={"mp": z + 1}, device_id_type=MESH)

    count = jnp.where((z > 0) & (z < mp - 1), 2, 1)
    if square:
        for other in partners(d)[1:]:
            pl.semaphore_signal(barrier, inc=1, device_id={"dp": other}, device_id_type=MESH)
        count = count + 3
    pl.semaphore_wait(barrier, count)

    if square:
        squares = [
            Square(
                d, shard, whole, square_sent.at[k], square_came.at[k], square_own.at[k]
            )
            for k, (shard, whole) in enumerate(((up_ref, up_half), (down_ref, w_down)))
        ]
        for item in squares:
            item.start()
    else:
        loads = [
            pltpu.make_async_copy(up_ref, up_half, square_own.at[0]),
            pltpu.make_async_copy(down_ref, w_down, square_own.at[1]),
        ]
        for item in loads:
            item.start()
    load_gate = pltpu.make_async_copy(
        gate_ref, w_up.at[:, pl.ds(0, hidden_width)], square_own.at[2]
    )
    load_gate.start()

    def chunk_rows(c):
        return pl.ds(c * step, step)

    def store(buffer, target, c, k):
        return pltpu.make_async_copy(buffer, target.at[chunk_rows(c), :], store_sem.at[k])

    def own_cot(c):
        return pltpu.make_async_copy(cot_ref.at[chunk_rows(c), :], cots.at[c, z], load_sem.at[c])

    for c in range(chunks):
        own_cot(c).start()

    gain_ref[...] = jnp.zeros_like(gain_ref)
    tiles = step // TILE

    def fill(fold, slot, left, weights):
        def body(j):
            rows = pl.ds(pl.multiple_of(j * part, part), part)
            fold.parts[slot, j] = inner_cols(left, weights[rows, :]).astype(BF16)

        tile_loop(mp, body)

    def branch(c):
        if c > 1:
            rs1.drain(c % 2)
        fill(rs1, c % 2, mixed_ref[chunk_rows(c), :], wout_ref)
        rs1.start(c % 2)

    def join(c):
        rs1.finish(c % 2)

        def body(t):
            rows = rows_at(t, TILE)
            base = pl.ds(pl.multiple_of(c * step + t * TILE, TILE), TILE)
            total = x_ref[base, :].astype(F32) + rs1.total(c % 2, rows)
            mid_mine[c, rows, :] = total
            mids[c, z, rows, :] = total.astype(BF16)

        tile_loop(tiles, body)

    def stats(c, rows):
        blocks = [mids[c, j, rows, :].astype(F32) for j in range(mp)]
        square_sum = sum(jnp.sum(b * b, axis=1, keepdims=True) for b in blocks)
        return blocks, lax.rsqrt(square_sum / features + EPS)

    def block_cols(j):
        return slice(j * part, (j + 1) * part)

    def normalise(c):
        def body(t):
            rows = rows_at(t, TILE)
            base = pl.ds(pl.multiple_of(c * step + t * TILE, TILE), TILE)
            blocks, s2 = stats(c, rows)
            live = live_ref[base, :][:, 0:1]
            for j in range(mp):
                norm[rows, block_cols(j)] = (
                    blocks[j] * s2 * gains_ref[1:2, block_cols(j)]
                ).astype(BF16)
                cots[c, j, rows, :] = (cots[c, j, rows, :].astype(F32) * live).astype(BF16)

        tile_loop(tiles, body)

    def grad_y_copies(c):
        return [
            pltpu.make_async_copy(
                cots.at[c, j], grady_ref.at[chunk_rows(c), pl.ds(j * part, part)],
                store_sem.at[8 + j],
            )
            for j in range(mp)
        ]

    def mlp_first(c):
        if c > 0:
            store(norm, norm_ref, c, 0).wait()
            store(hidden, hidden_ref, c, 1).wait()
            store(pulled, pulled_ref, c, 2).wait()
            for copy in grad_y_copies(c - 1):
                copy.wait()
        if c == 0:
            load_gate.wait()
            for item in squares if square else ():
                item.finish()
            for item in () if square else loads:
                item.wait()
        ag2.drain(c)
        normalise(c)
        store(norm, norm_ref, c, 0).start()
        for copy in grad_y_copies(c):
            copy.start()
        size = 256

        def body(t):
            near = pl.ds(pl.multiple_of(t * size, size), size)
            off = pl.ds(pl.multiple_of(hidden_width + t * size, size), size)
            gate = matmul(norm[...], w_up[:, near])
            up = matmul(norm[...], w_up[:, off])
            grad = sum(
                matmul(cots[c, j], w_down[block_cols(j), near]) for j in range(mp)
            )
            value, slope = gelu_and_slope(gate)
            hidden[:, near] = (value * up).astype(BF16)
            pulled[:, near] = (grad * up * slope).astype(BF16)
            pulled[:, off] = (grad * value).astype(BF16)

        tile_loop(hidden_width // size, body)
        store(hidden, hidden_ref, c, 1).start()
        store(pulled, pulled_ref, c, 2).start()

    def mlp_second(c):
        slot = c % 2
        if c > 1:
            rs3.drain(slot)
        fill(rs3, slot, pulled[...], w_up)
        rs3.start(slot)
        if square and c == chunks - 1:
            for item in squares:
                item.drain()
            for k, other in enumerate(partners(d)[1:]):
                pl.semaphore_signal(
                    free_sem.at[k], inc=1, device_id={"dp": other}, device_id_type=MESH
                )

    def mlp_third(c):
        slot = c % 2
        if c > 1:
            rs2.drain(slot)
        fill(rs2, slot, hidden[...], w_down)
        rs2.start(slot)

    def gather_grad(c):
        slot = c % 2
        rs3.finish(slot)

        def body(t):
            rows = rows_at(t, TILE)
            total = rs3.total(slot, rows)
            gn2_mine[slot, rows, :] = total
            gn2s[c, z, rows, :] = total.astype(BF16)

        tile_loop(tiles, body)
        ag4.step(c, 0)

    def norm_back(c):
        slot = c % 2
        ag4.finish(c)
        if c > 0:
            store(gbo, gbo_ref, c, 3).wait()
            store(local, local_ref, c, 4).wait()
            store(gm, gm_ref, c, 5).wait()

        def body(t):
            rows = rows_at(t, TILE)
            blocks, s2 = stats(c, rows)
            grads = [gn2s[c, j, rows, :].astype(F32) for j in range(mp)]
            scaled = [grads[j] * gains_ref[1:2, block_cols(j)] for j in range(mp)]
            mean = (
                sum(jnp.sum(scaled[j] * blocks[j], axis=1, keepdims=True) for j in range(mp))
                / features
            )
            fall = s2 * s2 * s2 * mean
            for j in range(mp):
                grad_y = cots[c, j, rows, :].astype(F32)
                gbo[rows, block_cols(j)] = (
                    grad_y + s2 * scaled[j] - blocks[j] * fall
                ).astype(BF16)
                gain_ref[:, block_cols(j)] += jnp.sum(
                    (grads[j] * (blocks[j] * s2)).reshape(-1, 8, part), axis=0
                )
            local[rows, :] = (
                cots[c, z, rows, :].astype(F32)
                + s2 * (gn2_mine[slot, rows, :] * mine_ref[1:2, :])
                - mid_mine[c, rows, :] * fall
            )

        tile_loop(tiles, body)
        gm[...] = matmul(gbo[...], wout_ref[...])
        store(gbo, gbo_ref, c, 3).start()
        store(local, local_ref, c, 4).start()
        store(gm, gm_ref, c, 5).start()

    def make_output(c):
        rs2.finish(c % 2)
        if c > 0:
            store(out, output_ref, c, 6).wait()

        def body(t):
            rows = rows_at(t, TILE)
            out[rows, :] = (mid_mine[c, rows, :] + rs2.total(c % 2, rows)).astype(BF16)

        tile_loop(tiles, body)
        store(out, output_ref, c, 6).start()

    own = features // 8
    count_tasks = 2 * hidden_width // part
    scatters, sending = [], [None] * 4
    buffers = [rights1.at[i // 2, i % 2] for i in range(4)]
    staged = [None]

    def left_block(i):
        return (cots if i < 2 else mids).at[i % 2]

    def left_copies():
        return [
            pltpu.make_async_copy(
                norm_ref.at[chunk_rows(i), pl.ds(j * part, part)], left_block(i).at[j],
                left_sem.at[i, j],
            )
            for i in range(chunks)
            for j in range(mp)
        ]

    def right_copies(k):
        return [
            pltpu.make_async_copy(
                pulled_ref.at[chunk_rows(i), pl.ds(k * part, part)], parts1.at[k % 2, i],
                right_sem.at[k % 2, i],
            )
            for i in range(chunks)
        ]

    def make_scatter(k):
        def compute(owner, target, add):
            j = lax.div(owner, 2)
            near = pl.ds(pl.multiple_of(lax.rem(owner, 2) * own, own), own)
            value = sum(
                inner_rows(left_block(i)[j, :, near], parts1[k % 2, i]) for i in range(chunks)
            )
            if add:
                value = value + target[...].astype(F32)
            target[...] = value.astype(BF16)

        cols = pl.ds(k * part, part)

        def place(first):
            return w_up.at[pl.ds(first, own), cols]

        def held(i):
            return w_up.at[pl.ds(pl.multiple_of(i * own, own), own), cols]

        return Scatter(
            d, own, compute, held, place(4 * own), place(5 * own), place(6 * own),
            task_sent.at[k], task_came.at[k],
        )

    def weight_first(k):
        if not square:
            return
        if k == 0:
            store(norm, norm_ref, chunks - 1, 0).wait()
            store(pulled, pulled_ref, chunks - 1, 2).wait()
            for slot in range(2):
                rs1.drain(slot)
            for c in range(2):
                ag3.drain(c)
            scatters.extend(make_scatter(i) for i in range(count_tasks))
            for copy in right_copies(0) + left_copies():
                copy.start()
            for i in range(3):
                pl.semaphore_wait(free_sem.at[i], 1)
        if k + 1 < count_tasks:
            for copy in right_copies(k + 1):
                copy.start()
        for copy in right_copies(k) + (left_copies() if k == 0 else []):
            copy.wait()
        scatters[k].far_core(buffers, sending)
        scatters[k].near_core()

    def weight_second(k):
        if square:
            scatters[k].onward()

    def weight_third(k):
        if not square:
            return
        if staged[0] is not None:
            staged[0].wait()
        scatters[k].finish(stage)
        half = count_tasks // 2
        target = grad_gate_ref if k < half else grad_up_ref
        staged[0] = pltpu.make_async_copy(
            stage, target.at[:, pl.ds((k % half) * part, part)], stage_sem
        )
        staged[0].start()

    steps = {
        "A": branch, "J": join, "H": mlp_first, "G": mlp_second, "O": mlp_third,
        "K": gather_grad, "B": norm_back, "Y": make_output, "D": weight_first,
        "W": weight_second, "Z": weight_third,
    }
    moves = {"a": (rs1, 2), "b": (rs2, 2), "c": (rs3, 2), "d": (ag2, 0), "e": (ag3, 0), "f": (ag4, 0)}
    for name, s, c in MIDDLE_ORDER:
        if name == "S":
            if square and s < 3:
                squares[s - 1].step_one()
            if square and s == 3:
                squares[0].step_two()
                squares[1].step_two()
        elif name in steps:
            steps[name](c)
        else:
            line, parity = moves[name]
            if s == mp - 1:
                line.finish(c)
                continue
            if name == "d" and s == 0:
                own_cot(c).wait()
            line.step(c % parity if parity else c, s)

    last = chunks - 1
    for k, (buffer, target) in enumerate(
        (
            (norm, norm_ref), (hidden, hidden_ref), (pulled, pulled_ref), (gbo, gbo_ref),
            (local, local_ref), (gm, gm_ref), (out, output_ref),
        )
    ):
        if not (square and k in (0, 2)):
            store(buffer, target, last, k).wait()
    for copy in grad_y_copies(last):
        copy.wait()
    for c in range(chunks):
        if c > 1 or not square:
            ag3.drain(c)
        ag4.drain(c)
    for slot in range(2):
        for fold in folds[1:] if square else folds:
            fold.drain(slot)
    if square:
        staged[0].wait()
        for copy in sending:
            copy.wait_send()
        for scatter in scatters:
            scatter.drain()


def middle(dp, mp, chunks, mixed, inputs, cotangent, live, gains, mine, w_out, gate, up, down):
    count, part = inputs.shape
    width, hidden_width = mixed.shape[1], down.shape[1]
    step, features = count // chunks, part * mp

    def fold_buffers():
        return [
            pltpu.VMEM((2, mp, step, part), BF16),
            pltpu.VMEM((2, mp - 1, step, part), BF16),
            pltpu.VMEM((2, mp - 1, step, part), BF16),
        ]

    dma = pltpu.SemaphoreType.DMA
    any_, vmem = pl.BlockSpec(memory_space=pl.ANY), pl.BlockSpec(memory_space=pltpu.VMEM)
    return pl.pallas_call(
        functools.partial(middle_kernel, dp, mp, chunks),
        in_specs=[vmem, vmem, any_, vmem, vmem, vmem, vmem, any_, any_, any_],
        out_specs=[any_] * 10 + [vmem],
        out_shape=(
            jax.ShapeDtypeStruct((count, part), BF16),
            jax.ShapeDtypeStruct((count, width), F32),
            jax.ShapeDtypeStruct((count, features), BF16),
            jax.ShapeDtypeStruct((count, part), F32),
            jax.ShapeDtypeStruct((count, hidden_width), BF16),
            jax.ShapeDtypeStruct((count, 2 * hidden_width), BF16),
            jax.ShapeDtypeStruct((count, features), BF16),
            jax.ShapeDtypeStruct((count, features), BF16),
            jax.ShapeDtypeStruct((features // 8, hidden_width), F32),
            jax.ShapeDtypeStruct((features // 8, hidden_width), F32),
            jax.ShapeDtypeStruct((8, features), F32),
        ),
        scratch_shapes=[
            pltpu.VMEM((features, 2 * hidden_width), BF16),
            pltpu.VMEM((features, hidden_width), BF16),
            pltpu.VMEM((chunks, mp, step, part), BF16),
            pltpu.VMEM((chunks, mp, step, part), BF16),
            pltpu.VMEM((chunks, mp, step, part), BF16),
            pltpu.VMEM((chunks, step, part), F32),
            pltpu.VMEM((2, step, part), F32),
        ]
        + fold_buffers() + fold_buffers() + fold_buffers()
        + [
            pltpu.VMEM((step, features), BF16),
            pltpu.VMEM((step, hidden_width), BF16),
            pltpu.VMEM((step, 2 * hidden_width), BF16),
            pltpu.VMEM((step, features), BF16),
            pltpu.VMEM((step, width), F32),
            pltpu.VMEM((step, part), F32),
            pltpu.VMEM((step, part), BF16),
            dma((3, chunks, 2 * mp)),
            dma((3, chunks, mp)),
            dma((3, 2, mp)),
            dma((3, 2, mp)),
            dma((3, 2, mp)),
            dma((2, 8)),
            dma((2, 8)),
            dma((3,)),
            dma((chunks,)),
            dma((12,)),
            pltpu.VMEM((features // 8, part), F32),
            pltpu.SemaphoreType.REGULAR((3,)),
            dma((2 * hidden_width // part, 8)),
            dma((2 * hidden_width // part, 8)),
            dma((chunks, mp)),
            dma((2, chunks)),
            dma,
        ],
        compiler_params=pltpu.CompilerParams(
            collective_id=0, has_side_effects=True, vmem_limit_bytes=62 * 1024 * 1024
        ),
        name="middle",
    )(mixed, inputs, cotangent, live, gains, mine, w_out, gate, up, down)


def tail_kernel(mp, tasks, names, *refs):
    ref = dict(zip(names, refs))
    pull, w_in, params = ref["pull"], ref["w_in_here"], ref["params"]
    chunks, _, step, part = ref["parts"].shape
    count, features = chunks * step, part * mp
    own, width = features // 8, params.shape[1]
    z, d = lax.axis_index("mp"), lax.axis_index("dp")
    _, by_core, by_x, by_y = partners(d)
    fold = Fold(
        z, mp, ref["parts"], ref["rights"], ref["lefts"], ref["fold_sent"], ref["fold_right"],
        ref["fold_left"],
    )
    near = z + 1 - 2 * lax.rem(z, 2)
    apart = z + 2 - 4 * lax.div(z, 2)

    def chunk_rows(c):
        return pl.ds(c * step, step)

    def recurrence_copies(c):
        copies = [
            pltpu.make_async_copy(
                ref[name].at[chunk_rows(c), :], ref[name + "_here"], ref["chunk_sem"].at[k]
            )
            for k, name in enumerate(("gm", "both", "conv", "r", "i", "state"))
        ]
        if c > 0:
            rows = pl.ds(c * step - 8, 8)
            copies += [
                pltpu.make_async_copy(
                    ref["both"].at[rows, pl.ds(0, width)], ref["halo"], ref["chunk_sem"].at[6]
                ),
                pltpu.make_async_copy(
                    ref["state"].at[rows, :], ref["start"], ref["chunk_sem"].at[7]
                ),
            ]
        return copies

    def norm_copy(c):
        return pltpu.make_async_copy(
            ref["norm1"].at[chunk_rows(c), :], ref["norm_here"], ref["norm_sem"]
        )

    def left_copy(name):
        return pltpu.make_async_copy(ref[name], ref["lhs"], ref["left_sem"])

    def right_copy(name, first, columns, slot):
        return pltpu.make_async_copy(
            ref[name].at[:, pl.ds(first, columns)], ref["rhs"].at[slot, :, pl.ds(0, columns)],
            ref["right_sem"].at[slot],
        )

    def end_copies(c):
        return [
            pltpu.make_async_copy(
                ref[name].at[chunk_rows(c), :], ref[name + "_here"], ref["end_sem"].at[k]
            )
            for k, name in enumerate(("local", "x", "s1"))
        ]

    whole_copies = [
        pltpu.make_async_copy(ref[name], ref[name + "_here"], ref["whole_sem"].at[k])
        for k, name in enumerate(("dense", "w_in"))
    ]
    last = chunks - 1
    for copy in recurrence_copies(last) + whole_copies:
        copy.start()
    norm_copy(last).start()
    left_copy("grady").start()
    first_rights = [
        right_copy(t[2], t[3], t[4], k) for k, t in enumerate(tasks[:2])
    ]
    for copy in first_rights + end_copies(last):
        copy.start()

    fold.clear()
    barrier = pltpu.get_barrier_semaphore()

    @pl.when(z > 0)
    def _():
        pl.semaphore_signal(barrier, inc=1, device_id={"mp": z - 1}, device_id_type=MESH)

    @pl.when(z < mp - 1)
    def _():
        pl.semaphore_signal(barrier, inc=1, device_id={"mp": z + 1}, device_id_type=MESH)

    pl.semaphore_signal(barrier, inc=1, device_id={"mp": apart}, device_id_type=MESH)
    for other in (by_core, by_x, by_y):
        pl.semaphore_signal(barrier, inc=1, device_id={"dp": other}, device_id_type=MESH)

    for name in ("back", "after", "gain", "dense_sum", "params_sum"):
        ref[name][...] = jnp.zeros_like(ref[name])
    gain = ref["gain"]

    def recur(c):
        for copy in recurrence_copies(c):
            copy.wait()
        if c == 0:
            ref["halo"][...] = jnp.zeros_like(ref["halo"])
            ref["start"][...] = jnp.zeros_like(ref["start"])
        if c == last:
            for copy in whole_copies:
                copy.wait()
        rnn_backward_kernel(
            ref["gm_here"], ref["both_here"], ref["halo"], ref["start"], ref["conv_here"],
            ref["r_here"], ref["i_here"], ref["state_here"],
            ref["mask"].at[pl.ds(c * step, step + 8), :], ref["dense_here"], params,
            ref["back"], ref["after"],
            pull.at[chunk_rows(c), :], ref["rates"], ref["dparams"], ref["back"], ref["after"],
            ref["dots"],
            ref["padded"], ref["before"], ref["decay"], ref["adjoint"], ref["coef"],
            ref["dconv"], ref["sums"],
        )
        ref["params_sum"][...] += ref["dparams"][...]
        ref["dense_sum"][...] += inner_rows(ref["conv_here"][...].astype(BF16), ref["rates"][...])
        if c > 0:
            for copy in recurrence_copies(c - 1):
                copy.start()
        for q in range(step // 128):
            turned = jnp.transpose(ref["dots"][q * 128 : (q + 1) * 128, :])
            ref["dots_row"][c, :, q * 128 : (q + 1) * 128] = turned[0:8, :]
        if c == last:
            pl.semaphore_wait(barrier, jnp.where((z > 0) & (z < mp - 1), 6, 5))
        dots_copy(c, 0).start()
        norm_copy(c).wait()

        def body(j):
            rows = pl.ds(pl.multiple_of(j * part, part), part)
            value = inner_cols(pull[chunk_rows(c), :], w_in[rows, :])
            fold.parts[c, j] = value.astype(BF16)
            gain[:, rows] += jnp.sum(
                (value * ref["norm_here"][:, rows].astype(F32)).reshape(-1, 8, part), axis=0
            )

        tile_loop(mp, body)
        fold.start(c)
        if c > 0:
            norm_copy(c - 1).start()

    def dots_copy(c, k):
        return pltpu.make_async_remote_copy(
            src_ref=ref["dots_row"].at[c], dst_ref=ref["dots_in"].at[c, k],
            send_sem=ref["dots_sent"].at[c, k], recv_sem=ref["dots_came"].at[c, k],
            device_id={"mp": near if k == 0 else apart}, device_id_type=MESH,
        )

    def dots_add(c, k):
        dots_copy(c, k).wait()
        ref["dots_row"][c] += ref["dots_in"][c, k]
        if k == 0:
            dots_copy(c, 1).start()

    def input_grad(c):
        dots_add(c, 1)
        for q in range(step // 128):
            row = ref["dots_row"][c, 0:1, q * 128 : (q + 1) * 128]
            ref["dots_col"][q * 128 : (q + 1) * 128, :] = jnp.transpose(
                jnp.broadcast_to(row, (128, 128))
            )
        fold.finish(c)
        for copy in end_copies(c):
            copy.wait()

        def body(t):
            rows = rows_at(t, TILE)
            base = pl.ds(pl.multiple_of(c * step + t * TILE, TILE), TILE)
            s1 = ref["s1_here"][rows, :][:, 0:1]
            dot = ref["dots_col"][rows, :][:, 0:1]
            grad = (
                ref["local_here"][rows, :]
                + s1 * (fold.total(c, rows) * ref["mine"][0:1, :])
                - ref["x_here"][rows, :].astype(F32) * (s1 * s1 * dot * (1.0 / features))
            )
            ref["grad_x"][base, :] = grad.astype(BF16)

        tile_loop(step // TILE, body)
        if c > 0:
            for copy in end_copies(c - 1):
                copy.start()

    sends, store_sem = ref["sends"], ref["store_sem"]
    slots = {k: k % 2 for k, t in enumerate(tasks) if t[2] in ("hidden", "mixed")}

    def build(k):
        _, left, right, first, columns, _ = tasks[k]

        def compute(owner, target, add):
            if left is None:
                rows = pl.ds(pl.multiple_of(owner * 32, 32), 32)
                value = ref["gates"][rows, first : first + columns].astype(F32)
            else:
                near = pl.ds(pl.multiple_of(owner * own, own), own)
                if right == "pull":
                    operand = pull[:, first : first + columns]
                else:
                    operand = ref["rhs"][slots[k], :, 0:columns]
                value = inner_rows(ref["lhs"][:, near], operand)
            if add:
                value = value + target[...].astype(F32)
            target[...] = value.astype(BF16)

        return Scatter(
            d, 32 if left is None else own, compute, ref["held%d" % k].at.__getitem__,
            ref["far%d" % k], ref["first%d" % k], ref["second%d" % k], ref["task_sent"].at[k],
            ref["task_came"].at[k],
        )

    scatters = [build(k) for k in range(len(tasks))]
    sending = [None] * 4

    def far_core(k):
        height, columns = scatters[k].count, tasks[k][4]
        scatters[k].far_core(
            [sends.at[slot, pl.ds(0, height), pl.ds(0, columns)] for slot in range(4)], sending
        )

    stage, stage_wait = ref["stage"], [None, None]

    def finish(k):
        scatter = scatters[k]
        name, columns, column = tasks[k][0], tasks[k][4], tasks[k][5]
        slot = k % 2
        if stage_wait[slot] is not None:
            stage_wait[slot].wait()
        view = stage.at[slot, pl.ds(0, scatter.count), pl.ds(0, columns)]
        scatter.finish(view)
        target = ref["grad_" + name].at[:, pl.ds(column, columns)]
        copy = pltpu.make_async_copy(view, target, store_sem.at[slot])
        copy.start()
        stage_wait[slot] = copy

    small, small_in = ref["small"], ref["small_in"]
    targets = (
        {"dp": by_core}, {"dp": by_x}, {"dp": by_y}, {"mp": near}, {"mp": apart},
    )

    def small_copy(k):
        rows = pl.ds(0, 16 if k < 3 else 8)
        return pltpu.make_async_remote_copy(
            src_ref=small.at[rows, :], dst_ref=small_in.at[k, rows, :],
            send_sem=ref["small_sent"].at[k], recv_sem=ref["small_came"].at[k],
            device_id=targets[k], device_id_type=MESH,
        )

    def small_first():
        small[...] = jnp.zeros_like(small)
        small[0:1, :] = jnp.sum(gain[...], axis=0, keepdims=True) / ref["gains"][0:1, :]
        small[1:2, :] = ref["gain2"][...] * (1.0 / mp)
        small[8:16, 0:width] = ref["params_sum"][...]
        small_copy(0).start()

    def small_next(k):
        rows = 16 if k < 3 else 8
        small_copy(k).wait()
        small[0:rows, :] += small_in[k, 0:rows, :]
        if k < 4:
            small_copy(k + 1).start()

    def gate_blocks():
        flat, gates = ref["flat"], ref["gates"]
        span = flat.shape[0] - 16
        rows = span // 8
        column = lax.broadcasted_iota(jnp.int32, (span, 2 * width), 1)
        column = jnp.where(column >= width, column - width, column)
        total = jnp.zeros((span, 2 * width), F32)
        for b in range(width // span):
            inside = (column >= b * span) & (column < (b + 1) * span)
            total = total + jnp.where(
                inside, ref["dense_sum"][b * span : (b + 1) * span, :], 0.0
            )
        flat[0:span, :] = total
        flat[span:, :] = jnp.zeros((16, 2 * width), F32)
        for k in range(8):
            gates[k * 32 : (k + 1) * 32, :] = flat[k * rows : k * rows + 32, :].astype(BF16)

    recur(3)
    for copy in first_rights:
        copy.wait()
    left_copy("grady").wait()
    far_core(0)
    scatters[0].near_core()
    fold.step(3, 1)
    recur(2)
    fold.step(3, 2)
    far_core(1)
    scatters[1].near_core()
    left_copy("gbo").start()
    out_right = right_copy("mixed", 0, tasks[2][4], 0)
    out_right.start()
    dots_add(3, 0)
    scatters[0].onward()
    fold.step(2, 1)
    recur(1)
    dots_add(2, 0)
    fold.step(2, 2)
    left_copy("gbo").wait()
    out_right.wait()
    far_core(2)
    scatters[2].near_core()
    left_copy("norm1").start()
    scatters[1].onward()
    fold.step(1, 1)
    input_grad(3)
    recur(0)
    small_first()
    gate_blocks()
    dots_add(1, 0)
    fold.step(1, 2)
    small_next(0)
    left_copy("norm1").wait()
    far_core(3)
    small_next(1)
    scatters[3].near_core()
    scatters[2].onward()
    small_next(2)
    fold.step(0, 1)
    input_grad(2)
    far_core(4)
    scatters[4].near_core()
    scatters[3].onward()
    dots_add(0, 0)
    fold.step(0, 2)
    for k in (5, 6):
        far_core(k)
        scatters[k].near_core()
    scatters[4].onward()
    finish(0)
    finish(1)
    input_grad(1)
    for k in (5, 6):
        scatters[k].onward()
    finish(2)
    small_next(3)
    finish(3)
    input_grad(0)
    for k in (4, 5, 6):
        finish(k)
    small_next(4)
    for copy in stage_wait:
        copy.wait()
    for copy in sending:
        copy.wait_send()
    for scatter in scatters:
        scatter.drain()
    for c in range(chunks):
        fold.drain(c)


def tail(mp, chunks, span, rnn, mask, params, dense, w_in, norm1, grady, hidden, gbo, mixed, s1, x,
         local, gains, mine, gain2):
    gm, both, conv, r, i, state = rnn
    count, part = x.shape
    features, width = part * mp, params.shape[1]
    own, step = features // 8, count // chunks
    widths = {
        "down": hidden.shape[1], "out": width, "in": 2 * width, "block": 2 * width,
    }
    heights = {name: 32 if name == "block" else own for name in widths}
    operands = {
        "down": ("grady", "hidden"), "out": ("gbo", "mixed"), "in": ("norm1", "pull"),
        "block": (None, "gates"),
    }
    tasks = []
    for name, columns in widths.items():
        left, right = operands[name]
        pieces = 1 if name == "out" else 2
        size = columns // pieces
        for piece in range(pieces):
            tasks.append((name, left, right, piece * size, size, piece * size))
    widest = max(t[4] for t in tasks)
    dma = pltpu.SemaphoreType.DMA
    any_, vmem = pl.BlockSpec(memory_space=pl.ANY), pl.BlockSpec(memory_space=pltpu.VMEM)
    ins = [
        ("gm", gm, any_), ("both", both, any_), ("conv", conv, any_), ("r", r, any_),
        ("i", i, any_), ("state", state, any_), ("mask", mask, vmem), ("params", params, vmem),
        ("dense", dense, any_), ("w_in", w_in, any_), ("norm1", norm1, any_),
        ("grady", grady, any_), ("hidden", hidden, any_), ("gbo", gbo, any_),
        ("mixed", mixed, any_), ("s1", s1, any_), ("x", x, any_), ("local", local, any_),
        ("gains", gains, vmem), ("mine", mine, vmem), ("gain2", gain2, vmem),
    ]
    shape = jax.ShapeDtypeStruct
    outs = [("grad_x", shape((count, part), BF16), vmem)]
    for name, columns in widths.items():
        outs.append(("grad_" + name, shape((heights[name], columns), F32), any_))
    outs.append(("small", shape((16, features), F32), vmem))
    wide = pltpu.VMEM((step, width), F32)
    tall = pltpu.VMEM((step + 8, width), F32)
    eight = pltpu.VMEM((8, width), F32)
    columns = pltpu.VMEM((width // 128, step, 128), F32)
    scratch = [
        ("gm_here", wide), ("both_here", pltpu.VMEM((step, 2 * width), F32)),
        ("conv_here", wide), ("r_here", wide), ("i_here", wide), ("state_here", wide),
        ("halo", eight), ("start", eight), ("back", eight), ("after", eight),
        ("dparams", eight), ("params_sum", eight),
        ("dense_here", pltpu.VMEM(dense.shape, BF16)), ("w_in_here", pltpu.VMEM(w_in.shape, BF16)),
        ("pull", pltpu.VMEM((count, 2 * width), BF16)),
        ("rates", pltpu.VMEM((step, 2 * width), BF16)),
        ("dots", pltpu.VMEM((step, 128), F32)),
        ("padded", tall), ("before", tall), ("decay", columns), ("adjoint", columns),
        ("coef", columns), ("dconv", tall), ("sums", pltpu.VMEM((8, 8, width), F32)),
        ("dense_sum", pltpu.VMEM((width, 2 * width), F32)),
        ("flat", pltpu.VMEM((span + 16, 2 * width), F32)),
        ("gates", pltpu.VMEM((256, 2 * width), BF16)),
        ("norm_here", pltpu.VMEM((step, features), BF16)),
        ("lhs", pltpu.VMEM((count, features), BF16)),
        ("rhs", pltpu.VMEM((2, count, widest), BF16)),
        ("local_here", pltpu.VMEM((step, part), F32)), ("x_here", pltpu.VMEM((step, part), BF16)),
        ("s1_here", pltpu.VMEM((step, 128), F32)),
        ("parts", pltpu.VMEM((chunks, mp, step, part), BF16)),
        ("rights", pltpu.VMEM((chunks, mp - 1, step, part), BF16)),
        ("lefts", pltpu.VMEM((chunks, mp - 1, step, part), BF16)),
        ("sends", pltpu.VMEM((4, own, widest), BF16)),
        ("stage", pltpu.VMEM((2, own, widest), F32)),
        ("gain", pltpu.VMEM((8, features), F32)),
        ("dots_row", pltpu.VMEM((chunks, 8, step), F32)),
        ("dots_in", pltpu.VMEM((chunks, 2, 8, step), F32)),
        ("dots_col", pltpu.VMEM((step, 128), F32)),
        ("small_in", pltpu.VMEM((5, 16, features), F32)),
        ("chunk_sem", dma((8,))), ("norm_sem", dma), ("left_sem", dma), ("right_sem", dma((2,))),
        ("end_sem", dma((3,))), ("whole_sem", dma((2,))), ("store_sem", dma((2,))),
        ("fold_sent", dma((chunks, mp))), ("fold_right", dma((chunks, mp))),
        ("fold_left", dma((chunks, mp))),
        ("task_sent", dma((len(tasks), 8))), ("task_came", dma((len(tasks), 8))),
        ("dots_sent", dma((chunks, 2))), ("dots_came", dma((chunks, 2))),
        ("small_sent", dma((5,))), ("small_came", dma((5,))),
    ]
    for k, (name, _, _, _, size, _) in enumerate(tasks):
        rows = heights[name]
        scratch.append(("held%d" % k, pltpu.VMEM((4, rows, size), BF16)))
        for kind in ("far", "first", "second"):
            scratch.append(("%s%d" % (kind, k), pltpu.VMEM((rows, size), BF16)))
    names = [i[0] for i in ins] + [o[0] for o in outs] + [k[0] for k in scratch]
    return pl.pallas_call(
        functools.partial(tail_kernel, mp, tuple(tasks), tuple(names)),
        in_specs=[i[2] for i in ins],
        out_specs=[o[2] for o in outs],
        out_shape=[o[1] for o in outs],
        scratch_shapes=[k[1] for k in scratch],
        compiler_params=pltpu.CompilerParams(
            collective_id=1, has_side_effects=True, vmem_limit_bytes=63 * 1024 * 1024
        ),
        name="tail",
    )(*[i[1] for i in ins])


def make_masks(row_lengths, count):
    ends = jnp.cumsum(row_lengths)
    places = jnp.arange(-TAPS, count, dtype=jnp.int32)
    segment = jnp.sum((places[:, None] >= ends[None, :]).astype(jnp.int32), axis=1)
    segment = jnp.where(places < 0, -1, segment)
    now = segment[TAPS:]
    same = [(segment[TAPS - k : TAPS - k + count] == now).astype(F32) for k in range(1, TAPS)]
    blank = jnp.zeros((count,), F32)
    columns = [same[0]] + same + [blank] * (LANES - TAPS)
    live = now < row_lengths.shape[0]
    return jnp.stack(columns, axis=1), live


def dense_gates(gates, width):
    span = gates.shape[0]
    tiled = jnp.tile(gates, (width // span, 1))
    row = lax.broadcasted_iota(jnp.int32, tiled.shape, 0) // span
    column = (lax.broadcasted_iota(jnp.int32, tiled.shape, 1) % width) // span
    return jnp.where(row == column, tiled, jnp.zeros((), tiled.dtype))


def diagonal_blocks(dense, span):
    width = dense.shape[0]
    column = (lax.broadcasted_iota(jnp.int32, (1, 2 * width), 1) % width) // span
    total = jnp.zeros((span, 2 * width), F32)
    for b in range(width // span):
        total = total + jnp.where(column == b, dense[b * span : (b + 1) * span], 0.0)
    return total


def per_device(
    dp, mp,
    inputs, lengths, cotangent, gains, rnn_params, rnn_in, branch_gate, recur_gate, input_gate,
    mlp_gate, mlp_up, rnn_out, mlp_down,
):
    count, part = inputs.shape
    width = rnn_in.shape[1]
    hidden_width = mlp_gate.shape[1]
    span = recur_gate.shape[0] * dp
    features = part * mp
    step = count // CHUNKS
    spot = lax.axis_index("mp") * part

    def cut(values):
        return [values[c * step : (c + 1) * step] for c in range(CHUNKS)]

    def mine(values):
        return lax.dynamic_slice_in_dim(values, spot, part, values.ndim - 1)

    in_shard = jnp.concatenate([rnn_in, branch_gate], axis=1)
    out_shard = rnn_out.T
    gates_shard = jnp.concatenate([recur_gate, input_gate], axis=1)
    gate, up, down = mlp_gate, mlp_up, mlp_down.T
    if dp == 8:
        gates_shard = jnp.pad(gates_shard, ((0, 32 - span // 8), (0, 0)))
    else:
        in_shard, out_shard = square_gather(in_shard, "dp", dp), square_gather(out_shard, "dp", dp)
        gate, up, down = [square_gather(w, "dp", dp) for w in (gate, up, down)]
        gates_shard = pair_gather(gates_shard, "dp", dp).reshape(8, span // 8, 2 * width)
        gates_shard = jnp.pad(gates_shard, ((0, 0), (0, 32 - span // 8), (0, 0)))
        gates_shard = gates_shard.reshape(256, 2 * width)

    mask, live = make_masks(lengths[0], count)
    mask_tail = jnp.concatenate([mask, jnp.zeros((8, LANES), F32)], axis=0)
    tail_masks = [mask_tail[c * step : (c + 1) * step + 8] for c in range(CHUNKS)]
    live = jnp.broadcast_to(live[:, None], (count, LANES)).astype(F32)
    w_in, w_out, w_gate, dense, normed, both, conv, r, i, state, mixed, s1 = head(
        dp, mp, 4, inputs, gains, rnn_params, mask, in_shard, out_shard, gate, gates_shard, span
    )
    (
        output, gm, gbo, local, hidden, pulled, normed2, grad_y, grad_gate, grad_up, gain2,
    ) = middle(
        dp, mp, 4, mixed, inputs, cotangent, live, gains, mine(gains), w_out,
        w_gate, up, down,
    )
    gain2 = jnp.sum(gain2, axis=0, keepdims=True)
    if dp == 8:
        rows = span // dp
        input_grad, grad_down, grad_out, grad_in, grad_gates, small = tail(
            mp, 4, span, (gm, both, conv, r, i, state), mask_tail, rnn_params, dense, w_in, normed,
            grad_y, hidden, gbo, mixed, s1, inputs, local, gains, mine(gains), gain2,
        )
        grad_gates = grad_gates[:rows]
        grad_gains, grad_params = small[0:2], small[8:16, :width]
    else:
        blank = jnp.zeros((8, width), F32)
        back, tail_rows = blank, blank
        pulls, rates, dots = [None] * CHUNKS, [None] * CHUNKS, [None] * CHUNKS
        params_total = 0.0
        gms, boths = cut(gm), cut(both)
        saves = list(zip(cut(conv), cut(r), cut(i), cut(state)))
        for c in reversed(range(CHUNKS)):
            low = c * step
            halo = blank if c == 0 else both[low - 8 : low, :width]
            start = blank if c == 0 else state[low - 8 : low]
            pull, rate, dparams, back, tail_rows, dot = rnn_backward(
                gms[c], boths[c], halo, start, saves[c], tail_masks[c], dense, rnn_params,
                back, tail_rows,
            )
            params_total = params_total + dparams
            pulls[c], rates[c], dots[c] = pull, rate, dot
        pull = jnp.concatenate(pulls)
        dots = jnp.concatenate(dots)
        grad_gates = diagonal_blocks(inner_rows(conv.astype(BF16), jnp.concatenate(rates)), span)

        parts = []
        gain1 = 0.0
        norms, s1 = cut(normed), s1[:, 0:1]
        for c in range(CHUNKS):
            gn1_part = inner_cols(pulls[c], w_in).astype(BF16)
            gain1 = gain1 + jnp.sum(gn1_part.astype(F32) * norms[c].astype(F32), axis=0)
            parts.append(line_scatter(gn1_part, "mp", mp))
        dot = line_sum(dots[:, 0].reshape(8, -1), "mp", mp).reshape(-1, 1)
        input_grad = (
            local + s1 * (jnp.concatenate(parts) * mine(gains[0]))
            - inputs.astype(F32) * (s1 * s1 * dot / features)
        ).astype(BF16)
        grad_both = square_scatter(inner_rows(normed2, pulled).astype(BF16), "dp", dp)
        grad_gate, grad_up = grad_both[:, :hidden_width], grad_both[:, hidden_width:]
        grad_down = square_scatter(inner_rows(grad_y, hidden).astype(BF16), "dp", dp)
        grad_out = square_scatter(inner_rows(gbo, mixed).astype(BF16), "dp", dp)
        grad_in = square_scatter(inner_rows(normed, pull).astype(BF16), "dp", dp)
        grad_gates = pair_scatter(grad_gates, "dp", dp)
        grad_params = line_sum(params_total, "dp", dp)
        both_gains = jnp.concatenate([(gain1 / gains[0])[None], gain2])
        both_gains = line_sum(both_gains, "dp", dp)
        grad_gains = jnp.concatenate([line_sum(both_gains[:1], "mp", mp), both_gains[1:]])
    return (
        output,
        input_grad,
        grad_gains,
        grad_params,
        grad_in[:, :width],
        grad_in[:, width:],
        grad_gates[:, :width],
        grad_gates[:, width:],
        grad_gate,
        grad_up,
        grad_out.T,
        grad_down.T,
    )


def solution(mesh):
    return jax.shard_map(
        functools.partial(per_device, mesh.shape["dp"], mesh.shape["mp"]),
        mesh=mesh,
        in_specs=(
            P("dp", "mp"),
            P("dp", None),
            P("dp", "mp"),
            P(),
            P(None, "mp"),
            P("dp", "mp"),
            P("dp", "mp"),
            P("dp", "mp"),
            P("dp", "mp"),
            P("dp", "mp"),
            P("dp", "mp"),
            P("mp", "dp"),
            P("mp", "dp"),
        ),
        out_specs=(
            P("dp", "mp"),
            P("dp", "mp"),
            P(),
            P(None, "mp"),
            P("dp", "mp"),
            P("dp", "mp"),
            P("dp", "mp"),
            P("dp", "mp"),
            P("dp", "mp"),
            P("dp", "mp"),
            P("mp", "dp"),
            P("mp", "dp"),
        ),
        check_vma=False,
    )
```

```python
import functools

import jax
import jax.numpy as jnp
from jax import lax
from jax.experimental import pallas as pl
from jax.experimental.pallas import tpu as pltpu
from jax.sharding import PartitionSpec as P

EPS = 1e-06
DECAY_SCALE = 8.0
ROOT_FLOOR = 0.0001
TAPS = 4
LANES = 8
CHUNKS = 1
TILE = 32
F32 = jnp.float32
BF16 = jnp.bfloat16
VMEM_BYTES = 56 * 1024 * 1024


def matmul(left, right):
    return jnp.dot(left, right, preferred_element_type=F32)


def inner_rows(left, right):
    return lax.dot_general(left, right, (((0,), (0,)), ((), ())), preferred_element_type=F32)


def inner_cols(left, right):
    return lax.dot_general(left, right, (((1,), (1,)), ((), ())), preferred_element_type=F32)


def gelu_and_slope(values):
    outer = 0.7978845608028654
    inner = 0.044715
    square = values * values
    bent = jnp.tanh(outer * values * (1.0 + inner * square))
    half = 0.5 * (1.0 + bent)
    slope = half + 0.5 * values * (1.0 - bent * bent) * outer * (1.0 + 3.0 * inner * square)
    return values * half, slope


def gelu(values):
    outer = 0.7978845608028654
    inner = 0.044715
    bent = jnp.tanh(outer * values * (1.0 + inner * values * values))
    return values * (0.5 * (1.0 + bent))


def one_less_exp(values):
    near = -values * (1.0 + 0.5 * values * (1.0 + (values / 3.0) * (1.0 + 0.25 * values)))
    return jnp.where(values > -0.02, near, 1.0 - jnp.exp(values))


def after(value, *earlier):
    return lax.optimization_barrier((value,) + earlier)[0]


def line_gather(mine, axis, size):
    place = lax.axis_index(axis)
    width = mine.shape[1]
    right, left = mine, mine
    rights, lefts = {}, {}
    for step in range(1, size):
        right = lax.ppermute(right, axis, [(i, i + 1) for i in range(step - 1, size - 1)])
        left = lax.ppermute(left, axis, [(i + 1, i) for i in range(size - step)])
        rights[step], lefts[step] = right, left
    whole = jnp.zeros((mine.shape[0], size * width), mine.dtype)
    for step in range(size):
        block = mine if step == 0 else lefts[step] + rights[size - step]
        spot = lax.rem(place + step, size) * width
        whole = lax.dynamic_update_slice_in_dim(whole, block, spot, 1)
    return whole


def line_scatter(part, axis, size):
    place = lax.axis_index(axis)
    width = part.shape[1] // size

    def block(index):
        spot = jnp.clip(index, 0, size - 1) * width
        return lax.dynamic_slice_in_dim(part, spot, width, 1).astype(F32)

    right, left = None, None
    for step in range(1, size):
        going = block(size - step + place)
        if right is not None:
            going = going + right.astype(F32)
        right = lax.ppermute(going.astype(BF16), axis, [(i, i + 1) for i in range(step)])
        going = block(place - (size - step))
        if left is not None:
            going = going + left.astype(F32)
        left = lax.ppermute(
            going.astype(BF16), axis, [(i, i - 1) for i in range(size - step, size)]
        )
    return block(place) + right.astype(F32) + left.astype(F32)


def line_sum(value, axis, size):
    bit = 1
    while bit < size:
        value = value + lax.ppermute(value, axis, [(i, i ^ bit) for i in range(size)])
        bit *= 2
    return value


def pair_gather(mine, axis, size):
    place = lax.axis_index(axis)
    bit = 1
    while bit < size:
        other = lax.ppermute(mine, axis, [(i, i ^ bit) for i in range(size)])
        upper = (place & bit) != 0
        mine = jnp.concatenate(
            [jnp.where(upper, other, mine), jnp.where(upper, mine, other)], axis=0
        )
        bit *= 2
    return mine


def pair_scatter(part, axis, size):
    place = lax.axis_index(axis)
    part = part.astype(F32)
    bit = size // 2
    while bit >= 1:
        upper = (place & bit) != 0
        low, high = jnp.split(part, 2, axis=0)
        going = jnp.where(upper, low, high).astype(BF16)
        came = lax.ppermute(going, axis, [(i, i ^ bit) for i in range(size)])
        part = jnp.where(upper, high, low) + came.astype(F32)
        bit //= 2
    return part


def swap(size, bit):
    return [(i, i ^ bit) for i in range(size)]


def cross(size):
    return [(i, i ^ 4 if i % 2 == 0 else i ^ 2) for i in range(size)]


def square_gather(mine, axis, size):
    if size != 8:
        return pair_gather(mine, axis, size)
    place = lax.axis_index(axis)
    rows = mine.shape[0]
    by_x = lax.ppermute(mine, axis, swap(size, 2))
    by_y = lax.ppermute(mine, axis, swap(size, 4))
    onward = jnp.where((place & 1) == 0, by_x, by_y)
    far = lax.ppermute(onward, axis, cross(size))
    held = {0: mine, 2: by_x, 4: by_y, 6: far}
    for bits in (0, 2, 4, 6):
        held[bits + 1] = lax.ppermute(held[bits], axis, swap(size, 1))
    whole = jnp.zeros((size * rows,) + mine.shape[1:], mine.dtype)
    for bits, block in held.items():
        whole = lax.dynamic_update_slice_in_dim(whole, block, (place ^ bits) * rows, 0)
    return whole


def square_scatter(part, axis, size):
    if size != 8:
        return pair_scatter(part, axis, size)
    place = lax.axis_index(axis)
    core = place & 1
    chip = lax.shift_right_logical(place, 1)
    split = part.reshape(size // 2, 2, part.shape[0] // size, part.shape[1])
    going = lax.dynamic_index_in_dim(split, 1 - core, 1, keepdims=False)
    came = lax.ppermute(going, axis, swap(size, 1))
    kept = lax.dynamic_index_in_dim(split, core, 1, keepdims=False)
    both = (kept.astype(F32) + came.astype(F32)).astype(BF16)

    def pick(index):
        return lax.dynamic_index_in_dim(both, index, 0, keepdims=False)

    far = lax.ppermute(pick(chip ^ 3), axis, cross(size)).astype(F32)
    none = jnp.zeros((), F32)
    to_x = pick(chip ^ 1).astype(F32) + jnp.where(core == 0, far, none)
    to_y = pick(chip ^ 2).astype(F32) + jnp.where(core == 1, far, none)
    by_x = lax.ppermute(to_x.astype(BF16), axis, swap(size, 2))
    by_y = lax.ppermute(to_y.astype(BF16), axis, swap(size, 4))
    return pick(chip).astype(F32) + by_x.astype(F32) + by_y.astype(F32)


def tile_loop(count, body):
    lax.fori_loop(0, count, lambda i, c: (body(i), c)[1], 0)


def rows_at(index, size):
    return pl.ds(pl.multiple_of(index * size, size), size)


def rnn_forward_kernel(
    both_ref, halo_ref, start_ref, mask_ref, gates_ref, params_ref,
    mixed_ref, conv_ref, r_ref, i_ref, state_ref, end_ref,
    padded, high, low,
):
    count, width = conv_ref.shape
    tiles = count // TILE
    padded[0:8, :] = halo_ref[...]
    padded[8:, :] = both_ref[:, 0:width]

    def convolve(t):
        span = padded[pl.ds(pl.multiple_of(t * TILE, TILE), TILE + 8), :]
        mask = mask_ref[rows_at(t, TILE), :]
        conv = params_ref[0:1, :] * span[8:, :] + params_ref[TAPS : TAPS + 1, :]
        for k in range(1, TAPS):
            moved = span[8 - k : 8 - k + TILE, :]
            conv = conv + params_ref[k : k + 1, :] * (moved * mask[:, k : k + 1])
        conv_ref[rows_at(t, TILE), :] = conv
        top = conv.astype(BF16)
        high[rows_at(t, TILE), :] = top
        low[rows_at(t, TILE), :] = (conv - top.astype(F32)).astype(BF16)

    tile_loop(tiles, convolve)

    block = min(256, count)

    def gate(t):
        rows = rows_at(t, block)
        weights = gates_ref[...]
        both = jnp.dot(high[rows, :], weights, preferred_element_type=F32)
        both = both + jnp.dot(low[rows, :], weights, preferred_element_type=F32)
        r_ref[rows, :] = both[:, 0:width]
        i_ref[rows, :] = both[:, width:]

    tile_loop(count // block, gate)

    strength = DECAY_SCALE * jax.nn.softplus(-params_ref[TAPS + 3 : TAPS + 4, :])

    place = lax.broadcasted_iota(jnp.int32, (8, width), 0)

    def advance(t, carry):
        rows = rows_at(t, TILE)
        keep = mask_ref[rows, :][:, 0:1]
        r = jax.nn.sigmoid(r_ref[rows, :] + params_ref[TAPS + 1 : TAPS + 2, :])
        i = jax.nn.sigmoid(i_ref[rows, :] + params_ref[TAPS + 2 : TAPS + 3, :])
        log_a = -strength * r
        scale = jnp.sqrt(jnp.maximum(one_less_exp(2.0 * log_a), ROOT_FLOOR))
        scale = jnp.where(keep > 0.0, scale, 1.0)
        decay = jnp.exp(log_a) * keep
        drive = scale * i * conv_ref[rows, :]
        r_ref[rows, :] = r
        i_ref[rows, :] = i
        states = []
        for g in range(0, TILE, 8):
            a, held = decay[g : g + 8, :], drive[g : g + 8, :]
            for s in (1, 2, 4):
                inside = place >= s
                held = held + a * jnp.where(inside, pltpu.roll(held, s, 0), 0.0)
                a = a * jnp.where(inside, pltpu.roll(a, s, 0), 1.0)
            held = held + a * carry
            carry = jnp.broadcast_to(held[7:8, :], (8, width))
            states.append(held)
        state = jnp.concatenate(states, axis=0)
        state_ref[rows, :] = state
        mixed_ref[rows, :] = (state * gelu(both_ref[rows, width:])).astype(BF16)
        return carry

    carry = jnp.broadcast_to(start_ref[0:1, :], (8, width))
    end_ref[...] = lax.fori_loop(0, tiles, advance, carry)


def rnn_forward(both, halo, start, mask, gates, params):
    count, width = both.shape[0], both.shape[1] // 2
    full = jax.ShapeDtypeStruct((count, width), F32)
    return pl.pallas_call(
        rnn_forward_kernel,
        out_shape=(
            jax.ShapeDtypeStruct((count, width), BF16),
            full, full, full, full,
            jax.ShapeDtypeStruct((8, width), F32),
        ),
        scratch_shapes=[
            pltpu.VMEM((count + 8, width), F32),
            pltpu.VMEM((count, width), BF16),
            pltpu.VMEM((count, width), BF16),
        ],
        compiler_params=pltpu.CompilerParams(vmem_limit_bytes=VMEM_BYTES),
        cost_estimate=pl.CostEstimate(
            flops=4 * count * width * 2 * width, bytes_accessed=count * width * 30,
            transcendentals=count * width * 6,
        ),
        name="rnn_forward",
    )(both, halo, start, mask, gates, params)


def rnn_backward_kernel(
    gm_ref, both_ref, halo_ref, start_ref, conv_ref, r_ref, i_ref, state_ref, mask_ref,
    gates_ref, params_ref, back_ref, tail_ref,
    grads_ref, rates_ref, dparams_ref, back_out_ref, tail_out_ref, dots_ref,
    padded, before, dconv, sums,
):
    count, width = conv_ref.shape
    tiles = count // TILE
    padded[0:8, :] = halo_ref[...]
    padded[8:, :] = both_ref[:, 0:width]
    before[0:8, :] = start_ref[...]
    before[8:, :] = state_ref[...]
    strength = DECAY_SCALE * jax.nn.softplus(-params_ref[TAPS + 3 : TAPS + 4, :])

    sums[...] = jnp.zeros_like(sums)
    place = lax.broadcasted_iota(jnp.int32, (8, width), 0)

    def fold(values):
        return jnp.sum(values.reshape(-1, 8, width), axis=0)

    def chain(t, carry):
        later, later_decay = carry
        base = pl.multiple_of((tiles - 1 - t) * TILE, TILE)
        rows = pl.ds(base, TILE)
        keep = mask_ref[rows, :][:, 0:1]
        gm = gm_ref[rows, :]
        value, slope = gelu_and_slope(both_ref[rows, width:])
        grads_ref[rows, width:] = (gm * state_ref[rows, :] * slope).astype(BF16)
        given = gm * value
        r, i, conv = r_ref[rows, :], i_ref[rows, :], conv_ref[rows, :]
        fall = jnp.exp(-strength * r) * keep
        adjoints = []
        for g in reversed(range(0, TILE, 8)):
            a = fall[g : g + 8, :]
            ahead = jnp.where(place == 7, later_decay, pltpu.roll(a, 7, 0))
            held = given[g : g + 8, :]
            for s in (1, 2, 4):
                inside = place < 8 - s
                held = held + ahead * jnp.where(inside, pltpu.roll(held, 8 - s, 0), 0.0)
                ahead = ahead * jnp.where(inside, pltpu.roll(ahead, 8 - s, 0), 1.0)
            held = held + ahead * later
            later = jnp.broadcast_to(held[0:1, :], (8, width))
            later_decay = jnp.broadcast_to(a[0:1, :], (8, width))
            adjoints.append(held)
        a = jnp.concatenate(adjoints[::-1], axis=0)
        prior = before[pl.ds(base, TILE + 8), :][7 : 7 + TILE, :]
        room = one_less_exp(-2.0 * strength * r)
        bound = jnp.maximum(room, ROOT_FLOOR)
        inverse = lax.rsqrt(bound)
        scale = jnp.where(keep > 0.0, bound * inverse, 1.0)
        open_ = jnp.where(room > ROOT_FLOOR, inverse, 0.0)
        driven = a * i
        dlog = fall * (a * prior - fall * driven * conv * open_)
        common = a * scale
        drec = dlog * (-strength) * r * (1.0 - r)
        dinp = common * conv * i * (1.0 - i)
        rates_ref[rows, 0:width] = drec.astype(BF16)
        rates_ref[rows, width:] = dinp.astype(BF16)
        dconv[rows, :] = common * i
        sums[5] += fold(drec)
        sums[6] += fold(dinp)
        sums[7] += fold(dlog * r)
        return later, later_decay

    later = jnp.broadcast_to(back_ref[0:1, :], (8, width))
    later, later_decay = lax.fori_loop(
        0, tiles, chain, (later, jnp.ones((8, width), F32))
    )
    back_out_ref[...] = later * later_decay

    block = min(256, count)

    def spread(t):
        rows = rows_at(t, block)
        dconv[rows, :] += lax.dot_general(
            rates_ref[rows, :], gates_ref[...], (((1,), (1,)), ((), ())),
            preferred_element_type=F32,
        )

    tile_loop(count // block, spread)
    dconv[count:, :] = tail_ref[...]
    tail_out_ref[...] = dconv[0:8, :]

    def unconvolve(t):
        base = pl.multiple_of(t * TILE, TILE)
        rows = pl.ds(base, TILE)
        span = dconv[pl.ds(base, TILE + 8), :]
        mask = mask_ref[pl.ds(base, TILE + 8), :]
        source = padded[pl.ds(base, TILE + 8), :]
        here = span[0:TILE, :]
        out = params_ref[0:1, :] * here
        sums[0] += fold(here * source[8:, :])
        sums[4] += fold(here)
        for k in range(1, TAPS):
            kept = span * mask[:, k : k + 1]
            out = out + params_ref[k : k + 1, :] * kept[k : k + TILE, :]
            sums[k] += fold(kept[0:TILE, :] * source[8 - k : 8 - k + TILE, :])
        grads_ref[rows, 0:width] = out.astype(BF16)
        dot = jnp.sum(
            out * source[8:, :] + grads_ref[rows, width:].astype(F32) * both_ref[rows, width:],
            axis=1, keepdims=True,
        )
        dots_ref[rows, :] = jnp.broadcast_to(dot, (TILE, 128))

    tile_loop(tiles, unconvolve)
    for k in range(8):
        dparams_ref[k : k + 1, :] = jnp.sum(sums[k], axis=0, keepdims=True)
    dparams_ref[TAPS + 3 : TAPS + 4, :] = (
        DECAY_SCALE
        * jax.nn.sigmoid(-params_ref[TAPS + 3 : TAPS + 4, :])
        * jnp.sum(sums[TAPS + 3], axis=0, keepdims=True)
    )


def rnn_backward(gm, both, halo, start, saved, mask, gates, params, back, tail):
    conv, r, i, state = saved
    count, width = conv.shape
    return pl.pallas_call(
        rnn_backward_kernel,
        out_shape=(
            jax.ShapeDtypeStruct((count, 2 * width), BF16),
            jax.ShapeDtypeStruct((count, 2 * width), BF16),
            jax.ShapeDtypeStruct((8, width), F32),
            jax.ShapeDtypeStruct((8, width), F32),
            jax.ShapeDtypeStruct((8, width), F32),
            jax.ShapeDtypeStruct((count, 128), F32),
        ),
        scratch_shapes=[
            pltpu.VMEM((count + 8, width), F32),
            pltpu.VMEM((count + 8, width), F32),
            pltpu.VMEM((count + 8, width), F32),
            pltpu.VMEM((8, 8, width), F32),
        ],
        compiler_params=pltpu.CompilerParams(vmem_limit_bytes=VMEM_BYTES),
        cost_estimate=pl.CostEstimate(
            flops=2 * count * width * 2 * width, bytes_accessed=count * width * 36,
            transcendentals=count * width * 6,
        ),
        name="rnn_backward",
    )(gm, both, halo, start, conv, r, i, state, mask, gates, params, back, tail)


MESH = pl.DeviceIdType.MESH


class Spread:
    def __init__(self, place, size, blocks, sent, came):
        self.place, self.size = place, size
        self.blocks, self.sent, self.came = blocks, sent, came

    def copy(self, slot, j, way, k):
        ref = self.blocks.at[slot, j]
        return pltpu.make_async_remote_copy(
            src_ref=ref, dst_ref=ref, send_sem=self.sent.at[slot, k],
            recv_sem=self.came.at[slot, j], device_id={"mp": self.place + way},
            device_id_type=MESH,
        )

    def moves(self, s):
        z, n = self.place, self.size
        return (
            ((z - s >= 0) & (z < n - 1), z - s, 1, 2 * s),
            ((z + s <= n - 1) & (z > 0), z + s, -1, 2 * s + 1),
        )

    def step(self, slot, s):
        for valid, j, way, k in self.moves(s):

            @pl.when(valid)
            def _(j=j, way=way, k=k):
                copy = self.copy(slot, j, way, k)
                if s > 0:
                    copy.wait_recv()
                copy.start()

    def finish(self, slot):
        z, n = self.place, self.size

        @pl.when(z == 0)
        def _():
            for j in range(1, n):
                self.copy(slot, j, 1, 0).wait_recv()

        @pl.when(z == n - 1)
        def _():
            for j in range(n - 1):
                self.copy(slot, j, -1, 0).wait_recv()

    def drain(self, slot):
        for s in range(self.size - 1):
            for valid, j, way, k in self.moves(s):

                @pl.when(valid)
                def _(j=j, way=way, k=k):
                    self.copy(slot, j, way, k).wait_send()


class Fold:
    def __init__(self, place, size, parts, rights, lefts, sent, came_right, came_left):
        self.place, self.size = place, size
        self.parts, self.rights, self.lefts = parts, rights, lefts
        self.sent, self.came_right, self.came_left = sent, came_right, came_left

    def right(self, slot, j, k):
        return pltpu.make_async_remote_copy(
            src_ref=self.parts.at[slot, j], dst_ref=self.rights.at[slot, k],
            send_sem=self.sent.at[slot, j], recv_sem=self.came_right.at[slot, k],
            device_id={"mp": self.place + 1}, device_id_type=MESH,
        )

    def left(self, slot, j, k):
        return pltpu.make_async_remote_copy(
            src_ref=self.parts.at[slot, j], dst_ref=self.lefts.at[slot, k],
            send_sem=self.sent.at[slot, j], recv_sem=self.came_left.at[slot, k],
            device_id={"mp": self.place - 1}, device_id_type=MESH,
        )

    def clear(self):
        for slot in range(self.parts.shape[0]):
            last = self.size - 2
            blank = jnp.zeros(self.rights.shape[2:], BF16)
            self.rights[slot, last] = blank
            self.lefts[slot, last] = blank

    def start(self, slot):
        z, n = self.place, self.size

        @pl.when(z == 0)
        def _():
            for j in reversed(range(1, n)):
                self.right(slot, j, n - 1 - j).start()

        @pl.when(z == n - 1)
        def _():
            for j in range(n - 1):
                self.left(slot, j, j).start()

    def step(self, slot, s):
        z, n = self.place, self.size
        back = n - 1 - z

        @pl.when((z >= 1) & (z <= n - 2) & (s >= z))
        def _():
            j = n - 1 + z - s
            self.right(slot, j, s - 1).wait_recv()
            self.add(slot, j, self.rights, s - 1)
            self.right(slot, j, s).start()

        @pl.when((back >= 1) & (back <= n - 2) & (s >= back))
        def _():
            j = s - back
            self.left(slot, j, s - 1).wait_recv()
            self.add(slot, j, self.lefts, s - 1)
            self.left(slot, j, s).start()

    def add(self, slot, j, came, k):
        self.parts[slot, j] = (
            self.parts[slot, j].astype(F32) + came[slot, k].astype(F32)
        ).astype(BF16)

    def finish(self, slot):
        z, n = self.place, self.size

        @pl.when(z >= 1)
        def _():
            self.right(slot, z, n - 2).wait_recv()

        @pl.when(z <= n - 2)
        def _():
            self.left(slot, z, n - 2).wait_recv()

    def total(self, slot, rows):
        z, n = self.place, self.size
        return (
            self.parts[slot, z, rows, :].astype(F32)
            + self.rights[slot, n - 2, rows, :].astype(F32)
            + self.lefts[slot, n - 2, rows, :].astype(F32)
        )

    def drain(self, slot):
        for j in range(self.size):

            @pl.when(j != self.place)
            def _(j=j):
                self.right(slot, j, 0).wait_send()


def partners(d):
    core, x, y = lax.rem(d, 2), lax.rem(lax.div(d, 2), 2), lax.div(d, 4)
    return core, d + 1 - 2 * core, d + 2 - 4 * x, d + 4 - 8 * y


class Square:
    def __init__(self, d, shard, whole, sent, came, own):
        self.d, self.shard, self.whole = d, shard, whole
        self.sent, self.came, self.own = sent, came, own
        self.core, self.by_core, self.by_x, self.by_y = partners(d)

    def rows(self, d):
        count = self.shard.shape[0]
        return self.whole.at[pl.ds(pl.multiple_of(d * count, count), count), :]

    def copy(self, src, origin, target, sent, came):
        return pltpu.make_async_remote_copy(
            src_ref=src, dst_ref=self.rows(origin), send_sem=self.sent.at[sent],
            recv_sem=self.came.at[came], device_id={"dp": target}, device_id_type=MESH,
        )

    def local(self):
        return pltpu.make_async_copy(self.shard, self.rows(self.d), self.own)

    def far(self):
        return partners(self.by_x)[3]

    def first(self):
        return (
            self.copy(self.shard, self.d, self.by_x, 0, 2),
            self.copy(self.shard, self.d, self.by_y, 1, 4),
            self.copy(self.shard, self.d, self.by_core, 2, 1),
        )

    def start(self):
        for copy in self.first():
            copy.start()
        self.local().start()

    def step_one(self):
        x_rows, y_rows = self.rows(self.by_x), self.rows(self.by_y)
        by_x = self.copy(x_rows, self.by_x, self.by_core, 3, 2)
        by_y = self.copy(y_rows, self.by_y, self.by_core, 4, 4)
        by_x.wait_recv()

        @pl.when(self.core == 0)
        def _():
            self.copy(x_rows, self.by_x, self.by_y, 5, 6).start()

        self.copy(x_rows, self.by_x, self.by_core, 3, 3).start()
        by_y.wait_recv()

        @pl.when(self.core == 1)
        def _():
            self.copy(y_rows, self.by_y, self.by_x, 5, 6).start()

        self.copy(y_rows, self.by_y, self.by_core, 4, 5).start()

    def step_two(self):
        far = self.far()
        rows = self.rows(far)
        self.copy(rows, far, self.by_core, 6, 6).wait_recv()
        self.copy(rows, far, self.by_core, 6, 7).start()

    def finish(self):
        for k in (1, 3, 5, 7):
            self.copy(self.shard, self.d, self.by_core, 0, k).wait_recv()
        self.local().wait()

    def drain(self):
        for k in range(7):
            self.copy(self.shard, self.d, self.by_core, k, 0).wait_send()


class Scatter:
    def __init__(self, d, count, compute, held, far, first, second, sent, came):
        self.d, self.count, self.compute = d, count, compute
        self.held, self.far_in, self.first_in, self.second_in = held, far, first, second
        self.sent, self.came = sent, came
        self.core, self.by_core, by_x, by_y = partners(d)
        even = self.core == 0
        self.first = jnp.where(even, by_y, by_x)
        self.second = jnp.where(even, by_x, by_y)
        self.first_at, self.second_at = 2 - self.core, 1 + self.core
        other = partners(self.by_core)
        self.away = (self.by_core, other[2], other[3], partners(other[2])[3])
        self.distant = partners(by_x)[3]

    def owners(self):
        return [self.away[k] for k in (3, 1, 2, 0)] + [
            self.distant, self.first, self.d, self.second
        ]

    def copy(self, src, dst, target, sent, came):
        return pltpu.make_async_remote_copy(
            src_ref=src, dst_ref=dst, send_sem=self.sent.at[sent], recv_sem=self.came.at[came],
            device_id={"dp": target}, device_id_type=MESH,
        )

    def to_core(self, buffer, k):
        return self.copy(buffer, self.held(k), self.by_core, k, k)

    def to_far(self):
        return self.copy(self.held(3), self.far_in, self.first, 4, 4)

    def to_first(self):
        return self.copy(self.held(self.first_at), self.first_in, self.first, 5, 5)

    def to_second(self):
        return self.copy(self.held(self.second_at), self.second_in, self.second, 6, 6)

    def far_core(self, buffers, sending):
        for slot, k in enumerate((3, 1, 2, 0)):
            if sending[slot] is not None:
                sending[slot].wait_send()
            self.compute(self.away[k], buffers[slot], False)
            copy = self.to_core(buffers[slot], k)
            copy.start()
            sending[slot] = copy

    def add_block(self, k, came, owner):
        self.copy(self.held(k), self.held(k), self.by_core, k, came).wait_recv()
        self.compute(owner, self.held(k), True)

    def near_core(self):
        self.add_block(3, 3, self.distant)
        self.to_far().start()
        self.add_block(self.first_at, self.first_at, self.first)
        self.to_first().start()
        self.add_block(0, 0, self.d)
        self.add_block(self.second_at, self.second_at, self.second)

    def onward(self):
        self.to_far().wait_recv()
        held = self.held(self.second_at)

        def body(t):
            rows = rows_at(t, 16)
            held[rows, :] = (
                held[rows, :].astype(F32) + self.far_in[rows, :].astype(F32)
            ).astype(BF16)

        tile_loop(self.count // 16, body)
        self.to_second().start()

    def finish(self, target):
        self.to_first().wait_recv()
        self.to_second().wait_recv()
        held = self.held(0)

        def body(t):
            rows = rows_at(t, 16)
            target[rows, :] = (
                held[rows, :].astype(F32)
                + self.first_in[rows, :].astype(F32)
                + self.second_in[rows, :].astype(F32)
            )

        tile_loop(self.count // 16, body)

    def drain(self):
        self.to_far().wait_send()
        self.to_first().wait_send()
        self.to_second().wait_send()


def head_kernel(dp, mp, names, *refs):
    ref = dict(zip(names, refs))
    blocks, w_in, norm, both = ref["blocks"], ref["w_in_here"], ref["norm"], ref["both_here"]
    chunks, _, step, part = blocks.shape
    features, width = part * mp, ref["mixed_here"].shape[2]
    z, d = lax.axis_index("mp"), lax.axis_index("dp")
    square = dp == 8
    gather = Spread(z, mp, blocks, ref["spread_sent"], ref["spread_came"])

    barrier = pltpu.get_barrier_semaphore()

    @pl.when(z > 0)
    def _():
        pl.semaphore_signal(barrier, inc=1, device_id={"mp": z - 1}, device_id_type=MESH)

    @pl.when(z < mp - 1)
    def _():
        pl.semaphore_signal(barrier, inc=1, device_id={"mp": z + 1}, device_id_type=MESH)

    count = jnp.where((z > 0) & (z < mp - 1), 2, 1)
    if square:
        for other in partners(d)[1:]:
            pl.semaphore_signal(barrier, inc=1, device_id={"dp": other}, device_id_type=MESH)
        count = count + 3

    def chunk_rows(c):
        return pl.ds(c * step, step)

    def own_block(c):
        return pltpu.make_async_copy(
            ref["x"].at[chunk_rows(c), :], blocks.at[c, z], ref["load_sem"].at[c]
        )

    for c in range(chunks):
        own_block(c).start()
    pl.semaphore_wait(barrier, count)

    wholes = (
        ("gates_shard", ref["gates_here"]), ("in_shard", w_in), ("out_shard", ref["w_out"]),
        ("gate_shard", ref["w_gate"]),
    )
    if square:
        squares = [
            Square(
                d, ref[name], whole, ref["square_sent"].at[k], ref["square_came"].at[k],
                ref["square_own"].at[k],
            )
            for k, (name, whole) in enumerate(wholes)
        ]
        for item in squares[:2]:
            item.start()
    else:
        loads = [
            pltpu.make_async_copy(ref[name], whole, ref["square_own"].at[k])
            for k, (name, whole) in enumerate(wholes)
        ]
        for item in loads:
            item.start()

    def begin(c):
        own_block(c).wait()
        gather.step(c, 0)

    begin(0)
    if chunks > 1:
        begin(1)

    def expand():
        span = ref["gates_flat"].shape[0]
        rows = span // 8
        for k in range(8):
            ref["gates_flat"][k * rows : (k + 1) * rows, :] = ref["gates_here"][
                k * 32 : k * 32 + 32, :
            ].astype(F32)[0:rows, :]
        column = lax.broadcasted_iota(jnp.int32, (span, 2 * width), 1)
        column = jnp.where(column >= width, column - width, column)
        for b in range(width // span):
            inside = (column >= b * span) & (column < (b + 1) * span)
            ref["dense_here"][b * span : (b + 1) * span, :] = jnp.where(
                inside, ref["gates_flat"][...], 0.0
            ).astype(BF16)

    stores = (
        ("norm", "norm"), ("both", "both_here"), ("conv", "conv_here"), ("r", "r_here"),
        ("i", "i_here"), ("state", "state_here"), ("mixed", "mixed_here"), ("s1", "s1_here"),
    )

    def store_all(c):
        return [
            pltpu.make_async_copy(
                ref[near].at[c % 2], ref[far + "_out"].at[chunk_rows(c), :],
                ref["store_sem"].at[c % 2, k],
            )
            for k, (far, near) in enumerate(stores)
        ]

    ref["halo"][...] = jnp.zeros_like(ref["halo"])
    ref["start"][...] = jnp.zeros_like(ref["start"])

    def compute(c):
        slot = c % 2
        if c > 1:
            for copy in store_all(c - 2):
                copy.wait()

        def body(t):
            rows = rows_at(t, TILE)
            values = [blocks[c, j, rows, :].astype(F32) for j in range(mp)]
            total = sum(jnp.sum(v * v, axis=1, keepdims=True) for v in values)
            s1 = lax.rsqrt(total / features + EPS)
            for j in range(mp):
                cols = slice(j * part, (j + 1) * part)
                norm[slot, rows, cols] = (values[j] * s1 * ref["gains"][0:1, cols]).astype(BF16)
            ref["s1_here"][slot, rows, :] = jnp.broadcast_to(s1, (TILE, 128))

        tile_loop(step // TILE, body)
        for k in range(2):
            cols = slice(k * width, (k + 1) * width)
            both[slot, :, cols] = matmul(norm[slot], w_in[:, cols])
        rnn_forward_kernel(
            both.at[slot], ref["halo"], ref["start"], ref["mask"].at[chunk_rows(c), :],
            ref["dense_here"], ref["params"],
            ref["mixed_here"].at[slot], ref["conv_here"].at[slot], ref["r_here"].at[slot],
            ref["i_here"].at[slot], ref["state_here"].at[slot], ref["end"],
            ref["padded"], ref["high"], ref["low"],
        )
        ref["halo"][...] = both[slot, step - 8 :, 0:width]
        ref["start"][...] = ref["end"][...]
        for copy in store_all(c):
            copy.start()

    for s in range(1, mp - 1):
        gather.step(0, s)
        if s == 1 and chunks > 2:
            begin(2)
    if square:
        for item in squares[:2]:
            item.step_one()
        for item in squares[2:]:
            item.start()
        for item in squares[:2]:
            item.step_two()
    gather.finish(0)
    for c in range(chunks):
        if c + 1 < chunks:
            gather.step(c + 1, 1)
        if c == 0:
            if square:
                for item in squares[:2]:
                    item.finish()
            else:
                for item in loads:
                    item.wait()
            expand()
            pass_on = [
                pltpu.make_async_copy(w_in, ref["w_in"], ref["pass_sem"].at[0]),
                pltpu.make_async_copy(ref["dense_here"], ref["dense"], ref["pass_sem"].at[1]),
            ]
            for copy in pass_on:
                copy.start()
        if c + 3 < chunks:
            begin(c + 3)
        compute(c)
        if square and (c + 1) * 4 == chunks:
            squares[2].step_one()
        if square and (c + 1) * 2 == chunks:
            squares[2].step_two()
            squares[3].step_one()
        if square and (c + 1) * 4 == 3 * chunks:
            squares[3].step_two()
        if c + 1 < chunks:
            for s in range(2, mp - 1):
                gather.step(c + 1, s)
            gather.finish(c + 1)
    if square:
        squares[2].finish()
        squares[3].finish()
        for item in squares:
            item.drain()
    for copy in pass_on:
        copy.wait()
    for c in range(max(0, chunks - 2), chunks):
        for copy in store_all(c):
            copy.wait()
    for c in range(chunks):
        gather.drain(c)


def head(
    dp, mp, chunks, x, gains, params, mask, in_shard, out_shard, gate_shard, gates_shard, span
):
    count, part = x.shape
    features, width = part * mp, params.shape[1]
    step = count // chunks
    dma = pltpu.SemaphoreType.DMA
    any_, vmem = pl.BlockSpec(memory_space=pl.ANY), pl.BlockSpec(memory_space=pltpu.VMEM)
    ins = [
        ("x", x, any_), ("gains", gains, vmem), ("params", params, vmem), ("mask", mask, vmem),
        ("in_shard", in_shard, any_), ("out_shard", out_shard, any_),
        ("gate_shard", gate_shard, any_), ("gates_shard", gates_shard, any_),
    ]
    gate_width = gate_shard.shape[1]
    shape = jax.ShapeDtypeStruct
    outs = [
        ("w_in", shape((features, 2 * width), BF16)), ("w_out", shape((features, width), BF16)),
        ("w_gate", shape((features, gate_width), BF16)), ("dense", shape((width, 2 * width), BF16)), ("norm_out", shape((count, features), BF16)),
        ("both_out", shape((count, 2 * width), F32)), ("conv_out", shape((count, width), F32)),
        ("r_out", shape((count, width), F32)), ("i_out", shape((count, width), F32)),
        ("state_out", shape((count, width), F32)), ("mixed_out", shape((count, width), BF16)),
        ("s1_out", shape((count, 128), F32)),
    ]
    wide = pltpu.VMEM((2, step, width), F32)
    scratch = [
        ("blocks", pltpu.VMEM((chunks, mp, step, part), BF16)),
        ("w_in_here", pltpu.VMEM((features, 2 * width), BF16)),
        ("gates_here", pltpu.VMEM((256, 2 * width), BF16)),
        ("gates_flat", pltpu.VMEM((span, 2 * width), F32)),
        ("dense_here", pltpu.VMEM((width, 2 * width), BF16)),
        ("norm", pltpu.VMEM((2, step, features), BF16)),
        ("both_here", pltpu.VMEM((2, step, 2 * width), F32)),
        ("conv_here", wide), ("r_here", wide), ("i_here", wide), ("state_here", wide),
        ("mixed_here", pltpu.VMEM((2, step, width), BF16)),
        ("s1_here", pltpu.VMEM((2, step, 128), F32)),
        ("halo", pltpu.VMEM((8, width), F32)), ("start", pltpu.VMEM((8, width), F32)),
        ("end", pltpu.VMEM((8, width), F32)),
        ("padded", pltpu.VMEM((step + 8, width), F32)),
        ("high", pltpu.VMEM((step, width), BF16)), ("low", pltpu.VMEM((step, width), BF16)),
        ("spread_sent", dma((chunks, 2 * mp))), ("spread_came", dma((chunks, mp))),
        ("square_sent", dma((4, 8))), ("square_came", dma((4, 8))), ("square_own", dma((4,))),
        ("load_sem", dma((chunks,))), ("store_sem", dma((2, 8))), ("pass_sem", dma((2,))),
    ]
    names = [i[0] for i in ins] + [o[0] for o in outs] + [k[0] for k in scratch]
    return pl.pallas_call(
        functools.partial(head_kernel, dp, mp, tuple(names)),
        in_specs=[i[2] for i in ins],
        out_specs=[any_] * len(outs),
        out_shape=[o[1] for o in outs],
        scratch_shapes=[k[1] for k in scratch],
        compiler_params=pltpu.CompilerParams(
            collective_id=2, has_side_effects=True, vmem_limit_bytes=60 * 1024 * 1024
        ),
        name="head",
    )(*[i[1] for i in ins])


MIDDLE_ORDER = (
    ("d", 0, 0), ("A", 0, 0), ("d", 0, 1), ("d", 1, 0), ("a", 1, 0), ("d", 2, 0), ("a", 2, 0),
    ("d", 0, 2), ("J", 0, 0), ("e", 0, 0), ("A", 0, 1), ("e", 1, 0), ("d", 1, 2), ("e", 2, 0),
    ("d", 3, 0), ("S", 1, 0), ("a", 1, 1), ("a", 2, 1), ("d", 2, 2), ("d", 1, 1), ("d", 0, 3),
    ("e", 3, 0), ("S", 2, 0), ("A", 0, 2), ("d", 2, 1), ("S", 3, 0), ("d", 1, 3), ("J", 0, 1),
    ("e", 0, 1), ("a", 1, 2), ("H", 0, 0), ("a", 2, 2), ("e", 1, 1), ("G", 0, 0), ("O", 0, 0),
    ("c", 1, 0), ("e", 2, 1), ("J", 0, 2), ("d", 2, 3), ("d", 3, 1), ("d", 3, 2), ("e", 3, 1),
    ("e", 0, 2), ("b", 1, 0), ("A", 0, 3), ("c", 2, 0), ("H", 0, 1), ("e", 1, 2), ("K", 0, 0),
    ("G", 0, 1), ("a", 1, 3), ("e", 2, 2), ("b", 2, 0), ("f", 1, 0), ("O", 0, 1), ("e", 3, 2),
    ("a", 2, 3), ("c", 1, 1), ("H", 0, 2), ("f", 2, 0), ("c", 2, 1), ("b", 1, 1), ("J", 0, 3),
    ("d", 3, 3), ("Y", 0, 0), ("B", 0, 0), ("e", 0, 3), ("K", 0, 1), ("b", 2, 1), ("G", 0, 2),
    ("f", 1, 1), ("c", 1, 2), ("e", 1, 3), ("f", 2, 1), ("Y", 0, 1), ("c", 2, 2), ("B", 0, 1),
    ("e", 2, 3), ("K", 0, 2), ("O", 0, 2), ("f", 1, 2), ("e", 3, 3), ("H", 0, 3), ("f", 2, 2),
    ("G", 0, 3), ("b", 1, 2), ("B", 0, 2), ("O", 0, 3), ("c", 1, 3), ("D", 0, 0), ("D", 0, 1),
    ("c", 2, 3), ("W", 0, 0), ("D", 0, 2), ("Z", 0, 0), ("W", 0, 1), ("K", 0, 3), ("D", 0, 3),
    ("W", 0, 2), ("f", 1, 3), ("Z", 0, 1), ("b", 2, 2), ("b", 1, 3), ("W", 0, 3), ("D", 0, 4),
    ("f", 2, 3), ("D", 0, 5), ("W", 0, 4), ("Z", 0, 2), ("W", 0, 5), ("b", 2, 3), ("Y", 0, 2),
    ("Z", 0, 3), ("B", 0, 3), ("Z", 0, 4), ("Y", 0, 3), ("Z", 0, 5),
)


def middle_kernel(dp, mp, chunks, *refs):
    (
        mixed_ref, x_ref, cot_ref, live_ref, gains_ref, wout_ref, gate_ref, up_ref,
        down_ref,
        output_ref, gm_ref, gbo_ref, local_ref, hidden_ref, pulled_ref, norm_ref, grady_ref,
        grad_gate_ref, grad_up_ref, gain_ref,
        w_up, w_down, cots, mids, gn2s, mid_mine, gn2_mine,
        parts1, rights1, lefts1, parts2, rights2, lefts2, parts3, rights3, lefts3,
        norm, hidden, pulled, gbo, gm, local, out,
        spread_sent, spread_came, fold_sent, fold_right, fold_left,
        square_sent, square_came, square_own, load_sem, store_sem,
        stage, free_sem, task_sent, task_came, left_sem, right_sem, stage_sem,
    ) = refs
    step, part = x_ref.shape[0] // chunks, x_ref.shape[1]
    features = part * mp
    hidden_width = w_down.shape[1]
    z, d = lax.axis_index("mp"), lax.axis_index("dp")
    square = dp == 8
    up_half = w_up.at[:, pl.ds(hidden_width, hidden_width)]
    own_cols = pl.ds(pl.multiple_of(z * part, part), part)

    folds = [
        Fold(z, mp, p, r, l, fold_sent.at[k], fold_right.at[k], fold_left.at[k])
        for k, (p, r, l) in enumerate(
            ((parts1, rights1, lefts1), (parts2, rights2, lefts2), (parts3, rights3, lefts3))
        )
    ]
    rs1, rs2, rs3 = folds
    ag2, ag3, ag4 = [
        Spread(z, mp, b, spread_sent.at[k], spread_came.at[k])
        for k, b in enumerate((cots, mids, gn2s))
    ]
    for fold in folds:
        fold.clear()

    barrier = pltpu.get_barrier_semaphore()

    @pl.when(z > 0)
    def _():
        pl.semaphore_signal(barrier, inc=1, device_id={"mp": z - 1}, device_id_type=MESH)

    @pl.when(z < mp - 1)
    def _():
        pl.semaphore_signal(barrier, inc=1, device_id={"mp": z + 1}, device_id_type=MESH)

    count = jnp.where((z > 0) & (z < mp - 1), 2, 1)
    if square:
        for other in partners(d)[1:]:
            pl.semaphore_signal(barrier, inc=1, device_id={"dp": other}, device_id_type=MESH)
        count = count + 3
    pl.semaphore_wait(barrier, count)

    if square:
        squares = [
            Square(
                d, shard, whole, square_sent.at[k], square_came.at[k], square_own.at[k]
            )
            for k, (shard, whole) in enumerate(((up_ref, up_half), (down_ref, w_down)))
        ]
        for item in squares:
            item.start()
    else:
        loads = [
            pltpu.make_async_copy(up_ref, up_half, square_own.at[0]),
            pltpu.make_async_copy(down_ref, w_down, square_own.at[1]),
        ]
        for item in loads:
            item.start()
    load_gate = pltpu.make_async_copy(
        gate_ref, w_up.at[:, pl.ds(0, hidden_width)], square_own.at[2]
    )
    load_gate.start()

    def chunk_rows(c):
        return pl.ds(c * step, step)

    def store(buffer, target, c, k):
        return pltpu.make_async_copy(buffer, target.at[chunk_rows(c), :], store_sem.at[k])

    def own_cot(c):
        return pltpu.make_async_copy(cot_ref.at[chunk_rows(c), :], cots.at[c, z], load_sem.at[c])

    for c in range(chunks):
        own_cot(c).start()

    gain_ref[...] = jnp.zeros_like(gain_ref)
    tiles = step // TILE

    def fill(fold, slot, left, weights):
        def body(j):
            rows = pl.ds(pl.multiple_of(j * part, part), part)
            fold.parts[slot, j] = inner_cols(left, weights[rows, :]).astype(BF16)

        tile_loop(mp, body)

    def branch(c):
        if c > 1:
            rs1.drain(c % 2)
        fill(rs1, c % 2, mixed_ref[chunk_rows(c), :], wout_ref)
        rs1.start(c % 2)

    def join(c):
        rs1.finish(c % 2)

        def body(t):
            rows = rows_at(t, TILE)
            base = pl.ds(pl.multiple_of(c * step + t * TILE, TILE), TILE)
            total = x_ref[base, :].astype(F32) + rs1.total(c % 2, rows)
            mid_mine[c, rows, :] = total
            mids[c, z, rows, :] = total.astype(BF16)

        tile_loop(tiles, body)

    def stats(c, rows):
        blocks = [mids[c, j, rows, :].astype(F32) for j in range(mp)]
        square_sum = sum(jnp.sum(b * b, axis=1, keepdims=True) for b in blocks)
        return blocks, lax.rsqrt(square_sum / features + EPS)

    def block_cols(j):
        return slice(j * part, (j + 1) * part)

    def normalise(c):
        def body(t):
            rows = rows_at(t, TILE)
            base = pl.ds(pl.multiple_of(c * step + t * TILE, TILE), TILE)
            blocks, s2 = stats(c, rows)
            live = live_ref[base, :][:, TAPS : TAPS + 1]
            for j in range(mp):
                norm[rows, block_cols(j)] = (
                    blocks[j] * s2 * gains_ref[1:2, block_cols(j)]
                ).astype(BF16)
                cots[c, j, rows, :] = (cots[c, j, rows, :].astype(F32) * live).astype(BF16)

        tile_loop(tiles, body)

    def grad_y_copies(c):
        return [
            pltpu.make_async_copy(
                cots.at[c, j], grady_ref.at[chunk_rows(c), pl.ds(j * part, part)],
                store_sem.at[8 + j],
            )
            for j in range(mp)
        ]

    def mlp_first(c):
        if c > 0:
            store(norm, norm_ref, c, 0).wait()
            store(hidden, hidden_ref, c, 1).wait()
            store(pulled, pulled_ref, c, 2).wait()
            for copy in grad_y_copies(c - 1):
                copy.wait()
        if c == 0:
            load_gate.wait()
            for item in squares if square else ():
                item.finish()
            for item in () if square else loads:
                item.wait()
        ag2.drain(c)
        normalise(c)
        store(norm, norm_ref, c, 0).start()
        for copy in grad_y_copies(c):
            copy.start()
        size = 256

        def body(t):
            near = pl.ds(pl.multiple_of(t * size, size), size)
            off = pl.ds(pl.multiple_of(hidden_width + t * size, size), size)
            gate = matmul(norm[...], w_up[:, near])
            up = matmul(norm[...], w_up[:, off])
            grad = sum(
                matmul(cots[c, j], w_down[block_cols(j), near]) for j in range(mp)
            )
            value, slope = gelu_and_slope(gate)
            hidden[:, near] = (value * up).astype(BF16)
            pulled[:, near] = (grad * up * slope).astype(BF16)
            pulled[:, off] = (grad * value).astype(BF16)

        tile_loop(hidden_width // size, body)
        store(hidden, hidden_ref, c, 1).start()
        store(pulled, pulled_ref, c, 2).start()

    def mlp_second(c):
        slot = c % 2
        if c > 1:
            rs3.drain(slot)
        fill(rs3, slot, pulled[...], w_up)
        rs3.start(slot)
        if square and c == chunks - 1:
            for item in squares:
                item.drain()
            for k, other in enumerate(partners(d)[1:]):
                pl.semaphore_signal(
                    free_sem.at[k], inc=1, device_id={"dp": other}, device_id_type=MESH
                )

    def mlp_third(c):
        slot = c % 2
        if c > 1:
            rs2.drain(slot)
        fill(rs2, slot, hidden[...], w_down)
        rs2.start(slot)

    def gather_grad(c):
        slot = c % 2
        rs3.finish(slot)

        def body(t):
            rows = rows_at(t, TILE)
            total = rs3.total(slot, rows)
            gn2_mine[slot, rows, :] = total
            gn2s[c, z, rows, :] = total.astype(BF16)

        tile_loop(tiles, body)
        ag4.step(c, 0)

    def norm_back(c):
        slot = c % 2
        ag4.finish(c)
        if c > 0:
            store(gbo, gbo_ref, c, 3).wait()
            store(local, local_ref, c, 4).wait()
            store(gm, gm_ref, c, 5).wait()

        def body(t):
            rows = rows_at(t, TILE)
            blocks, s2 = stats(c, rows)
            grads = [gn2s[c, j, rows, :].astype(F32) for j in range(mp)]
            scaled = [grads[j] * gains_ref[1:2, block_cols(j)] for j in range(mp)]
            mean = (
                sum(jnp.sum(scaled[j] * blocks[j], axis=1, keepdims=True) for j in range(mp))
                / features
            )
            fall = s2 * s2 * s2 * mean
            for j in range(mp):
                grad_y = cots[c, j, rows, :].astype(F32)
                gbo[rows, block_cols(j)] = (
                    grad_y + s2 * scaled[j] - blocks[j] * fall
                ).astype(BF16)
                gain_ref[:, block_cols(j)] += jnp.sum(
                    (grads[j] * (blocks[j] * s2)).reshape(-1, 8, part), axis=0
                )
            local[rows, :] = (
                cots[c, z, rows, :].astype(F32)
                + s2 * (gn2_mine[slot, rows, :] * gains_ref[1:2, own_cols])
                - mid_mine[c, rows, :] * fall
            )

        tile_loop(tiles, body)
        gm[...] = matmul(gbo[...], wout_ref[...])
        store(gbo, gbo_ref, c, 3).start()
        store(local, local_ref, c, 4).start()
        store(gm, gm_ref, c, 5).start()

    def make_output(c):
        rs2.finish(c % 2)
        if c > 0:
            store(out, output_ref, c, 6).wait()

        def body(t):
            rows = rows_at(t, TILE)
            out[rows, :] = (mid_mine[c, rows, :] + rs2.total(c % 2, rows)).astype(BF16)

        tile_loop(tiles, body)
        store(out, output_ref, c, 6).start()

    own = features // 8
    count_tasks = 2 * hidden_width // part
    scatters, sending = [], [None] * 4
    buffers = [rights1.at[i // 2, i % 2] for i in range(4)]
    staged = [None]

    def left_block(i):
        return (cots if i < 2 else mids).at[i % 2]

    def left_copies():
        return [
            pltpu.make_async_copy(
                norm_ref.at[chunk_rows(i), pl.ds(j * part, part)], left_block(i).at[j],
                left_sem.at[i, j],
            )
            for i in range(chunks)
            for j in range(mp)
        ]

    def right_copies(k):
        return [
            pltpu.make_async_copy(
                pulled_ref.at[chunk_rows(i), pl.ds(k * part, part)], parts1.at[k % 2, i],
                right_sem.at[k % 2, i],
            )
            for i in range(chunks)
        ]

    def make_scatter(k):
        def compute(owner, target, add):
            j = lax.div(owner, 2)
            near = pl.ds(pl.multiple_of(lax.rem(owner, 2) * own, own), own)
            value = sum(
                inner_rows(left_block(i)[j, :, near], parts1[k % 2, i]) for i in range(chunks)
            )
            if add:
                value = value + target[...].astype(F32)
            target[...] = value.astype(BF16)

        cols = pl.ds(k * part, part)

        def place(first):
            return w_up.at[pl.ds(first, own), cols]

        def held(i):
            return w_up.at[pl.ds(pl.multiple_of(i * own, own), own), cols]

        return Scatter(
            d, own, compute, held, place(4 * own), place(5 * own), place(6 * own),
            task_sent.at[k], task_came.at[k],
        )

    def weight_first(k):
        if not square:
            return
        if k == 0:
            store(norm, norm_ref, chunks - 1, 0).wait()
            store(pulled, pulled_ref, chunks - 1, 2).wait()
            for slot in range(2):
                rs1.drain(slot)
            for c in range(2):
                ag3.drain(c)
            scatters.extend(make_scatter(i) for i in range(count_tasks))
            for copy in right_copies(0) + left_copies():
                copy.start()
            for i in range(3):
                pl.semaphore_wait(free_sem.at[i], 1)
        if k + 1 < count_tasks:
            for copy in right_copies(k + 1):
                copy.start()
        for copy in right_copies(k) + (left_copies() if k == 0 else []):
            copy.wait()
        scatters[k].far_core(buffers, sending)
        scatters[k].near_core()

    def weight_second(k):
        if square:
            scatters[k].onward()

    def weight_third(k):
        if not square:
            return
        if staged[0] is not None:
            staged[0].wait()
        scatters[k].finish(stage)
        half = count_tasks // 2
        target = grad_gate_ref if k < half else grad_up_ref
        staged[0] = pltpu.make_async_copy(
            stage, target.at[:, pl.ds((k % half) * part, part)], stage_sem
        )
        staged[0].start()

    steps = {
        "A": branch, "J": join, "H": mlp_first, "G": mlp_second, "O": mlp_third,
        "K": gather_grad, "B": norm_back, "Y": make_output, "D": weight_first,
        "W": weight_second, "Z": weight_third,
    }
    moves = {"a": (rs1, 2), "b": (rs2, 2), "c": (rs3, 2), "d": (ag2, 0), "e": (ag3, 0), "f": (ag4, 0)}
    for name, s, c in MIDDLE_ORDER:
        if name == "S":
            if square and s < 3:
                squares[s - 1].step_one()
            if square and s == 3:
                squares[0].step_two()
                squares[1].step_two()
        elif name in steps:
            steps[name](c)
        else:
            line, parity = moves[name]
            if s == mp - 1:
                line.finish(c)
                continue
            if name == "d" and s == 0:
                own_cot(c).wait()
            line.step(c % parity if parity else c, s)

    last = chunks - 1
    for k, (buffer, target) in enumerate(
        (
            (norm, norm_ref), (hidden, hidden_ref), (pulled, pulled_ref), (gbo, gbo_ref),
            (local, local_ref), (gm, gm_ref), (out, output_ref),
        )
    ):
        if not (square and k in (0, 2)):
            store(buffer, target, last, k).wait()
    for copy in grad_y_copies(last):
        copy.wait()
    for c in range(chunks):
        if c > 1 or not square:
            ag3.drain(c)
        ag4.drain(c)
    for slot in range(2):
        for fold in folds[1:] if square else folds:
            fold.drain(slot)
    if square:
        staged[0].wait()
        for copy in sending:
            copy.wait_send()
        for scatter in scatters:
            scatter.drain()


def middle(dp, mp, chunks, mixed, inputs, cotangent, live, gains, w_out, gate, up, down):
    count, part = inputs.shape
    width, hidden_width = mixed.shape[1], down.shape[1]
    step, features = count // chunks, part * mp

    def fold_buffers():
        return [
            pltpu.VMEM((2, mp, step, part), BF16),
            pltpu.VMEM((2, mp - 1, step, part), BF16),
            pltpu.VMEM((2, mp - 1, step, part), BF16),
        ]

    dma = pltpu.SemaphoreType.DMA
    any_, vmem = pl.BlockSpec(memory_space=pl.ANY), pl.BlockSpec(memory_space=pltpu.VMEM)
    return pl.pallas_call(
        functools.partial(middle_kernel, dp, mp, chunks),
        in_specs=[vmem, vmem, any_, vmem, vmem, vmem, any_, any_, any_],
        out_specs=[any_] * 10 + [vmem],
        out_shape=(
            jax.ShapeDtypeStruct((count, part), BF16),
            jax.ShapeDtypeStruct((count, width), F32),
            jax.ShapeDtypeStruct((count, features), BF16),
            jax.ShapeDtypeStruct((count, part), F32),
            jax.ShapeDtypeStruct((count, hidden_width), BF16),
            jax.ShapeDtypeStruct((count, 2 * hidden_width), BF16),
            jax.ShapeDtypeStruct((count, features), BF16),
            jax.ShapeDtypeStruct((count, features), BF16),
            jax.ShapeDtypeStruct((features // 8, hidden_width), F32),
            jax.ShapeDtypeStruct((features // 8, hidden_width), F32),
            jax.ShapeDtypeStruct((8, features), F32),
        ),
        scratch_shapes=[
            pltpu.VMEM((features, 2 * hidden_width), BF16),
            pltpu.VMEM((features, hidden_width), BF16),
            pltpu.VMEM((chunks, mp, step, part), BF16),
            pltpu.VMEM((chunks, mp, step, part), BF16),
            pltpu.VMEM((chunks, mp, step, part), BF16),
            pltpu.VMEM((chunks, step, part), F32),
            pltpu.VMEM((2, step, part), F32),
        ]
        + fold_buffers() + fold_buffers() + fold_buffers()
        + [
            pltpu.VMEM((step, features), BF16),
            pltpu.VMEM((step, hidden_width), BF16),
            pltpu.VMEM((step, 2 * hidden_width), BF16),
            pltpu.VMEM((step, features), BF16),
            pltpu.VMEM((step, width), F32),
            pltpu.VMEM((step, part), F32),
            pltpu.VMEM((step, part), BF16),
            dma((3, chunks, 2 * mp)),
            dma((3, chunks, mp)),
            dma((3, 2, mp)),
            dma((3, 2, mp)),
            dma((3, 2, mp)),
            dma((2, 8)),
            dma((2, 8)),
            dma((3,)),
            dma((chunks,)),
            dma((12,)),
            pltpu.VMEM((features // 8, part), F32),
            pltpu.SemaphoreType.REGULAR((3,)),
            dma((2 * hidden_width // part, 8)),
            dma((2 * hidden_width // part, 8)),
            dma((chunks, mp)),
            dma((2, chunks)),
            dma,
        ],
        compiler_params=pltpu.CompilerParams(
            collective_id=0, has_side_effects=True, vmem_limit_bytes=62 * 1024 * 1024
        ),
        name="middle",
    )(mixed, inputs, cotangent, live, gains, w_out, gate, up, down)


TAIL_ORDER = (
    ("R", 0, 3), ("R", 0, 2), ("D", 0, 0), ("R", 0, 1), ("D", 0, 1), ("a", 0, 3), ("l", 0, 2),
    ("W", 0, 0), ("s", 1, 3), ("s", 1, 2), ("R", 0, 0), ("W", 0, 1), ("s", 2, 3), ("D", 0, 2),
    ("s", 2, 2), ("m", 0, 0), ("l", 0, 3), ("s", 1, 1), ("a", 0, 2), ("g", 0, 0), ("W", 0, 2),
    ("m", 0, 1), ("a", 0, 1), ("a", 0, 0), ("D", 0, 3), ("s", 1, 0), ("D", 0, 4), ("s", 2, 1),
    ("m", 0, 2), ("D", 0, 5), ("D", 0, 6), ("I", 0, 3), ("W", 0, 3), ("s", 2, 0), ("Z", 0, 0),
    ("I", 0, 2), ("W", 0, 4), ("W", 0, 5), ("Z", 0, 1), ("I", 0, 1), ("m", 0, 3), ("W", 0, 6),
    ("Z", 0, 2), ("I", 0, 0), ("m", 0, 4), ("Z", 0, 3), ("Z", 0, 4), ("Z", 0, 5), ("m", 0, 5),
    ("Z", 0, 6),
)


def tail_kernel(mp, tasks, names, *refs):
    ref = dict(zip(names, refs))
    pull, w_in, params = ref["pull"], ref["w_in_here"], ref["params"]
    chunks, _, step, part = ref["parts"].shape
    count, features = chunks * step, part * mp
    own, width = features // 8, params.shape[1]
    z, d = lax.axis_index("mp"), lax.axis_index("dp")
    _, by_core, by_x, by_y = partners(d)
    fold = Fold(
        z, mp, ref["parts"], ref["rights"], ref["lefts"], ref["fold_sent"], ref["fold_right"],
        ref["fold_left"],
    )
    near = z + 1 - 2 * lax.rem(z, 2)
    apart = z + 2 - 4 * lax.div(z, 2)
    own_cols = pl.ds(pl.multiple_of(z * part, part), part)

    def chunk_rows(c):
        return pl.ds(c * step, step)

    def recurrence_copies(c):
        copies = [
            pltpu.make_async_copy(
                ref[name].at[chunk_rows(c), :], ref[name + "_here"], ref["chunk_sem"].at[k]
            )
            for k, name in enumerate(("gm", "both", "conv", "r", "i", "state"))
        ]
        if c > 0:
            rows = pl.ds(c * step - 8, 8)
            copies += [
                pltpu.make_async_copy(
                    ref["both"].at[rows, pl.ds(0, width)], ref["halo"], ref["chunk_sem"].at[6]
                ),
                pltpu.make_async_copy(
                    ref["state"].at[rows, :], ref["start"], ref["chunk_sem"].at[7]
                ),
            ]
        return copies

    def norm_copy(c):
        return pltpu.make_async_copy(
            ref["norm1"].at[chunk_rows(c), :], ref["norm_here"], ref["norm_sem"]
        )

    def left_copy(name):
        return pltpu.make_async_copy(ref[name], ref["lhs"], ref["left_sem"])

    def right_copy(name, first, columns, slot):
        return pltpu.make_async_copy(
            ref[name].at[:, pl.ds(first, columns)], ref["rhs"].at[slot, :, pl.ds(0, columns)],
            ref["right_sem"].at[slot],
        )

    def end_copies(c):
        return [
            pltpu.make_async_copy(
                ref[name].at[chunk_rows(c), :], ref[name + "_here"], ref["end_sem"].at[k]
            )
            for k, name in enumerate(("local", "x", "s1"))
        ]

    whole_copies = [
        pltpu.make_async_copy(ref[name], ref[name + "_here"], ref["whole_sem"].at[k])
        for k, name in enumerate(("dense", "w_in"))
    ]
    last = chunks - 1
    for copy in recurrence_copies(last) + whole_copies:
        copy.start()
    norm_copy(last).start()
    left_copy("grady").start()
    first_rights = [
        right_copy(t[2], t[3], t[4], k) for k, t in enumerate(tasks[:2])
    ]
    for copy in first_rights + end_copies(last):
        copy.start()

    fold.clear()
    barrier = pltpu.get_barrier_semaphore()

    @pl.when(z > 0)
    def _():
        pl.semaphore_signal(barrier, inc=1, device_id={"mp": z - 1}, device_id_type=MESH)

    @pl.when(z < mp - 1)
    def _():
        pl.semaphore_signal(barrier, inc=1, device_id={"mp": z + 1}, device_id_type=MESH)

    pl.semaphore_signal(barrier, inc=1, device_id={"mp": apart}, device_id_type=MESH)
    for other in (by_core, by_x, by_y):
        pl.semaphore_signal(barrier, inc=1, device_id={"dp": other}, device_id_type=MESH)

    for name in ("back", "after", "gain", "dense_sum", "params_sum"):
        ref[name][...] = jnp.zeros_like(ref[name])
    gain = ref["gain"]

    def recur(c):
        for copy in recurrence_copies(c):
            copy.wait()
        if c == 0:
            ref["halo"][...] = jnp.zeros_like(ref["halo"])
            ref["start"][...] = jnp.zeros_like(ref["start"])
        if c == last:
            for copy in whole_copies:
                copy.wait()
        rnn_backward_kernel(
            ref["gm_here"], ref["both_here"], ref["halo"], ref["start"], ref["conv_here"],
            ref["r_here"], ref["i_here"], ref["state_here"],
            ref["mask"].at[pl.ds(c * step, step + 8), :], ref["dense_here"], params,
            ref["back"], ref["after"],
            pull.at[chunk_rows(c), :], ref["rates"], ref["dparams"], ref["back"], ref["after"],
            ref["dots"],
            ref["padded"], ref["before"], ref["dconv"], ref["sums"],
        )
        ref["params_sum"][...] += ref["dparams"][...]
        ref["dense_sum"][...] += inner_rows(ref["conv_here"][...].astype(BF16), ref["rates"][...])
        if c > 0:
            for copy in recurrence_copies(c - 1):
                copy.start()
        for q in range(step // 128):
            turned = jnp.transpose(ref["dots"][q * 128 : (q + 1) * 128, :])
            ref["dots_row"][c, :, q * 128 : (q + 1) * 128] = turned[0:8, :]
        if c == last:
            pl.semaphore_wait(barrier, jnp.where((z > 0) & (z < mp - 1), 6, 5))
        dots_copy(c, 0).start()
        norm_copy(c).wait()

        def body(j):
            rows = pl.ds(pl.multiple_of(j * part, part), part)
            value = inner_cols(pull[chunk_rows(c), :], w_in[rows, :])
            fold.parts[c, j] = value.astype(BF16)
            gain[:, rows] += jnp.sum(
                (value * ref["norm_here"][:, rows].astype(F32)).reshape(-1, 8, part), axis=0
            )

        tile_loop(mp, body)
        fold.start(c)
        if c > 0:
            norm_copy(c - 1).start()

    def dots_copy(c, k):
        return pltpu.make_async_remote_copy(
            src_ref=ref["dots_row"].at[c], dst_ref=ref["dots_in"].at[c, k],
            send_sem=ref["dots_sent"].at[c, k], recv_sem=ref["dots_came"].at[c, k],
            device_id={"mp": near if k == 0 else apart}, device_id_type=MESH,
        )

    def dots_add(c, k):
        dots_copy(c, k).wait()
        ref["dots_row"][c] += ref["dots_in"][c, k]
        if k == 0:
            dots_copy(c, 1).start()

    def input_grad(c):
        dots_add(c, 1)
        for q in range(step // 128):
            row = ref["dots_row"][c, 0:1, q * 128 : (q + 1) * 128]
            ref["dots_col"][q * 128 : (q + 1) * 128, :] = jnp.transpose(
                jnp.broadcast_to(row, (128, 128))
            )
        fold.finish(c)
        for copy in end_copies(c):
            copy.wait()

        def body(t):
            rows = rows_at(t, TILE)
            base = pl.ds(pl.multiple_of(c * step + t * TILE, TILE), TILE)
            s1 = ref["s1_here"][rows, :][:, 0:1]
            dot = ref["dots_col"][rows, :][:, 0:1]
            grad = (
                ref["local_here"][rows, :]
                + s1 * (fold.total(c, rows) * ref["gains"][0:1, own_cols])
                - ref["x_here"][rows, :].astype(F32) * (s1 * s1 * dot * (1.0 / features))
            )
            ref["grad_x"][base, :] = grad.astype(BF16)

        tile_loop(step // TILE, body)
        if c > 0:
            for copy in end_copies(c - 1):
                copy.start()

    sends, store_sem = ref["sends"], ref["store_sem"]
    slots = {k: k % 2 for k, t in enumerate(tasks) if t[2] in ("hidden", "mixed")}

    def build(k):
        _, left, right, first, columns, _ = tasks[k]

        def compute(owner, target, add):
            if left is None:
                rows = pl.ds(pl.multiple_of(owner * 32, 32), 32)
                value = ref["gates"][rows, first : first + columns].astype(F32)
            else:
                near = pl.ds(pl.multiple_of(owner * own, own), own)
                if right == "pull":
                    operand = pull[:, first : first + columns]
                else:
                    operand = ref["rhs"][slots[k], :, 0:columns]
                value = inner_rows(ref["lhs"][:, near], operand)
            if add:
                value = value + target[...].astype(F32)
            target[...] = value.astype(BF16)

        return Scatter(
            d, 32 if left is None else own, compute, ref["held%d" % k].at.__getitem__,
            ref["far%d" % k], ref["first%d" % k], ref["second%d" % k], ref["task_sent"].at[k],
            ref["task_came"].at[k],
        )

    scatters = [build(k) for k in range(len(tasks))]
    sending = [None] * 4

    def far_core(k):
        height, columns = scatters[k].count, tasks[k][4]
        scatters[k].far_core(
            [sends.at[slot, pl.ds(0, height), pl.ds(0, columns)] for slot in range(4)], sending
        )

    stage, stage_wait = ref["stage"], [None, None]

    def finish(k):
        scatter = scatters[k]
        name, columns, column = tasks[k][0], tasks[k][4], tasks[k][5]
        slot = k % 2
        if stage_wait[slot] is not None:
            stage_wait[slot].wait()
        view = stage.at[slot, pl.ds(0, scatter.count), pl.ds(0, columns)]
        scatter.finish(view)
        target = ref["grad_" + name].at[:, pl.ds(column, columns)]
        copy = pltpu.make_async_copy(view, target, store_sem.at[slot])
        copy.start()
        stage_wait[slot] = copy

    small, small_in = ref["small"], ref["small_in"]
    targets = (
        {"dp": by_core}, {"dp": by_x}, {"dp": by_y}, {"mp": near}, {"mp": apart},
    )

    def small_copy(k):
        rows = pl.ds(0, 16 if k < 3 else 8)
        return pltpu.make_async_remote_copy(
            src_ref=small.at[rows, :], dst_ref=small_in.at[k, rows, :],
            send_sem=ref["small_sent"].at[k], recv_sem=ref["small_came"].at[k],
            device_id=targets[k], device_id_type=MESH,
        )

    def small_first():
        small[...] = jnp.zeros_like(small)
        small[0:1, :] = jnp.sum(gain[...], axis=0, keepdims=True) / ref["gains"][0:1, :]
        small[1:2, :] = jnp.sum(ref["gain2"][...], axis=0, keepdims=True) * (1.0 / mp)
        small[8:16, 0:width] = ref["params_sum"][...]
        small_copy(0).start()

    def small_next(k):
        rows = 16 if k < 3 else 8
        small_copy(k).wait()
        small[0:rows, :] += small_in[k, 0:rows, :]
        if k < 4:
            small_copy(k + 1).start()

    def gate_blocks():
        flat, gates = ref["flat"], ref["gates"]
        span = flat.shape[0] - 16
        rows = span // 8
        column = lax.broadcasted_iota(jnp.int32, (span, 2 * width), 1)
        column = jnp.where(column >= width, column - width, column)
        total = jnp.zeros((span, 2 * width), F32)
        for b in range(width // span):
            inside = (column >= b * span) & (column < (b + 1) * span)
            total = total + jnp.where(
                inside, ref["dense_sum"][b * span : (b + 1) * span, :], 0.0
            )
        flat[0:span, :] = total
        flat[span:, :] = jnp.zeros((16, 2 * width), F32)
        for k in range(8):
            gates[k * 32 : (k + 1) * 32, :] = flat[k * rows : k * rows + 32, :].astype(BF16)

    out_right = right_copy("mixed", 0, tasks[2][4], 0)

    def load_next(k):
        left_copy("gbo" if k == 2 else "norm1").start()
        if k == 2:
            out_right.start()

    def weight(k):
        if k == 0:
            for copy in first_rights:
                copy.wait()
            left_copy("grady").wait()
        if k == 2:
            out_right.wait()
        if k in (2, 3):
            left_copy("norm1").wait()
        far_core(k)
        scatters[k].near_core()

    steps = {
        "R": recur, "I": input_grad, "D": weight, "W": lambda k: scatters[k].onward(),
        "Z": finish, "l": load_next, "g": lambda k: gate_blocks(), "a": lambda c: dots_add(c, 0),
        "m": lambda k: small_next(k - 1) if k else small_first(),
    }
    for name, s, c in TAIL_ORDER:
        if name == "s":
            fold.step(c, s)
        else:
            steps[name](c)
    for copy in stage_wait:
        copy.wait()
    for copy in sending:
        copy.wait_send()
    for scatter in scatters:
        scatter.drain()
    for c in range(chunks):
        fold.drain(c)


def tail(mp, chunks, span, rnn, mask, params, dense, w_in, norm1, grady, hidden, gbo, mixed, s1, x,
         local, gains, gain2):
    gm, both, conv, r, i, state = rnn
    count, part = x.shape
    features, width = part * mp, params.shape[1]
    own, step = features // 8, count // chunks
    widths = {
        "down": hidden.shape[1], "out": width, "in": 2 * width, "block": 2 * width,
    }
    heights = {name: 32 if name == "block" else own for name in widths}
    operands = {
        "down": ("grady", "hidden"), "out": ("gbo", "mixed"), "in": ("norm1", "pull"),
        "block": (None, "gates"),
    }
    tasks = []
    for name, columns in widths.items():
        left, right = operands[name]
        pieces = 1 if name == "out" else 2
        size = columns // pieces
        for piece in range(pieces):
            tasks.append((name, left, right, piece * size, size, piece * size))
    widest = max(t[4] for t in tasks)
    dma = pltpu.SemaphoreType.DMA
    any_, vmem = pl.BlockSpec(memory_space=pl.ANY), pl.BlockSpec(memory_space=pltpu.VMEM)
    ins = [
        ("gm", gm, any_), ("both", both, any_), ("conv", conv, any_), ("r", r, any_),
        ("i", i, any_), ("state", state, any_), ("mask", mask, vmem), ("params", params, vmem),
        ("dense", dense, any_), ("w_in", w_in, any_), ("norm1", norm1, any_),
        ("grady", grady, any_), ("hidden", hidden, any_), ("gbo", gbo, any_),
        ("mixed", mixed, any_), ("s1", s1, any_), ("x", x, any_), ("local", local, any_),
        ("gains", gains, vmem), ("gain2", gain2, vmem),
    ]
    shape = jax.ShapeDtypeStruct
    outs = [("grad_x", shape((count, part), BF16), vmem)]
    for name, columns in widths.items():
        outs.append(("grad_" + name, shape((heights[name], columns), F32), any_))
    outs.append(("small", shape((16, features), F32), vmem))
    wide = pltpu.VMEM((step, width), F32)
    tall = pltpu.VMEM((step + 8, width), F32)
    eight = pltpu.VMEM((8, width), F32)
    scratch = [
        ("gm_here", wide), ("both_here", pltpu.VMEM((step, 2 * width), F32)),
        ("conv_here", wide), ("r_here", wide), ("i_here", wide), ("state_here", wide),
        ("halo", eight), ("start", eight), ("back", eight), ("after", eight),
        ("dparams", eight), ("params_sum", eight),
        ("dense_here", pltpu.VMEM(dense.shape, BF16)), ("w_in_here", pltpu.VMEM(w_in.shape, BF16)),
        ("pull", pltpu.VMEM((count, 2 * width), BF16)),
        ("rates", pltpu.VMEM((step, 2 * width), BF16)),
        ("dots", pltpu.VMEM((step, 128), F32)),
        ("padded", tall), ("before", tall), ("dconv", tall), ("sums", pltpu.VMEM((8, 8, width), F32)),
        ("dense_sum", pltpu.VMEM((width, 2 * width), F32)),
        ("flat", pltpu.VMEM((span + 16, 2 * width), F32)),
        ("gates", pltpu.VMEM((256, 2 * width), BF16)),
        ("norm_here", pltpu.VMEM((step, features), BF16)),
        ("lhs", pltpu.VMEM((count, features), BF16)),
        ("rhs", pltpu.VMEM((2, count, widest), BF16)),
        ("local_here", pltpu.VMEM((step, part), F32)), ("x_here", pltpu.VMEM((step, part), BF16)),
        ("s1_here", pltpu.VMEM((step, 128), F32)),
        ("parts", pltpu.VMEM((chunks, mp, step, part), BF16)),
        ("rights", pltpu.VMEM((chunks, mp - 1, step, part), BF16)),
        ("lefts", pltpu.VMEM((chunks, mp - 1, step, part), BF16)),
        ("sends", pltpu.VMEM((4, own, widest), BF16)),
        ("stage", pltpu.VMEM((2, own, widest), F32)),
        ("gain", pltpu.VMEM((8, features), F32)),
        ("dots_row", pltpu.VMEM((chunks, 8, step), F32)),
        ("dots_in", pltpu.VMEM((chunks, 2, 8, step), F32)),
        ("dots_col", pltpu.VMEM((step, 128), F32)),
        ("small_in", pltpu.VMEM((5, 16, features), F32)),
        ("chunk_sem", dma((8,))), ("norm_sem", dma), ("left_sem", dma), ("right_sem", dma((2,))),
        ("end_sem", dma((3,))), ("whole_sem", dma((2,))), ("store_sem", dma((2,))),
        ("fold_sent", dma((chunks, mp))), ("fold_right", dma((chunks, mp))),
        ("fold_left", dma((chunks, mp))),
        ("task_sent", dma((len(tasks), 8))), ("task_came", dma((len(tasks), 8))),
        ("dots_sent", dma((chunks, 2))), ("dots_came", dma((chunks, 2))),
        ("small_sent", dma((5,))), ("small_came", dma((5,))),
    ]
    for k, (name, _, _, _, size, _) in enumerate(tasks):
        rows = heights[name]
        scratch.append(("held%d" % k, pltpu.VMEM((4, rows, size), BF16)))
        for kind in ("far", "first", "second"):
            scratch.append(("%s%d" % (kind, k), pltpu.VMEM((rows, size), BF16)))
    names = [i[0] for i in ins] + [o[0] for o in outs] + [k[0] for k in scratch]
    return pl.pallas_call(
        functools.partial(tail_kernel, mp, tuple(tasks), tuple(names)),
        in_specs=[i[2] for i in ins],
        out_specs=[o[2] for o in outs],
        out_shape=[o[1] for o in outs],
        scratch_shapes=[k[1] for k in scratch],
        compiler_params=pltpu.CompilerParams(
            collective_id=1, has_side_effects=True, vmem_limit_bytes=63 * 1024 * 1024
        ),
        name="tail",
    )(*[i[1] for i in ins])


def make_masks(row_lengths, count):
    ends = jnp.cumsum(row_lengths)
    places = jnp.arange(-TAPS, count, dtype=jnp.int32)
    segment = jnp.sum((places[:, None] >= ends[None, :]).astype(jnp.int32), axis=1)
    segment = jnp.where(places < 0, -1, segment)
    now = segment[TAPS:]
    same = [(segment[TAPS - k : TAPS - k + count] == now).astype(F32) for k in range(1, TAPS)]
    blank = jnp.zeros((count,), F32)
    live = (now < row_lengths.shape[0]).astype(F32)
    columns = [same[0]] + same + [live] + [blank] * (LANES - TAPS - 1)
    return jnp.stack(columns, axis=1)


def dense_gates(gates, width):
    span = gates.shape[0]
    tiled = jnp.tile(gates, (width // span, 1))
    row = lax.broadcasted_iota(jnp.int32, tiled.shape, 0) // span
    column = (lax.broadcasted_iota(jnp.int32, tiled.shape, 1) % width) // span
    return jnp.where(row == column, tiled, jnp.zeros((), tiled.dtype))


def diagonal_blocks(dense, span):
    width = dense.shape[0]
    column = (lax.broadcasted_iota(jnp.int32, (1, 2 * width), 1) % width) // span
    total = jnp.zeros((span, 2 * width), F32)
    for b in range(width // span):
        total = total + jnp.where(column == b, dense[b * span : (b + 1) * span], 0.0)
    return total


def per_device(
    dp, mp,
    inputs, lengths, cotangent, gains, rnn_params, rnn_in, branch_gate, recur_gate, input_gate,
    mlp_gate, mlp_up, rnn_out, mlp_down,
):
    count, part = inputs.shape
    width = rnn_in.shape[1]
    hidden_width = mlp_gate.shape[1]
    span = recur_gate.shape[0] * dp
    features = part * mp
    step = count // CHUNKS
    spot = lax.axis_index("mp") * part

    def cut(values):
        return [values[c * step : (c + 1) * step] for c in range(CHUNKS)]

    def mine(values):
        return lax.dynamic_slice_in_dim(values, spot, part, values.ndim - 1)

    in_shard = jnp.concatenate([rnn_in, branch_gate], axis=1)
    out_shard = rnn_out.T
    gates_shard = jnp.concatenate([recur_gate, input_gate], axis=1)
    gate, up, down = mlp_gate, mlp_up, mlp_down.T
    if dp == 8:
        gates_shard = jnp.pad(gates_shard, ((0, 32 - span // 8), (0, 0)))
    else:
        in_shard, out_shard = square_gather(in_shard, "dp", dp), square_gather(out_shard, "dp", dp)
        gate, up, down = [square_gather(w, "dp", dp) for w in (gate, up, down)]
        gates_shard = pair_gather(gates_shard, "dp", dp).reshape(8, span // 8, 2 * width)
        gates_shard = jnp.pad(gates_shard, ((0, 0), (0, 32 - span // 8), (0, 0)))
        gates_shard = gates_shard.reshape(256, 2 * width)

    mask = make_masks(lengths[0], count)
    mask_tail = jnp.concatenate([mask, jnp.zeros((8, LANES), F32)], axis=0)
    tail_masks = [mask_tail[c * step : (c + 1) * step + 8] for c in range(CHUNKS)]
    w_in, w_out, w_gate, dense, normed, both, conv, r, i, state, mixed, s1 = head(
        dp, mp, 4, inputs, gains, rnn_params, mask, in_shard, out_shard, gate, gates_shard, span
    )
    (
        output, gm, gbo, local, hidden, pulled, normed2, grad_y, grad_gate, grad_up, gain2,
    ) = middle(
        dp, mp, 4, mixed, inputs, cotangent, mask, gains, w_out,
        w_gate, up, down,
    )
    if dp == 8:
        rows = span // dp
        input_grad, grad_down, grad_out, grad_in, grad_gates, small = tail(
            mp, 4, span, (gm, both, conv, r, i, state), mask_tail, rnn_params, dense, w_in, normed,
            grad_y, hidden, gbo, mixed, s1, inputs, local, gains, gain2,
        )
        grad_gates = grad_gates[:rows]
        grad_gains, grad_params = small[0:2], small[8:16, :width]
    else:
        blank = jnp.zeros((8, width), F32)
        back, tail_rows = blank, blank
        pulls, rates, dots = [None] * CHUNKS, [None] * CHUNKS, [None] * CHUNKS
        params_total = 0.0
        gms, boths = cut(gm), cut(both)
        saves = list(zip(cut(conv), cut(r), cut(i), cut(state)))
        for c in reversed(range(CHUNKS)):
            low = c * step
            halo = blank if c == 0 else both[low - 8 : low, :width]
            start = blank if c == 0 else state[low - 8 : low]
            pull, rate, dparams, back, tail_rows, dot = rnn_backward(
                gms[c], boths[c], halo, start, saves[c], tail_masks[c], dense, rnn_params,
                back, tail_rows,
            )
            params_total = params_total + dparams
            pulls[c], rates[c], dots[c] = pull, rate, dot
        pull = jnp.concatenate(pulls)
        dots = jnp.concatenate(dots)
        grad_gates = diagonal_blocks(inner_rows(conv.astype(BF16), jnp.concatenate(rates)), span)

        parts = []
        gain1 = 0.0
        norms, s1 = cut(normed), s1[:, 0:1]
        for c in range(CHUNKS):
            gn1_part = inner_cols(pulls[c], w_in).astype(BF16)
            gain1 = gain1 + jnp.sum(gn1_part.astype(F32) * norms[c].astype(F32), axis=0)
            parts.append(line_scatter(gn1_part, "mp", mp))
        dot = line_sum(dots[:, 0].reshape(8, -1), "mp", mp).reshape(-1, 1)
        input_grad = (
            local + s1 * (jnp.concatenate(parts) * mine(gains[0]))
            - inputs.astype(F32) * (s1 * s1 * dot / features)
        ).astype(BF16)
        grad_both = square_scatter(inner_rows(normed2, pulled).astype(BF16), "dp", dp)
        grad_gate, grad_up = grad_both[:, :hidden_width], grad_both[:, hidden_width:]
        grad_down = square_scatter(inner_rows(grad_y, hidden).astype(BF16), "dp", dp)
        grad_out = square_scatter(inner_rows(gbo, mixed).astype(BF16), "dp", dp)
        grad_in = square_scatter(inner_rows(normed, pull).astype(BF16), "dp", dp)
        grad_gates = pair_scatter(grad_gates, "dp", dp)
        grad_params = line_sum(params_total, "dp", dp)
        gain2 = jnp.sum(gain2, axis=0, keepdims=True)
        both_gains = jnp.concatenate([(gain1 / gains[0])[None], gain2])
        both_gains = line_sum(both_gains, "dp", dp)
        grad_gains = jnp.concatenate([line_sum(both_gains[:1], "mp", mp), both_gains[1:]])
    return (
        output,
        input_grad,
        grad_gains,
        grad_params,
        grad_in[:, :width],
        grad_in[:, width:],
        grad_gates[:, :width],
        grad_gates[:, width:],
        grad_gate,
        grad_up,
        grad_out.T,
        grad_down.T,
    )


def solution(mesh):
    return jax.shard_map(
        functools.partial(per_device, mesh.shape["dp"], mesh.shape["mp"]),
        mesh=mesh,
        in_specs=(
            P("dp", "mp"),
            P("dp", None),
            P("dp", "mp"),
            P(),
            P(None, "mp"),
            P("dp", "mp"),
            P("dp", "mp"),
            P("dp", "mp"),
            P("dp", "mp"),
            P("dp", "mp"),
            P("dp", "mp"),
            P("mp", "dp"),
            P("mp", "dp"),
        ),
        out_specs=(
            P("dp", "mp"),
            P("dp", "mp"),
            P(),
            P(None, "mp"),
            P("dp", "mp"),
            P("dp", "mp"),
            P("dp", "mp"),
            P("dp", "mp"),
            P("dp", "mp"),
            P("dp", "mp"),
            P("mp", "dp"),
            P("mp", "dp"),
        ),
        check_vma=False,
    )
```

```python
import functools

import jax
import jax.numpy as jnp
from jax import lax
from jax.experimental import pallas as pl
from jax.experimental.pallas import tpu as pltpu
from jax.sharding import PartitionSpec as P

EPS = 1e-06
DECAY_SCALE = 8.0
ROOT_FLOOR = 0.0001
TAPS = 4
LANES = 8
CHUNKS = 1
TILE = 32
F32 = jnp.float32
BF16 = jnp.bfloat16
VMEM_BYTES = 56 * 1024 * 1024


def matmul(left, right):
    return jnp.dot(left, right, preferred_element_type=F32)


def inner_rows(left, right):
    return lax.dot_general(left, right, (((0,), (0,)), ((), ())), preferred_element_type=F32)


def inner_cols(left, right):
    return lax.dot_general(left, right, (((1,), (1,)), ((), ())), preferred_element_type=F32)


def gelu_and_slope(values):
    outer = 0.7978845608028654
    inner = 0.044715
    square = values * values
    bent = jnp.tanh(outer * values * (1.0 + inner * square))
    half = 0.5 * (1.0 + bent)
    slope = half + 0.5 * values * (1.0 - bent * bent) * outer * (1.0 + 3.0 * inner * square)
    return values * half, slope


def gelu(values):
    outer = 0.7978845608028654
    inner = 0.044715
    bent = jnp.tanh(outer * values * (1.0 + inner * values * values))
    return values * (0.5 * (1.0 + bent))


def one_less_exp(values):
    near = -values * (1.0 + 0.5 * values * (1.0 + (values / 3.0) * (1.0 + 0.25 * values)))
    return jnp.where(values > -0.02, near, 1.0 - jnp.exp(values))


def after(value, *earlier):
    return lax.optimization_barrier((value,) + earlier)[0]


def line_gather(mine, axis, size):
    place = lax.axis_index(axis)
    width = mine.shape[1]
    right, left = mine, mine
    rights, lefts = {}, {}
    for step in range(1, size):
        right = lax.ppermute(right, axis, [(i, i + 1) for i in range(step - 1, size - 1)])
        left = lax.ppermute(left, axis, [(i + 1, i) for i in range(size - step)])
        rights[step], lefts[step] = right, left
    whole = jnp.zeros((mine.shape[0], size * width), mine.dtype)
    for step in range(size):
        block = mine if step == 0 else lefts[step] + rights[size - step]
        spot = lax.rem(place + step, size) * width
        whole = lax.dynamic_update_slice_in_dim(whole, block, spot, 1)
    return whole


def line_scatter(part, axis, size):
    place = lax.axis_index(axis)
    width = part.shape[1] // size

    def block(index):
        spot = jnp.clip(index, 0, size - 1) * width
        return lax.dynamic_slice_in_dim(part, spot, width, 1).astype(F32)

    right, left = None, None
    for step in range(1, size):
        going = block(size - step + place)
        if right is not None:
            going = going + right.astype(F32)
        right = lax.ppermute(going.astype(BF16), axis, [(i, i + 1) for i in range(step)])
        going = block(place - (size - step))
        if left is not None:
            going = going + left.astype(F32)
        left = lax.ppermute(
            going.astype(BF16), axis, [(i, i - 1) for i in range(size - step, size)]
        )
    return block(place) + right.astype(F32) + left.astype(F32)


def line_sum(value, axis, size):
    bit = 1
    while bit < size:
        value = value + lax.ppermute(value, axis, [(i, i ^ bit) for i in range(size)])
        bit *= 2
    return value


def pair_gather(mine, axis, size):
    place = lax.axis_index(axis)
    bit = 1
    while bit < size:
        other = lax.ppermute(mine, axis, [(i, i ^ bit) for i in range(size)])
        upper = (place & bit) != 0
        mine = jnp.concatenate(
            [jnp.where(upper, other, mine), jnp.where(upper, mine, other)], axis=0
        )
        bit *= 2
    return mine


def pair_scatter(part, axis, size):
    place = lax.axis_index(axis)
    part = part.astype(F32)
    bit = size // 2
    while bit >= 1:
        upper = (place & bit) != 0
        low, high = jnp.split(part, 2, axis=0)
        going = jnp.where(upper, low, high).astype(BF16)
        came = lax.ppermute(going, axis, [(i, i ^ bit) for i in range(size)])
        part = jnp.where(upper, high, low) + came.astype(F32)
        bit //= 2
    return part


def swap(size, bit):
    return [(i, i ^ bit) for i in range(size)]


def cross(size):
    return [(i, i ^ 4 if i % 2 == 0 else i ^ 2) for i in range(size)]


def square_gather(mine, axis, size):
    if size != 8:
        return pair_gather(mine, axis, size)
    place = lax.axis_index(axis)
    rows = mine.shape[0]
    by_x = lax.ppermute(mine, axis, swap(size, 2))
    by_y = lax.ppermute(mine, axis, swap(size, 4))
    onward = jnp.where((place & 1) == 0, by_x, by_y)
    far = lax.ppermute(onward, axis, cross(size))
    held = {0: mine, 2: by_x, 4: by_y, 6: far}
    for bits in (0, 2, 4, 6):
        held[bits + 1] = lax.ppermute(held[bits], axis, swap(size, 1))
    whole = jnp.zeros((size * rows,) + mine.shape[1:], mine.dtype)
    for bits, block in held.items():
        whole = lax.dynamic_update_slice_in_dim(whole, block, (place ^ bits) * rows, 0)
    return whole


def square_scatter(part, axis, size):
    if size != 8:
        return pair_scatter(part, axis, size)
    place = lax.axis_index(axis)
    core = place & 1
    chip = lax.shift_right_logical(place, 1)
    split = part.reshape(size // 2, 2, part.shape[0] // size, part.shape[1])
    going = lax.dynamic_index_in_dim(split, 1 - core, 1, keepdims=False)
    came = lax.ppermute(going, axis, swap(size, 1))
    kept = lax.dynamic_index_in_dim(split, core, 1, keepdims=False)
    both = (kept.astype(F32) + came.astype(F32)).astype(BF16)

    def pick(index):
        return lax.dynamic_index_in_dim(both, index, 0, keepdims=False)

    far = lax.ppermute(pick(chip ^ 3), axis, cross(size)).astype(F32)
    none = jnp.zeros((), F32)
    to_x = pick(chip ^ 1).astype(F32) + jnp.where(core == 0, far, none)
    to_y = pick(chip ^ 2).astype(F32) + jnp.where(core == 1, far, none)
    by_x = lax.ppermute(to_x.astype(BF16), axis, swap(size, 2))
    by_y = lax.ppermute(to_y.astype(BF16), axis, swap(size, 4))
    return pick(chip).astype(F32) + by_x.astype(F32) + by_y.astype(F32)


def tile_loop(count, body):
    lax.fori_loop(0, count, lambda i, c: (body(i), c)[1], 0)


def rows_at(index, size):
    return pl.ds(pl.multiple_of(index * size, size), size)


def rnn_forward_kernel(
    both_ref, halo_ref, start_ref, mask_ref, gates_ref, params_ref,
    mixed_ref, conv_ref, r_ref, i_ref, state_ref, end_ref,
    padded, high, low,
):
    count, width = conv_ref.shape
    tiles = count // TILE
    padded[0:8, :] = halo_ref[...]
    padded[8:, :] = both_ref[:, 0:width]

    def convolve(t):
        span = padded[pl.ds(pl.multiple_of(t * TILE, TILE), TILE + 8), :]
        mask = mask_ref[rows_at(t, TILE), :]
        conv = params_ref[0:1, :] * span[8:, :] + params_ref[TAPS : TAPS + 1, :]
        for k in range(1, TAPS):
            moved = span[8 - k : 8 - k + TILE, :]
            conv = conv + params_ref[k : k + 1, :] * (moved * mask[:, k : k + 1])
        conv_ref[rows_at(t, TILE), :] = conv
        top = conv.astype(BF16)
        high[rows_at(t, TILE), :] = top
        low[rows_at(t, TILE), :] = (conv - top.astype(F32)).astype(BF16)

    tile_loop(tiles, convolve)

    block = min(256, count)

    def gate(t):
        rows = rows_at(t, block)
        weights = gates_ref[...]
        both = jnp.dot(high[rows, :], weights, preferred_element_type=F32)
        both = both + jnp.dot(low[rows, :], weights, preferred_element_type=F32)
        r_ref[rows, :] = both[:, 0:width]
        i_ref[rows, :] = both[:, width:]

    tile_loop(count // block, gate)

    strength = DECAY_SCALE * jax.nn.softplus(-params_ref[TAPS + 3 : TAPS + 4, :])

    place = lax.broadcasted_iota(jnp.int32, (8, width), 0)

    def advance(t, carry):
        rows = rows_at(t, TILE)
        keep = mask_ref[rows, :][:, 0:1]
        r = jax.nn.sigmoid(r_ref[rows, :] + params_ref[TAPS + 1 : TAPS + 2, :])
        i = jax.nn.sigmoid(i_ref[rows, :] + params_ref[TAPS + 2 : TAPS + 3, :])
        log_a = -strength * r
        scale = jnp.sqrt(jnp.maximum(one_less_exp(2.0 * log_a), ROOT_FLOOR))
        scale = jnp.where(keep > 0.0, scale, 1.0)
        decay = jnp.exp(log_a) * keep
        drive = scale * i * conv_ref[rows, :]
        r_ref[rows, :] = r
        i_ref[rows, :] = i
        states = []
        for g in range(0, TILE, 8):
            a, held = decay[g : g + 8, :], drive[g : g + 8, :]
            for s in (1, 2, 4):
                inside = place >= s
                held = held + a * jnp.where(inside, pltpu.roll(held, s, 0), 0.0)
                a = a * jnp.where(inside, pltpu.roll(a, s, 0), 1.0)
            held = held + a * carry
            carry = jnp.broadcast_to(held[7:8, :], (8, width))
            states.append(held)
        state = jnp.concatenate(states, axis=0)
        state_ref[rows, :] = state
        mixed_ref[rows, :] = (state * gelu(both_ref[rows, width:])).astype(BF16)
        return carry

    carry = jnp.broadcast_to(start_ref[0:1, :], (8, width))
    end_ref[...] = lax.fori_loop(0, tiles, advance, carry)


def rnn_forward(both, halo, start, mask, gates, params):
    count, width = both.shape[0], both.shape[1] // 2
    full = jax.ShapeDtypeStruct((count, width), F32)
    return pl.pallas_call(
        rnn_forward_kernel,
        out_shape=(
            jax.ShapeDtypeStruct((count, width), BF16),
            full, full, full, full,
            jax.ShapeDtypeStruct((8, width), F32),
        ),
        scratch_shapes=[
            pltpu.VMEM((count + 8, width), F32),
            pltpu.VMEM((count, width), BF16),
            pltpu.VMEM((count, width), BF16),
        ],
        compiler_params=pltpu.CompilerParams(vmem_limit_bytes=VMEM_BYTES),
        cost_estimate=pl.CostEstimate(
            flops=4 * count * width * 2 * width, bytes_accessed=count * width * 30,
            transcendentals=count * width * 6,
        ),
        name="rnn_forward",
    )(both, halo, start, mask, gates, params)


def rnn_backward_kernel(
    gm_ref, both_ref, halo_ref, start_ref, conv_ref, r_ref, i_ref, state_ref, mask_ref,
    gates_ref, params_ref, back_ref, tail_ref,
    grads_ref, rates_ref, dparams_ref, back_out_ref, tail_out_ref, dots_ref,
    padded, before, dconv, sums,
):
    count, width = conv_ref.shape
    tiles = count // TILE
    padded[0:8, :] = halo_ref[...]
    padded[8:, :] = both_ref[:, 0:width]
    before[0:8, :] = start_ref[...]
    before[8:, :] = state_ref[...]
    strength = DECAY_SCALE * jax.nn.softplus(-params_ref[TAPS + 3 : TAPS + 4, :])

    sums[...] = jnp.zeros_like(sums)
    place = lax.broadcasted_iota(jnp.int32, (8, width), 0)

    def fold(values):
        return jnp.sum(values.reshape(-1, 8, width), axis=0)

    def chain(t, carry):
        later, later_decay = carry
        base = pl.multiple_of((tiles - 1 - t) * TILE, TILE)
        rows = pl.ds(base, TILE)
        keep = mask_ref[rows, :][:, 0:1]
        gm = gm_ref[rows, :]
        value, slope = gelu_and_slope(both_ref[rows, width:])
        grads_ref[rows, width:] = (gm * state_ref[rows, :] * slope).astype(BF16)
        given = gm * value
        r, i, conv = r_ref[rows, :], i_ref[rows, :], conv_ref[rows, :]
        fall = jnp.exp(-strength * r) * keep
        adjoints = []
        for g in reversed(range(0, TILE, 8)):
            a = fall[g : g + 8, :]
            ahead = jnp.where(place == 7, later_decay, pltpu.roll(a, 7, 0))
            held = given[g : g + 8, :]
            for s in (1, 2, 4):
                inside = place < 8 - s
                held = held + ahead * jnp.where(inside, pltpu.roll(held, 8 - s, 0), 0.0)
                ahead = ahead * jnp.where(inside, pltpu.roll(ahead, 8 - s, 0), 1.0)
            held = held + ahead * later
            later = jnp.broadcast_to(held[0:1, :], (8, width))
            later_decay = jnp.broadcast_to(a[0:1, :], (8, width))
            adjoints.append(held)
        a = jnp.concatenate(adjoints[::-1], axis=0)
        prior = before[pl.ds(base, TILE + 8), :][7 : 7 + TILE, :]
        room = one_less_exp(-2.0 * strength * r)
        bound = jnp.maximum(room, ROOT_FLOOR)
        inverse = lax.rsqrt(bound)
        scale = jnp.where(keep > 0.0, bound * inverse, 1.0)
        open_ = jnp.where(room > ROOT_FLOOR, inverse, 0.0)
        driven = a * i
        dlog = fall * (a * prior - fall * driven * conv * open_)
        common = a * scale
        drec = dlog * (-strength) * r * (1.0 - r)
        dinp = common * conv * i * (1.0 - i)
        rates_ref[rows, 0:width] = drec.astype(BF16)
        rates_ref[rows, width:] = dinp.astype(BF16)
        dconv[rows, :] = common * i
        sums[5] += fold(drec)
        sums[6] += fold(dinp)
        sums[7] += fold(dlog * r)
        return later, later_decay

    later = jnp.broadcast_to(back_ref[0:1, :], (8, width))
    later, later_decay = lax.fori_loop(
        0, tiles, chain, (later, jnp.ones((8, width), F32))
    )
    back_out_ref[...] = later * later_decay

    block = min(256, count)

    def spread(t):
        rows = rows_at(t, block)
        dconv[rows, :] += lax.dot_general(
            rates_ref[rows, :], gates_ref[...], (((1,), (1,)), ((), ())),
            preferred_element_type=F32,
        )

    tile_loop(count // block, spread)
    dconv[count:, :] = tail_ref[...]
    tail_out_ref[...] = dconv[0:8, :]

    def unconvolve(t):
        base = pl.multiple_of(t * TILE, TILE)
        rows = pl.ds(base, TILE)
        span = dconv[pl.ds(base, TILE + 8), :]
        mask = mask_ref[pl.ds(base, TILE + 8), :]
        source = padded[pl.ds(base, TILE + 8), :]
        here = span[0:TILE, :]
        out = params_ref[0:1, :] * here
        sums[0] += fold(here * source[8:, :])
        sums[4] += fold(here)
        for k in range(1, TAPS):
            kept = span * mask[:, k : k + 1]
            out = out + params_ref[k : k + 1, :] * kept[k : k + TILE, :]
            sums[k] += fold(kept[0:TILE, :] * source[8 - k : 8 - k + TILE, :])
        grads_ref[rows, 0:width] = out.astype(BF16)
        dot = jnp.sum(
            out * source[8:, :] + grads_ref[rows, width:].astype(F32) * both_ref[rows, width:],
            axis=1, keepdims=True,
        )
        dots_ref[rows, :] = jnp.broadcast_to(dot, (TILE, 128))

    tile_loop(tiles, unconvolve)
    for k in range(8):
        dparams_ref[k : k + 1, :] = jnp.sum(sums[k], axis=0, keepdims=True)
    dparams_ref[TAPS + 3 : TAPS + 4, :] = (
        DECAY_SCALE
        * jax.nn.sigmoid(-params_ref[TAPS + 3 : TAPS + 4, :])
        * jnp.sum(sums[TAPS + 3], axis=0, keepdims=True)
    )


def rnn_backward(gm, both, halo, start, saved, mask, gates, params, back, tail):
    conv, r, i, state = saved
    count, width = conv.shape
    return pl.pallas_call(
        rnn_backward_kernel,
        out_shape=(
            jax.ShapeDtypeStruct((count, 2 * width), BF16),
            jax.ShapeDtypeStruct((count, 2 * width), BF16),
            jax.ShapeDtypeStruct((8, width), F32),
            jax.ShapeDtypeStruct((8, width), F32),
            jax.ShapeDtypeStruct((8, width), F32),
            jax.ShapeDtypeStruct((count, 128), F32),
        ),
        scratch_shapes=[
            pltpu.VMEM((count + 8, width), F32),
            pltpu.VMEM((count + 8, width), F32),
            pltpu.VMEM((count + 8, width), F32),
            pltpu.VMEM((8, 8, width), F32),
        ],
        compiler_params=pltpu.CompilerParams(vmem_limit_bytes=VMEM_BYTES),
        cost_estimate=pl.CostEstimate(
            flops=2 * count * width * 2 * width, bytes_accessed=count * width * 36,
            transcendentals=count * width * 6,
        ),
        name="rnn_backward",
    )(gm, both, halo, start, conv, r, i, state, mask, gates, params, back, tail)


MESH = pl.DeviceIdType.MESH


class Spread:
    def __init__(self, place, size, blocks, sent, came):
        self.place, self.size = place, size
        self.blocks, self.sent, self.came = blocks, sent, came

    def copy(self, slot, j, way, k):
        ref = self.blocks.at[slot, j]
        return pltpu.make_async_remote_copy(
            src_ref=ref, dst_ref=ref, send_sem=self.sent.at[slot, k],
            recv_sem=self.came.at[slot, j], device_id={"mp": self.place + way},
            device_id_type=MESH,
        )

    def moves(self, s):
        z, n = self.place, self.size
        return (
            ((z - s >= 0) & (z < n - 1), z - s, 1, 2 * s),
            ((z + s <= n - 1) & (z > 0), z + s, -1, 2 * s + 1),
        )

    def step(self, slot, s):
        for valid, j, way, k in self.moves(s):

            @pl.when(valid)
            def _(j=j, way=way, k=k):
                copy = self.copy(slot, j, way, k)
                if s > 0:
                    copy.wait_recv()
                copy.start()

    def finish(self, slot):
        z, n = self.place, self.size

        @pl.when(z == 0)
        def _():
            for j in range(1, n):
                self.copy(slot, j, 1, 0).wait_recv()

        @pl.when(z == n - 1)
        def _():
            for j in range(n - 1):
                self.copy(slot, j, -1, 0).wait_recv()

    def drain(self, slot):
        for s in range(self.size - 1):
            for valid, j, way, k in self.moves(s):

                @pl.when(valid)
                def _(j=j, way=way, k=k):
                    self.copy(slot, j, way, k).wait_send()


class Fold:
    def __init__(self, place, size, parts, rights, lefts, sent, came_right, came_left):
        self.place, self.size = place, size
        self.parts, self.rights, self.lefts = parts, rights, lefts
        self.sent, self.came_right, self.came_left = sent, came_right, came_left

    def right(self, slot, j, k):
        return pltpu.make_async_remote_copy(
            src_ref=self.parts.at[slot, j], dst_ref=self.rights.at[slot, k],
            send_sem=self.sent.at[slot, j], recv_sem=self.came_right.at[slot, k],
            device_id={"mp": self.place + 1}, device_id_type=MESH,
        )

    def left(self, slot, j, k):
        return pltpu.make_async_remote_copy(
            src_ref=self.parts.at[slot, j], dst_ref=self.lefts.at[slot, k],
            send_sem=self.sent.at[slot, j], recv_sem=self.came_left.at[slot, k],
            device_id={"mp": self.place - 1}, device_id_type=MESH,
        )

    def clear(self):
        for slot in range(self.parts.shape[0]):
            last = self.size - 2
            blank = jnp.zeros(self.rights.shape[2:], BF16)
            self.rights[slot, last] = blank
            self.lefts[slot, last] = blank

    def start(self, slot):
        z, n = self.place, self.size

        @pl.when(z == 0)
        def _():
            for j in reversed(range(1, n)):
                self.right(slot, j, n - 1 - j).start()

        @pl.when(z == n - 1)
        def _():
            for j in range(n - 1):
                self.left(slot, j, j).start()

    def step(self, slot, s):
        z, n = self.place, self.size
        back = n - 1 - z

        @pl.when((z >= 1) & (z <= n - 2) & (s >= z))
        def _():
            j = n - 1 + z - s
            self.right(slot, j, s - 1).wait_recv()
            self.add(slot, j, self.rights, s - 1)
            self.right(slot, j, s).start()

        @pl.when((back >= 1) & (back <= n - 2) & (s >= back))
        def _():
            j = s - back
            self.left(slot, j, s - 1).wait_recv()
            self.add(slot, j, self.lefts, s - 1)
            self.left(slot, j, s).start()

    def add(self, slot, j, came, k):
        self.parts[slot, j] = (
            self.parts[slot, j].astype(F32) + came[slot, k].astype(F32)
        ).astype(BF16)

    def finish(self, slot):
        z, n = self.place, self.size

        @pl.when(z >= 1)
        def _():
            self.right(slot, z, n - 2).wait_recv()

        @pl.when(z <= n - 2)
        def _():
            self.left(slot, z, n - 2).wait_recv()

    def total(self, slot, rows):
        z, n = self.place, self.size
        return (
            self.parts[slot, z, rows, :].astype(F32)
            + self.rights[slot, n - 2, rows, :].astype(F32)
            + self.lefts[slot, n - 2, rows, :].astype(F32)
        )

    def drain(self, slot):
        for j in range(self.size):

            @pl.when(j != self.place)
            def _(j=j):
                self.right(slot, j, 0).wait_send()


def partners(d):
    core, x, y = lax.rem(d, 2), lax.rem(lax.div(d, 2), 2), lax.div(d, 4)
    return core, d + 1 - 2 * core, d + 2 - 4 * x, d + 4 - 8 * y


class Square:
    def __init__(self, d, shard, whole, sent, came, own, axis=0):
        self.d, self.shard, self.whole, self.axis = d, shard, whole, axis
        self.sent, self.came, self.own = sent, came, own
        self.core, self.by_core, self.by_x, self.by_y = partners(d)

    def rows(self, d):
        count = self.shard.shape[self.axis]
        window = pl.ds(pl.multiple_of(d * count, count), count)
        return self.whole.at[:, window] if self.axis else self.whole.at[window, :]

    def copy(self, src, origin, target, sent, came):
        return pltpu.make_async_remote_copy(
            src_ref=src, dst_ref=self.rows(origin), send_sem=self.sent.at[sent],
            recv_sem=self.came.at[came], device_id={"dp": target}, device_id_type=MESH,
        )

    def local(self):
        return pltpu.make_async_copy(self.shard, self.rows(self.d), self.own)

    def far(self):
        return partners(self.by_x)[3]

    def first(self):
        return (
            self.copy(self.shard, self.d, self.by_x, 0, 2),
            self.copy(self.shard, self.d, self.by_y, 1, 4),
            self.copy(self.shard, self.d, self.by_core, 2, 1),
        )

    def start(self):
        for copy in self.first():
            copy.start()
        self.local().start()

    def step_one(self):
        x_rows, y_rows = self.rows(self.by_x), self.rows(self.by_y)
        by_x = self.copy(x_rows, self.by_x, self.by_core, 3, 2)
        by_y = self.copy(y_rows, self.by_y, self.by_core, 4, 4)
        by_x.wait_recv()

        @pl.when(self.core == 0)
        def _():
            self.copy(x_rows, self.by_x, self.by_y, 5, 6).start()

        self.copy(x_rows, self.by_x, self.by_core, 3, 3).start()
        by_y.wait_recv()

        @pl.when(self.core == 1)
        def _():
            self.copy(y_rows, self.by_y, self.by_x, 5, 6).start()

        self.copy(y_rows, self.by_y, self.by_core, 4, 5).start()

    def step_two(self):
        far = self.far()
        rows = self.rows(far)
        self.copy(rows, far, self.by_core, 6, 6).wait_recv()
        self.copy(rows, far, self.by_core, 6, 7).start()

    def finish(self):
        for k in (1, 3, 5, 7):
            self.copy(self.shard, self.d, self.by_core, 0, k).wait_recv()
        self.local().wait()

    def drain(self):
        for k in range(7):
            self.copy(self.shard, self.d, self.by_core, k, 0).wait_send()


class Scatter:
    def __init__(self, d, count, compute, held, far, first, second, sent, came):
        self.d, self.count, self.compute = d, count, compute
        self.held, self.far_in, self.first_in, self.second_in = held, far, first, second
        self.sent, self.came = sent, came
        self.core, self.by_core, by_x, by_y = partners(d)
        even = self.core == 0
        self.first = jnp.where(even, by_y, by_x)
        self.second = jnp.where(even, by_x, by_y)
        self.first_at, self.second_at = 2 - self.core, 1 + self.core
        other = partners(self.by_core)
        self.away = (self.by_core, other[2], other[3], partners(other[2])[3])
        self.distant = partners(by_x)[3]

    def owners(self):
        return [self.away[k] for k in (3, 1, 2, 0)] + [
            self.distant, self.first, self.d, self.second
        ]

    def copy(self, src, dst, target, sent, came):
        return pltpu.make_async_remote_copy(
            src_ref=src, dst_ref=dst, send_sem=self.sent.at[sent], recv_sem=self.came.at[came],
            device_id={"dp": target}, device_id_type=MESH,
        )

    def to_core(self, buffer, k):
        return self.copy(buffer, self.held(k), self.by_core, k, k)

    def to_far(self):
        return self.copy(self.held(3), self.far_in, self.first, 4, 4)

    def to_first(self):
        return self.copy(self.held(self.first_at), self.first_in, self.first, 5, 5)

    def to_second(self):
        return self.copy(self.held(self.second_at), self.second_in, self.second, 6, 6)

    def far_core(self, buffers, sending):
        for slot, k in enumerate((3, 1, 2, 0)):
            if sending[slot] is not None:
                sending[slot].wait_send()
            self.compute(self.away[k], buffers[slot], False)
            copy = self.to_core(buffers[slot], k)
            copy.start()
            sending[slot] = copy

    def add_block(self, k, came, owner):
        self.copy(self.held(k), self.held(k), self.by_core, k, came).wait_recv()
        self.compute(owner, self.held(k), True)

    def near_core(self):
        self.add_block(3, 3, self.distant)
        self.to_far().start()
        self.add_block(self.first_at, self.first_at, self.first)
        self.to_first().start()
        self.add_block(0, 0, self.d)
        self.add_block(self.second_at, self.second_at, self.second)

    def onward(self):
        self.to_far().wait_recv()
        held = self.held(self.second_at)

        def body(t):
            rows = rows_at(t, 16)
            held[rows, :] = (
                held[rows, :].astype(F32) + self.far_in[rows, :].astype(F32)
            ).astype(BF16)

        tile_loop(self.count // 16, body)
        self.to_second().start()

    def finish(self, target):
        self.to_first().wait_recv()
        self.to_second().wait_recv()
        held = self.held(0)

        def body(t):
            rows = rows_at(t, 16)
            target[rows, :] = (
                held[rows, :].astype(F32)
                + self.first_in[rows, :].astype(F32)
                + self.second_in[rows, :].astype(F32)
            )

        tile_loop(self.count // 16, body)

    def drain(self):
        self.to_far().wait_send()
        self.to_first().wait_send()
        self.to_second().wait_send()


def head_kernel(dp, mp, names, *refs):
    ref = dict(zip(names, refs))
    blocks, w_in, norm, both = ref["blocks"], ref["w_in_here"], ref["norm"], ref["both_here"]
    chunks, _, step, part = blocks.shape
    features, width = part * mp, ref["mixed_here"].shape[2]
    z, d = lax.axis_index("mp"), lax.axis_index("dp")
    square = dp == 8
    gather = Spread(z, mp, blocks, ref["spread_sent"], ref["spread_came"])

    barrier = pltpu.get_barrier_semaphore()

    @pl.when(z > 0)
    def _():
        pl.semaphore_signal(barrier, inc=1, device_id={"mp": z - 1}, device_id_type=MESH)

    @pl.when(z < mp - 1)
    def _():
        pl.semaphore_signal(barrier, inc=1, device_id={"mp": z + 1}, device_id_type=MESH)

    count = jnp.where((z > 0) & (z < mp - 1), 2, 1)
    if square:
        for other in partners(d)[1:]:
            pl.semaphore_signal(barrier, inc=1, device_id={"dp": other}, device_id_type=MESH)
        count = count + 3

    def chunk_rows(c):
        return pl.ds(c * step, step)

    def own_block(c):
        return pltpu.make_async_copy(
            ref["x"].at[chunk_rows(c), :], blocks.at[c, z], ref["load_sem"].at[c]
        )

    for c in range(chunks):
        own_block(c).start()
    pl.semaphore_wait(barrier, count)

    wholes = (
        ("gates_shard", ref["gates_here"], 0),
        ("rnn_in", w_in.at[:, pl.ds(0, width)], 0),
        ("branch_gate", w_in.at[:, pl.ds(width, width)], 0),
        ("rnn_out", ref["w_out"], 1),
        ("mlp_gate", ref["w_gate"], 0),
    )
    if square:
        squares = [
            Square(
                d, ref[name], whole, ref["square_sent"].at[k], ref["square_came"].at[k],
                ref["square_own"].at[k], axis,
            )
            for k, (name, whole, axis) in enumerate(wholes)
        ]
        for item in squares[:3]:
            item.start()
    else:
        loads = [
            pltpu.make_async_copy(ref[name], whole, ref["square_own"].at[k])
            for k, (name, whole, _) in enumerate(wholes)
        ]
        for item in loads:
            item.start()

    def begin(c):
        own_block(c).wait()
        gather.step(c, 0)

    begin(0)
    if chunks > 1:
        begin(1)

    def expand():
        span = ref["gates_flat"].shape[0]
        rows = span // 8
        for k in range(8):
            ref["gates_flat"][k * rows : (k + 1) * rows, :] = ref["gates_here"][
                k * 32 : k * 32 + 32, :
            ].astype(F32)[0:rows, :]
        column = lax.broadcasted_iota(jnp.int32, (span, 2 * width), 1)
        column = jnp.where(column >= width, column - width, column)
        for b in range(width // span):
            inside = (column >= b * span) & (column < (b + 1) * span)
            ref["dense_here"][b * span : (b + 1) * span, :] = jnp.where(
                inside, ref["gates_flat"][...], 0.0
            ).astype(BF16)

    stores = (
        ("norm", "norm"), ("both", "both_here"), ("conv", "conv_here"), ("r", "r_here"),
        ("i", "i_here"), ("state", "state_here"), ("mixed", "mixed_here"), ("s1", "s1_here"),
    )

    def store_all(c):
        return [
            pltpu.make_async_copy(
                ref[near].at[c % 2], ref[far + "_out"].at[chunk_rows(c), :],
                ref["store_sem"].at[c % 2, k],
            )
            for k, (far, near) in enumerate(stores)
        ]

    ref["halo"][...] = jnp.zeros_like(ref["halo"])
    ref["start"][...] = jnp.zeros_like(ref["start"])

    def compute(c):
        slot = c % 2
        if c > 1:
            for copy in store_all(c - 2):
                copy.wait()

        def body(t):
            rows = rows_at(t, TILE)
            values = [blocks[c, j, rows, :].astype(F32) for j in range(mp)]
            total = sum(jnp.sum(v * v, axis=1, keepdims=True) for v in values)
            s1 = lax.rsqrt(total / features + EPS)
            for j in range(mp):
                cols = slice(j * part, (j + 1) * part)
                norm[slot, rows, cols] = (values[j] * s1 * ref["gains"][0:1, cols]).astype(BF16)
            ref["s1_here"][slot, rows, :] = jnp.broadcast_to(s1, (TILE, 128))

        tile_loop(step // TILE, body)
        for k in range(2):
            cols = slice(k * width, (k + 1) * width)
            both[slot, :, cols] = matmul(norm[slot], w_in[:, cols])
        rnn_forward_kernel(
            both.at[slot], ref["halo"], ref["start"], ref["mask"].at[chunk_rows(c), :],
            ref["dense_here"], ref["params"],
            ref["mixed_here"].at[slot], ref["conv_here"].at[slot], ref["r_here"].at[slot],
            ref["i_here"].at[slot], ref["state_here"].at[slot], ref["end"],
            ref["padded"], ref["high"], ref["low"],
        )
        ref["halo"][...] = both[slot, step - 8 :, 0:width]
        ref["start"][...] = ref["end"][...]
        for copy in store_all(c):
            copy.start()

    for s in range(1, mp - 1):
        gather.step(0, s)
        if s == 1 and chunks > 2:
            begin(2)
    if square:
        for item in squares[:3]:
            item.step_one()
        for item in squares[3:]:
            item.start()
        for item in squares[:3]:
            item.step_two()
    gather.finish(0)
    for c in range(chunks):
        if c + 1 < chunks:
            gather.step(c + 1, 1)
        if c == 0:
            if square:
                for item in squares[:3]:
                    item.finish()
            else:
                for item in loads:
                    item.wait()
            expand()
            pass_on = [
                pltpu.make_async_copy(w_in, ref["w_in"], ref["pass_sem"].at[0]),
                pltpu.make_async_copy(ref["dense_here"], ref["dense"], ref["pass_sem"].at[1]),
            ]
            for copy in pass_on:
                copy.start()
        if c + 3 < chunks:
            begin(c + 3)
        compute(c)
        if square and (c + 1) * 4 == chunks:
            squares[3].step_one()
        if square and (c + 1) * 2 == chunks:
            squares[3].step_two()
            squares[4].step_one()
        if square and (c + 1) * 4 == 3 * chunks:
            squares[4].step_two()
        if c + 1 < chunks:
            for s in range(2, mp - 1):
                gather.step(c + 1, s)
            gather.finish(c + 1)
    if square:
        squares[3].finish()
        squares[4].finish()
        for item in squares:
            item.drain()
    for copy in pass_on:
        copy.wait()
    for c in range(max(0, chunks - 2), chunks):
        for copy in store_all(c):
            copy.wait()
    for c in range(chunks):
        gather.drain(c)


def head(
    dp, mp, chunks, x, gains, params, mask, rnn_in, branch_gate, rnn_out, mlp_gate, gates_shard,
    span,
):
    count, part = x.shape
    features, width = part * mp, params.shape[1]
    step = count // chunks
    dma = pltpu.SemaphoreType.DMA
    any_, vmem = pl.BlockSpec(memory_space=pl.ANY), pl.BlockSpec(memory_space=pltpu.VMEM)
    ins = [
        ("x", x, any_), ("gains", gains, vmem), ("params", params, vmem), ("mask", mask, vmem),
        ("rnn_in", rnn_in, any_), ("branch_gate", branch_gate, any_), ("rnn_out", rnn_out, any_),
        ("mlp_gate", mlp_gate, any_), ("gates_shard", gates_shard, any_),
    ]
    gate_width = mlp_gate.shape[1]
    shape = jax.ShapeDtypeStruct
    outs = [
        ("w_in", shape((features, 2 * width), BF16)), ("w_out", shape((width, features), BF16)),
        ("w_gate", shape((features, gate_width), BF16)), ("dense", shape((width, 2 * width), BF16)), ("norm_out", shape((count, features), BF16)),
        ("both_out", shape((count, 2 * width), F32)), ("conv_out", shape((count, width), F32)),
        ("r_out", shape((count, width), F32)), ("i_out", shape((count, width), F32)),
        ("state_out", shape((count, width), F32)), ("mixed_out", shape((count, width), BF16)),
        ("s1_out", shape((count, 128), F32)),
    ]
    wide = pltpu.VMEM((2, step, width), F32)
    scratch = [
        ("blocks", pltpu.VMEM((chunks, mp, step, part), BF16)),
        ("w_in_here", pltpu.VMEM((features, 2 * width), BF16)),
        ("gates_here", pltpu.VMEM((256, 2 * width), BF16)),
        ("gates_flat", pltpu.VMEM((span, 2 * width), F32)),
        ("dense_here", pltpu.VMEM((width, 2 * width), BF16)),
        ("norm", pltpu.VMEM((2, step, features), BF16)),
        ("both_here", pltpu.VMEM((2, step, 2 * width), F32)),
        ("conv_here", wide), ("r_here", wide), ("i_here", wide), ("state_here", wide),
        ("mixed_here", pltpu.VMEM((2, step, width), BF16)),
        ("s1_here", pltpu.VMEM((2, step, 128), F32)),
        ("halo", pltpu.VMEM((8, width), F32)), ("start", pltpu.VMEM((8, width), F32)),
        ("end", pltpu.VMEM((8, width), F32)),
        ("padded", pltpu.VMEM((step + 8, width), F32)),
        ("high", pltpu.VMEM((step, width), BF16)), ("low", pltpu.VMEM((step, width), BF16)),
        ("spread_sent", dma((chunks, 2 * mp))), ("spread_came", dma((chunks, mp))),
        ("square_sent", dma((5, 8))), ("square_came", dma((5, 8))), ("square_own", dma((5,))),
        ("load_sem", dma((chunks,))), ("store_sem", dma((2, 8))), ("pass_sem", dma((2,))),
    ]
    names = [i[0] for i in ins] + [o[0] for o in outs] + [k[0] for k in scratch]
    return pl.pallas_call(
        functools.partial(head_kernel, dp, mp, tuple(names)),
        in_specs=[i[2] for i in ins],
        out_specs=[any_] * len(outs),
        out_shape=[o[1] for o in outs],
        scratch_shapes=[k[1] for k in scratch],
        compiler_params=pltpu.CompilerParams(
            collective_id=2, has_side_effects=True, vmem_limit_bytes=60 * 1024 * 1024
        ),
        name="head",
    )(*[i[1] for i in ins])


MIDDLE_ORDER = (
    ("d", 0, 0), ("d", 0, 1), ("d", 1, 1), ("A", 0, 0), ("a", 1, 0), ("d", 1, 0), ("a", 2, 0),
    ("A", 0, 1), ("d", 2, 0), ("d", 2, 1), ("a", 1, 1), ("J", 0, 0), ("S", 1, 0), ("e", 0, 0),
    ("a", 2, 1), ("S", 2, 0), ("e", 1, 0), ("e", 2, 0), ("d", 0, 2), ("d", 0, 3), ("J", 0, 1),
    ("S", 3, 0), ("e", 0, 1), ("e", 3, 0), ("d", 1, 2), ("d", 1, 3), ("A", 0, 2), ("d", 3, 0),
    ("a", 1, 2), ("e", 1, 1), ("H", 0, 0), ("G", 0, 0), ("d", 2, 2), ("a", 2, 2), ("e", 2, 1),
    ("c", 1, 0), ("d", 2, 3), ("O", 0, 0), ("b", 1, 0), ("J", 0, 2), ("e", 3, 1), ("e", 0, 2),
    ("d", 3, 1), ("c", 2, 0), ("A", 0, 3), ("d", 3, 3), ("H", 0, 1), ("e", 1, 2), ("a", 1, 3),
    ("K", 0, 0), ("G", 0, 1), ("a", 2, 3), ("f", 1, 0), ("c", 1, 1), ("e", 2, 2), ("e", 3, 2),
    ("J", 0, 3), ("e", 0, 3), ("O", 0, 1), ("f", 2, 0), ("d", 3, 2), ("b", 2, 0), ("H", 0, 2),
    ("c", 2, 1), ("b", 1, 1), ("Y", 0, 0), ("e", 1, 3), ("B", 0, 0), ("K", 0, 1), ("e", 2, 3),
    ("G", 0, 2), ("b", 2, 1), ("e", 3, 3), ("f", 1, 1), ("O", 0, 2), ("c", 1, 2), ("H", 0, 3),
    ("Y", 0, 1), ("f", 2, 1), ("c", 2, 2), ("B", 0, 1), ("G", 0, 3), ("K", 0, 2), ("b", 1, 2),
    ("O", 0, 3), ("D", 0, 0), ("c", 1, 3), ("D", 0, 1), ("c", 2, 3), ("W", 0, 0), ("D", 0, 2),
    ("Z", 0, 0), ("f", 1, 2), ("W", 0, 1), ("b", 2, 2), ("D", 0, 3), ("f", 2, 2), ("K", 0, 3),
    ("Z", 0, 1), ("b", 1, 3), ("W", 0, 2), ("D", 0, 4), ("W", 0, 3), ("Z", 0, 2), ("f", 1, 3),
    ("W", 0, 4), ("D", 0, 5), ("Y", 0, 2), ("f", 2, 3), ("Z", 0, 3), ("B", 0, 2), ("b", 2, 3),
    ("W", 0, 5), ("B", 0, 3), ("Z", 0, 4), ("Z", 0, 5), ("Y", 0, 3),
)


def middle_kernel(dp, mp, chunks, *refs):
    (
        mixed_ref, x_ref, cot_ref, live_ref, gains_ref, wout_ref, gate_ref, up_ref,
        down_ref,
        output_ref, gm_ref, gbo_ref, local_ref, hidden_ref, pulled_ref, norm_ref, grady_ref,
        grad_gate_ref, grad_up_ref, gain_ref,
        w_up, w_down, cots, mids, gn2s, mid_mine, gn2_mine,
        parts1, rights1, lefts1, parts2, rights2, lefts2, parts3, rights3, lefts3,
        norm, hidden, pulled, gbo, gm, local, out,
        spread_sent, spread_came, fold_sent, fold_right, fold_left,
        square_sent, square_came, square_own, load_sem, store_sem,
        stage, free_sem, task_sent, task_came, left_sem, right_sem, stage_sem, slot_right,
        slot_left,
    ) = refs
    step, part = x_ref.shape[0] // chunks, x_ref.shape[1]
    features = part * mp
    hidden_width = w_down.shape[0]
    z, d = lax.axis_index("mp"), lax.axis_index("dp")
    square = dp == 8
    up_half = w_up.at[:, pl.ds(hidden_width, hidden_width)]
    own_cols = pl.ds(pl.multiple_of(z * part, part), part)

    folds = [
        Fold(z, mp, p, r, l, fold_sent.at[k], fold_right.at[k], fold_left.at[k])
        for k, (p, r, l) in enumerate(
            ((parts1, rights1, lefts1), (parts2, rights2, lefts2), (parts3, rights3, lefts3))
        )
    ]
    rs1, rs2, rs3 = folds
    ag2, ag3, ag4 = [
        Spread(z, mp, b, spread_sent.at[k], spread_came.at[k])
        for k, b in enumerate((cots, mids, gn2s))
    ]
    for fold in folds:
        fold.clear()

    barrier = pltpu.get_barrier_semaphore()

    @pl.when(z > 0)
    def _():
        pl.semaphore_signal(barrier, inc=1, device_id={"mp": z - 1}, device_id_type=MESH)

    @pl.when(z < mp - 1)
    def _():
        pl.semaphore_signal(barrier, inc=1, device_id={"mp": z + 1}, device_id_type=MESH)

    count = jnp.where((z > 0) & (z < mp - 1), 2, 1)
    if square:
        for other in partners(d)[1:]:
            pl.semaphore_signal(barrier, inc=1, device_id={"dp": other}, device_id_type=MESH)
        count = count + 3
    pl.semaphore_wait(barrier, count)

    if square:
        squares = [
            Square(
                d, shard, whole, square_sent.at[k], square_came.at[k], square_own.at[k], k
            )
            for k, (shard, whole) in enumerate(((up_ref, up_half), (down_ref, w_down)))
        ]
        for item in squares:
            item.start()
    else:
        loads = [
            pltpu.make_async_copy(up_ref, up_half, square_own.at[0]),
            pltpu.make_async_copy(down_ref, w_down, square_own.at[1]),
        ]
        for item in loads:
            item.start()
    load_gate = pltpu.make_async_copy(
        gate_ref, w_up.at[:, pl.ds(0, hidden_width)], square_own.at[2]
    )
    load_gate.start()

    def chunk_rows(c):
        return pl.ds(c * step, step)

    def store(buffer, target, c, k):
        return pltpu.make_async_copy(buffer, target.at[chunk_rows(c), :], store_sem.at[k])

    def own_cot(c):
        return pltpu.make_async_copy(cot_ref.at[chunk_rows(c), :], cots.at[c, z], load_sem.at[c])

    for c in range(chunks):
        own_cot(c).start()

    gain_ref[...] = jnp.zeros_like(gain_ref)
    tiles = step // TILE

    def fill(fold, slot, left, weights, columns=True):
        def body(j):
            near = pl.ds(pl.multiple_of(j * part, part), part)
            if columns:
                value = matmul(left, weights[:, near])
            else:
                value = inner_cols(left, weights[near, :])
            fold.parts[slot, j] = value.astype(BF16)

        tile_loop(mp, body)

    def branch(c):
        if c > 1:
            rs1.drain(c % 2)
        fill(rs1, c % 2, mixed_ref[chunk_rows(c), :], wout_ref)
        rs1.start(c % 2)

    def join(c):
        rs1.finish(c % 2)

        def body(t):
            rows = rows_at(t, TILE)
            base = pl.ds(pl.multiple_of(c * step + t * TILE, TILE), TILE)
            total = x_ref[base, :].astype(F32) + rs1.total(c % 2, rows)
            mid_mine[c, rows, :] = total
            mids[c, z, rows, :] = total.astype(BF16)

        tile_loop(tiles, body)

    def stats(c, rows):
        blocks = [mids[c, j, rows, :].astype(F32) for j in range(mp)]
        square_sum = sum(jnp.sum(b * b, axis=1, keepdims=True) for b in blocks)
        return blocks, lax.rsqrt(square_sum / features + EPS)

    def block_cols(j):
        return slice(j * part, (j + 1) * part)

    def normalise(c):
        def body(t):
            rows = rows_at(t, TILE)
            base = pl.ds(pl.multiple_of(c * step + t * TILE, TILE), TILE)
            blocks, s2 = stats(c, rows)
            live = live_ref[base, :][:, TAPS : TAPS + 1]
            for j in range(mp):
                norm[rows, block_cols(j)] = (
                    blocks[j] * s2 * gains_ref[1:2, block_cols(j)]
                ).astype(BF16)
                cots[c, j, rows, :] = (cots[c, j, rows, :].astype(F32) * live).astype(BF16)

        tile_loop(tiles, body)

    def grad_y_copies(c):
        return [
            pltpu.make_async_copy(
                cots.at[c, j], grady_ref.at[chunk_rows(c), pl.ds(j * part, part)],
                store_sem.at[8 + j],
            )
            for j in range(mp)
        ]

    def mlp_first(c):
        if c > 0:
            store(norm, norm_ref, c, 0).wait()
            store(hidden, hidden_ref, c, 1).wait()
            store(pulled, pulled_ref, c, 2).wait()
            for copy in grad_y_copies(c - 1):
                copy.wait()
        if c == 0:
            load_gate.wait()
            for item in squares if square else ():
                item.finish()
            for item in () if square else loads:
                item.wait()
        ag2.drain(c)
        normalise(c)
        store(norm, norm_ref, c, 0).start()
        for copy in grad_y_copies(c):
            copy.start()
        size = 256

        def body(t):
            near = pl.ds(pl.multiple_of(t * size, size), size)
            off = pl.ds(pl.multiple_of(hidden_width + t * size, size), size)
            gate = matmul(norm[...], w_up[:, near])
            up = matmul(norm[...], w_up[:, off])
            grad = sum(
                inner_cols(cots[c, j], w_down[near, block_cols(j)]) for j in range(mp)
            )
            value, slope = gelu_and_slope(gate)
            hidden[:, near] = (value * up).astype(BF16)
            pulled[:, near] = (grad * up * slope).astype(BF16)
            pulled[:, off] = (grad * value).astype(BF16)

        tile_loop(hidden_width // size, body)
        store(hidden, hidden_ref, c, 1).start()
        store(pulled, pulled_ref, c, 2).start()

    def mlp_second(c):
        slot = c % 2
        if c > 1:
            rs3.drain(slot)
        fill(rs3, slot, pulled[...], w_up, False)
        rs3.start(slot)
        if square and c == chunks - 1:
            for item in squares:
                item.drain()
            for k, other in enumerate(partners(d)[1:]):
                pl.semaphore_signal(
                    free_sem.at[k], inc=1, device_id={"dp": other}, device_id_type=MESH
                )

    def mlp_third(c):
        slot = c % 2
        if c > 1:
            rs2.drain(slot)
        fill(rs2, slot, hidden[...], w_down)
        if c > 1:

            @pl.when(z < mp - 1)
            def _():
                pl.semaphore_wait(slot_right.at[slot], 1)

            @pl.when(z > 0)
            def _():
                pl.semaphore_wait(slot_left.at[slot], 1)

        rs2.start(slot)

    def gather_grad(c):
        slot = c % 2
        rs3.finish(slot)

        def body(t):
            rows = rows_at(t, TILE)
            total = rs3.total(slot, rows)
            gn2_mine[slot, rows, :] = total
            gn2s[c, z, rows, :] = total.astype(BF16)

        tile_loop(tiles, body)
        ag4.step(c, 0)

    def norm_back(c):
        slot = c % 2
        ag4.finish(c)
        if c > 0:
            store(gbo, gbo_ref, c, 3).wait()
            store(local, local_ref, c, 4).wait()
            store(gm, gm_ref, c, 5).wait()

        def body(t):
            rows = rows_at(t, TILE)
            blocks, s2 = stats(c, rows)
            grads = [gn2s[c, j, rows, :].astype(F32) for j in range(mp)]
            scaled = [grads[j] * gains_ref[1:2, block_cols(j)] for j in range(mp)]
            mean = (
                sum(jnp.sum(scaled[j] * blocks[j], axis=1, keepdims=True) for j in range(mp))
                / features
            )
            fall = s2 * s2 * s2 * mean
            for j in range(mp):
                grad_y = cots[c, j, rows, :].astype(F32)
                gbo[rows, block_cols(j)] = (
                    grad_y + s2 * scaled[j] - blocks[j] * fall
                ).astype(BF16)
                gain_ref[:, block_cols(j)] += jnp.sum(
                    (grads[j] * (blocks[j] * s2)).reshape(-1, 8, part), axis=0
                )
            local[rows, :] = (
                cots[c, z, rows, :].astype(F32)
                + s2 * (gn2_mine[slot, rows, :] * gains_ref[1:2, own_cols])
                - mid_mine[c, rows, :] * fall
            )

        tile_loop(tiles, body)
        gm[...] = inner_cols(gbo[...], wout_ref[...])
        store(gbo, gbo_ref, c, 3).start()
        store(local, local_ref, c, 4).start()
        store(gm, gm_ref, c, 5).start()

    def make_output(c):
        rs2.finish(c % 2)
        if c > 0:
            store(out, output_ref, c, 6).wait()

        def body(t):
            rows = rows_at(t, TILE)
            out[rows, :] = (mid_mine[c, rows, :] + rs2.total(c % 2, rows)).astype(BF16)

        tile_loop(tiles, body)
        if c + 2 < chunks:
            slot = c % 2

            @pl.when(z > 0)
            def _():
                pl.semaphore_signal(
                    slot_right.at[slot], inc=1, device_id={"mp": z - 1}, device_id_type=MESH
                )

            @pl.when(z < mp - 1)
            def _():
                pl.semaphore_signal(
                    slot_left.at[slot], inc=1, device_id={"mp": z + 1}, device_id_type=MESH
                )

        store(out, output_ref, c, 6).start()

    own = features // 8
    count_tasks = 2 * hidden_width // part
    scatters, sending = [], [None] * 4
    buffers = [rights1.at[i // 2, i % 2] for i in range(4)]
    staged = [None]

    def left_block(i):
        return (cots if i < 2 else mids).at[i % 2]

    def left_copies():
        return [
            pltpu.make_async_copy(
                norm_ref.at[chunk_rows(i), pl.ds(j * part, part)], left_block(i).at[j],
                left_sem.at[i, j],
            )
            for i in range(chunks)
            for j in range(mp)
        ]

    def right_copies(k):
        return [
            pltpu.make_async_copy(
                pulled_ref.at[chunk_rows(i), pl.ds(k * part, part)], parts1.at[k % 2, i],
                right_sem.at[k % 2, i],
            )
            for i in range(chunks)
        ]

    def make_scatter(k):
        def compute(owner, target, add):
            j = lax.div(owner, 2)
            near = pl.ds(pl.multiple_of(lax.rem(owner, 2) * own, own), own)
            value = sum(
                inner_rows(left_block(i)[j, :, near], parts1[k % 2, i]) for i in range(chunks)
            )
            if add:
                value = value + target[...].astype(F32)
            target[...] = value.astype(BF16)

        cols = pl.ds(k * part, part)

        def place(first):
            return w_up.at[pl.ds(first, own), cols]

        def held(i):
            return w_up.at[pl.ds(pl.multiple_of(i * own, own), own), cols]

        return Scatter(
            d, own, compute, held, place(4 * own), place(5 * own), place(6 * own),
            task_sent.at[k], task_came.at[k],
        )

    def weight_first(k):
        if not square:
            return
        if k == 0:
            store(norm, norm_ref, chunks - 1, 0).wait()
            store(pulled, pulled_ref, chunks - 1, 2).wait()
            for slot in range(2):
                rs1.drain(slot)
            for c in range(2):
                ag3.drain(c)
            scatters.extend(make_scatter(i) for i in range(count_tasks))
            for copy in right_copies(0) + left_copies():
                copy.start()
            for i in range(3):
                pl.semaphore_wait(free_sem.at[i], 1)
        if k + 1 < count_tasks:
            for copy in right_copies(k + 1):
                copy.start()
        for copy in right_copies(k) + (left_copies() if k == 0 else []):
            copy.wait()
        scatters[k].far_core(buffers, sending)
        scatters[k].near_core()

    def weight_second(k):
        if square:
            scatters[k].onward()

    def weight_third(k):
        if not square:
            return
        if staged[0] is not None:
            staged[0].wait()
        scatters[k].finish(stage)
        half = count_tasks // 2
        target = grad_gate_ref if k < half else grad_up_ref
        staged[0] = pltpu.make_async_copy(
            stage, target.at[:, pl.ds((k % half) * part, part)], stage_sem
        )
        staged[0].start()

    steps = {
        "A": branch, "J": join, "H": mlp_first, "G": mlp_second, "O": mlp_third,
        "K": gather_grad, "B": norm_back, "Y": make_output, "D": weight_first,
        "W": weight_second, "Z": weight_third,
    }
    moves = {"a": (rs1, 2), "b": (rs2, 2), "c": (rs3, 2), "d": (ag2, 0), "e": (ag3, 0), "f": (ag4, 0)}
    for name, s, c in MIDDLE_ORDER:
        if name == "S":
            if square and s < 3:
                squares[s - 1].step_one()
            if square and s == 3:
                squares[0].step_two()
                squares[1].step_two()
        elif name in steps:
            steps[name](c)
        else:
            line, parity = moves[name]
            if s == mp - 1:
                line.finish(c)
                continue
            if name == "d" and s == 0:
                own_cot(c).wait()
            line.step(c % parity if parity else c, s)

    last = chunks - 1
    for k, (buffer, target) in enumerate(
        (
            (norm, norm_ref), (hidden, hidden_ref), (pulled, pulled_ref), (gbo, gbo_ref),
            (local, local_ref), (gm, gm_ref), (out, output_ref),
        )
    ):
        if not (square and k in (0, 2)):
            store(buffer, target, last, k).wait()
    for copy in grad_y_copies(last):
        copy.wait()
    for c in range(chunks):
        if c > 1 or not square:
            ag3.drain(c)
        ag4.drain(c)
    for slot in range(2):
        for fold in folds[1:] if square else folds:
            fold.drain(slot)
    if square:
        staged[0].wait()
        for copy in sending:
            copy.wait_send()
        for scatter in scatters:
            scatter.drain()


def middle(dp, mp, chunks, mixed, inputs, cotangent, live, gains, w_out, gate, up, down):
    count, part = inputs.shape
    width, hidden_width = mixed.shape[1], down.shape[0]
    step, features = count // chunks, part * mp

    def fold_buffers():
        return [
            pltpu.VMEM((2, mp, step, part), BF16),
            pltpu.VMEM((2, mp - 1, step, part), BF16),
            pltpu.VMEM((2, mp - 1, step, part), BF16),
        ]

    dma = pltpu.SemaphoreType.DMA
    any_, vmem = pl.BlockSpec(memory_space=pl.ANY), pl.BlockSpec(memory_space=pltpu.VMEM)
    return pl.pallas_call(
        functools.partial(middle_kernel, dp, mp, chunks),
        in_specs=[vmem, vmem, any_, vmem, vmem, vmem, any_, any_, any_],
        out_specs=[any_] * 10 + [vmem],
        out_shape=(
            jax.ShapeDtypeStruct((count, part), BF16),
            jax.ShapeDtypeStruct((count, width), F32),
            jax.ShapeDtypeStruct((count, features), BF16),
            jax.ShapeDtypeStruct((count, part), F32),
            jax.ShapeDtypeStruct((count, hidden_width), BF16),
            jax.ShapeDtypeStruct((count, 2 * hidden_width), BF16),
            jax.ShapeDtypeStruct((count, features), BF16),
            jax.ShapeDtypeStruct((count, features), BF16),
            jax.ShapeDtypeStruct((features // 8, hidden_width), F32),
            jax.ShapeDtypeStruct((features // 8, hidden_width), F32),
            jax.ShapeDtypeStruct((8, features), F32),
        ),
        scratch_shapes=[
            pltpu.VMEM((features, 2 * hidden_width), BF16),
            pltpu.VMEM((hidden_width, features), BF16),
            pltpu.VMEM((chunks, mp, step, part), BF16),
            pltpu.VMEM((chunks, mp, step, part), BF16),
            pltpu.VMEM((chunks, mp, step, part), BF16),
            pltpu.VMEM((chunks, step, part), F32),
            pltpu.VMEM((2, step, part), F32),
        ]
        + fold_buffers() + fold_buffers() + fold_buffers()
        + [
            pltpu.VMEM((step, features), BF16),
            pltpu.VMEM((step, hidden_width), BF16),
            pltpu.VMEM((step, 2 * hidden_width), BF16),
            pltpu.VMEM((step, features), BF16),
            pltpu.VMEM((step, width), F32),
            pltpu.VMEM((step, part), F32),
            pltpu.VMEM((step, part), BF16),
            dma((3, chunks, 2 * mp)),
            dma((3, chunks, mp)),
            dma((3, 2, mp)),
            dma((3, 2, mp)),
            dma((3, 2, mp)),
            dma((2, 8)),
            dma((2, 8)),
            dma((3,)),
            dma((chunks,)),
            dma((12,)),
            pltpu.VMEM((features // 8, part), F32),
            pltpu.SemaphoreType.REGULAR((3,)),
            dma((2 * hidden_width // part, 8)),
            dma((2 * hidden_width // part, 8)),
            dma((chunks, mp)),
            dma((2, chunks)),
            dma,
            pltpu.SemaphoreType.REGULAR((2,)),
            pltpu.SemaphoreType.REGULAR((2,)),
        ],
        compiler_params=pltpu.CompilerParams(
            collective_id=0, has_side_effects=True, vmem_limit_bytes=62 * 1024 * 1024
        ),
        name="middle",
    )(mixed, inputs, cotangent, live, gains, w_out, gate, up, down)


TAIL_ORDER = (
    ("R", 0, 3), ("R", 0, 2), ("D", 0, 0), ("R", 0, 1), ("D", 0, 1), ("a", 0, 3), ("l", 0, 2),
    ("W", 0, 0), ("s", 1, 3), ("s", 1, 2), ("R", 0, 0), ("W", 0, 1), ("s", 2, 3), ("D", 0, 2),
    ("s", 2, 2), ("m", 0, 0), ("l", 0, 3), ("s", 1, 1), ("a", 0, 2), ("g", 0, 0), ("W", 0, 2),
    ("m", 0, 1), ("a", 0, 1), ("a", 0, 0), ("D", 0, 3), ("s", 1, 0), ("D", 0, 4), ("s", 2, 1),
    ("m", 0, 2), ("D", 0, 5), ("D", 0, 6), ("I", 0, 3), ("W", 0, 3), ("s", 2, 0), ("Z", 0, 0),
    ("I", 0, 2), ("W", 0, 4), ("W", 0, 5), ("Z", 0, 1), ("I", 0, 1), ("m", 0, 3), ("W", 0, 6),
    ("Z", 0, 2), ("I", 0, 0), ("m", 0, 4), ("Z", 0, 3), ("Z", 0, 4), ("Z", 0, 5), ("m", 0, 5),
    ("Z", 0, 6),
)


def tail_kernel(mp, tasks, names, *refs):
    ref = dict(zip(names, refs))
    pull, w_in, params = ref["pull"], ref["w_in_here"], ref["params"]
    chunks, _, step, part = ref["parts"].shape
    count, features = chunks * step, part * mp
    own, width = features // 8, params.shape[1]
    z, d = lax.axis_index("mp"), lax.axis_index("dp")
    _, by_core, by_x, by_y = partners(d)
    fold = Fold(
        z, mp, ref["parts"], ref["rights"], ref["lefts"], ref["fold_sent"], ref["fold_right"],
        ref["fold_left"],
    )
    near = z + 1 - 2 * lax.rem(z, 2)
    apart = z + 2 - 4 * lax.div(z, 2)
    own_cols = pl.ds(pl.multiple_of(z * part, part), part)

    def chunk_rows(c):
        return pl.ds(c * step, step)

    def recurrence_copies(c):
        copies = [
            pltpu.make_async_copy(
                ref[name].at[chunk_rows(c), :], ref[name + "_here"], ref["chunk_sem"].at[k]
            )
            for k, name in enumerate(("gm", "both", "conv", "r", "i", "state"))
        ]
        if c > 0:
            rows = pl.ds(c * step - 8, 8)
            copies += [
                pltpu.make_async_copy(
                    ref["both"].at[rows, pl.ds(0, width)], ref["halo"], ref["chunk_sem"].at[6]
                ),
                pltpu.make_async_copy(
                    ref["state"].at[rows, :], ref["start"], ref["chunk_sem"].at[7]
                ),
            ]
        return copies

    def norm_copy(c):
        return pltpu.make_async_copy(
            ref["norm1"].at[chunk_rows(c), :], ref["norm_here"], ref["norm_sem"]
        )

    def left_copy(name):
        return pltpu.make_async_copy(ref[name], ref["lhs"], ref["left_sem"])

    def right_copy(name, first, columns, slot):
        return pltpu.make_async_copy(
            ref[name].at[:, pl.ds(first, columns)], ref["rhs"].at[slot, :, pl.ds(0, columns)],
            ref["right_sem"].at[slot],
        )

    def end_copies(c):
        return [
            pltpu.make_async_copy(
                ref[name].at[chunk_rows(c), :], ref[name + "_here"], ref["end_sem"].at[k]
            )
            for k, name in enumerate(("local", "x", "s1"))
        ]

    whole_copies = [
        pltpu.make_async_copy(ref[name], ref[name + "_here"], ref["whole_sem"].at[k])
        for k, name in enumerate(("dense", "w_in"))
    ]
    last = chunks - 1
    for copy in recurrence_copies(last) + whole_copies:
        copy.start()
    norm_copy(last).start()
    left_copy("grady").start()
    first_rights = [
        right_copy(t[2], t[3], t[4], k) for k, t in enumerate(tasks[:2])
    ]
    for copy in first_rights + end_copies(last):
        copy.start()

    fold.clear()
    barrier = pltpu.get_barrier_semaphore()

    @pl.when(z > 0)
    def _():
        pl.semaphore_signal(barrier, inc=1, device_id={"mp": z - 1}, device_id_type=MESH)

    @pl.when(z < mp - 1)
    def _():
        pl.semaphore_signal(barrier, inc=1, device_id={"mp": z + 1}, device_id_type=MESH)

    pl.semaphore_signal(barrier, inc=1, device_id={"mp": apart}, device_id_type=MESH)
    for other in (by_core, by_x, by_y):
        pl.semaphore_signal(barrier, inc=1, device_id={"dp": other}, device_id_type=MESH)

    for name in ("back", "after", "gain", "dense_sum", "params_sum"):
        ref[name][...] = jnp.zeros_like(ref[name])
    gain = ref["gain"]

    def recur(c):
        for copy in recurrence_copies(c):
            copy.wait()
        if c == 0:
            ref["halo"][...] = jnp.zeros_like(ref["halo"])
            ref["start"][...] = jnp.zeros_like(ref["start"])
        if c == last:
            for copy in whole_copies:
                copy.wait()
        rnn_backward_kernel(
            ref["gm_here"], ref["both_here"], ref["halo"], ref["start"], ref["conv_here"],
            ref["r_here"], ref["i_here"], ref["state_here"],
            ref["mask"].at[pl.ds(c * step, step + 8), :], ref["dense_here"], params,
            ref["back"], ref["after"],
            pull.at[chunk_rows(c), :], ref["rates"], ref["dparams"], ref["back"], ref["after"],
            ref["dots"],
            ref["padded"], ref["before"], ref["dconv"], ref["sums"],
        )
        ref["params_sum"][...] += ref["dparams"][...]
        ref["dense_sum"][...] += inner_rows(ref["conv_here"][...].astype(BF16), ref["rates"][...])
        if c > 0:
            for copy in recurrence_copies(c - 1):
                copy.start()
        for q in range(step // 128):
            turned = jnp.transpose(ref["dots"][q * 128 : (q + 1) * 128, :])
            ref["dots_row"][c, :, q * 128 : (q + 1) * 128] = turned[0:8, :]
        if c == last:
            pl.semaphore_wait(barrier, jnp.where((z > 0) & (z < mp - 1), 6, 5))
        dots_copy(c, 0).start()
        norm_copy(c).wait()

        def body(j):
            rows = pl.ds(pl.multiple_of(j * part, part), part)
            value = inner_cols(pull[chunk_rows(c), :], w_in[rows, :])
            fold.parts[c, j] = value.astype(BF16)
            gain[:, rows] += jnp.sum(
                (value * ref["norm_here"][:, rows].astype(F32)).reshape(-1, 8, part), axis=0
            )

        tile_loop(mp, body)
        fold.start(c)
        if c > 0:
            norm_copy(c - 1).start()

    def dots_copy(c, k):
        return pltpu.make_async_remote_copy(
            src_ref=ref["dots_row"].at[c], dst_ref=ref["dots_in"].at[c, k],
            send_sem=ref["dots_sent"].at[c, k], recv_sem=ref["dots_came"].at[c, k],
            device_id={"mp": near if k == 0 else apart}, device_id_type=MESH,
        )

    def dots_add(c, k):
        dots_copy(c, k).wait()
        ref["dots_row"][c] += ref["dots_in"][c, k]
        if k == 0:
            dots_copy(c, 1).start()

    def input_grad(c):
        dots_add(c, 1)
        for q in range(step // 128):
            row = ref["dots_row"][c, 0:1, q * 128 : (q + 1) * 128]
            ref["dots_col"][q * 128 : (q + 1) * 128, :] = jnp.transpose(
                jnp.broadcast_to(row, (128, 128))
            )
        fold.finish(c)
        for copy in end_copies(c):
            copy.wait()

        def body(t):
            rows = rows_at(t, TILE)
            base = pl.ds(pl.multiple_of(c * step + t * TILE, TILE), TILE)
            s1 = ref["s1_here"][rows, :][:, 0:1]
            dot = ref["dots_col"][rows, :][:, 0:1]
            grad = (
                ref["local_here"][rows, :]
                + s1 * (fold.total(c, rows) * ref["gains"][0:1, own_cols])
                - ref["x_here"][rows, :].astype(F32) * (s1 * s1 * dot * (1.0 / features))
            )
            ref["grad_x"][base, :] = grad.astype(BF16)

        tile_loop(step // TILE, body)
        if c > 0:
            for copy in end_copies(c - 1):
                copy.start()

    sends, store_sem = ref["sends"], ref["store_sem"]
    slots = {k: k % 2 for k, t in enumerate(tasks) if t[2] in ("hidden", "mixed")}

    def build(k):
        _, left, right, first, columns, _ = tasks[k]

        def compute(owner, target, add):
            if left is None:
                rows = pl.ds(pl.multiple_of(owner * 32, 32), 32)
                value = ref["gates"][rows, first : first + columns].astype(F32)
            else:
                near = pl.ds(pl.multiple_of(owner * own, own), own)
                if right == "pull":
                    operand = pull[:, first : first + columns]
                else:
                    operand = ref["rhs"][slots[k], :, 0:columns]
                value = inner_rows(ref["lhs"][:, near], operand)
            if add:
                value = value + target[...].astype(F32)
            target[...] = value.astype(BF16)

        return Scatter(
            d, 32 if left is None else own, compute, ref["held%d" % k].at.__getitem__,
            ref["far%d" % k], ref["first%d" % k], ref["second%d" % k], ref["task_sent"].at[k],
            ref["task_came"].at[k],
        )

    scatters = [build(k) for k in range(len(tasks))]
    sending = [None] * 4

    def far_core(k):
        height, columns = scatters[k].count, tasks[k][4]
        scatters[k].far_core(
            [sends.at[slot, pl.ds(0, height), pl.ds(0, columns)] for slot in range(4)], sending
        )

    stage, stage_wait = ref["stage"], [None, None]

    def finish(k):
        scatter = scatters[k]
        name, columns, column = tasks[k][0], tasks[k][4], tasks[k][5]
        slot = k % 2
        if stage_wait[slot] is not None:
            stage_wait[slot].wait()
        view = stage.at[slot, pl.ds(0, scatter.count), pl.ds(0, columns)]
        scatter.finish(view)
        target = ref["grad_" + name].at[:, pl.ds(column, columns)]
        copy = pltpu.make_async_copy(view, target, store_sem.at[slot])
        copy.start()
        stage_wait[slot] = copy

    small, small_in = ref["small"], ref["small_in"]
    targets = (
        {"dp": by_core}, {"dp": by_x}, {"dp": by_y}, {"mp": near}, {"mp": apart},
    )

    def small_copy(k):
        rows = pl.ds(0, 16 if k < 3 else 8)
        return pltpu.make_async_remote_copy(
            src_ref=small.at[rows, :], dst_ref=small_in.at[k, rows, :],
            send_sem=ref["small_sent"].at[k], recv_sem=ref["small_came"].at[k],
            device_id=targets[k], device_id_type=MESH,
        )

    def small_first():
        small[...] = jnp.zeros_like(small)
        small[0:1, :] = jnp.sum(gain[...], axis=0, keepdims=True) / ref["gains"][0:1, :]
        small[1:2, :] = jnp.sum(ref["gain2"][...], axis=0, keepdims=True) * (1.0 / mp)
        small[8:16, 0:width] = ref["params_sum"][...]
        small_copy(0).start()

    def small_next(k):
        rows = 16 if k < 3 else 8
        small_copy(k).wait()
        small[0:rows, :] += small_in[k, 0:rows, :]
        if k < 4:
            small_copy(k + 1).start()

    def gate_blocks():
        flat, gates = ref["flat"], ref["gates"]
        span = flat.shape[0] - 16
        rows = span // 8
        column = lax.broadcasted_iota(jnp.int32, (span, 2 * width), 1)
        column = jnp.where(column >= width, column - width, column)
        total = jnp.zeros((span, 2 * width), F32)
        for b in range(width // span):
            inside = (column >= b * span) & (column < (b + 1) * span)
            total = total + jnp.where(
                inside, ref["dense_sum"][b * span : (b + 1) * span, :], 0.0
            )
        flat[0:span, :] = total
        flat[span:, :] = jnp.zeros((16, 2 * width), F32)
        for k in range(8):
            gates[k * 32 : (k + 1) * 32, :] = flat[k * rows : k * rows + 32, :].astype(BF16)

    out_right = right_copy("mixed", 0, tasks[2][4], 0)

    def load_next(k):
        left_copy("gbo" if k == 2 else "norm1").start()
        if k == 2:
            out_right.start()

    def weight(k):
        if k == 0:
            for copy in first_rights:
                copy.wait()
            left_copy("grady").wait()
        if k == 2:
            out_right.wait()
        if k in (2, 3):
            left_copy("norm1").wait()
        far_core(k)
        scatters[k].near_core()

    steps = {
        "R": recur, "I": input_grad, "D": weight, "W": lambda k: scatters[k].onward(),
        "Z": finish, "l": load_next, "g": lambda k: gate_blocks(), "a": lambda c: dots_add(c, 0),
        "m": lambda k: small_next(k - 1) if k else small_first(),
    }
    for name, s, c in TAIL_ORDER:
        if name == "s":
            fold.step(c, s)
        else:
            steps[name](c)
    for copy in stage_wait:
        copy.wait()
    for copy in sending:
        copy.wait_send()
    for scatter in scatters:
        scatter.drain()
    for c in range(chunks):
        fold.drain(c)


def tail(mp, chunks, span, rnn, mask, params, dense, w_in, norm1, grady, hidden, gbo, mixed, s1, x,
         local, gains, gain2):
    gm, both, conv, r, i, state = rnn
    count, part = x.shape
    features, width = part * mp, params.shape[1]
    own, step = features // 8, count // chunks
    widths = {
        "down": hidden.shape[1], "out": width, "in": 2 * width, "block": 2 * width,
    }
    heights = {name: 32 if name == "block" else own for name in widths}
    operands = {
        "down": ("grady", "hidden"), "out": ("gbo", "mixed"), "in": ("norm1", "pull"),
        "block": (None, "gates"),
    }
    tasks = []
    for name, columns in widths.items():
        left, right = operands[name]
        pieces = 1 if name == "out" else 2
        size = columns // pieces
        for piece in range(pieces):
            tasks.append((name, left, right, piece * size, size, piece * size))
    widest = max(t[4] for t in tasks)
    dma = pltpu.SemaphoreType.DMA
    any_, vmem = pl.BlockSpec(memory_space=pl.ANY), pl.BlockSpec(memory_space=pltpu.VMEM)
    ins = [
        ("gm", gm, any_), ("both", both, any_), ("conv", conv, any_), ("r", r, any_),
        ("i", i, any_), ("state", state, any_), ("mask", mask, vmem), ("params", params, vmem),
        ("dense", dense, any_), ("w_in", w_in, any_), ("norm1", norm1, any_),
        ("grady", grady, any_), ("hidden", hidden, any_), ("gbo", gbo, any_),
        ("mixed", mixed, any_), ("s1", s1, any_), ("x", x, any_), ("local", local, any_),
        ("gains", gains, vmem), ("gain2", gain2, vmem),
    ]
    shape = jax.ShapeDtypeStruct
    outs = [("grad_x", shape((count, part), BF16), vmem)]
    for name, columns in widths.items():
        outs.append(("grad_" + name, shape((heights[name], columns), F32), any_))
    outs.append(("small", shape((16, features), F32), vmem))
    wide = pltpu.VMEM((step, width), F32)
    tall = pltpu.VMEM((step + 8, width), F32)
    eight = pltpu.VMEM((8, width), F32)
    scratch = [
        ("gm_here", wide), ("both_here", pltpu.VMEM((step, 2 * width), F32)),
        ("conv_here", wide), ("r_here", wide), ("i_here", wide), ("state_here", wide),
        ("halo", eight), ("start", eight), ("back", eight), ("after", eight),
        ("dparams", eight), ("params_sum", eight),
        ("dense_here", pltpu.VMEM(dense.shape, BF16)), ("w_in_here", pltpu.VMEM(w_in.shape, BF16)),
        ("pull", pltpu.VMEM((count, 2 * width), BF16)),
        ("rates", pltpu.VMEM((step, 2 * width), BF16)),
        ("dots", pltpu.VMEM((step, 128), F32)),
        ("padded", tall), ("before", tall), ("dconv", tall), ("sums", pltpu.VMEM((8, 8, width), F32)),
        ("dense_sum", pltpu.VMEM((width, 2 * width), F32)),
        ("flat", pltpu.VMEM((span + 16, 2 * width), F32)),
        ("gates", pltpu.VMEM((256, 2 * width), BF16)),
        ("norm_here", pltpu.VMEM((step, features), BF16)),
        ("lhs", pltpu.VMEM((count, features), BF16)),
        ("rhs", pltpu.VMEM((2, count, widest), BF16)),
        ("local_here", pltpu.VMEM((step, part), F32)), ("x_here", pltpu.VMEM((step, part), BF16)),
        ("s1_here", pltpu.VMEM((step, 128), F32)),
        ("parts", pltpu.VMEM((chunks, mp, step, part), BF16)),
        ("rights", pltpu.VMEM((chunks, mp - 1, step, part), BF16)),
        ("lefts", pltpu.VMEM((chunks, mp - 1, step, part), BF16)),
        ("sends", pltpu.VMEM((4, own, widest), BF16)),
        ("stage", pltpu.VMEM((2, own, widest), F32)),
        ("gain", pltpu.VMEM((8, features), F32)),
        ("dots_row", pltpu.VMEM((chunks, 8, step), F32)),
        ("dots_in", pltpu.VMEM((chunks, 2, 8, step), F32)),
        ("dots_col", pltpu.VMEM((step, 128), F32)),
        ("small_in", pltpu.VMEM((5, 16, features), F32)),
        ("chunk_sem", dma((8,))), ("norm_sem", dma), ("left_sem", dma), ("right_sem", dma((2,))),
        ("end_sem", dma((3,))), ("whole_sem", dma((2,))), ("store_sem", dma((2,))),
        ("fold_sent", dma((chunks, mp))), ("fold_right", dma((chunks, mp))),
        ("fold_left", dma((chunks, mp))),
        ("task_sent", dma((len(tasks), 8))), ("task_came", dma((len(tasks), 8))),
        ("dots_sent", dma((chunks, 2))), ("dots_came", dma((chunks, 2))),
        ("small_sent", dma((5,))), ("small_came", dma((5,))),
    ]
    for k, (name, _, _, _, size, _) in enumerate(tasks):
        rows = heights[name]
        scratch.append(("held%d" % k, pltpu.VMEM((4, rows, size), BF16)))
        for kind in ("far", "first", "second"):
            scratch.append(("%s%d" % (kind, k), pltpu.VMEM((rows, size), BF16)))
    names = [i[0] for i in ins] + [o[0] for o in outs] + [k[0] for k in scratch]
    return pl.pallas_call(
        functools.partial(tail_kernel, mp, tuple(tasks), tuple(names)),
        in_specs=[i[2] for i in ins],
        out_specs=[o[2] for o in outs],
        out_shape=[o[1] for o in outs],
        scratch_shapes=[k[1] for k in scratch],
        compiler_params=pltpu.CompilerParams(
            collective_id=1, has_side_effects=True, vmem_limit_bytes=63 * 1024 * 1024
        ),
        name="tail",
    )(*[i[1] for i in ins])


def make_masks(row_lengths, count):
    ends = jnp.cumsum(row_lengths)
    places = jnp.arange(-TAPS, count, dtype=jnp.int32)
    segment = jnp.sum((places[:, None] >= ends[None, :]).astype(jnp.int32), axis=1)
    segment = jnp.where(places < 0, -1, segment)
    now = segment[TAPS:]
    same = [(segment[TAPS - k : TAPS - k + count] == now).astype(F32) for k in range(1, TAPS)]
    blank = jnp.zeros((count,), F32)
    live = (now < row_lengths.shape[0]).astype(F32)
    columns = [same[0]] + same + [live] + [blank] * (LANES - TAPS - 1)
    return jnp.stack(columns, axis=1)


def dense_gates(gates, width):
    span = gates.shape[0]
    tiled = jnp.tile(gates, (width // span, 1))
    row = lax.broadcasted_iota(jnp.int32, tiled.shape, 0) // span
    column = (lax.broadcasted_iota(jnp.int32, tiled.shape, 1) % width) // span
    return jnp.where(row == column, tiled, jnp.zeros((), tiled.dtype))


def diagonal_blocks(dense, span):
    width = dense.shape[0]
    column = (lax.broadcasted_iota(jnp.int32, (1, 2 * width), 1) % width) // span
    total = jnp.zeros((span, 2 * width), F32)
    for b in range(width // span):
        total = total + jnp.where(column == b, dense[b * span : (b + 1) * span], 0.0)
    return total


def per_device(
    dp, mp,
    inputs, lengths, cotangent, gains, rnn_params, rnn_in, branch_gate, recur_gate, input_gate,
    mlp_gate, mlp_up, rnn_out, mlp_down,
):
    count, part = inputs.shape
    width = rnn_in.shape[1]
    hidden_width = mlp_gate.shape[1]
    span = recur_gate.shape[0] * dp
    features = part * mp
    step = count // CHUNKS
    spot = lax.axis_index("mp") * part

    def cut(values):
        return [values[c * step : (c + 1) * step] for c in range(CHUNKS)]

    def mine(values):
        return lax.dynamic_slice_in_dim(values, spot, part, values.ndim - 1)

    gates_shard = jnp.concatenate([recur_gate, input_gate], axis=1)
    if dp == 8:
        gates_shard = jnp.pad(gates_shard, ((0, 32 - span // 8), (0, 0)))
    else:
        rnn_in, branch_gate, mlp_gate, mlp_up = [
            square_gather(w, "dp", dp) for w in (rnn_in, branch_gate, mlp_gate, mlp_up)
        ]
        rnn_out, mlp_down = [square_gather(w.T, "dp", dp).T for w in (rnn_out, mlp_down)]
        gates_shard = pair_gather(gates_shard, "dp", dp).reshape(8, span // 8, 2 * width)
        gates_shard = jnp.pad(gates_shard, ((0, 0), (0, 32 - span // 8), (0, 0)))
        gates_shard = gates_shard.reshape(256, 2 * width)

    mask = make_masks(lengths[0], count)
    mask_tail = jnp.concatenate([mask, jnp.zeros((8, LANES), F32)], axis=0)
    tail_masks = [mask_tail[c * step : (c + 1) * step + 8] for c in range(CHUNKS)]
    w_in, w_out, w_gate, dense, normed, both, conv, r, i, state, mixed, s1 = head(
        dp, mp, 4, inputs, gains, rnn_params, mask, rnn_in, branch_gate, rnn_out, mlp_gate,
        gates_shard, span,
    )
    (
        output, gm, gbo, local, hidden, pulled, normed2, grad_y, grad_gate, grad_up, gain2,
    ) = middle(
        dp, mp, 4, mixed, inputs, cotangent, mask, gains, w_out,
        w_gate, mlp_up, mlp_down,
    )
    if dp == 8:
        rows = span // dp
        input_grad, grad_down, grad_out, grad_in, grad_gates, small = tail(
            mp, 4, span, (gm, both, conv, r, i, state), mask_tail, rnn_params, dense, w_in, normed,
            grad_y, hidden, gbo, mixed, s1, inputs, local, gains, gain2,
        )
        grad_gates = grad_gates[:rows]
        grad_gains, grad_params = small[0:2], small[8:16, :width]
    else:
        blank = jnp.zeros((8, width), F32)
        back, tail_rows = blank, blank
        pulls, rates, dots = [None] * CHUNKS, [None] * CHUNKS, [None] * CHUNKS
        params_total = 0.0
        gms, boths = cut(gm), cut(both)
        saves = list(zip(cut(conv), cut(r), cut(i), cut(state)))
        for c in reversed(range(CHUNKS)):
            low = c * step
            halo = blank if c == 0 else both[low - 8 : low, :width]
            start = blank if c == 0 else state[low - 8 : low]
            pull, rate, dparams, back, tail_rows, dot = rnn_backward(
                gms[c], boths[c], halo, start, saves[c], tail_masks[c], dense, rnn_params,
                back, tail_rows,
            )
            params_total = params_total + dparams
            pulls[c], rates[c], dots[c] = pull, rate, dot
        pull = jnp.concatenate(pulls)
        dots = jnp.concatenate(dots)
        grad_gates = diagonal_blocks(inner_rows(conv.astype(BF16), jnp.concatenate(rates)), span)

        parts = []
        gain1 = 0.0
        norms, s1 = cut(normed), s1[:, 0:1]
        for c in range(CHUNKS):
            gn1_part = inner_cols(pulls[c], w_in).astype(BF16)
            gain1 = gain1 + jnp.sum(gn1_part.astype(F32) * norms[c].astype(F32), axis=0)
            parts.append(line_scatter(gn1_part, "mp", mp))
        dot = line_sum(dots[:, 0].reshape(8, -1), "mp", mp).reshape(-1, 1)
        input_grad = (
            local + s1 * (jnp.concatenate(parts) * mine(gains[0]))
            - inputs.astype(F32) * (s1 * s1 * dot / features)
        ).astype(BF16)
        grad_both = square_scatter(inner_rows(normed2, pulled).astype(BF16), "dp", dp)
        grad_gate, grad_up = grad_both[:, :hidden_width], grad_both[:, hidden_width:]
        grad_down = square_scatter(inner_rows(grad_y, hidden).astype(BF16), "dp", dp)
        grad_out = square_scatter(inner_rows(gbo, mixed).astype(BF16), "dp", dp)
        grad_in = square_scatter(inner_rows(normed, pull).astype(BF16), "dp", dp)
        grad_gates = pair_scatter(grad_gates, "dp", dp)
        grad_params = line_sum(params_total, "dp", dp)
        gain2 = jnp.sum(gain2, axis=0, keepdims=True)
        both_gains = jnp.concatenate([(gain1 / gains[0])[None], gain2])
        both_gains = line_sum(both_gains, "dp", dp)
        grad_gains = jnp.concatenate([line_sum(both_gains[:1], "mp", mp), both_gains[1:]])
    return (
        output,
        input_grad,
        grad_gains,
        grad_params,
        grad_in[:, :width],
        grad_in[:, width:],
        grad_gates[:, :width],
        grad_gates[:, width:],
        grad_gate,
        grad_up,
        grad_out.T,
        grad_down.T,
    )


def solution(mesh):
    return jax.shard_map(
        functools.partial(per_device, mesh.shape["dp"], mesh.shape["mp"]),
        mesh=mesh,
        in_specs=(
            P("dp", "mp"),
            P("dp", None),
            P("dp", "mp"),
            P(),
            P(None, "mp"),
            P("dp", "mp"),
            P("dp", "mp"),
            P("dp", "mp"),
            P("dp", "mp"),
            P("dp", "mp"),
            P("dp", "mp"),
            P("mp", "dp"),
            P("mp", "dp"),
        ),
        out_specs=(
            P("dp", "mp"),
            P("dp", "mp"),
            P(),
            P(None, "mp"),
            P("dp", "mp"),
            P("dp", "mp"),
            P("dp", "mp"),
            P("dp", "mp"),
            P("dp", "mp"),
            P("dp", "mp"),
            P("mp", "dp"),
            P("mp", "dp"),
        ),
        check_vma=False,
    )
```

```python
import functools

import jax
import jax.numpy as jnp
from jax import lax
from jax.experimental import pallas as pl
from jax.experimental.pallas import tpu as pltpu
from jax.sharding import PartitionSpec as P

EPS = 1e-06
DECAY_SCALE = 8.0
ROOT_FLOOR = 0.0001
TAPS = 4
LANES = 8
CHUNKS = 1
TILE = 32
RNN_TILE = 64
F32 = jnp.float32
BF16 = jnp.bfloat16
VMEM_BYTES = 56 * 1024 * 1024


def matmul(left, right):
    return jnp.dot(left, right, preferred_element_type=F32)


def inner_rows(left, right):
    return lax.dot_general(left, right, (((0,), (0,)), ((), ())), preferred_element_type=F32)


def inner_cols(left, right):
    return lax.dot_general(left, right, (((1,), (1,)), ((), ())), preferred_element_type=F32)


def gelu_and_slope(values):
    outer = 0.7978845608028654
    inner = 0.044715
    square = values * values
    bent = jnp.tanh(outer * values * (1.0 + inner * square))
    half = 0.5 * (1.0 + bent)
    slope = half + 0.5 * values * (1.0 - bent * bent) * outer * (1.0 + 3.0 * inner * square)
    return values * half, slope


def gelu(values):
    outer = 0.7978845608028654
    inner = 0.044715
    bent = jnp.tanh(outer * values * (1.0 + inner * values * values))
    return values * (0.5 * (1.0 + bent))


def one_less_exp(values):
    near = -values * (1.0 + 0.5 * values * (1.0 + (values / 3.0) * (1.0 + 0.25 * values)))
    return jnp.where(values > -0.02, near, 1.0 - jnp.exp(values))


def after(value, *earlier):
    return lax.optimization_barrier((value,) + earlier)[0]


def line_gather(mine, axis, size):
    place = lax.axis_index(axis)
    width = mine.shape[1]
    right, left = mine, mine
    rights, lefts = {}, {}
    for step in range(1, size):
        right = lax.ppermute(right, axis, [(i, i + 1) for i in range(step - 1, size - 1)])
        left = lax.ppermute(left, axis, [(i + 1, i) for i in range(size - step)])
        rights[step], lefts[step] = right, left
    whole = jnp.zeros((mine.shape[0], size * width), mine.dtype)
    for step in range(size):
        block = mine if step == 0 else lefts[step] + rights[size - step]
        spot = lax.rem(place + step, size) * width
        whole = lax.dynamic_update_slice_in_dim(whole, block, spot, 1)
    return whole


def line_scatter(part, axis, size):
    place = lax.axis_index(axis)
    width = part.shape[1] // size

    def block(index):
        spot = jnp.clip(index, 0, size - 1) * width
        return lax.dynamic_slice_in_dim(part, spot, width, 1).astype(F32)

    right, left = None, None
    for step in range(1, size):
        going = block(size - step + place)
        if right is not None:
            going = going + right.astype(F32)
        right = lax.ppermute(going.astype(BF16), axis, [(i, i + 1) for i in range(step)])
        going = block(place - (size - step))
        if left is not None:
            going = going + left.astype(F32)
        left = lax.ppermute(
            going.astype(BF16), axis, [(i, i - 1) for i in range(size - step, size)]
        )
    return block(place) + right.astype(F32) + left.astype(F32)


def line_sum(value, axis, size):
    bit = 1
    while bit < size:
        value = value + lax.ppermute(value, axis, [(i, i ^ bit) for i in range(size)])
        bit *= 2
    return value


def pair_gather(mine, axis, size):
    place = lax.axis_index(axis)
    bit = 1
    while bit < size:
        other = lax.ppermute(mine, axis, [(i, i ^ bit) for i in range(size)])
        upper = (place & bit) != 0
        mine = jnp.concatenate(
            [jnp.where(upper, other, mine), jnp.where(upper, mine, other)], axis=0
        )
        bit *= 2
    return mine


def pair_scatter(part, axis, size):
    place = lax.axis_index(axis)
    part = part.astype(F32)
    bit = size // 2
    while bit >= 1:
        upper = (place & bit) != 0
        low, high = jnp.split(part, 2, axis=0)
        going = jnp.where(upper, low, high).astype(BF16)
        came = lax.ppermute(going, axis, [(i, i ^ bit) for i in range(size)])
        part = jnp.where(upper, high, low) + came.astype(F32)
        bit //= 2
    return part


def swap(size, bit):
    return [(i, i ^ bit) for i in range(size)]


def cross(size):
    return [(i, i ^ 4 if i % 2 == 0 else i ^ 2) for i in range(size)]


def square_gather(mine, axis, size):
    if size != 8:
        return pair_gather(mine, axis, size)
    place = lax.axis_index(axis)
    rows = mine.shape[0]
    by_x = lax.ppermute(mine, axis, swap(size, 2))
    by_y = lax.ppermute(mine, axis, swap(size, 4))
    onward = jnp.where((place & 1) == 0, by_x, by_y)
    far = lax.ppermute(onward, axis, cross(size))
    held = {0: mine, 2: by_x, 4: by_y, 6: far}
    for bits in (0, 2, 4, 6):
        held[bits + 1] = lax.ppermute(held[bits], axis, swap(size, 1))
    whole = jnp.zeros((size * rows,) + mine.shape[1:], mine.dtype)
    for bits, block in held.items():
        whole = lax.dynamic_update_slice_in_dim(whole, block, (place ^ bits) * rows, 0)
    return whole


def square_scatter(part, axis, size):
    if size != 8:
        return pair_scatter(part, axis, size)
    place = lax.axis_index(axis)
    core = place & 1
    chip = lax.shift_right_logical(place, 1)
    split = part.reshape(size // 2, 2, part.shape[0] // size, part.shape[1])
    going = lax.dynamic_index_in_dim(split, 1 - core, 1, keepdims=False)
    came = lax.ppermute(going, axis, swap(size, 1))
    kept = lax.dynamic_index_in_dim(split, core, 1, keepdims=False)
    both = (kept.astype(F32) + came.astype(F32)).astype(BF16)

    def pick(index):
        return lax.dynamic_index_in_dim(both, index, 0, keepdims=False)

    far = lax.ppermute(pick(chip ^ 3), axis, cross(size)).astype(F32)
    none = jnp.zeros((), F32)
    to_x = pick(chip ^ 1).astype(F32) + jnp.where(core == 0, far, none)
    to_y = pick(chip ^ 2).astype(F32) + jnp.where(core == 1, far, none)
    by_x = lax.ppermute(to_x.astype(BF16), axis, swap(size, 2))
    by_y = lax.ppermute(to_y.astype(BF16), axis, swap(size, 4))
    return pick(chip).astype(F32) + by_x.astype(F32) + by_y.astype(F32)


def tile_loop(count, body):
    lax.fori_loop(0, count, lambda i, c: (body(i), c)[1], 0)


def rows_at(index, size):
    return pl.ds(pl.multiple_of(index * size, size), size)


def rnn_forward_kernel(
    both_ref, halo_ref, start_ref, mask_ref, gates_ref, params_ref,
    mixed_ref, conv_ref, r_ref, i_ref, state_ref, end_ref,
    padded, high, low,
):
    count, width = conv_ref.shape
    tiles = count // RNN_TILE
    padded[0:8, :] = halo_ref[...]
    padded[8:, :] = both_ref[:, 0:width]

    def convolve(t):
        span = padded[pl.ds(pl.multiple_of(t * RNN_TILE, RNN_TILE), RNN_TILE + 8), :]
        mask = mask_ref[rows_at(t, RNN_TILE), :]
        conv = params_ref[0:1, :] * span[8:, :] + params_ref[TAPS : TAPS + 1, :]
        for k in range(1, TAPS):
            moved = span[8 - k : 8 - k + RNN_TILE, :]
            conv = conv + params_ref[k : k + 1, :] * (moved * mask[:, k : k + 1])
        conv_ref[rows_at(t, RNN_TILE), :] = conv
        top = conv.astype(BF16)
        high[rows_at(t, RNN_TILE), :] = top
        low[rows_at(t, RNN_TILE), :] = (conv - top.astype(F32)).astype(BF16)

    tile_loop(tiles, convolve)

    block = min(256, count)

    def gate(t):
        rows = rows_at(t, block)
        weights = gates_ref[...]
        both = jnp.dot(high[rows, :], weights, preferred_element_type=F32)
        both = both + jnp.dot(low[rows, :], weights, preferred_element_type=F32)
        r_ref[rows, :] = both[:, 0:width]
        i_ref[rows, :] = both[:, width:]

    tile_loop(count // block, gate)

    strength = DECAY_SCALE * jax.nn.softplus(-params_ref[TAPS + 3 : TAPS + 4, :])

    place = lax.broadcasted_iota(jnp.int32, (8, width), 0)

    def advance(t, carry):
        rows = rows_at(t, RNN_TILE)
        keep = mask_ref[rows, :][:, 0:1]
        r = jax.nn.sigmoid(r_ref[rows, :] + params_ref[TAPS + 1 : TAPS + 2, :])
        i = jax.nn.sigmoid(i_ref[rows, :] + params_ref[TAPS + 2 : TAPS + 3, :])
        log_a = -strength * r
        scale = jnp.sqrt(jnp.maximum(one_less_exp(2.0 * log_a), ROOT_FLOOR))
        scale = jnp.where(keep > 0.0, scale, 1.0)
        decay = jnp.exp(log_a) * keep
        drive = scale * i * conv_ref[rows, :]
        r_ref[rows, :] = r
        i_ref[rows, :] = i
        states = []
        for g in range(0, RNN_TILE, 8):
            a, held = decay[g : g + 8, :], drive[g : g + 8, :]
            for s in (1, 2, 4):
                inside = place >= s
                held = held + a * jnp.where(inside, pltpu.roll(held, s, 0), 0.0)
                a = a * jnp.where(inside, pltpu.roll(a, s, 0), 1.0)
            held = held + a * carry
            carry = jnp.broadcast_to(held[7:8, :], (8, width))
            states.append(held)
        state = jnp.concatenate(states, axis=0)
        state_ref[rows, :] = state
        mixed_ref[rows, :] = (state * gelu(both_ref[rows, width:])).astype(BF16)
        return carry

    carry = jnp.broadcast_to(start_ref[0:1, :], (8, width))
    end_ref[...] = lax.fori_loop(0, tiles, advance, carry)


def rnn_forward(both, halo, start, mask, gates, params):
    count, width = both.shape[0], both.shape[1] // 2
    full = jax.ShapeDtypeStruct((count, width), F32)
    return pl.pallas_call(
        rnn_forward_kernel,
        out_shape=(
            jax.ShapeDtypeStruct((count, width), BF16),
            full, full, full, full,
            jax.ShapeDtypeStruct((8, width), F32),
        ),
        scratch_shapes=[
            pltpu.VMEM((count + 8, width), F32),
            pltpu.VMEM((count, width), BF16),
            pltpu.VMEM((count, width), BF16),
        ],
        compiler_params=pltpu.CompilerParams(vmem_limit_bytes=VMEM_BYTES),
        cost_estimate=pl.CostEstimate(
            flops=4 * count * width * 2 * width, bytes_accessed=count * width * 30,
            transcendentals=count * width * 6,
        ),
        name="rnn_forward",
    )(both, halo, start, mask, gates, params)


def rnn_backward_kernel(
    gm_ref, both_ref, halo_ref, start_ref, conv_ref, r_ref, i_ref, state_ref, mask_ref,
    gates_ref, params_ref, back_ref, tail_ref,
    grads_ref, rates_ref, dparams_ref, back_out_ref, tail_out_ref, dots_ref,
    padded, before, dconv, sums,
):
    count, width = conv_ref.shape
    tiles = count // RNN_TILE
    padded[0:8, :] = halo_ref[...]
    padded[8:, :] = both_ref[:, 0:width]
    before[0:8, :] = start_ref[...]
    before[8:, :] = state_ref[...]
    strength = DECAY_SCALE * jax.nn.softplus(-params_ref[TAPS + 3 : TAPS + 4, :])

    sums[...] = jnp.zeros_like(sums)
    place = lax.broadcasted_iota(jnp.int32, (8, width), 0)

    def fold(values):
        return jnp.sum(values.reshape(-1, 8, width), axis=0)

    def chain(t, carry):
        later, later_decay = carry
        base = pl.multiple_of((tiles - 1 - t) * RNN_TILE, RNN_TILE)
        rows = pl.ds(base, RNN_TILE)
        keep = mask_ref[rows, :][:, 0:1]
        gm = gm_ref[rows, :]
        value, slope = gelu_and_slope(both_ref[rows, width:])
        grads_ref[rows, width:] = (gm * state_ref[rows, :] * slope).astype(BF16)
        given = gm * value
        r, i, conv = r_ref[rows, :], i_ref[rows, :], conv_ref[rows, :]
        fall = jnp.exp(-strength * r) * keep
        adjoints = []
        for g in reversed(range(0, RNN_TILE, 8)):
            a = fall[g : g + 8, :]
            ahead = jnp.where(place == 7, later_decay, pltpu.roll(a, 7, 0))
            held = given[g : g + 8, :]
            for s in (1, 2, 4):
                inside = place < 8 - s
                held = held + ahead * jnp.where(inside, pltpu.roll(held, 8 - s, 0), 0.0)
                ahead = ahead * jnp.where(inside, pltpu.roll(ahead, 8 - s, 0), 1.0)
            held = held + ahead * later
            later = jnp.broadcast_to(held[0:1, :], (8, width))
            later_decay = jnp.broadcast_to(a[0:1, :], (8, width))
            adjoints.append(held)
        a = jnp.concatenate(adjoints[::-1], axis=0)
        prior = before[pl.ds(base, RNN_TILE + 8), :][7 : 7 + RNN_TILE, :]
        room = one_less_exp(-2.0 * strength * r)
        bound = jnp.maximum(room, ROOT_FLOOR)
        inverse = lax.rsqrt(bound)
        scale = jnp.where(keep > 0.0, bound * inverse, 1.0)
        open_ = jnp.where(room > ROOT_FLOOR, inverse, 0.0)
        driven = a * i
        dlog = fall * (a * prior - fall * driven * conv * open_)
        common = a * scale
        drec = dlog * (-strength) * r * (1.0 - r)
        dinp = common * conv * i * (1.0 - i)
        rates_ref[rows, 0:width] = drec.astype(BF16)
        rates_ref[rows, width:] = dinp.astype(BF16)
        dconv[rows, :] = common * i
        sums[5] += fold(drec)
        sums[6] += fold(dinp)
        sums[7] += fold(dlog * r)
        return later, later_decay

    later = jnp.broadcast_to(back_ref[0:1, :], (8, width))
    later, later_decay = lax.fori_loop(
        0, tiles, chain, (later, jnp.ones((8, width), F32))
    )
    back_out_ref[...] = later * later_decay

    block = min(256, count)

    def spread(t):
        rows = rows_at(t, block)
        dconv[rows, :] += lax.dot_general(
            rates_ref[rows, :], gates_ref[...], (((1,), (1,)), ((), ())),
            preferred_element_type=F32,
        )

    tile_loop(count // block, spread)
    dconv[count:, :] = tail_ref[...]
    tail_out_ref[...] = dconv[0:8, :]

    def unconvolve(t):
        base = pl.multiple_of(t * RNN_TILE, RNN_TILE)
        rows = pl.ds(base, RNN_TILE)
        span = dconv[pl.ds(base, RNN_TILE + 8), :]
        mask = mask_ref[pl.ds(base, RNN_TILE + 8), :]
        source = padded[pl.ds(base, RNN_TILE + 8), :]
        here = span[0:RNN_TILE, :]
        out = params_ref[0:1, :] * here
        sums[0] += fold(here * source[8:, :])
        sums[4] += fold(here)
        for k in range(1, TAPS):
            kept = span * mask[:, k : k + 1]
            out = out + params_ref[k : k + 1, :] * kept[k : k + RNN_TILE, :]
            sums[k] += fold(kept[0:RNN_TILE, :] * source[8 - k : 8 - k + RNN_TILE, :])
        grads_ref[rows, 0:width] = out.astype(BF16)
        dot = jnp.sum(
            out * source[8:, :] + grads_ref[rows, width:].astype(F32) * both_ref[rows, width:],
            axis=1, keepdims=True,
        )
        dots_ref[rows, :] = jnp.broadcast_to(dot, (RNN_TILE, 128))

    tile_loop(tiles, unconvolve)
    for k in range(8):
        dparams_ref[k : k + 1, :] = jnp.sum(sums[k], axis=0, keepdims=True)
    dparams_ref[TAPS + 3 : TAPS + 4, :] = (
        DECAY_SCALE
        * jax.nn.sigmoid(-params_ref[TAPS + 3 : TAPS + 4, :])
        * jnp.sum(sums[TAPS + 3], axis=0, keepdims=True)
    )


def rnn_backward(gm, both, halo, start, saved, mask, gates, params, back, tail):
    conv, r, i, state = saved
    count, width = conv.shape
    return pl.pallas_call(
        rnn_backward_kernel,
        out_shape=(
            jax.ShapeDtypeStruct((count, 2 * width), BF16),
            jax.ShapeDtypeStruct((count, 2 * width), BF16),
            jax.ShapeDtypeStruct((8, width), F32),
            jax.ShapeDtypeStruct((8, width), F32),
            jax.ShapeDtypeStruct((8, width), F32),
            jax.ShapeDtypeStruct((count, 128), F32),
        ),
        scratch_shapes=[
            pltpu.VMEM((count + 8, width), F32),
            pltpu.VMEM((count + 8, width), F32),
            pltpu.VMEM((count + 8, width), F32),
            pltpu.VMEM((8, 8, width), F32),
        ],
        compiler_params=pltpu.CompilerParams(vmem_limit_bytes=VMEM_BYTES),
        cost_estimate=pl.CostEstimate(
            flops=2 * count * width * 2 * width, bytes_accessed=count * width * 36,
            transcendentals=count * width * 6,
        ),
        name="rnn_backward",
    )(gm, both, halo, start, conv, r, i, state, mask, gates, params, back, tail)


MESH = pl.DeviceIdType.MESH


class Spread:
    def __init__(self, place, size, blocks, sent, came):
        self.place, self.size = place, size
        self.blocks, self.sent, self.came = blocks, sent, came

    def copy(self, slot, j, way, k):
        ref = self.blocks.at[slot, j]
        return pltpu.make_async_remote_copy(
            src_ref=ref, dst_ref=ref, send_sem=self.sent.at[slot, k],
            recv_sem=self.came.at[slot, j], device_id={"mp": self.place + way},
            device_id_type=MESH,
        )

    def moves(self, s):
        z, n = self.place, self.size
        return (
            ((z - s >= 0) & (z < n - 1), z - s, 1, 2 * s),
            ((z + s <= n - 1) & (z > 0), z + s, -1, 2 * s + 1),
        )

    def step(self, slot, s):
        for valid, j, way, k in self.moves(s):

            @pl.when(valid)
            def _(j=j, way=way, k=k):
                copy = self.copy(slot, j, way, k)
                if s > 0:
                    copy.wait_recv()
                copy.start()

    def finish(self, slot):
        z, n = self.place, self.size

        @pl.when(z == 0)
        def _():
            for j in range(1, n):
                self.copy(slot, j, 1, 0).wait_recv()

        @pl.when(z == n - 1)
        def _():
            for j in range(n - 1):
                self.copy(slot, j, -1, 0).wait_recv()

    def drain(self, slot):
        for s in range(self.size - 1):
            for valid, j, way, k in self.moves(s):

                @pl.when(valid)
                def _(j=j, way=way, k=k):
                    self.copy(slot, j, way, k).wait_send()


class Fold:
    def __init__(self, place, size, parts, rights, lefts, sent, came_right, came_left):
        self.place, self.size = place, size
        self.parts, self.rights, self.lefts = parts, rights, lefts
        self.sent, self.came_right, self.came_left = sent, came_right, came_left

    def right(self, slot, j, k):
        return pltpu.make_async_remote_copy(
            src_ref=self.parts.at[slot, j], dst_ref=self.rights.at[slot, k],
            send_sem=self.sent.at[slot, j], recv_sem=self.came_right.at[slot, k],
            device_id={"mp": self.place + 1}, device_id_type=MESH,
        )

    def left(self, slot, j, k):
        return pltpu.make_async_remote_copy(
            src_ref=self.parts.at[slot, j], dst_ref=self.lefts.at[slot, k],
            send_sem=self.sent.at[slot, j], recv_sem=self.came_left.at[slot, k],
            device_id={"mp": self.place - 1}, device_id_type=MESH,
        )

    def clear(self):
        for slot in range(self.parts.shape[0]):
            last = self.size - 2
            blank = jnp.zeros(self.rights.shape[2:], BF16)
            self.rights[slot, last] = blank
            self.lefts[slot, last] = blank

    def start(self, slot):
        z, n = self.place, self.size

        @pl.when(z == 0)
        def _():
            for j in reversed(range(1, n)):
                self.right(slot, j, n - 1 - j).start()

        @pl.when(z == n - 1)
        def _():
            for j in range(n - 1):
                self.left(slot, j, j).start()

    def step(self, slot, s):
        z, n = self.place, self.size
        back = n - 1 - z

        @pl.when((z >= 1) & (z <= n - 2) & (s >= z))
        def _():
            j = n - 1 + z - s
            self.right(slot, j, s - 1).wait_recv()
            self.add(slot, j, self.rights, s - 1)
            self.right(slot, j, s).start()

        @pl.when((back >= 1) & (back <= n - 2) & (s >= back))
        def _():
            j = s - back
            self.left(slot, j, s - 1).wait_recv()
            self.add(slot, j, self.lefts, s - 1)
            self.left(slot, j, s).start()

    def add(self, slot, j, came, k):
        self.parts[slot, j] = (
            self.parts[slot, j].astype(F32) + came[slot, k].astype(F32)
        ).astype(BF16)

    def finish(self, slot):
        z, n = self.place, self.size

        @pl.when(z >= 1)
        def _():
            self.right(slot, z, n - 2).wait_recv()

        @pl.when(z <= n - 2)
        def _():
            self.left(slot, z, n - 2).wait_recv()

    def total(self, slot, rows):
        z, n = self.place, self.size
        return (
            self.parts[slot, z, rows, :].astype(F32)
            + self.rights[slot, n - 2, rows, :].astype(F32)
            + self.lefts[slot, n - 2, rows, :].astype(F32)
        )

    def drain(self, slot):
        for j in range(self.size):

            @pl.when(j != self.place)
            def _(j=j):
                self.right(slot, j, 0).wait_send()


def partners(d):
    core, x, y = lax.rem(d, 2), lax.rem(lax.div(d, 2), 2), lax.div(d, 4)
    return core, d + 1 - 2 * core, d + 2 - 4 * x, d + 4 - 8 * y


class Square:
    def __init__(self, d, shard, whole, sent, came, own, axis=0):
        self.d, self.shard, self.whole, self.axis = d, shard, whole, axis
        self.sent, self.came, self.own = sent, came, own
        self.core, self.by_core, self.by_x, self.by_y = partners(d)

    def rows(self, d):
        count = self.shard.shape[self.axis]
        window = pl.ds(pl.multiple_of(d * count, count), count)
        return self.whole.at[:, window] if self.axis else self.whole.at[window, :]

    def copy(self, src, origin, target, sent, came):
        return pltpu.make_async_remote_copy(
            src_ref=src, dst_ref=self.rows(origin), send_sem=self.sent.at[sent],
            recv_sem=self.came.at[came], device_id={"dp": target}, device_id_type=MESH,
        )

    def local(self):
        return pltpu.make_async_copy(self.shard, self.rows(self.d), self.own)

    def far(self):
        return partners(self.by_x)[3]

    def first(self):
        return (
            self.copy(self.shard, self.d, self.by_x, 0, 2),
            self.copy(self.shard, self.d, self.by_y, 1, 4),
            self.copy(self.shard, self.d, self.by_core, 2, 1),
        )

    def start(self):
        for copy in self.first():
            copy.start()
        self.local().start()

    def step_one(self):
        x_rows, y_rows = self.rows(self.by_x), self.rows(self.by_y)
        by_x = self.copy(x_rows, self.by_x, self.by_core, 3, 2)
        by_y = self.copy(y_rows, self.by_y, self.by_core, 4, 4)
        by_x.wait_recv()

        @pl.when(self.core == 0)
        def _():
            self.copy(x_rows, self.by_x, self.by_y, 5, 6).start()

        self.copy(x_rows, self.by_x, self.by_core, 3, 3).start()
        by_y.wait_recv()

        @pl.when(self.core == 1)
        def _():
            self.copy(y_rows, self.by_y, self.by_x, 5, 6).start()

        self.copy(y_rows, self.by_y, self.by_core, 4, 5).start()

    def step_two(self):
        far = self.far()
        rows = self.rows(far)
        self.copy(rows, far, self.by_core, 6, 6).wait_recv()
        self.copy(rows, far, self.by_core, 6, 7).start()

    def finish(self):
        for k in (1, 3, 5, 7):
            self.copy(self.shard, self.d, self.by_core, 0, k).wait_recv()
        self.local().wait()

    def drain(self):
        for k in range(7):
            self.copy(self.shard, self.d, self.by_core, k, 0).wait_send()


class Scatter:
    def __init__(self, d, count, compute, held, far, first, second, sent, came):
        self.d, self.count, self.compute = d, count, compute
        self.held, self.far_in, self.first_in, self.second_in = held, far, first, second
        self.sent, self.came = sent, came
        self.core, self.by_core, by_x, by_y = partners(d)
        even = self.core == 0
        self.first = jnp.where(even, by_y, by_x)
        self.second = jnp.where(even, by_x, by_y)
        self.first_at, self.second_at = 2 - self.core, 1 + self.core
        other = partners(self.by_core)
        self.away = (self.by_core, other[2], other[3], partners(other[2])[3])
        self.distant = partners(by_x)[3]

    def owners(self):
        return [self.away[k] for k in (3, 1, 2, 0)] + [
            self.distant, self.first, self.d, self.second
        ]

    def copy(self, src, dst, target, sent, came):
        return pltpu.make_async_remote_copy(
            src_ref=src, dst_ref=dst, send_sem=self.sent.at[sent], recv_sem=self.came.at[came],
            device_id={"dp": target}, device_id_type=MESH,
        )

    def to_core(self, buffer, k):
        return self.copy(buffer, self.held(k), self.by_core, k, k)

    def to_far(self):
        return self.copy(self.held(3), self.far_in, self.first, 4, 4)

    def to_first(self):
        return self.copy(self.held(self.first_at), self.first_in, self.first, 5, 5)

    def to_second(self):
        return self.copy(self.held(self.second_at), self.second_in, self.second, 6, 6)

    def far_core(self, buffers, sending):
        for slot, k in enumerate((3, 1, 2, 0)):
            if sending[slot] is not None:
                sending[slot].wait_send()
            self.compute(self.away[k], buffers[slot], False)
            copy = self.to_core(buffers[slot], k)
            copy.start()
            sending[slot] = copy

    def add_block(self, k, came, owner):
        self.copy(self.held(k), self.held(k), self.by_core, k, came).wait_recv()
        self.compute(owner, self.held(k), True)

    def near_core(self):
        self.add_block(3, 3, self.distant)
        self.to_far().start()
        self.add_block(self.first_at, self.first_at, self.first)
        self.to_first().start()
        self.add_block(0, 0, self.d)
        self.add_block(self.second_at, self.second_at, self.second)

    def onward(self):
        self.to_far().wait_recv()
        held = self.held(self.second_at)

        def body(t):
            rows = rows_at(t, 32)
            held[rows, :] = (
                held[rows, :].astype(F32) + self.far_in[rows, :].astype(F32)
            ).astype(BF16)

        tile_loop(self.count // 32, body)
        self.to_second().start()

    def finish(self, target):
        self.to_first().wait_recv()
        self.to_second().wait_recv()
        held = self.held(0)

        def body(t):
            rows = rows_at(t, 32)
            target[rows, :] = (
                held[rows, :].astype(F32)
                + self.first_in[rows, :].astype(F32)
                + self.second_in[rows, :].astype(F32)
            )

        tile_loop(self.count // 32, body)

    def drain(self):
        self.to_far().wait_send()
        self.to_first().wait_send()
        self.to_second().wait_send()


def head_kernel(dp, mp, names, *refs):
    ref = dict(zip(names, refs))
    blocks, w_in, norm, both = ref["blocks"], ref["w_in_here"], ref["norm"], ref["both_here"]
    chunks, _, step, part = blocks.shape
    features, width = part * mp, ref["mixed_here"].shape[2]
    z, d = lax.axis_index("mp"), lax.axis_index("dp")
    square = dp == 8
    gather = Spread(z, mp, blocks, ref["spread_sent"], ref["spread_came"])

    barrier = pltpu.get_barrier_semaphore()

    @pl.when(z > 0)
    def _():
        pl.semaphore_signal(barrier, inc=1, device_id={"mp": z - 1}, device_id_type=MESH)

    @pl.when(z < mp - 1)
    def _():
        pl.semaphore_signal(barrier, inc=1, device_id={"mp": z + 1}, device_id_type=MESH)

    count = jnp.where((z > 0) & (z < mp - 1), 2, 1)
    if square:
        for other in partners(d)[1:]:
            pl.semaphore_signal(barrier, inc=1, device_id={"dp": other}, device_id_type=MESH)
        count = count + 3

    def chunk_rows(c):
        return pl.ds(c * step, step)

    def own_block(c):
        return pltpu.make_async_copy(
            ref["x"].at[chunk_rows(c), :], blocks.at[c, z], ref["load_sem"].at[c]
        )

    for c in range(chunks):
        own_block(c).start()
    pl.semaphore_wait(barrier, count)

    wholes = (
        ("gates_shard", ref["gates_here"], 0),
        ("rnn_in", w_in.at[:, pl.ds(0, width)], 0),
        ("branch_gate", w_in.at[:, pl.ds(width, width)], 0),
        ("rnn_out", ref["w_out"], 1),
        ("mlp_gate", ref["w_gate"], 0),
    )
    if square:
        squares = [
            Square(
                d, ref[name], whole, ref["square_sent"].at[k], ref["square_came"].at[k],
                ref["square_own"].at[k], axis,
            )
            for k, (name, whole, axis) in enumerate(wholes)
        ]
        for item in squares[:3]:
            item.start()
    else:
        loads = [
            pltpu.make_async_copy(ref[name], whole, ref["square_own"].at[k])
            for k, (name, whole, _) in enumerate(wholes)
        ]
        for item in loads:
            item.start()

    def begin(c):
        own_block(c).wait()
        gather.step(c, 0)

    begin(0)
    if chunks > 1:
        begin(1)

    def expand():
        span = ref["gates_flat"].shape[0]
        rows = span // 8
        for k in range(8):
            ref["gates_flat"][k * rows : (k + 1) * rows, :] = ref["gates_here"][
                k * 32 : k * 32 + 32, :
            ].astype(F32)[0:rows, :]
        column = lax.broadcasted_iota(jnp.int32, (span, 2 * width), 1)
        column = jnp.where(column >= width, column - width, column)
        for b in range(width // span):
            inside = (column >= b * span) & (column < (b + 1) * span)
            ref["dense_here"][b * span : (b + 1) * span, :] = jnp.where(
                inside, ref["gates_flat"][...], 0.0
            ).astype(BF16)

    stores = (
        ("norm", "norm"), ("both", "both_here"), ("conv", "conv_here"), ("r", "r_here"),
        ("i", "i_here"), ("state", "state_here"), ("mixed", "mixed_here"), ("s1", "s1_here"),
    )

    def store_all(c):
        return [
            pltpu.make_async_copy(
                ref[near].at[c % 2], ref[far + "_out"].at[chunk_rows(c), :],
                ref["store_sem"].at[c % 2, k],
            )
            for k, (far, near) in enumerate(stores)
        ]

    ref["halo"][...] = jnp.zeros_like(ref["halo"])
    ref["start"][...] = jnp.zeros_like(ref["start"])

    def compute(c):
        slot = c % 2
        if c > 1:
            for copy in store_all(c - 2):
                copy.wait()

        def body(t):
            rows = rows_at(t, TILE)
            values = [blocks[c, j, rows, :].astype(F32) for j in range(mp)]
            total = sum(jnp.sum(v * v, axis=1, keepdims=True) for v in values)
            s1 = lax.rsqrt(total / features + EPS)
            for j in range(mp):
                cols = slice(j * part, (j + 1) * part)
                norm[slot, rows, cols] = (values[j] * s1 * ref["gains"][0:1, cols]).astype(BF16)
            ref["s1_here"][slot, rows, :] = jnp.broadcast_to(s1, (TILE, 128))

        tile_loop(step // TILE, body)
        for k in range(2):
            cols = slice(k * width, (k + 1) * width)
            both[slot, :, cols] = matmul(norm[slot], w_in[:, cols])
        rnn_forward_kernel(
            both.at[slot], ref["halo"], ref["start"], ref["mask"].at[chunk_rows(c), :],
            ref["dense_here"], ref["params"],
            ref["mixed_here"].at[slot], ref["conv_here"].at[slot], ref["r_here"].at[slot],
            ref["i_here"].at[slot], ref["state_here"].at[slot], ref["end"],
            ref["padded"], ref["high"], ref["low"],
        )
        ref["halo"][...] = both[slot, step - 8 :, 0:width]
        ref["start"][...] = ref["end"][...]
        for copy in store_all(c):
            copy.start()

    for s in range(1, mp - 1):
        gather.step(0, s)
        if s == 1 and chunks > 2:
            begin(2)
    if square:
        for item in squares[:3]:
            item.step_one()
        for item in squares[3:]:
            item.start()
        for item in squares[:3]:
            item.step_two()
    gather.finish(0)
    for c in range(chunks):
        if c + 1 < chunks:
            gather.step(c + 1, 1)
        if c == 0:
            if square:
                for item in squares[:3]:
                    item.finish()
            else:
                for item in loads:
                    item.wait()
            expand()
            pass_on = [
                pltpu.make_async_copy(w_in, ref["w_in"], ref["pass_sem"].at[0]),
                pltpu.make_async_copy(ref["dense_here"], ref["dense"], ref["pass_sem"].at[1]),
            ]
            for copy in pass_on:
                copy.start()
        if c + 3 < chunks:
            begin(c + 3)
        compute(c)
        if square and (c + 1) * 4 == chunks:
            squares[3].step_one()
        if square and (c + 1) * 2 == chunks:
            squares[3].step_two()
            squares[4].step_one()
        if square and (c + 1) * 4 == 3 * chunks:
            squares[4].step_two()
        if c + 1 < chunks:
            for s in range(2, mp - 1):
                gather.step(c + 1, s)
            gather.finish(c + 1)
    if square:
        squares[3].finish()
        squares[4].finish()
        for item in squares:
            item.drain()
    for copy in pass_on:
        copy.wait()
    for c in range(max(0, chunks - 2), chunks):
        for copy in store_all(c):
            copy.wait()
    for c in range(chunks):
        gather.drain(c)


def head(
    dp, mp, chunks, x, gains, params, mask, rnn_in, branch_gate, rnn_out, mlp_gate, gates_shard,
    span,
):
    count, part = x.shape
    features, width = part * mp, params.shape[1]
    step = count // chunks
    dma = pltpu.SemaphoreType.DMA
    any_, vmem = pl.BlockSpec(memory_space=pl.ANY), pl.BlockSpec(memory_space=pltpu.VMEM)
    ins = [
        ("x", x, any_), ("gains", gains, vmem), ("params", params, vmem), ("mask", mask, vmem),
        ("rnn_in", rnn_in, any_), ("branch_gate", branch_gate, any_), ("rnn_out", rnn_out, any_),
        ("mlp_gate", mlp_gate, any_), ("gates_shard", gates_shard, any_),
    ]
    gate_width = mlp_gate.shape[1]
    shape = jax.ShapeDtypeStruct
    outs = [
        ("w_in", shape((features, 2 * width), BF16)), ("w_out", shape((width, features), BF16)),
        ("w_gate", shape((features, gate_width), BF16)), ("dense", shape((width, 2 * width), BF16)), ("norm_out", shape((count, features), BF16)),
        ("both_out", shape((count, 2 * width), F32)), ("conv_out", shape((count, width), F32)),
        ("r_out", shape((count, width), F32)), ("i_out", shape((count, width), F32)),
        ("state_out", shape((count, width), F32)), ("mixed_out", shape((count, width), BF16)),
        ("s1_out", shape((count, 128), F32)),
    ]
    wide = pltpu.VMEM((2, step, width), F32)
    scratch = [
        ("blocks", pltpu.VMEM((chunks, mp, step, part), BF16)),
        ("w_in_here", pltpu.VMEM((features, 2 * width), BF16)),
        ("gates_here", pltpu.VMEM((256, 2 * width), BF16)),
        ("gates_flat", pltpu.VMEM((span, 2 * width), F32)),
        ("dense_here", pltpu.VMEM((width, 2 * width), BF16)),
        ("norm", pltpu.VMEM((2, step, features), BF16)),
        ("both_here", pltpu.VMEM((2, step, 2 * width), F32)),
        ("conv_here", wide), ("r_here", wide), ("i_here", wide), ("state_here", wide),
        ("mixed_here", pltpu.VMEM((2, step, width), BF16)),
        ("s1_here", pltpu.VMEM((2, step, 128), F32)),
        ("halo", pltpu.VMEM((8, width), F32)), ("start", pltpu.VMEM((8, width), F32)),
        ("end", pltpu.VMEM((8, width), F32)),
        ("padded", pltpu.VMEM((step + 8, width), F32)),
        ("high", pltpu.VMEM((step, width), BF16)), ("low", pltpu.VMEM((step, width), BF16)),
        ("spread_sent", dma((chunks, 2 * mp))), ("spread_came", dma((chunks, mp))),
        ("square_sent", dma((5, 8))), ("square_came", dma((5, 8))), ("square_own", dma((5,))),
        ("load_sem", dma((chunks,))), ("store_sem", dma((2, 8))), ("pass_sem", dma((2,))),
    ]
    names = [i[0] for i in ins] + [o[0] for o in outs] + [k[0] for k in scratch]
    return pl.pallas_call(
        functools.partial(head_kernel, dp, mp, tuple(names)),
        in_specs=[i[2] for i in ins],
        out_specs=[any_] * len(outs),
        out_shape=[o[1] for o in outs],
        scratch_shapes=[k[1] for k in scratch],
        compiler_params=pltpu.CompilerParams(
            collective_id=2, has_side_effects=True, vmem_limit_bytes=60 * 1024 * 1024
        ),
        name="head",
    )(*[i[1] for i in ins])


MIDDLE_ORDER = (
    ("d", 0, 0), ("d", 0, 1), ("d", 1, 1), ("A", 0, 0), ("a", 1, 0), ("d", 1, 0), ("a", 2, 0),
    ("A", 0, 1), ("d", 2, 0), ("d", 2, 1), ("a", 1, 1), ("J", 0, 0), ("S", 1, 0), ("e", 0, 0),
    ("a", 2, 1), ("S", 2, 0), ("e", 1, 0), ("e", 2, 0), ("d", 0, 2), ("d", 0, 3), ("J", 0, 1),
    ("S", 3, 0), ("e", 0, 1), ("e", 3, 0), ("d", 1, 2), ("d", 1, 3), ("A", 0, 2), ("d", 3, 0),
    ("a", 1, 2), ("e", 1, 1), ("H", 0, 0), ("G", 0, 0), ("d", 2, 2), ("a", 2, 2), ("e", 2, 1),
    ("c", 1, 0), ("d", 2, 3), ("O", 0, 0), ("b", 1, 0), ("J", 0, 2), ("e", 3, 1), ("e", 0, 2),
    ("d", 3, 1), ("c", 2, 0), ("A", 0, 3), ("d", 3, 3), ("H", 0, 1), ("e", 1, 2), ("a", 1, 3),
    ("K", 0, 0), ("G", 0, 1), ("a", 2, 3), ("f", 1, 0), ("c", 1, 1), ("e", 2, 2), ("e", 3, 2),
    ("J", 0, 3), ("e", 0, 3), ("O", 0, 1), ("f", 2, 0), ("d", 3, 2), ("b", 2, 0), ("H", 0, 2),
    ("c", 2, 1), ("b", 1, 1), ("Y", 0, 0), ("e", 1, 3), ("B", 0, 0), ("K", 0, 1), ("e", 2, 3),
    ("G", 0, 2), ("b", 2, 1), ("e", 3, 3), ("f", 1, 1), ("O", 0, 2), ("c", 1, 2), ("H", 0, 3),
    ("Y", 0, 1), ("f", 2, 1), ("c", 2, 2), ("B", 0, 1), ("G", 0, 3), ("K", 0, 2), ("b", 1, 2),
    ("O", 0, 3), ("D", 0, 0), ("c", 1, 3), ("D", 0, 1), ("c", 2, 3), ("W", 0, 0), ("D", 0, 2),
    ("Z", 0, 0), ("f", 1, 2), ("W", 0, 1), ("b", 2, 2), ("D", 0, 3), ("f", 2, 2), ("K", 0, 3),
    ("Z", 0, 1), ("b", 1, 3), ("W", 0, 2), ("D", 0, 4), ("W", 0, 3), ("Z", 0, 2), ("f", 1, 3),
    ("W", 0, 4), ("D", 0, 5), ("Y", 0, 2), ("f", 2, 3), ("Z", 0, 3), ("B", 0, 2), ("b", 2, 3),
    ("W", 0, 5), ("B", 0, 3), ("Z", 0, 4), ("Z", 0, 5), ("Y", 0, 3),
)


def middle_kernel(dp, mp, chunks, *refs):
    (
        mixed_ref, x_ref, cot_ref, live_ref, gains_ref, wout_ref, gate_ref, up_ref,
        down_ref,
        output_ref, gm_ref, gbo_ref, local_ref, hidden_ref, pulled_ref, norm_ref, grady_ref,
        grad_gate_ref, grad_up_ref, gain_ref,
        w_up, w_down, cots, mids, gn2s, mid_mine, gn2_mine,
        parts1, rights1, lefts1, parts2, rights2, lefts2, parts3, rights3, lefts3,
        norm, hidden, pulled, gbo, gm, local, out,
        spread_sent, spread_came, fold_sent, fold_right, fold_left,
        square_sent, square_came, square_own, load_sem, store_sem,
        stage, free_sem, task_sent, task_came, left_sem, right_sem, stage_sem, slot_right,
        slot_left,
    ) = refs
    step, part = x_ref.shape[0] // chunks, x_ref.shape[1]
    features = part * mp
    hidden_width = w_down.shape[0]
    z, d = lax.axis_index("mp"), lax.axis_index("dp")
    square = dp == 8
    up_half = w_up.at[:, pl.ds(hidden_width, hidden_width)]
    own_cols = pl.ds(pl.multiple_of(z * part, part), part)

    folds = [
        Fold(z, mp, p, r, l, fold_sent.at[k], fold_right.at[k], fold_left.at[k])
        for k, (p, r, l) in enumerate(
            ((parts1, rights1, lefts1), (parts2, rights2, lefts2), (parts3, rights3, lefts3))
        )
    ]
    rs1, rs2, rs3 = folds
    ag2, ag3, ag4 = [
        Spread(z, mp, b, spread_sent.at[k], spread_came.at[k])
        for k, b in enumerate((cots, mids, gn2s))
    ]
    for fold in folds:
        fold.clear()

    barrier = pltpu.get_barrier_semaphore()

    @pl.when(z > 0)
    def _():
        pl.semaphore_signal(barrier, inc=1, device_id={"mp": z - 1}, device_id_type=MESH)

    @pl.when(z < mp - 1)
    def _():
        pl.semaphore_signal(barrier, inc=1, device_id={"mp": z + 1}, device_id_type=MESH)

    count = jnp.where((z > 0) & (z < mp - 1), 2, 1)
    if square:
        for other in partners(d)[1:]:
            pl.semaphore_signal(barrier, inc=1, device_id={"dp": other}, device_id_type=MESH)
        count = count + 3
    pl.semaphore_wait(barrier, count)

    if square:
        squares = [
            Square(
                d, shard, whole, square_sent.at[k], square_came.at[k], square_own.at[k], k
            )
            for k, (shard, whole) in enumerate(((up_ref, up_half), (down_ref, w_down)))
        ]
        for item in squares:
            item.start()
    else:
        loads = [
            pltpu.make_async_copy(up_ref, up_half, square_own.at[0]),
            pltpu.make_async_copy(down_ref, w_down, square_own.at[1]),
        ]
        for item in loads:
            item.start()
    load_gate = pltpu.make_async_copy(
        gate_ref, w_up.at[:, pl.ds(0, hidden_width)], square_own.at[2]
    )
    load_gate.start()

    def chunk_rows(c):
        return pl.ds(c * step, step)

    def store(buffer, target, c, k):
        return pltpu.make_async_copy(buffer, target.at[chunk_rows(c), :], store_sem.at[k])

    def own_cot(c):
        return pltpu.make_async_copy(cot_ref.at[chunk_rows(c), :], cots.at[c, z], load_sem.at[c])

    for c in range(chunks):
        own_cot(c).start()

    gain_ref[...] = jnp.zeros_like(gain_ref)
    tiles = step // TILE

    def fill(fold, slot, left, weights, columns=True):
        def body(j):
            near = pl.ds(pl.multiple_of(j * part, part), part)
            if columns:
                value = matmul(left, weights[:, near])
            else:
                value = inner_cols(left, weights[near, :])
            fold.parts[slot, j] = value.astype(BF16)

        tile_loop(mp, body)

    def branch(c):
        if c > 1:
            rs1.drain(c % 2)
        fill(rs1, c % 2, mixed_ref[chunk_rows(c), :], wout_ref)
        rs1.start(c % 2)

    def join(c):
        rs1.finish(c % 2)

        def body(t):
            rows = rows_at(t, TILE)
            base = pl.ds(pl.multiple_of(c * step + t * TILE, TILE), TILE)
            total = x_ref[base, :].astype(F32) + rs1.total(c % 2, rows)
            mid_mine[c, rows, :] = total
            mids[c, z, rows, :] = total.astype(BF16)

        tile_loop(tiles, body)

    def stats(c, rows):
        blocks = [mids[c, j, rows, :].astype(F32) for j in range(mp)]
        square_sum = sum(jnp.sum(b * b, axis=1, keepdims=True) for b in blocks)
        return blocks, lax.rsqrt(square_sum / features + EPS)

    def block_cols(j):
        return slice(j * part, (j + 1) * part)

    def normalise(c):
        def body(t):
            rows = rows_at(t, TILE)
            base = pl.ds(pl.multiple_of(c * step + t * TILE, TILE), TILE)
            blocks, s2 = stats(c, rows)
            live = live_ref[base, :][:, TAPS : TAPS + 1]
            for j in range(mp):
                norm[rows, block_cols(j)] = (
                    blocks[j] * s2 * gains_ref[1:2, block_cols(j)]
                ).astype(BF16)
                cots[c, j, rows, :] = (cots[c, j, rows, :].astype(F32) * live).astype(BF16)

        tile_loop(tiles, body)

    def grad_y_copies(c):
        return [
            pltpu.make_async_copy(
                cots.at[c, j], grady_ref.at[chunk_rows(c), pl.ds(j * part, part)],
                store_sem.at[8 + j],
            )
            for j in range(mp)
        ]

    def mlp_first(c):
        if c > 0:
            store(norm, norm_ref, c, 0).wait()
            store(hidden, hidden_ref, c, 1).wait()
            store(pulled, pulled_ref, c, 2).wait()
            for copy in grad_y_copies(c - 1):
                copy.wait()
        if c == 0:
            load_gate.wait()
            for item in squares if square else ():
                item.finish()
            for item in () if square else loads:
                item.wait()
        ag2.drain(c)
        normalise(c)
        store(norm, norm_ref, c, 0).start()
        for copy in grad_y_copies(c):
            copy.start()
        size = 256

        def body(t):
            near = pl.ds(pl.multiple_of(t * size, size), size)
            off = pl.ds(pl.multiple_of(hidden_width + t * size, size), size)
            gate = matmul(norm[...], w_up[:, near])
            up = matmul(norm[...], w_up[:, off])
            grad = sum(
                inner_cols(cots[c, j], w_down[near, block_cols(j)]) for j in range(mp)
            )
            value, slope = gelu_and_slope(gate)
            hidden[:, near] = (value * up).astype(BF16)
            pulled[:, near] = (grad * up * slope).astype(BF16)
            pulled[:, off] = (grad * value).astype(BF16)

        tile_loop(hidden_width // size, body)
        store(hidden, hidden_ref, c, 1).start()
        store(pulled, pulled_ref, c, 2).start()

    def mlp_second(c):
        slot = c % 2
        if c > 1:
            rs3.drain(slot)
        fill(rs3, slot, pulled[...], w_up, False)
        rs3.start(slot)
        if square and c == chunks - 1:
            for item in squares:
                item.drain()
            for k, other in enumerate(partners(d)[1:]):
                pl.semaphore_signal(
                    free_sem.at[k], inc=1, device_id={"dp": other}, device_id_type=MESH
                )

    def mlp_third(c):
        slot = c % 2
        if c > 1:
            rs2.drain(slot)
        fill(rs2, slot, hidden[...], w_down)
        if c > 1:

            @pl.when(z < mp - 1)
            def _():
                pl.semaphore_wait(slot_right.at[slot], 1)

            @pl.when(z > 0)
            def _():
                pl.semaphore_wait(slot_left.at[slot], 1)

        rs2.start(slot)

    def gather_grad(c):
        slot = c % 2
        rs3.finish(slot)

        def body(t):
            rows = rows_at(t, TILE)
            total = rs3.total(slot, rows)
            gn2_mine[slot, rows, :] = total
            gn2s[c, z, rows, :] = total.astype(BF16)

        tile_loop(tiles, body)
        ag4.step(c, 0)

    def norm_back(c):
        slot = c % 2
        ag4.finish(c)
        if c > 0:
            store(gbo, gbo_ref, c, 3).wait()
            store(local, local_ref, c, 4).wait()
            store(gm, gm_ref, c, 5).wait()

        def body(t):
            rows = rows_at(t, TILE)
            blocks, s2 = stats(c, rows)
            grads = [gn2s[c, j, rows, :].astype(F32) for j in range(mp)]
            scaled = [grads[j] * gains_ref[1:2, block_cols(j)] for j in range(mp)]
            mean = (
                sum(jnp.sum(scaled[j] * blocks[j], axis=1, keepdims=True) for j in range(mp))
                / features
            )
            fall = s2 * s2 * s2 * mean
            for j in range(mp):
                grad_y = cots[c, j, rows, :].astype(F32)
                gbo[rows, block_cols(j)] = (
                    grad_y + s2 * scaled[j] - blocks[j] * fall
                ).astype(BF16)
                gain_ref[:, block_cols(j)] += jnp.sum(
                    (grads[j] * (blocks[j] * s2)).reshape(-1, 8, part), axis=0
                )
            local[rows, :] = (
                cots[c, z, rows, :].astype(F32)
                + s2 * (gn2_mine[slot, rows, :] * gains_ref[1:2, own_cols])
                - mid_mine[c, rows, :] * fall
            )

        tile_loop(tiles, body)
        gm[...] = inner_cols(gbo[...], wout_ref[...])
        store(gbo, gbo_ref, c, 3).start()
        store(local, local_ref, c, 4).start()
        store(gm, gm_ref, c, 5).start()

    def make_output(c):
        rs2.finish(c % 2)
        if c > 0:
            store(out, output_ref, c, 6).wait()

        def body(t):
            rows = rows_at(t, TILE)
            out[rows, :] = (mid_mine[c, rows, :] + rs2.total(c % 2, rows)).astype(BF16)

        tile_loop(tiles, body)
        if c + 2 < chunks:
            slot = c % 2

            @pl.when(z > 0)
            def _():
                pl.semaphore_signal(
                    slot_right.at[slot], inc=1, device_id={"mp": z - 1}, device_id_type=MESH
                )

            @pl.when(z < mp - 1)
            def _():
                pl.semaphore_signal(
                    slot_left.at[slot], inc=1, device_id={"mp": z + 1}, device_id_type=MESH
                )

        store(out, output_ref, c, 6).start()

    own = features // 8
    count_tasks = 2 * hidden_width // part
    scatters, sending = [], [None] * 4
    buffers = [rights1.at[i // 2, i % 2] for i in range(4)]
    staged = [None]

    def left_block(i):
        return (cots if i < 2 else mids).at[i % 2]

    def left_copies():
        return [
            pltpu.make_async_copy(
                norm_ref.at[chunk_rows(i), pl.ds(j * part, part)], left_block(i).at[j],
                left_sem.at[i, j],
            )
            for i in range(chunks)
            for j in range(mp)
        ]

    def right_copies(k):
        return [
            pltpu.make_async_copy(
                pulled_ref.at[chunk_rows(i), pl.ds(k * part, part)], parts1.at[k % 2, i],
                right_sem.at[k % 2, i],
            )
            for i in range(chunks)
        ]

    def make_scatter(k):
        def compute(owner, target, add):
            j = lax.div(owner, 2)
            near = pl.ds(pl.multiple_of(lax.rem(owner, 2) * own, own), own)
            value = sum(
                inner_rows(left_block(i)[j, :, near], parts1[k % 2, i]) for i in range(chunks)
            )
            if add:
                value = value + target[...].astype(F32)
            target[...] = value.astype(BF16)

        cols = pl.ds(k * part, part)

        def place(first):
            return w_up.at[pl.ds(first, own), cols]

        def held(i):
            return w_up.at[pl.ds(pl.multiple_of(i * own, own), own), cols]

        return Scatter(
            d, own, compute, held, place(4 * own), place(5 * own), place(6 * own),
            task_sent.at[k], task_came.at[k],
        )

    def weight_first(k):
        if not square:
            return
        if k == 0:
            store(norm, norm_ref, chunks - 1, 0).wait()
            store(pulled, pulled_ref, chunks - 1, 2).wait()
            for slot in range(2):
                rs1.drain(slot)
            for c in range(2):
                ag3.drain(c)
            scatters.extend(make_scatter(i) for i in range(count_tasks))
            for copy in right_copies(0) + left_copies():
                copy.start()
            for i in range(3):
                pl.semaphore_wait(free_sem.at[i], 1)
        if k + 1 < count_tasks:
            for copy in right_copies(k + 1):
                copy.start()
        for copy in right_copies(k) + (left_copies() if k == 0 else []):
            copy.wait()
        scatters[k].far_core(buffers, sending)
        scatters[k].near_core()

    def weight_second(k):
        if square:
            scatters[k].onward()

    def weight_third(k):
        if not square:
            return
        if staged[0] is not None:
            staged[0].wait()
        scatters[k].finish(stage)
        half = count_tasks // 2
        target = grad_gate_ref if k < half else grad_up_ref
        staged[0] = pltpu.make_async_copy(
            stage, target.at[:, pl.ds((k % half) * part, part)], stage_sem
        )
        staged[0].start()

    steps = {
        "A": branch, "J": join, "H": mlp_first, "G": mlp_second, "O": mlp_third,
        "K": gather_grad, "B": norm_back, "Y": make_output, "D": weight_first,
        "W": weight_second, "Z": weight_third,
    }
    moves = {"a": (rs1, 2), "b": (rs2, 2), "c": (rs3, 2), "d": (ag2, 0), "e": (ag3, 0), "f": (ag4, 0)}
    for name, s, c in MIDDLE_ORDER:
        if name == "S":
            if square and s < 3:
                squares[s - 1].step_one()
            if square and s == 3:
                squares[0].step_two()
                squares[1].step_two()
        elif name in steps:
            steps[name](c)
        else:
            line, parity = moves[name]
            if s == mp - 1:
                line.finish(c)
                continue
            if name == "d" and s == 0:
                own_cot(c).wait()
            line.step(c % parity if parity else c, s)

    last = chunks - 1
    for k, (buffer, target) in enumerate(
        (
            (norm, norm_ref), (hidden, hidden_ref), (pulled, pulled_ref), (gbo, gbo_ref),
            (local, local_ref), (gm, gm_ref), (out, output_ref),
        )
    ):
        if not (square and k in (0, 2)):
            store(buffer, target, last, k).wait()
    for copy in grad_y_copies(last):
        copy.wait()
    for c in range(chunks):
        if c > 1 or not square:
            ag3.drain(c)
        ag4.drain(c)
    for slot in range(2):
        for fold in folds[1:] if square else folds:
            fold.drain(slot)
    if square:
        staged[0].wait()
        for copy in sending:
            copy.wait_send()
        for scatter in scatters:
            scatter.drain()


def middle(dp, mp, chunks, mixed, inputs, cotangent, live, gains, w_out, gate, up, down):
    count, part = inputs.shape
    width, hidden_width = mixed.shape[1], down.shape[0]
    step, features = count // chunks, part * mp

    def fold_buffers():
        return [
            pltpu.VMEM((2, mp, step, part), BF16),
            pltpu.VMEM((2, mp - 1, step, part), BF16),
            pltpu.VMEM((2, mp - 1, step, part), BF16),
        ]

    dma = pltpu.SemaphoreType.DMA
    any_, vmem = pl.BlockSpec(memory_space=pl.ANY), pl.BlockSpec(memory_space=pltpu.VMEM)
    return pl.pallas_call(
        functools.partial(middle_kernel, dp, mp, chunks),
        in_specs=[vmem, vmem, any_, vmem, vmem, vmem, any_, any_, any_],
        out_specs=[any_] * 10 + [vmem],
        out_shape=(
            jax.ShapeDtypeStruct((count, part), BF16),
            jax.ShapeDtypeStruct((count, width), F32),
            jax.ShapeDtypeStruct((count, features), BF16),
            jax.ShapeDtypeStruct((count, part), F32),
            jax.ShapeDtypeStruct((count, hidden_width), BF16),
            jax.ShapeDtypeStruct((count, 2 * hidden_width), BF16),
            jax.ShapeDtypeStruct((count, features), BF16),
            jax.ShapeDtypeStruct((count, features), BF16),
            jax.ShapeDtypeStruct((features // 8, hidden_width), F32),
            jax.ShapeDtypeStruct((features // 8, hidden_width), F32),
            jax.ShapeDtypeStruct((8, features), F32),
        ),
        scratch_shapes=[
            pltpu.VMEM((features, 2 * hidden_width), BF16),
            pltpu.VMEM((hidden_width, features), BF16),
            pltpu.VMEM((chunks, mp, step, part), BF16),
            pltpu.VMEM((chunks, mp, step, part), BF16),
            pltpu.VMEM((chunks, mp, step, part), BF16),
            pltpu.VMEM((chunks, step, part), F32),
            pltpu.VMEM((2, step, part), F32),
        ]
        + fold_buffers() + fold_buffers() + fold_buffers()
        + [
            pltpu.VMEM((step, features), BF16),
            pltpu.VMEM((step, hidden_width), BF16),
            pltpu.VMEM((step, 2 * hidden_width), BF16),
            pltpu.VMEM((step, features), BF16),
            pltpu.VMEM((step, width), F32),
            pltpu.VMEM((step, part), F32),
            pltpu.VMEM((step, part), BF16),
            dma((3, chunks, 2 * mp)),
            dma((3, chunks, mp)),
            dma((3, 2, mp)),
            dma((3, 2, mp)),
            dma((3, 2, mp)),
            dma((2, 8)),
            dma((2, 8)),
            dma((3,)),
            dma((chunks,)),
            dma((12,)),
            pltpu.VMEM((features // 8, part), F32),
            pltpu.SemaphoreType.REGULAR((3,)),
            dma((2 * hidden_width // part, 8)),
            dma((2 * hidden_width // part, 8)),
            dma((chunks, mp)),
            dma((2, chunks)),
            dma,
            pltpu.SemaphoreType.REGULAR((2,)),
            pltpu.SemaphoreType.REGULAR((2,)),
        ],
        compiler_params=pltpu.CompilerParams(
            collective_id=0, has_side_effects=True, vmem_limit_bytes=62 * 1024 * 1024
        ),
        name="middle",
    )(mixed, inputs, cotangent, live, gains, w_out, gate, up, down)


TAIL_ORDER = (
    ("R", 0, 3), ("R", 0, 2), ("D", 0, 0), ("R", 0, 1), ("D", 0, 1), ("a", 0, 3), ("l", 0, 2),
    ("W", 0, 0), ("s", 1, 3), ("s", 1, 2), ("R", 0, 0), ("W", 0, 1), ("s", 2, 3), ("D", 0, 2),
    ("s", 2, 2), ("m", 0, 0), ("l", 0, 3), ("s", 1, 1), ("a", 0, 2), ("g", 0, 0), ("W", 0, 2),
    ("m", 0, 1), ("a", 0, 1), ("a", 0, 0), ("D", 0, 3), ("s", 1, 0), ("D", 0, 4), ("s", 2, 1),
    ("m", 0, 2), ("D", 0, 5), ("D", 0, 6), ("I", 0, 3), ("W", 0, 3), ("s", 2, 0), ("Z", 0, 0),
    ("I", 0, 2), ("W", 0, 4), ("W", 0, 5), ("Z", 0, 1), ("I", 0, 1), ("m", 0, 3), ("W", 0, 6),
    ("Z", 0, 2), ("I", 0, 0), ("m", 0, 4), ("Z", 0, 3), ("Z", 0, 4), ("Z", 0, 5), ("m", 0, 5),
    ("Z", 0, 6),
)


def tail_kernel(mp, tasks, names, *refs):
    ref = dict(zip(names, refs))
    pull, w_in, params = ref["pull"], ref["w_in_here"], ref["params"]
    chunks, _, step, part = ref["parts"].shape
    count, features = chunks * step, part * mp
    own, width = features // 8, params.shape[1]
    z, d = lax.axis_index("mp"), lax.axis_index("dp")
    _, by_core, by_x, by_y = partners(d)
    fold = Fold(
        z, mp, ref["parts"], ref["rights"], ref["lefts"], ref["fold_sent"], ref["fold_right"],
        ref["fold_left"],
    )
    near = z + 1 - 2 * lax.rem(z, 2)
    apart = z + 2 - 4 * lax.div(z, 2)
    own_cols = pl.ds(pl.multiple_of(z * part, part), part)

    def chunk_rows(c):
        return pl.ds(c * step, step)

    def recurrence_copies(c):
        copies = [
            pltpu.make_async_copy(
                ref[name].at[chunk_rows(c), :], ref[name + "_here"], ref["chunk_sem"].at[k]
            )
            for k, name in enumerate(("gm", "both", "conv", "r", "i", "state"))
        ]
        if c > 0:
            rows = pl.ds(c * step - 8, 8)
            copies += [
                pltpu.make_async_copy(
                    ref["both"].at[rows, pl.ds(0, width)], ref["halo"], ref["chunk_sem"].at[6]
                ),
                pltpu.make_async_copy(
                    ref["state"].at[rows, :], ref["start"], ref["chunk_sem"].at[7]
                ),
            ]
        return copies

    def norm_copy(c):
        return pltpu.make_async_copy(
            ref["norm1"].at[chunk_rows(c), :], ref["norm_here"], ref["norm_sem"]
        )

    def left_copy(name):
        return pltpu.make_async_copy(ref[name], ref["lhs"], ref["left_sem"])

    def right_copy(name, first, columns, slot):
        return pltpu.make_async_copy(
            ref[name].at[:, pl.ds(first, columns)], ref["rhs"].at[slot, :, pl.ds(0, columns)],
            ref["right_sem"].at[slot],
        )

    def end_copies(c):
        return [
            pltpu.make_async_copy(
                ref[name].at[chunk_rows(c), :], ref[name + "_here"], ref["end_sem"].at[k]
            )
            for k, name in enumerate(("local", "x", "s1"))
        ]

    whole_copies = [
        pltpu.make_async_copy(ref[name], ref[name + "_here"], ref["whole_sem"].at[k])
        for k, name in enumerate(("dense", "w_in"))
    ]
    last = chunks - 1
    for copy in recurrence_copies(last) + whole_copies:
        copy.start()
    norm_copy(last).start()
    left_copy("grady").start()
    first_rights = [
        right_copy(t[2], t[3], t[4], k) for k, t in enumerate(tasks[:2])
    ]
    for copy in first_rights + end_copies(last):
        copy.start()

    fold.clear()
    barrier = pltpu.get_barrier_semaphore()

    @pl.when(z > 0)
    def _():
        pl.semaphore_signal(barrier, inc=1, device_id={"mp": z - 1}, device_id_type=MESH)

    @pl.when(z < mp - 1)
    def _():
        pl.semaphore_signal(barrier, inc=1, device_id={"mp": z + 1}, device_id_type=MESH)

    pl.semaphore_signal(barrier, inc=1, device_id={"mp": apart}, device_id_type=MESH)
    for other in (by_core, by_x, by_y):
        pl.semaphore_signal(barrier, inc=1, device_id={"dp": other}, device_id_type=MESH)

    for name in ("back", "after", "gain", "dense_sum", "params_sum"):
        ref[name][...] = jnp.zeros_like(ref[name])
    gain = ref["gain"]

    def recur(c):
        for copy in recurrence_copies(c):
            copy.wait()
        if c == 0:
            ref["halo"][...] = jnp.zeros_like(ref["halo"])
            ref["start"][...] = jnp.zeros_like(ref["start"])
        if c == last:
            whole_copies[0].wait()
        rnn_backward_kernel(
            ref["gm_here"], ref["both_here"], ref["halo"], ref["start"], ref["conv_here"],
            ref["r_here"], ref["i_here"], ref["state_here"],
            ref["mask"].at[pl.ds(c * step, step + 8), :], ref["dense_here"], params,
            ref["back"], ref["after"],
            pull.at[chunk_rows(c), :], ref["rates"], ref["dparams"], ref["back"], ref["after"],
            ref["dots"],
            ref["padded"], ref["before"], ref["dconv"], ref["sums"],
        )
        ref["params_sum"][...] += ref["dparams"][...]
        ref["dense_sum"][...] += inner_rows(ref["conv_here"][...].astype(BF16), ref["rates"][...])
        if c > 0:
            for copy in recurrence_copies(c - 1):
                copy.start()
        for q in range(step // 128):
            turned = jnp.transpose(ref["dots"][q * 128 : (q + 1) * 128, :])
            ref["dots_row"][c, :, q * 128 : (q + 1) * 128] = turned[0:8, :]
        if c == last:
            whole_copies[1].wait()
            pl.semaphore_wait(barrier, jnp.where((z > 0) & (z < mp - 1), 6, 5))
        dots_copy(c, 0).start()
        norm_copy(c).wait()

        def body(j):
            rows = pl.ds(pl.multiple_of(j * part, part), part)
            value = inner_cols(pull[chunk_rows(c), :], w_in[rows, :])
            fold.parts[c, j] = value.astype(BF16)
            gain[:, rows] += jnp.sum(
                (value * ref["norm_here"][:, rows].astype(F32)).reshape(-1, 8, part), axis=0
            )

        tile_loop(mp, body)
        fold.start(c)
        if c > 0:
            norm_copy(c - 1).start()

    def dots_copy(c, k):
        return pltpu.make_async_remote_copy(
            src_ref=ref["dots_row"].at[c], dst_ref=ref["dots_in"].at[c, k],
            send_sem=ref["dots_sent"].at[c, k], recv_sem=ref["dots_came"].at[c, k],
            device_id={"mp": near if k == 0 else apart}, device_id_type=MESH,
        )

    def dots_add(c, k):
        dots_copy(c, k).wait()
        ref["dots_row"][c] += ref["dots_in"][c, k]
        if k == 0:
            dots_copy(c, 1).start()

    def input_grad(c):
        dots_add(c, 1)
        for q in range(step // 128):
            row = ref["dots_row"][c, 0:1, q * 128 : (q + 1) * 128]
            ref["dots_col"][q * 128 : (q + 1) * 128, :] = jnp.transpose(
                jnp.broadcast_to(row, (128, 128))
            )
        fold.finish(c)
        for copy in end_copies(c):
            copy.wait()

        def body(t):
            rows = rows_at(t, TILE)
            base = pl.ds(pl.multiple_of(c * step + t * TILE, TILE), TILE)
            s1 = ref["s1_here"][rows, :][:, 0:1]
            dot = ref["dots_col"][rows, :][:, 0:1]
            grad = (
                ref["local_here"][rows, :]
                + s1 * (fold.total(c, rows) * ref["gains"][0:1, own_cols])
                - ref["x_here"][rows, :].astype(F32) * (s1 * s1 * dot * (1.0 / features))
            )
            ref["grad_x"][base, :] = grad.astype(BF16)

        tile_loop(step // TILE, body)
        if c > 0:
            for copy in end_copies(c - 1):
                copy.start()

    sends, store_sem = ref["sends"], ref["store_sem"]
    slots = {k: k % 2 for k, t in enumerate(tasks) if t[2] in ("hidden", "mixed")}

    def build(k):
        _, left, right, first, columns, _ = tasks[k]

        def compute(owner, target, add):
            if left is None:
                rows = pl.ds(pl.multiple_of(owner * 32, 32), 32)
                value = ref["gates"][rows, first : first + columns].astype(F32)
            else:
                near = pl.ds(pl.multiple_of(owner * own, own), own)
                if right == "pull":
                    operand = pull[:, first : first + columns]
                else:
                    operand = ref["rhs"][slots[k], :, 0:columns]
                value = inner_rows(ref["lhs"][:, near], operand)
            if add:
                value = value + target[...].astype(F32)
            target[...] = value.astype(BF16)

        return Scatter(
            d, 32 if left is None else own, compute, ref["held%d" % k].at.__getitem__,
            ref["far%d" % k], ref["first%d" % k], ref["second%d" % k], ref["task_sent"].at[k],
            ref["task_came"].at[k],
        )

    scatters = [build(k) for k in range(len(tasks))]
    sending = [None] * 4

    def far_core(k):
        height, columns = scatters[k].count, tasks[k][4]
        scatters[k].far_core(
            [sends.at[slot, pl.ds(0, height), pl.ds(0, columns)] for slot in range(4)], sending
        )

    stage, stage_wait = ref["stage"], [None, None]

    def finish(k):
        scatter = scatters[k]
        name, columns, column = tasks[k][0], tasks[k][4], tasks[k][5]
        slot = k % 2
        if stage_wait[slot] is not None:
            stage_wait[slot].wait()
        view = stage.at[slot, pl.ds(0, scatter.count), pl.ds(0, columns)]
        scatter.finish(view)
        target = ref["grad_" + name].at[:, pl.ds(column, columns)]
        copy = pltpu.make_async_copy(view, target, store_sem.at[slot])
        copy.start()
        stage_wait[slot] = copy

    small, small_in = ref["small"], ref["small_in"]
    targets = (
        {"dp": by_core}, {"dp": by_x}, {"dp": by_y}, {"mp": near}, {"mp": apart},
    )

    def small_copy(k):
        rows = pl.ds(0, 16 if k < 3 else 8)
        return pltpu.make_async_remote_copy(
            src_ref=small.at[rows, :], dst_ref=small_in.at[k, rows, :],
            send_sem=ref["small_sent"].at[k], recv_sem=ref["small_came"].at[k],
            device_id=targets[k], device_id_type=MESH,
        )

    def small_first():
        small[...] = jnp.zeros_like(small)
        small[0:1, :] = jnp.sum(gain[...], axis=0, keepdims=True) / ref["gains"][0:1, :]
        small[1:2, :] = jnp.sum(ref["gain2"][...], axis=0, keepdims=True) * (1.0 / mp)
        small[8:16, 0:width] = ref["params_sum"][...]
        small_copy(0).start()

    def small_next(k):
        rows = 16 if k < 3 else 8
        small_copy(k).wait()
        small[0:rows, :] += small_in[k, 0:rows, :]
        if k < 4:
            small_copy(k + 1).start()
        else:
            ref["grad_gains"][...] = small[0:2, :]
            ref["grad_params"][...] = small[8:16, 0:width]

    def gate_blocks():
        flat, gates = ref["flat"], ref["gates"]
        span = flat.shape[0] - 16
        rows = span // 8
        column = lax.broadcasted_iota(jnp.int32, (span, 2 * width), 1)
        column = jnp.where(column >= width, column - width, column)
        total = jnp.zeros((span, 2 * width), F32)
        for b in range(width // span):
            inside = (column >= b * span) & (column < (b + 1) * span)
            total = total + jnp.where(
                inside, ref["dense_sum"][b * span : (b + 1) * span, :], 0.0
            )
        flat[0:span, :] = total
        flat[span:, :] = jnp.zeros((16, 2 * width), F32)
        for k in range(8):
            gates[k * 32 : (k + 1) * 32, :] = flat[k * rows : k * rows + 32, :].astype(BF16)

    out_right = right_copy("mixed", 0, tasks[2][4], 0)

    def load_next(k):
        left_copy("gbo" if k == 2 else "norm1").start()
        if k == 2:
            out_right.start()

    def weight(k):
        if k == 0:
            for copy in first_rights:
                copy.wait()
            left_copy("grady").wait()
        if k == 2:
            out_right.wait()
        if k in (2, 3):
            left_copy("norm1").wait()
        far_core(k)
        scatters[k].near_core()

    steps = {
        "R": recur, "I": input_grad, "D": weight, "W": lambda k: scatters[k].onward(),
        "Z": finish, "l": load_next, "g": lambda k: gate_blocks(), "a": lambda c: dots_add(c, 0),
        "m": lambda k: small_next(k - 1) if k else small_first(),
    }
    for name, s, c in TAIL_ORDER:
        if name == "s":
            fold.step(c, s)
        else:
            steps[name](c)
    for copy in stage_wait:
        copy.wait()
    for copy in sending:
        copy.wait_send()
    for scatter in scatters:
        scatter.drain()
    for c in range(chunks):
        fold.drain(c)


def tail(mp, chunks, span, rnn, mask, params, dense, w_in, norm1, grady, hidden, gbo, mixed, s1, x,
         local, gains, gain2):
    gm, both, conv, r, i, state = rnn
    count, part = x.shape
    features, width = part * mp, params.shape[1]
    own, step = features // 8, count // chunks
    widths = {
        "down": hidden.shape[1], "out": width, "in": 2 * width, "block": 2 * width,
    }
    heights = {name: 32 if name == "block" else own for name in widths}
    operands = {
        "down": ("grady", "hidden"), "out": ("gbo", "mixed"), "in": ("norm1", "pull"),
        "block": (None, "gates"),
    }
    tasks = []
    for name, columns in widths.items():
        left, right = operands[name]
        pieces = 1 if name == "out" else 2
        size = columns // pieces
        for piece in range(pieces):
            tasks.append((name, left, right, piece * size, size, piece * size))
    widest = max(t[4] for t in tasks)
    dma = pltpu.SemaphoreType.DMA
    any_, vmem = pl.BlockSpec(memory_space=pl.ANY), pl.BlockSpec(memory_space=pltpu.VMEM)
    ins = [
        ("gm", gm, any_), ("both", both, any_), ("conv", conv, any_), ("r", r, any_),
        ("i", i, any_), ("state", state, any_), ("mask", mask, vmem), ("params", params, vmem),
        ("dense", dense, any_), ("w_in", w_in, any_), ("norm1", norm1, any_),
        ("grady", grady, any_), ("hidden", hidden, any_), ("gbo", gbo, any_),
        ("mixed", mixed, any_), ("s1", s1, any_), ("x", x, any_), ("local", local, any_),
        ("gains", gains, vmem), ("gain2", gain2, vmem),
    ]
    shape = jax.ShapeDtypeStruct
    outs = [("grad_x", shape((count, part), BF16), vmem)]
    for name, columns in widths.items():
        outs.append(("grad_" + name, shape((heights[name], columns), F32), any_))
    outs.append(("grad_gains", shape((2, features), F32), vmem))
    outs.append(("grad_params", shape((8, width), F32), vmem))
    wide = pltpu.VMEM((step, width), F32)
    tall = pltpu.VMEM((step + 8, width), F32)
    eight = pltpu.VMEM((8, width), F32)
    scratch = [
        ("gm_here", wide), ("both_here", pltpu.VMEM((step, 2 * width), F32)),
        ("conv_here", wide), ("r_here", wide), ("i_here", wide), ("state_here", wide),
        ("halo", eight), ("start", eight), ("back", eight), ("after", eight),
        ("dparams", eight), ("params_sum", eight),
        ("dense_here", pltpu.VMEM(dense.shape, BF16)), ("w_in_here", pltpu.VMEM(w_in.shape, BF16)),
        ("pull", pltpu.VMEM((count, 2 * width), BF16)),
        ("rates", pltpu.VMEM((step, 2 * width), BF16)),
        ("dots", pltpu.VMEM((step, 128), F32)),
        ("padded", tall), ("before", tall), ("dconv", tall), ("sums", pltpu.VMEM((8, 8, width), F32)),
        ("dense_sum", pltpu.VMEM((width, 2 * width), F32)),
        ("flat", pltpu.VMEM((span + 16, 2 * width), F32)),
        ("gates", pltpu.VMEM((256, 2 * width), BF16)),
        ("norm_here", pltpu.VMEM((step, features), BF16)),
        ("lhs", pltpu.VMEM((count, features), BF16)),
        ("rhs", pltpu.VMEM((2, count, widest), BF16)),
        ("local_here", pltpu.VMEM((step, part), F32)), ("x_here", pltpu.VMEM((step, part), BF16)),
        ("s1_here", pltpu.VMEM((step, 128), F32)),
        ("parts", pltpu.VMEM((chunks, mp, step, part), BF16)),
        ("rights", pltpu.VMEM((chunks, mp - 1, step, part), BF16)),
        ("lefts", pltpu.VMEM((chunks, mp - 1, step, part), BF16)),
        ("sends", pltpu.VMEM((4, own, widest), BF16)),
        ("stage", pltpu.VMEM((2, own, widest), F32)),
        ("gain", pltpu.VMEM((8, features), F32)),
        ("dots_row", pltpu.VMEM((chunks, 8, step), F32)),
        ("dots_in", pltpu.VMEM((chunks, 2, 8, step), F32)),
        ("dots_col", pltpu.VMEM((step, 128), F32)),
        ("small", pltpu.VMEM((16, features), F32)),
        ("small_in", pltpu.VMEM((5, 16, features), F32)),
        ("chunk_sem", dma((8,))), ("norm_sem", dma), ("left_sem", dma), ("right_sem", dma((2,))),
        ("end_sem", dma((3,))), ("whole_sem", dma((2,))), ("store_sem", dma((2,))),
        ("fold_sent", dma((chunks, mp))), ("fold_right", dma((chunks, mp))),
        ("fold_left", dma((chunks, mp))),
        ("task_sent", dma((len(tasks), 8))), ("task_came", dma((len(tasks), 8))),
        ("dots_sent", dma((chunks, 2))), ("dots_came", dma((chunks, 2))),
        ("small_sent", dma((5,))), ("small_came", dma((5,))),
    ]
    for k, (name, _, _, _, size, _) in enumerate(tasks):
        rows = heights[name]
        scratch.append(("held%d" % k, pltpu.VMEM((4, rows, size), BF16)))
        for kind in ("far", "first", "second"):
            scratch.append(("%s%d" % (kind, k), pltpu.VMEM((rows, size), BF16)))
    names = [i[0] for i in ins] + [o[0] for o in outs] + [k[0] for k in scratch]
    return pl.pallas_call(
        functools.partial(tail_kernel, mp, tuple(tasks), tuple(names)),
        in_specs=[i[2] for i in ins],
        out_specs=[o[2] for o in outs],
        out_shape=[o[1] for o in outs],
        scratch_shapes=[k[1] for k in scratch],
        compiler_params=pltpu.CompilerParams(
            collective_id=1, has_side_effects=True, vmem_limit_bytes=63 * 1024 * 1024
        ),
        name="tail",
    )(*[i[1] for i in ins])


def make_masks(row_lengths, count):
    ends = jnp.cumsum(row_lengths)
    places = jnp.arange(-TAPS, count, dtype=jnp.int32)
    segment = jnp.sum((places[:, None] >= ends[None, :]).astype(jnp.int32), axis=1)
    segment = jnp.where(places < 0, -1, segment)
    now = segment[TAPS:]
    same = [(segment[TAPS - k : TAPS - k + count] == now).astype(F32) for k in range(1, TAPS)]
    blank = jnp.zeros((count,), F32)
    live = (now < row_lengths.shape[0]).astype(F32)
    columns = [same[0]] + same + [live] + [blank] * (LANES - TAPS - 1)
    return jnp.stack(columns, axis=1)


def dense_gates(gates, width):
    span = gates.shape[0]
    tiled = jnp.tile(gates, (width // span, 1))
    row = lax.broadcasted_iota(jnp.int32, tiled.shape, 0) // span
    column = (lax.broadcasted_iota(jnp.int32, tiled.shape, 1) % width) // span
    return jnp.where(row == column, tiled, jnp.zeros((), tiled.dtype))


def diagonal_blocks(dense, span):
    width = dense.shape[0]
    column = (lax.broadcasted_iota(jnp.int32, (1, 2 * width), 1) % width) // span
    total = jnp.zeros((span, 2 * width), F32)
    for b in range(width // span):
        total = total + jnp.where(column == b, dense[b * span : (b + 1) * span], 0.0)
    return total


def per_device(
    dp, mp,
    inputs, lengths, cotangent, gains, rnn_params, rnn_in, branch_gate, recur_gate, input_gate,
    mlp_gate, mlp_up, rnn_out, mlp_down,
):
    count, part = inputs.shape
    width = rnn_in.shape[1]
    hidden_width = mlp_gate.shape[1]
    span = recur_gate.shape[0] * dp
    features = part * mp
    step = count // CHUNKS
    spot = lax.axis_index("mp") * part

    def cut(values):
        return [values[c * step : (c + 1) * step] for c in range(CHUNKS)]

    def mine(values):
        return lax.dynamic_slice_in_dim(values, spot, part, values.ndim - 1)

    gates_shard = jnp.concatenate([recur_gate, input_gate], axis=1)
    if dp == 8:
        gates_shard = jnp.pad(gates_shard, ((0, 32 - span // 8), (0, 0)))
    else:
        rnn_in, branch_gate, mlp_gate, mlp_up = [
            square_gather(w, "dp", dp) for w in (rnn_in, branch_gate, mlp_gate, mlp_up)
        ]
        rnn_out, mlp_down = [square_gather(w.T, "dp", dp).T for w in (rnn_out, mlp_down)]
        gates_shard = pair_gather(gates_shard, "dp", dp).reshape(8, span // 8, 2 * width)
        gates_shard = jnp.pad(gates_shard, ((0, 0), (0, 32 - span // 8), (0, 0)))
        gates_shard = gates_shard.reshape(256, 2 * width)

    mask = make_masks(lengths[0], count)
    mask_tail = jnp.concatenate([mask, jnp.zeros((8, LANES), F32)], axis=0)
    tail_masks = [mask_tail[c * step : (c + 1) * step + 8] for c in range(CHUNKS)]
    w_in, w_out, w_gate, dense, normed, both, conv, r, i, state, mixed, s1 = head(
        dp, mp, 4, inputs, gains, rnn_params, mask, rnn_in, branch_gate, rnn_out, mlp_gate,
        gates_shard, span,
    )
    (
        output, gm, gbo, local, hidden, pulled, normed2, grad_y, grad_gate, grad_up, gain2,
    ) = middle(
        dp, mp, 4, mixed, inputs, cotangent, mask, gains, w_out,
        w_gate, mlp_up, mlp_down,
    )
    if dp == 8:
        rows = span // dp
        input_grad, grad_down, grad_out, grad_in, grad_gates, grad_gains, grad_params = tail(
            mp, 4, span, (gm, both, conv, r, i, state), mask_tail, rnn_params, dense, w_in, normed,
            grad_y, hidden, gbo, mixed, s1, inputs, local, gains, gain2,
        )
        grad_gates = grad_gates[:rows]
    else:
        blank = jnp.zeros((8, width), F32)
        back, tail_rows = blank, blank
        pulls, rates, dots = [None] * CHUNKS, [None] * CHUNKS, [None] * CHUNKS
        params_total = 0.0
        gms, boths = cut(gm), cut(both)
        saves = list(zip(cut(conv), cut(r), cut(i), cut(state)))
        for c in reversed(range(CHUNKS)):
            low = c * step
            halo = blank if c == 0 else both[low - 8 : low, :width]
            start = blank if c == 0 else state[low - 8 : low]
            pull, rate, dparams, back, tail_rows, dot = rnn_backward(
                gms[c], boths[c], halo, start, saves[c], tail_masks[c], dense, rnn_params,
                back, tail_rows,
            )
            params_total = params_total + dparams
            pulls[c], rates[c], dots[c] = pull, rate, dot
        pull = jnp.concatenate(pulls)
        dots = jnp.concatenate(dots)
        grad_gates = diagonal_blocks(inner_rows(conv.astype(BF16), jnp.concatenate(rates)), span)

        parts = []
        gain1 = 0.0
        norms, s1 = cut(normed), s1[:, 0:1]
        for c in range(CHUNKS):
            gn1_part = inner_cols(pulls[c], w_in).astype(BF16)
            gain1 = gain1 + jnp.sum(gn1_part.astype(F32) * norms[c].astype(F32), axis=0)
            parts.append(line_scatter(gn1_part, "mp", mp))
        dot = line_sum(dots[:, 0].reshape(8, -1), "mp", mp).reshape(-1, 1)
        input_grad = (
            local + s1 * (jnp.concatenate(parts) * mine(gains[0]))
            - inputs.astype(F32) * (s1 * s1 * dot / features)
        ).astype(BF16)
        grad_both = square_scatter(inner_rows(normed2, pulled).astype(BF16), "dp", dp)
        grad_gate, grad_up = grad_both[:, :hidden_width], grad_both[:, hidden_width:]
        grad_down = square_scatter(inner_rows(grad_y, hidden).astype(BF16), "dp", dp)
        grad_out = square_scatter(inner_rows(gbo, mixed).astype(BF16), "dp", dp)
        grad_in = square_scatter(inner_rows(normed, pull).astype(BF16), "dp", dp)
        grad_gates = pair_scatter(grad_gates, "dp", dp)
        grad_params = line_sum(params_total, "dp", dp)
        gain2 = jnp.sum(gain2, axis=0, keepdims=True)
        both_gains = jnp.concatenate([(gain1 / gains[0])[None], gain2])
        both_gains = line_sum(both_gains, "dp", dp)
        grad_gains = jnp.concatenate([line_sum(both_gains[:1], "mp", mp), both_gains[1:]])
    return (
        output,
        input_grad,
        grad_gains,
        grad_params,
        grad_in[:, :width],
        grad_in[:, width:],
        grad_gates[:, :width],
        grad_gates[:, width:],
        grad_gate,
        grad_up,
        grad_out.T,
        grad_down.T,
    )


def solution(mesh):
    return jax.shard_map(
        functools.partial(per_device, mesh.shape["dp"], mesh.shape["mp"]),
        mesh=mesh,
        in_specs=(
            P("dp", "mp"),
            P("dp", None),
            P("dp", "mp"),
            P(),
            P(None, "mp"),
            P("dp", "mp"),
            P("dp", "mp"),
            P("dp", "mp"),
            P("dp", "mp"),
            P("dp", "mp"),
            P("dp", "mp"),
            P("mp", "dp"),
            P("mp", "dp"),
        ),
        out_specs=(
            P("dp", "mp"),
            P("dp", "mp"),
            P(),
            P(None, "mp"),
            P("dp", "mp"),
            P("dp", "mp"),
            P("dp", "mp"),
            P("dp", "mp"),
            P("dp", "mp"),
            P("dp", "mp"),
            P("mp", "dp"),
            P("mp", "dp"),
        ),
        check_vma=False,
    )
```
